32 devices in a mesh: dp: 4 (over y, x), gx: 2 (over core), gy: 4 (over z).
Axes of the slice: x: 2, y: 2, z: 4, core: 2. Of those that a mesh axis runs over, the one named last changes fastest.
Arguments:
- tokens: bfloat16 [18464, 1024], P(('dp', 'gy'), 'gx'), may hold values from -6 to 6
- segment_ids: int32 [16, 1154], P(('dp', 'gx')), may hold values from 0 to 1, as said below
- norm1_gain: bfloat16 [1024], P('gx'), may hold values from 0.5 to 1.5
- norm1_shift: bfloat16 [1024], P('gx'), may hold values from -3 to 3
- qkv_weight: bfloat16 [1024, 3, 1024], P('gx', None, 'gy'), may hold values from -0.1875 to 0.1875
- qv_bias: bfloat16 [2, 1024], P(None, 'gy'), may hold values from -3 to 3
- out_weight: bfloat16 [1024, 1024], P('gy', 'gx'), may hold values from -4 to 4
- out_bias: bfloat16 [1024], P('gx'), may hold values from -3 to 3
- norm2_gain: bfloat16 [1024], P('gx'), may hold values from 0.5 to 1.5
- norm2_shift: bfloat16 [1024], P('gx'), may hold values from -3 to 3
- up_weight: bfloat16 [1024, 4096], P('gx', 'gy'), may hold values from -0.1875 to 0.1875
- up_bias: bfloat16 [4096], P('gy'), may hold values from -3 to 3
- down_weight: bfloat16 [4096, 1024], P('gy', 'gx'), may hold values from -0.09375 to 0.09375
- down_bias: bfloat16 [1024], P('gx'), may hold values from -3 to 3
- cotangent: bfloat16 [18464, 1024], P(('dp', 'gy'), 'gx'), may hold values from -6 to 6
Outputs:
- output: bfloat16 [18464, 1024], P(('dp', 'gy'), 'gx')
- input_grad: bfloat16 [18464, 1024], P(('dp', 'gy'), 'gx')
- norm1_gain_grad: float32 [1024], P('gx')
- norm1_shift_grad: float32 [1024], P('gx')
- qkv_weight_grad: float32 [2, 512, 3, 1024], P('gx', 'dp', None, 'gy')
- qv_bias_grad: float32 [2, 1024], P(None, 'gy')
- out_weight_grad: float32 [1024, 2, 512], P('gy', 'gx', 'dp')
- out_bias_grad: float32 [1024], P('gx')
- norm2_gain_grad: float32 [1024], P('gx')
- norm2_shift_grad: float32 [1024], P('gx')
- up_weight_grad: float32 [2, 512, 4096], P('gx', 'dp', 'gy')
- up_bias_grad: float32 [4096], P('gy')
- down_weight_grad: float32 [4, 1024, 1024], P('gy', 'dp', 'gx')
- down_bias_grad: float32 [1024], P('gx')
The draws below stay inside these ranges and needn't reach their ends.
Inputs may be any that keep to these rules, and one draw needn't show every extreme that they name: `segment_ids`: each row holds two images: ids 0 then 1, never falling; each image has from 289 to 865 positions, and some row's first image has exactly 865.
All inputs are finite; a program needn't handle non-finite values.
Results may differ from the reference program's by a relative error of at most 0.012.
The reference program's roundings to bfloat16 on the way count: a program that leaves them out, or rounds other values in their place, can miss the bound.
Values may be sent and summed in bfloat16 or wider, within the bound.
A program may use at most 256 MiB of HBM per device.

```python
import math
import jax
import jax.numpy as jnp
from jax import lax

D = 1024
HEADS = 16
HD = 64
FF = 4096
IMG = 577
SEQ = 1154
ROWS_ALL = 16
TOKENS = 18464
N_GX = 2
N_GY = 4


def draw_segment_ids(key, part):
    longest = 3 * IMG // 2
    shortest = SEQ - longest
    first_len = jax.random.randint(jax.random.fold_in(key, 11), (ROWS_ALL,), shortest, longest + 1)
    chosen = jax.random.randint(jax.random.fold_in(key, 12), (), 0, ROWS_ALL)
    row_index = jnp.arange(ROWS_ALL, dtype=jnp.int32)
    first_len = jnp.where(row_index == chosen, longest, first_len).astype(jnp.int32)
    positions = jnp.arange(SEQ, dtype=jnp.int32)
    return (positions[None, :] >= first_len[:, None]).astype(jnp.int32)


def steps_of(stream_key, dims, shards, smallest, largest):
    def one(dim, shards_of):
        heights = jax.random.uniform(jax.random.fold_in(jax.random.fold_in(stream_key, 6), dim), (shards_of,), jnp.float32, smallest / len(shards), largest / len(shards))
        return jnp.repeat(jnp.exp(heights), dims[dim] // shards_of).reshape((-1,) + (1,) * (len(dims) - dim - 1))

    loudness = one(*shards[0])
    for cut in shards[1:]:
        loudness = loudness * one(*cut)
    return loudness


def scatter_about(stream_key, extent, deviation, limit, pieces=(), kind=jnp.bfloat16):
    factor_of = steps_of(stream_key, extent, pieces, -0.22, 0.18) if pieces else 1.0
    drawn = jax.random.normal(stream_key, extent, jnp.float32) * deviation * factor_of
    return jnp.minimum(jnp.maximum(drawn, -limit), limit).astype(kind)


def setup_inputs(seed: int = 0) -> dict:
    splits = jax.random.split(jax.random.key(seed), 16)
    tokens = scatter_about(splits[0], (TOKENS, D), 1.0, 6.0, ((0, 16), (1, 2)))
    segment_ids = draw_segment_ids(jax.random.fold_in(splits[15], 71), 0)
    norm1_gain = jnp.clip(1.0 + 0.1 * jax.random.normal(splits[2], (D,), jnp.float32), 0.5, 1.5).astype(jnp.bfloat16)
    norm1_shift = scatter_about(splits[3], (D,), 0.3, 3.0, ((0, 2),))
    qkv_weight = scatter_about(splits[4], (D, 3, D), D ** -0.5, 0.1875, ((0, 2), (2, 4)))
    qv_bias = scatter_about(splits[5], (2, D), 0.3, 3.0, ((1, 4),))
    out_weight = scatter_about(splits[6], (D, D), 0.75, 4.0, ((0, 4), (1, 2)))
    out_bias = scatter_about(splits[7], (D,), 0.3, 3.0, ((0, 2),))
    norm2_gain = jnp.clip(1.0 + 0.1 * jax.random.normal(splits[8], (D,), jnp.float32), 0.5, 1.5).astype(jnp.bfloat16)
    norm2_shift = scatter_about(splits[9], (D,), 0.3, 3.0, ((0, 2),))
    up_weight = scatter_about(splits[10], (D, FF), D ** -0.5, 0.1875, ((0, 2), (1, 4)))
    up_bias = scatter_about(splits[11], (FF,), 0.3, 3.0, ((0, 4),))
    down_weight = scatter_about(splits[12], (FF, D), FF ** -0.5, 0.09375, ((0, 4), (1, 2)))
    down_bias = scatter_about(splits[13], (D,), 0.3, 3.0, ((0, 2),))
    cotangent = scatter_about(splits[14], (TOKENS, D), 1.0, 6.0, ((0, 16), (1, 2)))
    return {"tokens": tokens, "segment_ids": segment_ids, "norm1_gain": norm1_gain, "norm1_shift": norm1_shift, "qkv_weight": qkv_weight, "qv_bias": qv_bias, "out_weight": out_weight, "out_bias": out_bias, "norm2_gain": norm2_gain, "norm2_shift": norm2_shift, "up_weight": up_weight, "up_bias": up_bias, "down_weight": down_weight, "down_bias": down_bias, "cotangent": cotangent}


@jax.custom_vjp
def low(v):
    return lax.optimization_barrier(v.astype(jnp.bfloat16)).astype(jnp.float32)

@jax.custom_vjp
def low_back(v):
    return v

def low_keep(v):
    return (low(v), None)

def low_pass(kept, grad):
    return (grad,)

def back_keep(v):
    return (v, None)

def back_low(kept, grad):
    return (low(grad),)
low.defvjp(low_keep, low_pass)
low_back.defvjp(back_keep, back_low)
norm_eps = 1e-06
highest = lax.Precision.HIGHEST

def product(left, right):
    return jnp.dot(left, right, precision=highest, preferred_element_type=jnp.float32)

def normalize(values, gain, shift):
    mean_val = lax.optimization_barrier(jnp.mean(values, axis=-1, keepdims=True))
    square_mean = lax.optimization_barrier(jnp.mean(values * values, axis=-1, keepdims=True))
    return (values - mean_val) * lax.rsqrt(square_mean - mean_val * mean_val + norm_eps) * gain + shift

def attend_row(item):
    packed, segment = item
    query_part = packed[:, 0]
    key_part = packed[:, 1]
    value_part = packed[:, 2]
    scaling = 1.0 / math.sqrt(HD)
    scores = jnp.einsum('qhd,khd->hqk', query_part, key_part, precision=highest) * scaling
    scores = low_back(scores)
    same = segment[:, None] == segment[None, :]
    scores = jnp.where(same[None], scores, -1e+30)
    probs = low(jax.nn.softmax(scores, axis=-1))
    return jnp.einsum('hqk,khd->qhd', probs, value_part, precision=highest)

def layer(block, segment, norm1_gain, norm1_shift, qkv_weight, qv_bias, out_weight, out_bias, norm2_gain, norm2_shift, up_weight, up_bias, down_weight, down_bias):
    normed = low(normalize(block, norm1_gain, norm1_shift))
    qkv_all = product(normed, qkv_weight.reshape(D, 3 * D)).reshape(-1, 3, D)
    bias_full = jnp.stack([qv_bias[0], jnp.zeros_like(qv_bias[0]), qv_bias[1]])
    qkv_all = low(low_back(qkv_all + bias_full[None]))
    packed = qkv_all.reshape(-1, SEQ, 3, HEADS, HD)
    mixed = lax.map(jax.checkpoint(attend_row), (packed, segment)).reshape(-1, D)
    mixed = low(low_back(mixed))
    branch = low_back(product(mixed, out_weight) + out_bias)
    middle = block + branch
    normed_two = low(normalize(middle, norm2_gain, norm2_shift))
    hidden = low_back(product(normed_two, up_weight) + up_bias)
    active = low(jax.nn.gelu(hidden, approximate=False))
    branch_two = low_back(product(active, down_weight) + down_bias)
    return middle + branch_two

def reference(tokens, segment_ids, norm1_gain, norm1_shift, qkv_weight, qv_bias, out_weight, out_bias, norm2_gain, norm2_shift, up_weight, up_bias, down_weight, down_bias, cotangent):
    weights = tuple((item.astype(jnp.float32) for item in (norm1_gain, norm1_shift, qkv_weight, qv_bias, out_weight, out_bias, norm2_gain, norm2_shift, up_weight, up_bias, down_weight, down_bias)))
    blocks = tokens.astype(jnp.float32).reshape(ROWS_ALL // 2, 2 * SEQ, D)
    cot_blocks = cotangent.astype(jnp.float32).reshape(ROWS_ALL // 2, 2 * SEQ, D)
    seg_blocks = segment_ids.reshape(ROWS_ALL // 2, 2, SEQ)

    def advance(totals, item):
        block, cot_block, seg_block = item

        def apply(block_in, *params):
            return layer(block_in, seg_block, *params)
        result, pull = jax.vjp(apply, block, *weights)
        grads = pull(cot_block)
        totals = tuple((total + grad for total, grad in zip(totals, grads[1:])))
        return (totals, (result.astype(jnp.bfloat16), grads[0].astype(jnp.bfloat16)))
    start = tuple((jnp.zeros_like(item) for item in weights))
    totals, (results, input_grads) = lax.scan(advance, start, (blocks, cot_blocks, seg_blocks))
    return (results.reshape(TOKENS, D), input_grads.reshape(TOKENS, D), totals[0], totals[1], totals[2].reshape(N_GX, D // N_GX, 3, D), totals[3], totals[4].reshape(D, N_GX, D // N_GX), totals[5], totals[6], totals[7], totals[8].reshape(N_GX, D // N_GX, FF), totals[9], totals[10].reshape(N_GY, FF // N_GY, D), totals[11])
```

```python
import functools
import math

import jax
import jax.numpy as jnp
from jax import lax
from jax.experimental import pallas as pl
from jax.experimental.pallas import tpu as pltpu
from jax.sharding import PartitionSpec as P

D = 1024
HD = 64
MESH = pl.DeviceIdType.MESH
F32 = jnp.float32
BF = jnp.bfloat16
ANY = pl.BlockSpec(memory_space=pl.ANY)
SMEM = pl.BlockSpec(memory_space=pltpu.SMEM)
VMEM = pl.BlockSpec(memory_space=pltpu.VMEM)
norm_eps = 1e-06


def times_right(left, right):
    return jnp.dot(left, right, preferred_element_type=jnp.float32)


def times_back(left, right):
    return lax.dot_general(
        left, right, (((1,), (1,)), ((), ())), preferred_element_type=jnp.float32
    )


def times_outer(left, right):
    return lax.dot_general(
        left, right, (((0,), (0,)), ((), ())), preferred_element_type=jnp.float32
    )


def exact_gelu(values):
    return jax.nn.gelu(values, approximate=False)


def norm_forward(values, gain, shift):
    moments = lax.psum((jnp.sum(values, axis=1), jnp.sum(values * values, axis=1)), "gx")
    mean_val = moments[0] / D
    inverse = lax.rsqrt(moments[1] / D - mean_val * mean_val + norm_eps)
    hat_vals = (values - mean_val[:, None]) * inverse[:, None]
    return (hat_vals * gain + shift, hat_vals, inverse)


def norm_backward(grad_norm, hat_vals, inverse, gain):
    scaled = grad_norm * gain
    moments = lax.psum((jnp.sum(scaled, axis=1), jnp.sum(scaled * hat_vals, axis=1)), "gx")
    grad_in = inverse[:, None] * (
        scaled - (moments[0] / D)[:, None] - hat_vals * (moments[1] / D)[:, None]
    )
    return (grad_in, jnp.sum(grad_norm * hat_vals, axis=0), jnp.sum(grad_norm, axis=0))


def gather_gy(values):
    return lax.all_gather(values, "gy", axis=0, tiled=True)


def gather_gx(values):
    return lax.all_gather(values, "gx", axis=0, tiled=True)


def sum_over_gx(left, multiply):
    keep_rows = left.shape[0] // lax.axis_size("gx")

    def term(start, count):
        return multiply(left)

    return lax.psum_scatter(
        term(jnp.int32(0), keep_rows * lax.axis_size("gx")), "gx", scatter_dimension=0, tiled=True
    )


def sum_over_gy(left, multiply):
    keep_rows = left.shape[0] // lax.axis_size("gy")

    def term(start, count):
        return multiply(left)

    return lax.psum_scatter(
        term(jnp.int32(0), keep_rows * lax.axis_size("gy")), "gy", scatter_dimension=0, tiled=True
    )


def masked_scores(query_part, key_part, segment):
    scaling = 1.0 / math.sqrt(query_part.shape[-1])
    scores = (
        jnp.einsum("qhd,khd->hqk", query_part, key_part, preferred_element_type=jnp.float32)
        * scaling
    )
    same = segment[:, None] == segment[None, :]
    return jnp.where(same[None], scores, -1e30)


def attend_forward(item):
    packed, segment = item
    scores = masked_scores(packed[:, 0], packed[:, 1], segment)
    top_val = jnp.max(scores, axis=-1, keepdims=True)
    expo = jnp.exp(scores - top_val)
    total = jnp.sum(expo, axis=-1, keepdims=True)
    probs = (expo / total).astype(jnp.bfloat16)
    mixed = jnp.einsum("hqk,khd->qhd", probs, packed[:, 2], preferred_element_type=jnp.float32)
    return (mixed.astype(jnp.bfloat16), (top_val + jnp.log(total))[..., 0])


def attend_backward(item):
    packed, segment, log_sum, grad_out = item
    query_part = packed[:, 0]
    key_part = packed[:, 1]
    value_part = packed[:, 2]
    scaling = 1.0 / math.sqrt(query_part.shape[-1])
    scores = masked_scores(query_part, key_part, segment)
    probs = jnp.exp(scores - log_sum[..., None])
    probs_low = probs.astype(jnp.bfloat16)
    grad_prob = jnp.einsum("qhd,khd->hqk", grad_out, value_part, preferred_element_type=jnp.float32)
    grad_value = jnp.einsum("hqk,qhd->khd", probs_low, grad_out, preferred_element_type=jnp.float32)
    delta = jnp.sum(probs * grad_prob, axis=-1, keepdims=True)
    grad_score = (probs * (grad_prob - delta)).astype(jnp.bfloat16)
    grad_query = (
        jnp.einsum("hqk,khd->qhd", grad_score, key_part, preferred_element_type=jnp.float32)
        * scaling
    )
    grad_key = (
        jnp.einsum("hqk,qhd->khd", grad_score, query_part, preferred_element_type=jnp.float32)
        * scaling
    )
    return jnp.stack([grad_query, grad_key, grad_value], axis=1).astype(jnp.bfloat16)


def local(
    tokens,
    segment_ids,
    norm1_gain,
    norm1_shift,
    qkv_weight,
    qv_bias,
    out_weight,
    out_bias,
    norm2_gain,
    norm2_shift,
    up_weight,
    up_bias,
    down_weight,
    down_bias,
    cotangent,
):
    head_width = qkv_weight.shape[2]
    local_heads = head_width // HD
    seq_len = segment_ids.shape[1]
    qkv_flat = qkv_weight.reshape(qkv_weight.shape[0], 3 * head_width)
    gain_one = norm1_gain.astype(jnp.float32)
    gain_two = norm2_gain.astype(jnp.float32)
    resid = tokens.astype(jnp.float32)
    normed, hat_one, inv_one = norm_forward(resid, gain_one, norm1_shift.astype(jnp.float32))
    first_low = normed.astype(jnp.bfloat16)
    first_rows = gather_gy(first_low)
    qkv_all = sum_over_gx(first_rows, lambda piece: times_right(piece, qkv_flat))
    bias_full = jnp.stack([qv_bias[0], jnp.zeros_like(qv_bias[0]), qv_bias[1]]).astype(jnp.float32)
    qkv_low = (qkv_all.reshape(-1, 3, head_width) + bias_full[None]).astype(jnp.bfloat16)
    packed = qkv_low.reshape(-1, seq_len, 3, local_heads, HD)
    mixed, log_sums = lax.map(attend_forward, (packed, segment_ids))
    mixed_low = mixed.reshape(-1, head_width)
    mixed_rows = gather_gx(mixed_low)
    branch = sum_over_gy(
        mixed_rows, lambda piece: times_right(piece, out_weight)
    ) + out_bias.astype(jnp.float32)
    middle = resid + branch
    normed_two, hat_two, inv_two = norm_forward(middle, gain_two, norm2_shift.astype(jnp.float32))
    second_low = normed_two.astype(jnp.bfloat16)
    second_rows = gather_gy(second_low)
    hidden = sum_over_gx(second_rows, lambda piece: times_right(piece, up_weight)) + up_bias.astype(
        jnp.float32
    )
    active, gelu_pull = jax.vjp(exact_gelu, hidden)
    active_low = active.astype(jnp.bfloat16)
    active_rows = gather_gx(active_low)
    branch_two = sum_over_gy(
        active_rows, lambda piece: times_right(piece, down_weight)
    ) + down_bias.astype(jnp.float32)
    output = (middle + branch_two).astype(jnp.bfloat16)
    grad_top = cotangent.astype(jnp.float32)
    down_bias_grad = jnp.sum(grad_top, axis=0)
    grad_top_rows = gather_gy(cotangent)
    down_weight_grad = times_outer(active_rows, grad_top_rows)
    grad_active = sum_over_gx(grad_top_rows, lambda piece: times_back(piece, down_weight))
    grad_hidden = gelu_pull(grad_active)[0].astype(jnp.bfloat16)
    up_bias_grad = jnp.sum(grad_hidden.astype(jnp.float32), axis=0)
    hidden_rows = gather_gx(grad_hidden)
    up_weight_grad = times_outer(second_rows, hidden_rows)
    grad_norm_two = sum_over_gy(hidden_rows, lambda piece: times_back(piece, up_weight))
    grad_in_two, norm2_gain_grad, norm2_shift_grad = norm_backward(
        grad_norm_two, hat_two, inv_two, gain_two
    )
    grad_middle = grad_top + grad_in_two
    grad_branch = grad_middle.astype(jnp.bfloat16)
    out_bias_grad = jnp.sum(grad_branch.astype(jnp.float32), axis=0)
    branch_rows = gather_gy(grad_branch)
    out_weight_grad = times_outer(mixed_rows, branch_rows)
    grad_mixed = sum_over_gx(branch_rows, lambda piece: times_back(piece, out_weight)).astype(
        jnp.bfloat16
    )
    grad_mixed = grad_mixed.reshape(-1, seq_len, local_heads, HD)
    grad_packed = lax.map(attend_backward, (packed, segment_ids, log_sums, grad_mixed))
    grad_qkv = grad_packed.reshape(-1, 3 * head_width)
    third_sums = jnp.sum(grad_qkv.astype(jnp.float32), axis=0).reshape(3, head_width)
    qv_bias_grad = jnp.stack([third_sums[0], third_sums[2]])
    qkv_rows = gather_gx(grad_qkv)
    qkv_weight_grad = times_outer(first_rows, qkv_rows).reshape(qkv_weight.shape)
    grad_norm_one = sum_over_gy(qkv_rows, lambda piece: times_back(piece, qkv_flat))
    grad_in_one, norm1_gain_grad, norm1_shift_grad = norm_backward(
        grad_norm_one, hat_one, inv_one, gain_one
    )
    input_grad = (grad_middle + grad_in_one).astype(jnp.bfloat16)
    qkv_weight_grad, out_weight_grad, up_weight_grad, down_weight_grad = (
        lax.psum_scatter(qkv_weight_grad, "dp", scatter_dimension=0, tiled=True),
        lax.psum_scatter(out_weight_grad, "dp", scatter_dimension=1, tiled=True),
        lax.psum_scatter(up_weight_grad, "dp", scatter_dimension=0, tiled=True),
        lax.psum_scatter(down_weight_grad, "dp", scatter_dimension=0, tiled=True),
    )
    qkv_weight_grad = qkv_weight_grad[None]
    out_weight_grad = out_weight_grad[:, None, :]
    up_weight_grad = up_weight_grad[None]
    down_weight_grad = down_weight_grad[None]
    (
        norm1_gain_grad,
        norm1_shift_grad,
        norm2_gain_grad,
        norm2_shift_grad,
        out_bias_grad,
        down_bias_grad,
    ) = lax.psum(
        (
            norm1_gain_grad,
            norm1_shift_grad,
            norm2_gain_grad,
            norm2_shift_grad,
            out_bias_grad,
            down_bias_grad,
        ),
        ("dp", "gy"),
    )
    up_bias_grad, qv_bias_grad = lax.psum((up_bias_grad, qv_bias_grad), ("dp", "gx"))
    return (
        output,
        input_grad,
        norm1_gain_grad,
        norm1_shift_grad,
        qkv_weight_grad,
        qv_bias_grad,
        out_weight_grad,
        out_bias_grad,
        norm2_gain_grad,
        norm2_shift_grad,
        up_weight_grad,
        up_bias_grad,
        down_weight_grad,
        down_bias_grad,
    )


def flip1(i):
    return i + 1 - 2 * lax.rem(i, 2)


def flip2(i):
    return i + 2 - 4 * lax.div(i, 2)


def place():
    dp, c, z = lax.axis_index("dp"), lax.axis_index("gx"), lax.axis_index("gy")
    dps = (dp, flip1(dp), flip2(dp), 3 - dp)
    zs = (z, flip1(z), flip2(z), 3 - z)
    x_dev = (dps[1], c, z)
    y_dev = (dps[2], c, z)
    c_dev = (dp, 1 - c, z)
    z_devs = (None,) + tuple((dp, c, zz) for zz in zs[1:])
    return dps, zs, x_dev, y_dev, c_dev, z_devs


def greet(devices):
    barrier = pltpu.get_barrier_semaphore()
    for device in devices:
        pl.semaphore_signal(barrier, inc=1, device_id=device, device_id_type=MESH)
    pl.semaphore_wait(barrier, len(devices))


def gather_kernel(
    x_own, g_own, vec_own, bias_own,
    q_mine, q_theirs, o_mine, o_theirs, u_mine, u_theirs, d_mine, d_theirs,
    x_oth, g_oth, vec_oth, bias_all, wq, wo, wu, wd,
    ss, rs, ls,
):
    dps, zs, x_dev, y_dev, c_dev, z_devs = place()
    d, z = dps[0], zs[0]
    greet((x_dev, y_dev, c_dev) + z_devs[1:])
    count = [0]

    def remote(src, dst, device):
        i = count[0]
        count[0] += 1
        return pltpu.make_async_remote_copy(src, dst, ss.at[i], rs.at[i], device_id=device, device_id_type=MESH)

    half = pl.ds(512, 512)
    low = pl.ds(0, 512)
    pieces = (
        lambda zz, dd: wq.at[zz, :, dd],
        lambda zz, dd: wo.at[zz, dd],
        lambda zz, dd: wu.at[zz, :, dd],
        lambda zz, dd: wd.at[zz, dd],
    )
    local = [
        pltpu.make_async_copy(src, dst, ls.at[i])
        for i, (src, dst) in enumerate(
            ((q_mine, wq.at[z, 0]), (o_mine, wo.at[z, :, :, low]), (u_mine, wu.at[z, 0]), (d_mine, wd.at[z, :, :, low]), (bias_own, bias_all.at[z]))
        )
    ]
    for copy in local:
        copy.start()
    pair = [
        remote(q_theirs, wq.at[z, 1], c_dev),
        remote(o_theirs, wo.at[z, :, :, half], c_dev),
        remote(u_theirs, wu.at[z, 1], c_dev),
        remote(d_theirs, wd.at[z, :, :, half], c_dev),
    ]
    extra = [remote(x_own, x_oth, c_dev), remote(vec_own, vec_oth, c_dev), remote(g_own, g_oth, c_dev)]
    extra += [remote(bias_own, bias_all.at[z], z_devs[k]) for k in (1, 2, 3)]
    pair[0].start()
    extra[0].start()
    extra[1].start()
    for copy in extra[3:] + pair[1:] + extra[2:3]:
        copy.start()
    z_copies = {}
    x_copies = {}
    y_copies = {}
    d_copies = {}
    for m, piece in enumerate(pieces):
        local[m].wait()
        pair[m].wait_recv()
        for k in (1, 2, 3):
            send = remote(piece(z, d), piece(z, d), z_devs[k])
            z_copies[m, k] = send
            send.start()
    order = [(m, k) for m in range(4) for k in (1, 2, 3)]

    def forward(m, k):
        piece = pieces[m]
        if (k == 2) == (m in (0, 2)):
            x_copies[m, k].wait_recv()
            src = piece(zs[k], dps[1])
            copy = remote(src, src, y_dev)
        else:
            y_copies[m, k].wait_recv()
            src = piece(zs[k], dps[2])
            copy = remote(src, src, x_dev)
        d_copies[m, k] = copy
        copy.start()

    for step, (m, k) in enumerate(order):
        z_copies[m, k].wait_recv()
        src = pieces[m](zs[k], d)
        x_copies[m, k] = remote(src, src, x_dev)
        y_copies[m, k] = remote(src, src, y_dev)
        x_copies[m, k].start()
        y_copies[m, k].start()
        if step >= 1:
            forward(*order[step - 1])
    forward(*order[-1])
    local[4].wait()
    for copy in extra:
        copy.wait()
    for copy in pair:
        copy.wait_send()
    for m, k in order:
        z_copies[m, k].wait_send()
        x_copies[m, k].wait_send()
        y_copies[m, k].wait_send()
        if (k == 2) == (m in (0, 2)):
            y_copies[m, k].wait_recv()
        else:
            x_copies[m, k].wait_recv()
        d_copies[m, k].wait()


def gather_all(x_own, g_own, vec_own, bias_own, weights):
    n = 7 + 3 + 48
    shapes = [
        x_own.shape, g_own.shape, vec_own.shape, (4,) + bias_own.shape,
        (4, 2, 4, 128, 384), (4, 4, 32, 1024), (4, 2, 4, 128, 512), (4, 4, 128, 1024),
    ]
    return pl.pallas_call(
        gather_kernel,
        out_shape=[jax.ShapeDtypeStruct(s, BF) for s in shapes],
        in_specs=[ANY] * 12,
        out_specs=[ANY] * 8,
        scratch_shapes=[pltpu.SemaphoreType.DMA((n,)), pltpu.SemaphoreType.DMA((n,)), pltpu.SemaphoreType.DMA((5,))],
        compiler_params=pltpu.CompilerParams(collective_id=0, has_side_effects=True),
        name="gather_weights",
    )(x_own, g_own, vec_own, bias_own, *weights)


BLOCKS = ((128, 1024), (256, 512), (128, 256), (256, 384))


def scatter_kernel(*refs):
    g = refs[:4]
    keep = refs[4:8]
    got = refs[8:12]
    rx, ry, aa, bb, rz, sw = (refs[12 + 4 * i : 16 + 4 * i] for i in range(6))
    ss, rs = refs[36:]
    dps, zs, x_dev, y_dev, c_dev, z_devs = place()
    greet((x_dev, y_dev, c_dev) + z_devs[1:])
    count = [0]

    def remote(src, dst, device):
        i = count[0]
        count[0] += 1
        return pltpu.make_async_remote_copy(src, dst, ss.at[i], rs.at[i], device_id=device, device_id_type=MESH)

    first = {}
    second = {}
    third = {}
    last = {}
    zorder = (1, 2, 3, 0)

    def stage1(m):
        for zr in zorder:
            if zr < 2:
                dev, rels = x_dev, (1, 3)
            else:
                dev, rels = y_dev, (2, 3)
            for slot in (1, 0):
                copy = remote(g[m].at[zs[zr], dps[rels[slot]]], rx[m].at[zr, slot], dev)
                first[m, zr, slot] = copy
                copy.start()

    def stage2(m):
        for zr in zorder:
            dev, rel = (y_dev, 2) if zr < 2 else (x_dev, 1)
            first[m, zr, 1].wait_recv()
            aa[m][zr] = (g[m][zs[zr], dps[rel]].astype(F32) + rx[m][zr, 1].astype(F32)).astype(BF)
            copy = remote(aa[m].at[zr], ry[m].at[zr], dev)
            second[m, zr] = copy
            copy.start()

    def stage3(m):
        for zr in zorder:
            first[m, zr, 0].wait_recv()
            second[m, zr].wait_recv()
            bb[m][zr] = (g[m][zs[zr], dps[0]].astype(F32) + rx[m][zr, 0].astype(F32) + ry[m][zr].astype(F32)).astype(BF)
            if zr > 0:
                copy = remote(bb[m].at[zr], rz[m].at[zr - 1], z_devs[zr])
                third[m, zr] = copy
                copy.start()

    def stage4(m):
        for zr in (1, 2, 3):
            third[m, zr].wait_recv()
        total = bb[m][0].astype(F32) + rz[m][0].astype(F32) + rz[m][1].astype(F32) + rz[m][2].astype(F32)
        rows, cols = BLOCKS[m]
        if m in (1, 3):
            keep[m][...] = total[: rows // 2]
            sw[m][...] = total[rows // 2 :]
        else:
            keep[m][...] = total[:, : cols // 2]
            sw[m][...] = total[:, cols // 2 :]
        copy = remote(sw[m], got[m], c_dev)
        last[m] = copy
        copy.start()

    for m in range(4):
        stage1(m)
    for i in range(6):
        if i < 4:
            stage2(i)
        if 0 <= i - 1 < 4:
            stage3(i - 1)
        if 0 <= i - 2 < 4:
            stage4(i - 2)
    for copies in (first, second, third):
        for copy in copies.values():
            copy.wait_send()
    for copy in last.values():
        copy.wait()


def half_block(m):
    rows, cols = BLOCKS[m]
    return (rows // 2, cols) if m in (1, 3) else (rows, cols // 2)


def scatter_all(grads):
    n = 4 * (8 + 4 + 3 + 1)
    halves = [half_block(m) for m in range(4)]
    scratch = [pltpu.VMEM((4, 2) + b, BF) for b in BLOCKS]
    for lead in (4, 4, 4, 3):
        scratch += [pltpu.VMEM((lead,) + b, BF) for b in BLOCKS]
    scratch += [pltpu.VMEM(h, F32) for h in halves]
    return pl.pallas_call(
        scatter_kernel,
        out_shape=[jax.ShapeDtypeStruct(h, F32) for h in halves * 2],
        in_specs=[VMEM] * 4,
        out_specs=[VMEM] * 8,
        scratch_shapes=scratch + [pltpu.SemaphoreType.DMA((n,)), pltpu.SemaphoreType.DMA((n,))],
        compiler_params=pltpu.CompilerParams(collective_id=1, has_side_effects=True, vmem_limit_bytes=60 << 20),
        name="scatter_grads",
    )(*grads)


def dot_nt(a, b):
    return lax.dot_general(a, b, (((1,), (1,)), ((), ())), preferred_element_type=F32)


def dot_tn(a, b):
    return lax.dot_general(a, b, (((0,), (0,)), ((), ())), preferred_element_type=F32)


def dot_nn(a, b):
    return lax.dot_general(a, b, (((1,), (0,)), ((), ())), preferred_element_type=F32)


BQ = 256


def segments(shape, axis, start, n1, seq):
    pos = lax.broadcasted_iota(jnp.int32, shape, axis) + start
    return (pos >= n1).astype(jnp.int32) + (pos >= seq).astype(jnp.int32)


def attend_fwd_kernel(seq, n1_ref, q_ref, k_ref, v_ref, o_ref, lse_ref):
    n1 = n1_ref[0]
    tp = q_ref.shape[0]
    lane = lax.broadcasted_iota(jnp.int32, (1, 128), 1)
    seg_k = segments((1, tp), 1, 0, n1, seq)

    @pl.loop(0, tp // BQ)
    def _(i):
        start = pl.multiple_of(i * BQ, BQ)
        rows = pl.ds(start, BQ)
        q = q_ref[rows, :] * BF(0.125)
        seg_q = segments((BQ, 1), 0, start, n1, seq)
        same = seg_q == seg_k
        out = jnp.zeros((BQ, 128), F32)
        for h in range(2):
            mask = lax.div(lane, 64) == h
            s = dot_nt(jnp.where(mask, q, BF(0)), k_ref[...])
            s = jnp.where(same, s, -1e30)
            top = jnp.max(s, axis=1, keepdims=True)
            e = jnp.exp(s - top)
            total = jnp.sum(e, axis=1, keepdims=True)
            mixed = dot_nn(e.astype(BF), v_ref[...]) / total
            out = jnp.where(mask, mixed, out)
            lse = jnp.broadcast_to(top + jnp.log(total), (BQ, 128))
            lse_ref[0, h : h + 1, rows] = jnp.transpose(lse)[0:1]
        o_ref[rows, :] = out.astype(BF)


def attend_fwd(n1, qkv, seq):
    tp = qkv.shape[0]
    spec = lambda j: pl.BlockSpec((tp, 128), lambda i: (0, 3 * i + j))
    return pl.pallas_call(
        functools.partial(attend_fwd_kernel, seq),
        grid=(4,),
        out_shape=[jax.ShapeDtypeStruct((tp, 512), BF), jax.ShapeDtypeStruct((4, 2, tp), F32)],
        in_specs=[SMEM, spec(0), spec(1), spec(2)],
        out_specs=[pl.BlockSpec((tp, 128), lambda i: (0, i)), pl.BlockSpec((1, 2, tp), lambda i: (i, 0, 0))],
        compiler_params=pltpu.CompilerParams(vmem_limit_bytes=48 << 20),
        name="attend_fwd",
    )(n1, qkv, qkv, qkv)


def attend_bwd_kernel(seq, n1_ref, q_ref, k_ref, v_ref, o_ref, do_ref, lse_ref, out_ref, dk_acc, dv_acc):
    n1 = n1_ref[0]
    tp = q_ref.shape[0]
    lane = lax.broadcasted_iota(jnp.int32, (1, 128), 1)
    dk_acc[...] = jnp.zeros_like(dk_acc)
    dv_acc[...] = jnp.zeros_like(dv_acc)

    @pl.loop(0, tp // BQ)
    def _(i):
        start = pl.multiple_of(i * BQ, BQ)
        rows = pl.ds(start, BQ)
        q = q_ref[rows, :]
        do = do_ref[rows, :]
        prod = do.astype(F32) * o_ref[rows, :].astype(F32)
        seg_q = segments((1, BQ), 1, start, n1, seq)
        dq = jnp.zeros((BQ, 128), F32)
        for h in range(2):
            mask = lax.div(lane, 64) == h
            lse = lse_ref[0, h : h + 1, rows]
            delta = jnp.sum(jnp.where(mask, prod, 0.0), axis=1, keepdims=True)
            delta = jnp.transpose(jnp.broadcast_to(delta, (BQ, 128)))[0:1]
            qm = jnp.where(mask, q, BF(0)) * BF(0.125)
            dom = jnp.where(mask, do, BF(0))
            for kb in range(tp // BQ):
                keys = pl.ds(kb * BQ, BQ)
                same = segments((BQ, 1), 0, kb * BQ, n1, seq) == seg_q
                k = k_ref[keys, :]
                s = dot_nt(k, qm)
                p = jnp.where(same, jnp.exp(s - lse), 0.0)
                dp = dot_nt(v_ref[keys, :], dom)
                ds = (p * (dp - delta)).astype(BF)
                dv_acc[keys, :] += dot_nn(p.astype(BF), dom)
                dk_acc[keys, :] += dot_nn(ds, qm)
                dq += jnp.where(mask, dot_tn(ds, k), 0.0)
        out_ref[rows, 0:128] = (dq * 0.125).astype(BF)

    out_ref[:, 128:256] = dk_acc[...].astype(BF)
    out_ref[:, 256:384] = dv_acc[...].astype(BF)


def attend_bwd(n1, qkv, o, do, lse, seq):
    tp = qkv.shape[0]
    spec = lambda j: pl.BlockSpec((tp, 128), lambda i: (0, 3 * i + j))
    one = pl.BlockSpec((tp, 128), lambda i: (0, i))
    return pl.pallas_call(
        functools.partial(attend_bwd_kernel, seq),
        grid=(4,),
        out_shape=jax.ShapeDtypeStruct((tp, 1536), BF),
        in_specs=[SMEM, spec(0), spec(1), spec(2), one, one, pl.BlockSpec((1, 2, tp), lambda i: (i, 0, 0))],
        out_specs=pl.BlockSpec((tp, 384), lambda i: (0, i)),
        scratch_shapes=[pltpu.VMEM((tp, 128), F32)] * 2,
        compiler_params=pltpu.CompilerParams(vmem_limit_bytes=48 << 20),
        name="attend_bwd",
    )(n1, qkv, qkv, qkv, o, do, lse)


def swap_halves(v):
    return jnp.concatenate([v[:, 512:], v[:, :512]], axis=1)


def to_partner(v):
    return lax.ppermute(v, "gx", [(0, 1), (1, 0)])


def norm_stats(values):
    mean = jnp.mean(values, axis=1, keepdims=True)
    inverse = lax.rsqrt(jnp.mean(values * values, axis=1, keepdims=True) - mean * mean + norm_eps)
    return mean, inverse


def norm_pull(grad_norm, hat, inverse, gain):
    scaled = grad_norm * gain
    first = jnp.mean(scaled, axis=1, keepdims=True)
    second = jnp.mean(scaled * hat, axis=1, keepdims=True)
    return inverse * (scaled - first - hat * second)


def local_chip(
    tokens, segment_ids, norm1_gain, norm1_shift, qkv_weight, qv_bias, out_weight, out_bias,
    norm2_gain, norm2_shift, up_weight, up_bias, down_weight, down_bias, cotangent,
):
    seq = segment_ids.shape[1]
    tp = -(-seq // BQ) * BQ
    c = lax.axis_index("gx")
    z = lax.axis_index("gy")
    pad = ((0, tp - seq), (0, 0))
    x_own = jnp.pad(tokens, pad)
    g_own = jnp.pad(cotangent, pad)
    vec_own = jnp.pad(
        jnp.stack([norm1_gain, norm1_shift, out_bias, norm2_gain, norm2_shift, down_bias]), ((0, 10), (0, 0))
    )
    up_mine = lax.dynamic_index_in_dim(up_bias.reshape(4, 2, 128), c, 1, False).reshape(1, 512)
    qv_mine = lax.dynamic_index_in_dim(qv_bias.reshape(2, 2, 128), c, 1, False).reshape(1, 256)
    bias_own = jnp.concatenate([up_mine, jnp.pad(qv_mine, ((0, 0), (0, 256))), jnp.zeros((14, 512), BF)], axis=0)
    weights = []
    for side in (c, 1 - c):
        q = lax.dynamic_slice_in_dim(qkv_weight, side * 128, 128, 2).reshape(4, 128, 384)
        o = lax.dynamic_slice_in_dim(out_weight, side * 128, 128, 0).reshape(4, 32, 512)
        u = lax.dynamic_index_in_dim(up_weight.reshape(512, 4, 2, 128), side, 2, False).reshape(4, 128, 512)
        dn = lax.dynamic_index_in_dim(down_weight.reshape(4, 2, 128, 512), side, 1, False)
        weights.append((q, o, u, dn))
    weights = [w for pair in zip(*weights) for w in pair]
    x_oth, g_oth, vec_oth, bias_all, wq, wo, wu, wd = gather_all(x_own, g_own, vec_own, bias_own, weights)
    wq = wq.reshape(4, 1024, 384)
    wo = wo.reshape(512, 1024)
    wu = wu.reshape(4, 1024, 512)
    wd = wd.reshape(4 * 512, 1024)
    vec = jnp.concatenate([vec_own[:6], vec_oth[:6]], axis=1).astype(F32)
    gain1, shift1, ob, gain2, shift2, db = (vec[i] for i in range(6))
    ids = jnp.concatenate([segment_ids, to_partner(segment_ids)], axis=0)
    row = lax.rem(z, 2) + 2 * jnp.where(lax.div(z, 2) == c, 0, 1)
    n1 = jnp.sum((lax.dynamic_index_in_dim(ids, row, 0, False) == 0).astype(jnp.int32)).reshape(1)

    x = jnp.concatenate([x_own, x_oth], axis=1).astype(F32)
    g = jnp.concatenate([g_own, g_oth], axis=1)
    mean1, inv1 = norm_stats(x)
    hat1 = (x - mean1) * inv1
    a1 = (hat1 * gain1 + shift1).astype(BF)
    qb = bias_all[:, 1, :128]
    vb = bias_all[:, 1, 128:256]
    bias_full = jnp.stack([qb, jnp.zeros_like(qb), vb], axis=1).reshape(4, 384).astype(F32)
    qkv = (jnp.einsum("tw,zwk->tzk", a1, wq, preferred_element_type=F32) + bias_full[None]).astype(BF).reshape(tp, 1536)
    o, lse = attend_fwd(n1, qkv, seq)
    part = dot_nn(o, wo)
    m = x + part + swap_halves(to_partner(part.astype(BF))).astype(F32) + ob
    mean2, inv2 = norm_stats(m)
    hat2 = (m - mean2) * inv2
    a2 = (hat2 * gain2 + shift2).astype(BF)
    ub = bias_all[:, 0].astype(F32)
    h = jnp.einsum("tw,zwk->tzk", a2, wu, preferred_element_type=F32) + ub[None]
    h = h.reshape(tp, 2048)
    cdf = 0.5 * (1.0 + lax.erf(h * math.sqrt(0.5)))
    u = (h * cdf).astype(BF)
    gp = cdf + h * jnp.exp(-0.5 * h * h) * (1.0 / math.sqrt(2 * math.pi))
    part2 = dot_nn(u, wd)
    got2 = to_partner(part2[:, 512:].astype(BF)).astype(F32)
    output = (m[:, :512] + part2[:, :512] + got2 + db[:512])[:seq].astype(BF)
    g_f = g.astype(F32)
    down_bias_grad = jnp.sum(g_f[:, :512], axis=0)
    gd = dot_tn(u, g).astype(BF).reshape(4, 4, 128, 1024)
    dh = (dot_nt(g, wd) * gp).astype(BF)
    up_bias_grad = jnp.sum(dh.astype(F32), axis=0)
    gu = dot_tn(a2, dh).astype(BF).reshape(2, 4, 128, 4, 512).transpose(3, 1, 0, 2, 4).reshape(4, 4, 256, 512)
    part3 = jnp.einsum("tzk,zwk->tw", dh.reshape(tp, 4, 512), wu, preferred_element_type=F32)
    da2 = part3 + swap_halves(to_partner(part3.astype(BF))).astype(F32)
    norm2_gain_grad = jnp.sum(da2[:, :512] * hat2[:, :512], axis=0)
    norm2_shift_grad = jnp.sum(da2[:, :512], axis=0)
    dm = g_f + norm_pull(da2, hat2, inv2, gain2)
    dr = dm.astype(BF)
    out_bias_grad = jnp.sum(dr[:, :512].astype(F32), axis=0)
    go = dot_tn(o, dr).astype(BF).reshape(4, 128, 2, 4, 128).transpose(0, 3, 1, 2, 4).reshape(4, 4, 128, 256)
    do = dot_nt(dr, wo).astype(BF)
    dqkv = attend_bwd(n1, qkv, o, do, lse, seq)
    sums = jnp.sum(dqkv.astype(F32), axis=0).reshape(4, 3, 128)
    gq = dot_tn(a1, dqkv).astype(BF).reshape(2, 4, 128, 4, 384).transpose(3, 1, 0, 2, 4).reshape(4, 4, 256, 384)
    part4 = jnp.einsum("tzk,zwk->tw", dqkv.reshape(tp, 4, 384), wq, preferred_element_type=F32)
    da1 = part4 + swap_halves(to_partner(part4.astype(BF))).astype(F32)
    norm1_gain_grad = jnp.sum(da1[:, :512] * hat1[:, :512], axis=0)
    norm1_shift_grad = jnp.sum(da1[:, :512], axis=0)
    input_grad = (dm + norm_pull(da1, hat1, inv1, gain1))[:seq, :512].astype(BF)

    width = jnp.stack([norm1_gain_grad, norm1_shift_grad, out_bias_grad, norm2_gain_grad, norm2_shift_grad, down_bias_grad])
    mine = (jnp.arange(2) == c).astype(F32)
    flat = jnp.concatenate(
        [
            (mine[:, None, None] * width[None]).reshape(-1),
            (mine[None, None, :, None] * up_bias_grad.reshape(4, 4, 1, 128)).reshape(-1),
            (mine[None, None, :, None] * sums[:, 0::2, :].reshape(4, 2, 1, 128)).reshape(-1),
        ]
    )
    flat = lax.psum(flat, ("dp", "gx", "gy"))
    width = lax.dynamic_index_in_dim(flat[:6144].reshape(2, 6, 512), c, 0, False)
    up_bias_grad = lax.dynamic_index_in_dim(flat[6144:10240].reshape(4, 1024), z, 0, False)
    qv_bias_grad = lax.dynamic_index_in_dim(flat[10240:].reshape(4, 2, 256), z, 0, False)

    kd, ku, ko, kq, td, tu, to, tq = scatter_all((gd, gu, go, gq))

    def by_core(keep, got, axis):
        return jnp.where(c == 0, jnp.stack([keep, got], axis), jnp.stack([got, keep], axis))

    down_grad = by_core(kd, td, 0).reshape(1, 256, 512)
    up_grad = by_core(ku.reshape(128, 4, 128), tu.reshape(128, 4, 128), 2).reshape(1, 128, 1024)
    out_grad = by_core(ko, to, 0).reshape(256, 1, 128)
    qkv_grad = by_core(kq.reshape(128, 3, 128), tq.reshape(128, 3, 128), 2).reshape(1, 128, 3, 256)
    return (
        output, input_grad, width[0], width[1], qkv_grad, qv_bias_grad, out_grad, width[2],
        width[3], width[4], up_grad, up_bias_grad, down_grad, width[5],
    )


def solution(mesh):
    sizes = dict(mesh.shape)
    chip_rows = sizes["dp"] == 4 and sizes["gx"] == 2 and sizes["gy"] == 4

    def whole(*args):
        rows, seq = args[1].shape
        fast = chip_rows and rows * seq == args[0].shape[0] and rows == 16
        body = local_chip if fast else local
        return jax.shard_map(
            body,
            mesh=mesh,
            in_specs=(
                P(("dp", "gy"), "gx"), P(("dp", "gx"), None), P("gx"), P("gx"), P("gx", None, "gy"), P(None, "gy"),
                P("gy", "gx"), P("gx"), P("gx"), P("gx"), P("gx", "gy"), P("gy"), P("gy", "gx"), P("gx"), P(("dp", "gy"), "gx"),
            ),
            out_specs=(
                P(("dp", "gy"), "gx"), P(("dp", "gy"), "gx"), P("gx"), P("gx"), P("gx", "dp", None, "gy"), P(None, "gy"),
                P("gy", "gx", "dp"), P("gx"), P("gx"), P("gx"), P("gx", "dp", "gy"), P("gy"), P("gy", "dp", "gx"), P("gx"),
            ),
            check_vma=False,
        )(*args)

    return whole
```

```python
import functools
import math

import jax
import jax.numpy as jnp
from jax import lax
from jax.experimental import pallas as pl
from jax.experimental.pallas import tpu as pltpu
from jax.sharding import PartitionSpec as P

D = 1024
HD = 64
MESH = pl.DeviceIdType.MESH
F32 = jnp.float32
BF = jnp.bfloat16
ANY = pl.BlockSpec(memory_space=pl.ANY)
SMEM = pl.BlockSpec(memory_space=pltpu.SMEM)
VMEM = pl.BlockSpec(memory_space=pltpu.VMEM)
norm_eps = 1e-06


def times_right(left, right):
    return jnp.dot(left, right, preferred_element_type=jnp.float32)


def times_back(left, right):
    return lax.dot_general(
        left, right, (((1,), (1,)), ((), ())), preferred_element_type=jnp.float32
    )


def times_outer(left, right):
    return lax.dot_general(
        left, right, (((0,), (0,)), ((), ())), preferred_element_type=jnp.float32
    )


def exact_gelu(values):
    return jax.nn.gelu(values, approximate=False)


def norm_forward(values, gain, shift):
    moments = lax.psum((jnp.sum(values, axis=1), jnp.sum(values * values, axis=1)), "gx")
    mean_val = moments[0] / D
    inverse = lax.rsqrt(moments[1] / D - mean_val * mean_val + norm_eps)
    hat_vals = (values - mean_val[:, None]) * inverse[:, None]
    return (hat_vals * gain + shift, hat_vals, inverse)


def norm_backward(grad_norm, hat_vals, inverse, gain):
    scaled = grad_norm * gain
    moments = lax.psum((jnp.sum(scaled, axis=1), jnp.sum(scaled * hat_vals, axis=1)), "gx")
    grad_in = inverse[:, None] * (
        scaled - (moments[0] / D)[:, None] - hat_vals * (moments[1] / D)[:, None]
    )
    return (grad_in, jnp.sum(grad_norm * hat_vals, axis=0), jnp.sum(grad_norm, axis=0))


def gather_gy(values):
    return lax.all_gather(values, "gy", axis=0, tiled=True)


def gather_gx(values):
    return lax.all_gather(values, "gx", axis=0, tiled=True)


def sum_over_gx(left, multiply):
    keep_rows = left.shape[0] // lax.axis_size("gx")

    def term(start, count):
        return multiply(left)

    return lax.psum_scatter(
        term(jnp.int32(0), keep_rows * lax.axis_size("gx")), "gx", scatter_dimension=0, tiled=True
    )


def sum_over_gy(left, multiply):
    keep_rows = left.shape[0] // lax.axis_size("gy")

    def term(start, count):
        return multiply(left)

    return lax.psum_scatter(
        term(jnp.int32(0), keep_rows * lax.axis_size("gy")), "gy", scatter_dimension=0, tiled=True
    )


def masked_scores(query_part, key_part, segment):
    scaling = 1.0 / math.sqrt(query_part.shape[-1])
    scores = (
        jnp.einsum("qhd,khd->hqk", query_part, key_part, preferred_element_type=jnp.float32)
        * scaling
    )
    same = segment[:, None] == segment[None, :]
    return jnp.where(same[None], scores, -1e30)


def attend_forward(item):
    packed, segment = item
    scores = masked_scores(packed[:, 0], packed[:, 1], segment)
    top_val = jnp.max(scores, axis=-1, keepdims=True)
    expo = jnp.exp(scores - top_val)
    total = jnp.sum(expo, axis=-1, keepdims=True)
    probs = (expo / total).astype(jnp.bfloat16)
    mixed = jnp.einsum("hqk,khd->qhd", probs, packed[:, 2], preferred_element_type=jnp.float32)
    return (mixed.astype(jnp.bfloat16), (top_val + jnp.log(total))[..., 0])


def attend_backward(item):
    packed, segment, log_sum, grad_out = item
    query_part = packed[:, 0]
    key_part = packed[:, 1]
    value_part = packed[:, 2]
    scaling = 1.0 / math.sqrt(query_part.shape[-1])
    scores = masked_scores(query_part, key_part, segment)
    probs = jnp.exp(scores - log_sum[..., None])
    probs_low = probs.astype(jnp.bfloat16)
    grad_prob = jnp.einsum("qhd,khd->hqk", grad_out, value_part, preferred_element_type=jnp.float32)
    grad_value = jnp.einsum("hqk,qhd->khd", probs_low, grad_out, preferred_element_type=jnp.float32)
    delta = jnp.sum(probs * grad_prob, axis=-1, keepdims=True)
    grad_score = (probs * (grad_prob - delta)).astype(jnp.bfloat16)
    grad_query = (
        jnp.einsum("hqk,khd->qhd", grad_score, key_part, preferred_element_type=jnp.float32)
        * scaling
    )
    grad_key = (
        jnp.einsum("hqk,qhd->khd", grad_score, query_part, preferred_element_type=jnp.float32)
        * scaling
    )
    return jnp.stack([grad_query, grad_key, grad_value], axis=1).astype(jnp.bfloat16)


def local(
    tokens,
    segment_ids,
    norm1_gain,
    norm1_shift,
    qkv_weight,
    qv_bias,
    out_weight,
    out_bias,
    norm2_gain,
    norm2_shift,
    up_weight,
    up_bias,
    down_weight,
    down_bias,
    cotangent,
):
    head_width = qkv_weight.shape[2]
    local_heads = head_width // HD
    seq_len = segment_ids.shape[1]
    qkv_flat = qkv_weight.reshape(qkv_weight.shape[0], 3 * head_width)
    gain_one = norm1_gain.astype(jnp.float32)
    gain_two = norm2_gain.astype(jnp.float32)
    resid = tokens.astype(jnp.float32)
    normed, hat_one, inv_one = norm_forward(resid, gain_one, norm1_shift.astype(jnp.float32))
    first_low = normed.astype(jnp.bfloat16)
    first_rows = gather_gy(first_low)
    qkv_all = sum_over_gx(first_rows, lambda piece: times_right(piece, qkv_flat))
    bias_full = jnp.stack([qv_bias[0], jnp.zeros_like(qv_bias[0]), qv_bias[1]]).astype(jnp.float32)
    qkv_low = (qkv_all.reshape(-1, 3, head_width) + bias_full[None]).astype(jnp.bfloat16)
    packed = qkv_low.reshape(-1, seq_len, 3, local_heads, HD)
    mixed, log_sums = lax.map(attend_forward, (packed, segment_ids))
    mixed_low = mixed.reshape(-1, head_width)
    mixed_rows = gather_gx(mixed_low)
    branch = sum_over_gy(
        mixed_rows, lambda piece: times_right(piece, out_weight)
    ) + out_bias.astype(jnp.float32)
    middle = resid + branch
    normed_two, hat_two, inv_two = norm_forward(middle, gain_two, norm2_shift.astype(jnp.float32))
    second_low = normed_two.astype(jnp.bfloat16)
    second_rows = gather_gy(second_low)
    hidden = sum_over_gx(second_rows, lambda piece: times_right(piece, up_weight)) + up_bias.astype(
        jnp.float32
    )
    active, gelu_pull = jax.vjp(exact_gelu, hidden)
    active_low = active.astype(jnp.bfloat16)
    active_rows = gather_gx(active_low)
    branch_two = sum_over_gy(
        active_rows, lambda piece: times_right(piece, down_weight)
    ) + down_bias.astype(jnp.float32)
    output = (middle + branch_two).astype(jnp.bfloat16)
    grad_top = cotangent.astype(jnp.float32)
    down_bias_grad = jnp.sum(grad_top, axis=0)
    grad_top_rows = gather_gy(cotangent)
    down_weight_grad = times_outer(active_rows, grad_top_rows)
    grad_active = sum_over_gx(grad_top_rows, lambda piece: times_back(piece, down_weight))
    grad_hidden = gelu_pull(grad_active)[0].astype(jnp.bfloat16)
    up_bias_grad = jnp.sum(grad_hidden.astype(jnp.float32), axis=0)
    hidden_rows = gather_gx(grad_hidden)
    up_weight_grad = times_outer(second_rows, hidden_rows)
    grad_norm_two = sum_over_gy(hidden_rows, lambda piece: times_back(piece, up_weight))
    grad_in_two, norm2_gain_grad, norm2_shift_grad = norm_backward(
        grad_norm_two, hat_two, inv_two, gain_two
    )
    grad_middle = grad_top + grad_in_two
    grad_branch = grad_middle.astype(jnp.bfloat16)
    out_bias_grad = jnp.sum(grad_branch.astype(jnp.float32), axis=0)
    branch_rows = gather_gy(grad_branch)
    out_weight_grad = times_outer(mixed_rows, branch_rows)
    grad_mixed = sum_over_gx(branch_rows, lambda piece: times_back(piece, out_weight)).astype(
        jnp.bfloat16
    )
    grad_mixed = grad_mixed.reshape(-1, seq_len, local_heads, HD)
    grad_packed = lax.map(attend_backward, (packed, segment_ids, log_sums, grad_mixed))
    grad_qkv = grad_packed.reshape(-1, 3 * head_width)
    third_sums = jnp.sum(grad_qkv.astype(jnp.float32), axis=0).reshape(3, head_width)
    qv_bias_grad = jnp.stack([third_sums[0], third_sums[2]])
    qkv_rows = gather_gx(grad_qkv)
    qkv_weight_grad = times_outer(first_rows, qkv_rows).reshape(qkv_weight.shape)
    grad_norm_one = sum_over_gy(qkv_rows, lambda piece: times_back(piece, qkv_flat))
    grad_in_one, norm1_gain_grad, norm1_shift_grad = norm_backward(
        grad_norm_one, hat_one, inv_one, gain_one
    )
    input_grad = (grad_middle + grad_in_one).astype(jnp.bfloat16)
    qkv_weight_grad, out_weight_grad, up_weight_grad, down_weight_grad = (
        lax.psum_scatter(qkv_weight_grad, "dp", scatter_dimension=0, tiled=True),
        lax.psum_scatter(out_weight_grad, "dp", scatter_dimension=1, tiled=True),
        lax.psum_scatter(up_weight_grad, "dp", scatter_dimension=0, tiled=True),
        lax.psum_scatter(down_weight_grad, "dp", scatter_dimension=0, tiled=True),
    )
    qkv_weight_grad = qkv_weight_grad[None]
    out_weight_grad = out_weight_grad[:, None, :]
    up_weight_grad = up_weight_grad[None]
    down_weight_grad = down_weight_grad[None]
    (
        norm1_gain_grad,
        norm1_shift_grad,
        norm2_gain_grad,
        norm2_shift_grad,
        out_bias_grad,
        down_bias_grad,
    ) = lax.psum(
        (
            norm1_gain_grad,
            norm1_shift_grad,
            norm2_gain_grad,
            norm2_shift_grad,
            out_bias_grad,
            down_bias_grad,
        ),
        ("dp", "gy"),
    )
    up_bias_grad, qv_bias_grad = lax.psum((up_bias_grad, qv_bias_grad), ("dp", "gx"))
    return (
        output,
        input_grad,
        norm1_gain_grad,
        norm1_shift_grad,
        qkv_weight_grad,
        qv_bias_grad,
        out_weight_grad,
        out_bias_grad,
        norm2_gain_grad,
        norm2_shift_grad,
        up_weight_grad,
        up_bias_grad,
        down_weight_grad,
        down_bias_grad,
    )


def flip1(i):
    return i + 1 - 2 * lax.rem(i, 2)


def flip2(i):
    return i + 2 - 4 * lax.div(i, 2)


def place():
    dp, c, z = lax.axis_index("dp"), lax.axis_index("gx"), lax.axis_index("gy")
    dps = (dp, flip1(dp), flip2(dp), 3 - dp)
    zs = (z, flip1(z), flip2(z), 3 - z)
    x_dev = (dps[1], c, z)
    y_dev = (dps[2], c, z)
    c_dev = (dp, 1 - c, z)
    z_devs = (None,) + tuple((dp, c, zz) for zz in zs[1:])
    return dps, zs, x_dev, y_dev, c_dev, z_devs


def greet(devices):
    barrier = pltpu.get_barrier_semaphore()
    for device in devices:
        pl.semaphore_signal(barrier, inc=1, device_id=device, device_id_type=MESH)
    pl.semaphore_wait(barrier, len(devices))


WINDOW = 3
ORDER = tuple((m, k) for m in range(4) for k in (1, 2, 3))
N_PAIR = 9


class Sems:
    def __init__(self, ss, rs):
        self.ss, self.rs, self.n = ss, rs, 0

    def remote(self, src, dst, device):
        i = self.n
        self.n += 1
        return pltpu.make_async_remote_copy(
            src, dst, self.ss.at[i], self.rs.at[i], device_id=device, device_id_type=MESH
        )


class Locals:
    def __init__(self, ls):
        self.ls, self.n, self.open = ls, 0, []

    def copy(self, src, dst):
        copy = pltpu.make_async_copy(src, dst, self.ls.at[self.n])
        self.n += 1
        copy.start()
        return copy

    def later(self, src, dst):
        self.open.append(self.copy(src, dst))

    def close(self):
        for copy in self.open:
            copy.wait()


def weight_cuts(side, raw, full, crel):
    qf, ow, up, dn = raw
    wq, wo, wu, wd = full
    cols = pl.ds(crel * 512, 512)
    cuts = [[], [], [], []]
    for t in range(3):
        off = pl.multiple_of(t * 256 + side * 128, 128)
        cuts[0].append((qf.at[:, :, pl.ds(off, 128)], wq.at[0, crel, :, :, pl.ds(t * 128, 128)]))
    cuts[1].append((ow.at[side], wo.at[0, :, :, cols]))
    for t in range(4):
        off = pl.multiple_of(t * 256 + side * 128, 128)
        cuts[2].append((up.at[:, :, pl.ds(off, 128)], wu.at[0, crel, :, :, pl.ds(t * 128, 128)]))
    cuts[3].append((dn.at[:, side], wd.at[0, :, :, cols]))
    return cuts


def gather_steps(sems, loc, here, raw, full):
    dps, zs, x_dev, y_dev, c_dev, z_devs, c = here
    d = dps[0]
    wq, wo, wu, wd = full
    pieces = (
        lambda k, dd: wq.at[k, :, dd],
        lambda k, dd: wo.at[k, dd],
        lambda k, dd: wu.at[k, :, dd],
        lambda k, dd: wd.at[k, dd],
    )
    theirs = [[sems.remote(src, dst, c_dev) for src, dst in group] for group in weight_cuts(1 - c, raw, full, 1)]
    copies = {}
    own = []
    ready = set()

    def pair_start():
        for m, group in enumerate(weight_cuts(c, raw, full, 0)):
            for copy in theirs[m]:
                copy.start()
            own.append([loc.copy(src, dst) for src, dst in group])

    def own_ready(m):
        if m not in ready:
            ready.add(m)
            for copy in own[m]:
                copy.wait()
            for copy in theirs[m]:
                copy.wait_recv()

    def z_send(s):
        m, k = ORDER[s]
        own_ready(m)
        src = pieces[m](0, d)
        copy = sems.remote(src, pieces[m](k, d), z_devs[k])
        copies["z", m, k] = copy
        copy.start()

    def forward(s):
        m, k = ORDER[s]
        if (k == 2) == (m in (0, 2)):
            copies["x", m, k].wait_recv()
            src = pieces[m](k, dps[1])
            copy = sems.remote(src, src, y_dev)
        else:
            copies["y", m, k].wait_recv()
            src = pieces[m](k, dps[2])
            copy = sems.remote(src, src, x_dev)
        copies["d", m, k] = copy
        copy.start()

    def steps():
        for s in range(len(ORDER)):
            m, k = ORDER[s]
            copies["z", m, k].wait_recv()
            src = pieces[m](k, d)
            for axis, dev in (("x", x_dev), ("y", y_dev)):
                copy = sems.remote(src, src, dev)
                copies[axis, m, k] = copy
                copy.start()
            if s + WINDOW < len(ORDER):
                copies["z", m, k].wait_send()
                z_send(s + WINDOW)
            if s > 0:
                forward(s - 1)
            yield
        forward(len(ORDER) - 1)
        yield

    def slot_ready(m, k):
        if k == 0:
            own_ready(m)
            return
        copies["y" if (k == 2) == (m in (0, 2)) else "x", m, k].wait_recv()
        copies["d", m, k].wait_recv()

    def close():
        for group in theirs:
            for copy in group:
                copy.wait_send()
        for s, (m, k) in enumerate(ORDER):
            if s + WINDOW >= len(ORDER):
                copies["z", m, k].wait_send()
            for axis in "xyd":
                copies[axis, m, k].wait_send()

    return pair_start, z_send, steps(), slot_ready, close


def dot_nt(a, b):
    return lax.dot_general(a, b, (((1,), (1,)), ((), ())), preferred_element_type=F32)


def dot_tn(a, b):
    return lax.dot_general(a, b, (((0,), (0,)), ((), ())), preferred_element_type=F32)


def dot_nn(a, b):
    return lax.dot_general(a, b, (((1,), (0,)), ((), ())), preferred_element_type=F32)


BQ = 256


def segments(shape, axis, start, n1, seq):
    pos = (lax.broadcasted_iota(jnp.int32, shape, axis) + start).astype(F32)
    return (pos >= n1).astype(F32) + (pos >= float(seq)).astype(F32)


def attend_fwd_rows(qkv, o, lse_ref, zr, lo, hi, n1, seq):
    tp = qkv.shape[0]
    lane = lax.broadcasted_iota(jnp.int32, (1, 128), 1)
    base = zr * 384

    @pl.loop(lo, hi)
    def _(i):
        start = pl.multiple_of(i * BQ, BQ)
        rows = pl.ds(start, BQ)
        q = qkv[rows, base : base + 128] * BF(0.125)
        same = segments((BQ, 1), 0, start, n1, seq) == segments((1, tp), 1, 0, n1, seq)
        out = jnp.zeros((BQ, 128), F32)
        for h in range(2):
            mask = lax.div(lane, 64) == h
            s = dot_nt(jnp.where(mask, q, BF(0)), qkv[:, base + 128 : base + 256])
            s = jnp.where(same, s, -1e30)
            top = jnp.max(s, axis=1, keepdims=True)
            e = jnp.exp(s - top)
            total = jnp.sum(e, axis=1, keepdims=True)
            mixed = dot_nn(e.astype(BF), qkv[:, base + 256 : base + 384]) / total
            out = jnp.where(mask, mixed, out)
            lse = jnp.broadcast_to(top + jnp.log(total), (BQ, 128))
            lse_ref[2 * zr + h : 2 * zr + h + 1, rows] = jnp.transpose(lse)[0:1]
        o[rows, zr * 128 : zr * 128 + 128] = out.astype(BF)


def halves_mean(a, b):
    return (jnp.sum(a, axis=1, keepdims=True) + jnp.sum(b, axis=1, keepdims=True)) * (1.0 / D)


def forward_kernel(
    seq, x_own, g_own, vec_own, bias_own, ids, qf, ow, up, dn,
    wq, wo, wu, wd, n1_out, x_out, g_out, vec_out, bias_out, a1_out, qkv_out, o_out, lse_out, m_out, a2_out, u_out, gp_out, gd_out,
    x_oth, g_oth, vec_oth, bias_all, cnt, wq_v, wo_v, wu_v, a1, qkv, o, lse, m, pb, pr, a2, u, gp, gd,
    ss, rs, ls,
):
    tp = x_own.shape[0]
    nb = tp // BQ
    dps, zs, x_dev, y_dev, c_dev, z_devs = place()
    c, z = lax.axis_index("gx"), zs[0]
    sems, loc = Sems(ss, rs), Locals(ls)
    pair_start, z_send, steps, slot_ready, close = gather_steps(
        sems, loc, (dps, zs, x_dev, y_dev, c_dev, z_devs, c), (qf, ow, up, dn), (wq, wo, wu, wd)
    )

    def poll(n=1):
        for _ in range(n):
            next(steps, None)

    ids_low = (ids[...] == 0).astype(F32)
    for r in range(2):
        cnt[0, r] = jnp.broadcast_to(jnp.sum(ids_low[r : r + 1], axis=1, keepdims=True), (8, 128))
    bias_all[0] = bias_own[...]
    greet((x_dev, y_dev, c_dev) + z_devs[1:])
    pair_start()
    x_copy = sems.remote(x_own, x_oth, c_dev)
    x_copy.start()
    small = [sems.remote(vec_own, vec_oth, c_dev), sems.remote(cnt.at[0], cnt.at[1], c_dev)]
    small += [sems.remote(bias_own, bias_all.at[k], z_devs[k]) for k in (1, 2, 3)]
    for copy in small:
        copy.start()
    g_copy = sems.remote(g_own, g_oth, c_dev)
    g_copy.start()
    for s in range(WINDOW):
        z_send(s)
    for copy in small:
        copy.wait_recv()
    x_copy.wait_recv()
    vec = [(vec_own[i : i + 1, :].astype(F32), vec_oth[i : i + 1, :].astype(F32)) for i in range(6)]
    n1 = cnt[lax.rem(lax.div(z, 2) + c, 2), lax.rem(z, 2)]
    n1_out[...] = n1
    n1 = n1[0:1, 0:1]
    loc.later(x_oth, x_out)
    loc.later(vec_oth, vec_out)
    loc.later(bias_all, bias_out)

    @pl.loop(0, nb)
    def _(i):
        rows = pl.ds(pl.multiple_of(i * BQ, BQ), BQ)
        xo, xt = x_own[rows, :].astype(F32), x_oth[rows, :].astype(F32)
        mean = halves_mean(xo, xt)
        inv = lax.rsqrt(halves_mean(xo * xo, xt * xt) - mean * mean + norm_eps)
        a1[rows, 0:512] = ((xo - mean) * inv * vec[0][0] + vec[1][0]).astype(BF)
        a1[rows, 512:1024] = ((xt - mean) * inv * vec[0][1] + vec[1][1]).astype(BF)

    loc.later(a1, a1_out)
    for zr in range(4):
        slot_ready(0, zr)
        loc.copy(wq.at[zr], wq_v.at[zr]).wait()
        qb, vb = bias_all[zr, 1:2, 0:128].astype(F32), bias_all[zr, 1:2, 128:256].astype(F32)
        bias = jnp.concatenate([qb, jnp.zeros_like(qb), vb], axis=1)

        @pl.loop(0, nb)
        def _(i):
            rows = pl.ds(pl.multiple_of(i * BQ, BQ), BQ)
            qkv[rows, zr * 384 : zr * 384 + 384] = (dot_nn(a1[rows, :], wq_v[zr].reshape(1024, 384)) + bias).astype(BF)

        if zr == 0:
            poll()
        attend_fwd_rows(qkv, o, lse, zr, 0, 2, n1, seq)
        poll()
        attend_fwd_rows(qkv, o, lse, zr, 2, nb, n1, seq)
        if zr < 3:
            poll()
    loc.later(qkv, qkv_out)
    loc.later(o, o_out)
    loc.later(lse, lse_out)
    for zr in range(4):
        slot_ready(1, zr)
    loc.copy(wo, wo_v).wait()
    swaps = []
    for i in range(nb):
        rows = pl.ds(i * BQ, BQ)
        part = dot_nn(o[rows, :], wo_v[...].reshape(512, 1024))
        pb[rows, 0:512] = part[:, 512:].astype(BF)
        pb[rows, 512:1024] = part[:, :512].astype(BF)
        copy = sems.remote(pb.at[rows], pr.at[rows], c_dev)
        copy.start()
        swaps.append(copy)
        m[rows, :] = part
    poll()
    for i in range(nb):
        rows = pl.ds(i * BQ, BQ)
        swaps[i].wait_recv()
        mo = x_own[rows, :].astype(F32) + m[rows, 0:512] + pr[rows, 0:512].astype(F32) + vec[2][0]
        mt = x_oth[rows, :].astype(F32) + m[rows, 512:1024] + pr[rows, 512:1024].astype(F32) + vec[2][1]
        mean = halves_mean(mo, mt)
        inv = lax.rsqrt(halves_mean(mo * mo, mt * mt) - mean * mean + norm_eps)
        m[rows, 0:512] = mo
        m[rows, 512:1024] = mt
        a2[rows, 0:512] = ((mo - mean) * inv * vec[3][0] + vec[4][0]).astype(BF)
        a2[rows, 512:1024] = ((mt - mean) * inv * vec[3][1] + vec[4][1]).astype(BF)
    loc.later(m, m_out)
    loc.later(a2, a2_out)
    g_copy.wait_recv()
    loc.later(g_oth, g_out)
    for zr in range(4):
        slot_ready(2, zr)
        loc.copy(wu.at[zr], wu_v.at[zr]).wait()
        bias = bias_all[zr, 0:1, :].astype(F32)

        @pl.loop(0, nb)
        def _(i):
            rows = pl.ds(pl.multiple_of(i * BQ, BQ), BQ)
            h = dot_nn(a2[rows, :], wu_v[zr].reshape(1024, 512)) + bias
            cdf = 0.5 * (1.0 + lax.erf(h * math.sqrt(0.5)))
            u[rows, zr * 512 : zr * 512 + 512] = (h * cdf).astype(BF)
            gp[rows, zr * 512 : zr * 512 + 512] = (cdf + h * jnp.exp(-0.5 * h * h) * (1.0 / math.sqrt(2 * math.pi))).astype(BF)

        for j, gref in enumerate((g_own, g_oth)):
            gd[zr, :, :, 512 * j : 512 * j + 512] = (
                dot_tn(u[:, zr * 512 : zr * 512 + 512], gref[...]).astype(BF).reshape(4, 128, 512)
            )
        loc.later(gd.at[zr], gd_out.at[zr])
        poll()
    loc.later(u, u_out)
    loc.later(gp, gp_out)
    poll(99)
    for copy in small + [x_copy, g_copy] + swaps:
        copy.wait_send()
    for k in (1, 2, 3):
        slot_ready(3, k)
    close()
    loc.close()


def forward_all(x_own, g_own, vec_own, bias_own, ids, qf, ow, up, dn):
    tp = x_own.shape[0]
    seq = ids.shape[1]
    n_remote = N_PAIR + 7 + 48 + tp // BQ
    n_local = N_PAIR + 32
    hbm = [
        (4, 2, 4, 128, 384), (4, 4, 32, 1024), (4, 2, 4, 128, 512), (4, 4, 128, 1024),
    ]
    sds = jax.ShapeDtypeStruct
    out_shape = [sds(s, BF) for s in hbm] + [
        sds((8, 128), F32), sds((tp, 512), BF), sds((tp, 512), BF), sds(vec_own.shape, BF), sds((4,) + bias_own.shape, BF),
        sds((tp, 1024), BF), sds((tp, 1536), BF), sds((tp, 512), BF), sds((8, tp), F32), sds((tp, 1024), F32),
        sds((tp, 1024), BF), sds((tp, 2048), BF), sds((tp, 2048), BF), sds((4, 4, 128, 1024), BF),
    ]
    scratch = [
        pltpu.VMEM((tp, 512), BF), pltpu.VMEM((tp, 512), BF), pltpu.VMEM(vec_own.shape, BF), pltpu.VMEM((4,) + bias_own.shape, BF),
        pltpu.VMEM((2, 2, 8, 128), F32), pltpu.VMEM(hbm[0], BF), pltpu.VMEM(hbm[1], BF), pltpu.VMEM(hbm[2], BF),
        pltpu.VMEM((tp, 1024), BF), pltpu.VMEM((tp, 1536), BF), pltpu.VMEM((tp, 512), BF), pltpu.VMEM((8, tp), F32),
        pltpu.VMEM((tp, 1024), F32), pltpu.VMEM((tp, 1024), BF), pltpu.VMEM((tp, 1024), BF), pltpu.VMEM((tp, 1024), BF),
        pltpu.VMEM((tp, 2048), BF), pltpu.VMEM((tp, 2048), BF), pltpu.VMEM((4, 4, 128, 1024), BF),
        pltpu.SemaphoreType.DMA((n_remote,)), pltpu.SemaphoreType.DMA((n_remote,)), pltpu.SemaphoreType.DMA((n_local,)),
    ]
    return pl.pallas_call(
        functools.partial(forward_kernel, seq),
        out_shape=out_shape,
        in_specs=[VMEM] * 5 + [ANY] * 4,
        out_specs=[ANY] * 4 + [VMEM] + [ANY] * 13,
        scratch_shapes=scratch,
        compiler_params=pltpu.CompilerParams(collective_id=0, has_side_effects=True, vmem_limit_bytes=62 << 20),
        cost_estimate=pl.CostEstimate(flops=25 * 10**9, bytes_accessed=80 * 10**6, transcendentals=10**7),
        name="forward",
    )(x_own, g_own, vec_own, bias_own, ids, qf, ow, up, dn)


BLOCKS = ((128, 1024), (256, 512), (128, 256), (256, 384))


def scatter_kernel(*refs):
    g = refs[:4]
    keep = refs[4:8]
    got = refs[8:12]
    rx, ry, aa, bb, rz, sw = (refs[12 + 4 * i : 16 + 4 * i] for i in range(6))
    ss, rs = refs[36:]
    dps, zs, x_dev, y_dev, c_dev, z_devs = place()
    greet((x_dev, y_dev, c_dev) + z_devs[1:])
    count = [0]

    def remote(src, dst, device):
        i = count[0]
        count[0] += 1
        return pltpu.make_async_remote_copy(src, dst, ss.at[i], rs.at[i], device_id=device, device_id_type=MESH)

    first = {}
    second = {}
    third = {}
    last = {}
    zorder = (1, 2, 3, 0)

    def stage1(m):
        for zr in zorder:
            if zr < 2:
                dev, rels = x_dev, (1, 3)
            else:
                dev, rels = y_dev, (2, 3)
            for slot in (1, 0):
                copy = remote(g[m].at[zr, dps[rels[slot]]], rx[m].at[zr, slot], dev)
                first[m, zr, slot] = copy
                copy.start()

    def stage2(m):
        for zr in zorder:
            dev, rel = (y_dev, 2) if zr < 2 else (x_dev, 1)
            first[m, zr, 1].wait_recv()
            aa[m][zr] = (g[m][zr, dps[rel]].astype(F32) + rx[m][zr, 1].astype(F32)).astype(BF)
            copy = remote(aa[m].at[zr], ry[m].at[zr], dev)
            second[m, zr] = copy
            copy.start()

    def stage3(m):
        for zr in zorder:
            first[m, zr, 0].wait_recv()
            second[m, zr].wait_recv()
            bb[m][zr] = (g[m][zr, dps[0]].astype(F32) + rx[m][zr, 0].astype(F32) + ry[m][zr].astype(F32)).astype(BF)
            if zr > 0:
                copy = remote(bb[m].at[zr], rz[m].at[zr - 1], z_devs[zr])
                third[m, zr] = copy
                copy.start()

    def stage4(m):
        for zr in (1, 2, 3):
            third[m, zr].wait_recv()
        total = bb[m][0].astype(F32) + rz[m][0].astype(F32) + rz[m][1].astype(F32) + rz[m][2].astype(F32)
        rows, cols = BLOCKS[m]
        if m in (1, 3):
            keep[m][...] = total[: rows // 2]
            sw[m][...] = total[rows // 2 :]
        else:
            keep[m][...] = total[:, : cols // 2]
            sw[m][...] = total[:, cols // 2 :]
        copy = remote(sw[m], got[m], c_dev)
        last[m] = copy
        copy.start()

    for m in range(4):
        stage1(m)
    for i in range(6):
        if i < 4:
            stage2(i)
        if 0 <= i - 1 < 4:
            stage3(i - 1)
        if 0 <= i - 2 < 4:
            stage4(i - 2)
    for copies in (first, second, third):
        for copy in copies.values():
            copy.wait_send()
    for copy in last.values():
        copy.wait()


def half_block(m):
    rows, cols = BLOCKS[m]
    return (rows // 2, cols) if m in (1, 3) else (rows, cols // 2)


def scatter_all(grads):
    n = 4 * (8 + 4 + 3 + 1)
    halves = [half_block(m) for m in range(4)]
    scratch = [pltpu.VMEM((4, 2) + b, BF) for b in BLOCKS]
    for lead in (4, 4, 4, 3):
        scratch += [pltpu.VMEM((lead,) + b, BF) for b in BLOCKS]
    scratch += [pltpu.VMEM(h, F32) for h in halves]
    return pl.pallas_call(
        scatter_kernel,
        out_shape=[jax.ShapeDtypeStruct(h, F32) for h in halves * 2],
        in_specs=[VMEM] * 4,
        out_specs=[VMEM] * 8,
        scratch_shapes=scratch + [pltpu.SemaphoreType.DMA((n,)), pltpu.SemaphoreType.DMA((n,))],
        compiler_params=pltpu.CompilerParams(collective_id=1, has_side_effects=True, vmem_limit_bytes=60 << 20),
        name="scatter_grads",
    )(*grads)


def attend_bwd_kernel(seq, n1_ref, q_ref, k_ref, v_ref, o_ref, do_ref, lse_ref, out_ref, dk_acc, dv_acc):
    n1 = n1_ref[0:1, 0:1]
    tp = q_ref.shape[0]
    lane = lax.broadcasted_iota(jnp.int32, (1, 128), 1)
    dk_acc[...] = jnp.zeros_like(dk_acc)
    dv_acc[...] = jnp.zeros_like(dv_acc)

    @pl.loop(0, tp // BQ)
    def _(i):
        start = pl.multiple_of(i * BQ, BQ)
        rows = pl.ds(start, BQ)
        q = q_ref[rows, :]
        do = do_ref[rows, :]
        prod = do.astype(F32) * o_ref[rows, :].astype(F32)
        seg_q = segments((1, BQ), 1, start, n1, seq)
        dq = jnp.zeros((BQ, 128), F32)
        for h in range(2):
            mask = lax.div(lane, 64) == h
            lse = lse_ref[0, h : h + 1, rows]
            delta = jnp.sum(jnp.where(mask, prod, 0.0), axis=1, keepdims=True)
            delta = jnp.transpose(jnp.broadcast_to(delta, (BQ, 128)))[0:1]
            qm = jnp.where(mask, q, BF(0)) * BF(0.125)
            dom = jnp.where(mask, do, BF(0))
            for kb in range(tp // BQ):
                keys = pl.ds(kb * BQ, BQ)
                same = segments((BQ, 1), 0, kb * BQ, n1, seq) == seg_q
                k = k_ref[keys, :]
                s = dot_nt(k, qm)
                p = jnp.where(same, jnp.exp(s - lse), 0.0)
                dp = dot_nt(v_ref[keys, :], dom)
                ds = (p * (dp - delta)).astype(BF)
                dv_acc[keys, :] += dot_nn(p.astype(BF), dom)
                dk_acc[keys, :] += dot_nn(ds, qm)
                dq += jnp.where(mask, dot_tn(ds, k), 0.0)
        out_ref[rows, 0:128] = (dq * 0.125).astype(BF)

    out_ref[:, 128:256] = dk_acc[...].astype(BF)
    out_ref[:, 256:384] = dv_acc[...].astype(BF)


def attend_bwd(n1, qkv, o, do, lse, seq):
    tp = qkv.shape[0]
    spec = lambda j: pl.BlockSpec((tp, 128), lambda i: (0, 3 * i + j))
    one = pl.BlockSpec((tp, 128), lambda i: (0, i))
    return pl.pallas_call(
        functools.partial(attend_bwd_kernel, seq),
        grid=(4,),
        out_shape=jax.ShapeDtypeStruct((tp, 1536), BF),
        in_specs=[VMEM, spec(0), spec(1), spec(2), one, one, pl.BlockSpec((1, 2, tp), lambda i: (i, 0, 0))],
        out_specs=pl.BlockSpec((tp, 384), lambda i: (0, i)),
        scratch_shapes=[pltpu.VMEM((tp, 128), F32)] * 2,
        compiler_params=pltpu.CompilerParams(vmem_limit_bytes=48 << 20),
        name="attend_bwd",
    )(n1, qkv, qkv, qkv, o, do, lse)


def swap_halves(v):
    return jnp.concatenate([v[:, 512:], v[:, :512]], axis=1)


def to_partner(v):
    return lax.ppermute(v, "gx", [(0, 1), (1, 0)])


def norm_stats(values):
    mean = jnp.mean(values, axis=1, keepdims=True)
    inverse = lax.rsqrt(jnp.mean(values * values, axis=1, keepdims=True) - mean * mean + norm_eps)
    return mean, inverse


def norm_pull(grad_norm, hat, inverse, gain):
    scaled = grad_norm * gain
    first = jnp.mean(scaled, axis=1, keepdims=True)
    second = jnp.mean(scaled * hat, axis=1, keepdims=True)
    return inverse * (scaled - first - hat * second)


def local_chip(
    tokens, segment_ids, norm1_gain, norm1_shift, qkv_weight, qv_bias, out_weight, out_bias,
    norm2_gain, norm2_shift, up_weight, up_bias, down_weight, down_bias, cotangent,
):
    seq = segment_ids.shape[1]
    tp = -(-seq // BQ) * BQ
    c = lax.axis_index("gx")
    z = lax.axis_index("gy")
    pad = ((0, tp - seq), (0, 0))
    x_own = jnp.pad(tokens, pad)
    g_own = jnp.pad(cotangent, pad)
    vec_own = jnp.pad(
        jnp.stack([norm1_gain, norm1_shift, out_bias, norm2_gain, norm2_shift, down_bias]), ((0, 10), (0, 0))
    )
    up_mine = lax.dynamic_index_in_dim(up_bias.reshape(4, 2, 128), c, 1, False).reshape(1, 512)
    qv_mine = lax.dynamic_index_in_dim(qv_bias.reshape(2, 2, 128), c, 1, False).reshape(1, 256)
    bias_own = jnp.concatenate([up_mine, jnp.pad(qv_mine, ((0, 0), (0, 256))), jnp.zeros((14, 512), BF)], axis=0)
    qf = qkv_weight.reshape(4, 128, 768)
    ow = out_weight.reshape(2, 4, 32, 512)
    up = up_weight.reshape(4, 128, 1024)
    dn = down_weight.reshape(4, 2, 128, 512)
    (wq, wo, wu, wd, n1, x_oth, g_oth, vec_oth, bias_all, a1, qkv, o, lse, m, a2, u, gp, gd) = forward_all(
        x_own, g_own, vec_own, bias_own, segment_ids, qf, ow, up, dn
    )
    lse = lse.reshape(4, 2, tp)
    gp = gp.astype(F32)
    wq = wq.reshape(4, 1024, 384)
    wo = wo.reshape(512, 1024)
    wu = wu.reshape(4, 1024, 512)
    wd = wd.reshape(4 * 512, 1024)
    vec = jnp.concatenate([vec_own[:6], vec_oth[:6]], axis=1).astype(F32)
    gain1, shift1, ob, gain2, shift2, db = (vec[i] for i in range(6))
    x = jnp.concatenate([x_own, x_oth], axis=1).astype(F32)
    g = jnp.concatenate([g_own, g_oth], axis=1)
    mean1, inv1 = norm_stats(x)
    hat1 = (x - mean1) * inv1
    mean2, inv2 = norm_stats(m)
    hat2 = (m - mean2) * inv2
    part2 = dot_nn(u, wd)
    got2 = to_partner(part2[:, 512:].astype(BF)).astype(F32)
    output = (m[:, :512] + part2[:, :512] + got2 + db[:512])[:seq].astype(BF)
    g_f = g.astype(F32)
    down_bias_grad = jnp.sum(g_f[:, :512], axis=0)
    dh = (dot_nt(g, wd) * gp).astype(BF)
    up_bias_grad = jnp.sum(dh.astype(F32), axis=0)
    gu = dot_tn(a2, dh).astype(BF).reshape(2, 4, 128, 4, 512).transpose(3, 1, 0, 2, 4).reshape(4, 4, 256, 512)
    part3 = jnp.einsum("tzk,zwk->tw", dh.reshape(tp, 4, 512), wu, preferred_element_type=F32)
    da2 = part3 + swap_halves(to_partner(part3.astype(BF))).astype(F32)
    norm2_gain_grad = jnp.sum(da2[:, :512] * hat2[:, :512], axis=0)
    norm2_shift_grad = jnp.sum(da2[:, :512], axis=0)
    dm = g_f + norm_pull(da2, hat2, inv2, gain2)
    dr = dm.astype(BF)
    out_bias_grad = jnp.sum(dr[:, :512].astype(F32), axis=0)
    go = dot_tn(o, dr).astype(BF).reshape(4, 128, 2, 4, 128).transpose(0, 3, 1, 2, 4).reshape(4, 4, 128, 256)
    do = dot_nt(dr, wo).astype(BF)
    dqkv = attend_bwd(n1, qkv, o, do, lse, seq)
    sums = jnp.sum(dqkv.astype(F32), axis=0).reshape(4, 3, 128)
    gq = dot_tn(a1, dqkv).astype(BF).reshape(2, 4, 128, 4, 384).transpose(3, 1, 0, 2, 4).reshape(4, 4, 256, 384)
    part4 = jnp.einsum("tzk,zwk->tw", dqkv.reshape(tp, 4, 384), wq, preferred_element_type=F32)
    da1 = part4 + swap_halves(to_partner(part4.astype(BF))).astype(F32)
    norm1_gain_grad = jnp.sum(da1[:, :512] * hat1[:, :512], axis=0)
    norm1_shift_grad = jnp.sum(da1[:, :512], axis=0)
    input_grad = (dm + norm_pull(da1, hat1, inv1, gain1))[:seq, :512].astype(BF)

    width = jnp.stack([norm1_gain_grad, norm1_shift_grad, out_bias_grad, norm2_gain_grad, norm2_shift_grad, down_bias_grad])
    mine = (jnp.arange(2) == c).astype(F32)
    zrel = jnp.stack([z, flip1(z), flip2(z), 3 - z])
    at_z = (jnp.arange(4)[:, None] == zrel[None, :]).astype(F32)[:, :, None]

    def by_z(v):
        return jnp.sum(at_z * v.reshape(1, 4, -1), axis=1)

    flat = jnp.concatenate(
        [
            (mine[:, None, None] * width[None]).reshape(-1),
            (mine[None, None, :, None] * by_z(up_bias_grad).reshape(4, 4, 1, 128)).reshape(-1),
            (mine[None, None, :, None] * by_z(sums[:, 0::2, :]).reshape(4, 2, 1, 128)).reshape(-1),
        ]
    )
    flat = lax.psum(flat, ("dp", "gx", "gy"))
    width = lax.dynamic_index_in_dim(flat[:6144].reshape(2, 6, 512), c, 0, False)
    up_bias_grad = lax.dynamic_index_in_dim(flat[6144:10240].reshape(4, 1024), z, 0, False)
    qv_bias_grad = lax.dynamic_index_in_dim(flat[10240:].reshape(4, 2, 256), z, 0, False)

    kd, ku, ko, kq, td, tu, to, tq = scatter_all((gd, gu, go, gq))

    def by_core(keep, got, axis):
        return jnp.where(c == 0, jnp.stack([keep, got], axis), jnp.stack([got, keep], axis))

    down_grad = by_core(kd, td, 0).reshape(1, 256, 512)
    up_grad = by_core(ku.reshape(128, 4, 128), tu.reshape(128, 4, 128), 2).reshape(1, 128, 1024)
    out_grad = by_core(ko, to, 0).reshape(256, 1, 128)
    qkv_grad = by_core(kq.reshape(128, 3, 128), tq.reshape(128, 3, 128), 2).reshape(1, 128, 3, 256)
    return (
        output, input_grad, width[0], width[1], qkv_grad, qv_bias_grad, out_grad, width[2],
        width[3], width[4], up_grad, up_bias_grad, down_grad, width[5],
    )


def solution(mesh):
    sizes = dict(mesh.shape)
    chip_rows = sizes["dp"] == 4 and sizes["gx"] == 2 and sizes["gy"] == 4

    def whole(*args):
        rows, seq = args[1].shape
        fast = chip_rows and rows * seq == args[0].shape[0] and rows == 16
        body = local_chip if fast else local
        return jax.shard_map(
            body,
            mesh=mesh,
            in_specs=(
                P(("dp", "gy"), "gx"), P(("dp", "gx"), None), P("gx"), P("gx"), P("gx", None, "gy"), P(None, "gy"),
                P("gy", "gx"), P("gx"), P("gx"), P("gx"), P("gx", "gy"), P("gy"), P("gy", "gx"), P("gx"), P(("dp", "gy"), "gx"),
            ),
            out_specs=(
                P(("dp", "gy"), "gx"), P(("dp", "gy"), "gx"), P("gx"), P("gx"), P("gx", "dp", None, "gy"), P(None, "gy"),
                P("gy", "gx", "dp"), P("gx"), P("gx"), P("gx"), P("gx", "dp", "gy"), P("gy"), P("gy", "dp", "gx"), P("gx"),
            ),
            check_vma=False,
        )(*args)

    return whole
```

```python
import functools
import math

import jax
import jax.numpy as jnp
from jax import lax
from jax.experimental import pallas as pl
from jax.experimental.pallas import tpu as pltpu
from jax.sharding import PartitionSpec as P

D = 1024
HD = 64
MESH = pl.DeviceIdType.MESH
F32 = jnp.float32
BF = jnp.bfloat16
ANY = pl.BlockSpec(memory_space=pl.ANY)
SMEM = pl.BlockSpec(memory_space=pltpu.SMEM)
VMEM = pl.BlockSpec(memory_space=pltpu.VMEM)
norm_eps = 1e-06


def times_right(left, right):
    return jnp.dot(left, right, preferred_element_type=jnp.float32)


def times_back(left, right):
    return lax.dot_general(
        left, right, (((1,), (1,)), ((), ())), preferred_element_type=jnp.float32
    )


def times_outer(left, right):
    return lax.dot_general(
        left, right, (((0,), (0,)), ((), ())), preferred_element_type=jnp.float32
    )


def exact_gelu(values):
    return jax.nn.gelu(values, approximate=False)


def norm_forward(values, gain, shift):
    moments = lax.psum((jnp.sum(values, axis=1), jnp.sum(values * values, axis=1)), "gx")
    mean_val = moments[0] / D
    inverse = lax.rsqrt(moments[1] / D - mean_val * mean_val + norm_eps)
    hat_vals = (values - mean_val[:, None]) * inverse[:, None]
    return (hat_vals * gain + shift, hat_vals, inverse)


def norm_backward(grad_norm, hat_vals, inverse, gain):
    scaled = grad_norm * gain
    moments = lax.psum((jnp.sum(scaled, axis=1), jnp.sum(scaled * hat_vals, axis=1)), "gx")
    grad_in = inverse[:, None] * (
        scaled - (moments[0] / D)[:, None] - hat_vals * (moments[1] / D)[:, None]
    )
    return (grad_in, jnp.sum(grad_norm * hat_vals, axis=0), jnp.sum(grad_norm, axis=0))


def gather_gy(values):
    return lax.all_gather(values, "gy", axis=0, tiled=True)


def gather_gx(values):
    return lax.all_gather(values, "gx", axis=0, tiled=True)


def sum_over_gx(left, multiply):
    keep_rows = left.shape[0] // lax.axis_size("gx")

    def term(start, count):
        return multiply(left)

    return lax.psum_scatter(
        term(jnp.int32(0), keep_rows * lax.axis_size("gx")), "gx", scatter_dimension=0, tiled=True
    )


def sum_over_gy(left, multiply):
    keep_rows = left.shape[0] // lax.axis_size("gy")

    def term(start, count):
        return multiply(left)

    return lax.psum_scatter(
        term(jnp.int32(0), keep_rows * lax.axis_size("gy")), "gy", scatter_dimension=0, tiled=True
    )


def masked_scores(query_part, key_part, segment):
    scaling = 1.0 / math.sqrt(query_part.shape[-1])
    scores = (
        jnp.einsum("qhd,khd->hqk", query_part, key_part, preferred_element_type=jnp.float32)
        * scaling
    )
    same = segment[:, None] == segment[None, :]
    return jnp.where(same[None], scores, -1e30)


def attend_forward(item):
    packed, segment = item
    scores = masked_scores(packed[:, 0], packed[:, 1], segment)
    top_val = jnp.max(scores, axis=-1, keepdims=True)
    expo = jnp.exp(scores - top_val)
    total = jnp.sum(expo, axis=-1, keepdims=True)
    probs = (expo / total).astype(jnp.bfloat16)
    mixed = jnp.einsum("hqk,khd->qhd", probs, packed[:, 2], preferred_element_type=jnp.float32)
    return (mixed.astype(jnp.bfloat16), (top_val + jnp.log(total))[..., 0])


def attend_backward(item):
    packed, segment, log_sum, grad_out = item
    query_part = packed[:, 0]
    key_part = packed[:, 1]
    value_part = packed[:, 2]
    scaling = 1.0 / math.sqrt(query_part.shape[-1])
    scores = masked_scores(query_part, key_part, segment)
    probs = jnp.exp(scores - log_sum[..., None])
    probs_low = probs.astype(jnp.bfloat16)
    grad_prob = jnp.einsum("qhd,khd->hqk", grad_out, value_part, preferred_element_type=jnp.float32)
    grad_value = jnp.einsum("hqk,qhd->khd", probs_low, grad_out, preferred_element_type=jnp.float32)
    delta = jnp.sum(probs * grad_prob, axis=-1, keepdims=True)
    grad_score = (probs * (grad_prob - delta)).astype(jnp.bfloat16)
    grad_query = (
        jnp.einsum("hqk,khd->qhd", grad_score, key_part, preferred_element_type=jnp.float32)
        * scaling
    )
    grad_key = (
        jnp.einsum("hqk,qhd->khd", grad_score, query_part, preferred_element_type=jnp.float32)
        * scaling
    )
    return jnp.stack([grad_query, grad_key, grad_value], axis=1).astype(jnp.bfloat16)


def local(
    tokens,
    segment_ids,
    norm1_gain,
    norm1_shift,
    qkv_weight,
    qv_bias,
    out_weight,
    out_bias,
    norm2_gain,
    norm2_shift,
    up_weight,
    up_bias,
    down_weight,
    down_bias,
    cotangent,
):
    head_width = qkv_weight.shape[2]
    local_heads = head_width // HD
    seq_len = segment_ids.shape[1]
    qkv_flat = qkv_weight.reshape(qkv_weight.shape[0], 3 * head_width)
    gain_one = norm1_gain.astype(jnp.float32)
    gain_two = norm2_gain.astype(jnp.float32)
    resid = tokens.astype(jnp.float32)
    normed, hat_one, inv_one = norm_forward(resid, gain_one, norm1_shift.astype(jnp.float32))
    first_low = normed.astype(jnp.bfloat16)
    first_rows = gather_gy(first_low)
    qkv_all = sum_over_gx(first_rows, lambda piece: times_right(piece, qkv_flat))
    bias_full = jnp.stack([qv_bias[0], jnp.zeros_like(qv_bias[0]), qv_bias[1]]).astype(jnp.float32)
    qkv_low = (qkv_all.reshape(-1, 3, head_width) + bias_full[None]).astype(jnp.bfloat16)
    packed = qkv_low.reshape(-1, seq_len, 3, local_heads, HD)
    mixed, log_sums = lax.map(attend_forward, (packed, segment_ids))
    mixed_low = mixed.reshape(-1, head_width)
    mixed_rows = gather_gx(mixed_low)
    branch = sum_over_gy(
        mixed_rows, lambda piece: times_right(piece, out_weight)
    ) + out_bias.astype(jnp.float32)
    middle = resid + branch
    normed_two, hat_two, inv_two = norm_forward(middle, gain_two, norm2_shift.astype(jnp.float32))
    second_low = normed_two.astype(jnp.bfloat16)
    second_rows = gather_gy(second_low)
    hidden = sum_over_gx(second_rows, lambda piece: times_right(piece, up_weight)) + up_bias.astype(
        jnp.float32
    )
    active, gelu_pull = jax.vjp(exact_gelu, hidden)
    active_low = active.astype(jnp.bfloat16)
    active_rows = gather_gx(active_low)
    branch_two = sum_over_gy(
        active_rows, lambda piece: times_right(piece, down_weight)
    ) + down_bias.astype(jnp.float32)
    output = (middle + branch_two).astype(jnp.bfloat16)
    grad_top = cotangent.astype(jnp.float32)
    down_bias_grad = jnp.sum(grad_top, axis=0)
    grad_top_rows = gather_gy(cotangent)
    down_weight_grad = times_outer(active_rows, grad_top_rows)
    grad_active = sum_over_gx(grad_top_rows, lambda piece: times_back(piece, down_weight))
    grad_hidden = gelu_pull(grad_active)[0].astype(jnp.bfloat16)
    up_bias_grad = jnp.sum(grad_hidden.astype(jnp.float32), axis=0)
    hidden_rows = gather_gx(grad_hidden)
    up_weight_grad = times_outer(second_rows, hidden_rows)
    grad_norm_two = sum_over_gy(hidden_rows, lambda piece: times_back(piece, up_weight))
    grad_in_two, norm2_gain_grad, norm2_shift_grad = norm_backward(
        grad_norm_two, hat_two, inv_two, gain_two
    )
    grad_middle = grad_top + grad_in_two
    grad_branch = grad_middle.astype(jnp.bfloat16)
    out_bias_grad = jnp.sum(grad_branch.astype(jnp.float32), axis=0)
    branch_rows = gather_gy(grad_branch)
    out_weight_grad = times_outer(mixed_rows, branch_rows)
    grad_mixed = sum_over_gx(branch_rows, lambda piece: times_back(piece, out_weight)).astype(
        jnp.bfloat16
    )
    grad_mixed = grad_mixed.reshape(-1, seq_len, local_heads, HD)
    grad_packed = lax.map(attend_backward, (packed, segment_ids, log_sums, grad_mixed))
    grad_qkv = grad_packed.reshape(-1, 3 * head_width)
    third_sums = jnp.sum(grad_qkv.astype(jnp.float32), axis=0).reshape(3, head_width)
    qv_bias_grad = jnp.stack([third_sums[0], third_sums[2]])
    qkv_rows = gather_gx(grad_qkv)
    qkv_weight_grad = times_outer(first_rows, qkv_rows).reshape(qkv_weight.shape)
    grad_norm_one = sum_over_gy(qkv_rows, lambda piece: times_back(piece, qkv_flat))
    grad_in_one, norm1_gain_grad, norm1_shift_grad = norm_backward(
        grad_norm_one, hat_one, inv_one, gain_one
    )
    input_grad = (grad_middle + grad_in_one).astype(jnp.bfloat16)
    qkv_weight_grad, out_weight_grad, up_weight_grad, down_weight_grad = (
        lax.psum_scatter(qkv_weight_grad, "dp", scatter_dimension=0, tiled=True),
        lax.psum_scatter(out_weight_grad, "dp", scatter_dimension=1, tiled=True),
        lax.psum_scatter(up_weight_grad, "dp", scatter_dimension=0, tiled=True),
        lax.psum_scatter(down_weight_grad, "dp", scatter_dimension=0, tiled=True),
    )
    qkv_weight_grad = qkv_weight_grad[None]
    out_weight_grad = out_weight_grad[:, None, :]
    up_weight_grad = up_weight_grad[None]
    down_weight_grad = down_weight_grad[None]
    (
        norm1_gain_grad,
        norm1_shift_grad,
        norm2_gain_grad,
        norm2_shift_grad,
        out_bias_grad,
        down_bias_grad,
    ) = lax.psum(
        (
            norm1_gain_grad,
            norm1_shift_grad,
            norm2_gain_grad,
            norm2_shift_grad,
            out_bias_grad,
            down_bias_grad,
        ),
        ("dp", "gy"),
    )
    up_bias_grad, qv_bias_grad = lax.psum((up_bias_grad, qv_bias_grad), ("dp", "gx"))
    return (
        output,
        input_grad,
        norm1_gain_grad,
        norm1_shift_grad,
        qkv_weight_grad,
        qv_bias_grad,
        out_weight_grad,
        out_bias_grad,
        norm2_gain_grad,
        norm2_shift_grad,
        up_weight_grad,
        up_bias_grad,
        down_weight_grad,
        down_bias_grad,
    )


def flip1(i):
    return i + 1 - 2 * lax.rem(i, 2)


def flip2(i):
    return i + 2 - 4 * lax.div(i, 2)


def place():
    dp, c, z = lax.axis_index("dp"), lax.axis_index("gx"), lax.axis_index("gy")
    dps = (dp, flip1(dp), flip2(dp), 3 - dp)
    zs = (z, flip1(z), flip2(z), 3 - z)
    x_dev = (dps[1], c, z)
    y_dev = (dps[2], c, z)
    c_dev = (dp, 1 - c, z)
    z_devs = (None,) + tuple((dp, c, zz) for zz in zs[1:])
    return dps, zs, x_dev, y_dev, c_dev, z_devs


def greet(devices):
    barrier = pltpu.get_barrier_semaphore()
    for device in devices:
        pl.semaphore_signal(barrier, inc=1, device_id=device, device_id_type=MESH)
    pl.semaphore_wait(barrier, len(devices))


WINDOW = 3
ORDER = tuple((m, k) for m in range(4) for k in (1, 2, 3))
N_PAIR = 9


class Sems:
    def __init__(self, ss, rs):
        self.ss, self.rs, self.n = ss, rs, 0

    def remote(self, src, dst, device):
        i = self.n
        self.n += 1
        return pltpu.make_async_remote_copy(
            src, dst, self.ss.at[i], self.rs.at[i], device_id=device, device_id_type=MESH
        )


class Locals:
    def __init__(self, ls):
        self.ls, self.n, self.open = ls, 0, []

    def copy(self, src, dst):
        copy = pltpu.make_async_copy(src, dst, self.ls.at[self.n])
        self.n += 1
        copy.start()
        return copy

    def later(self, src, dst):
        self.open.append(self.copy(src, dst))

    def close(self):
        for copy in self.open:
            copy.wait()


def weight_cuts(side, raw, full, crel):
    qf, ow, up, dn = raw
    wq, wo, wu, wd = full
    cols = pl.ds(crel * 512, 512)
    cuts = [[], [], [], []]
    for t in range(3):
        off = pl.multiple_of(t * 256 + side * 128, 128)
        cuts[0].append((qf.at[:, :, pl.ds(off, 128)], wq.at[0, crel, :, :, pl.ds(t * 128, 128)]))
    cuts[1].append((ow.at[side], wo.at[0, :, :, cols]))
    for t in range(4):
        off = pl.multiple_of(t * 256 + side * 128, 128)
        cuts[2].append((up.at[:, :, pl.ds(off, 128)], wu.at[0, crel, :, :, pl.ds(t * 128, 128)]))
    cuts[3].append((dn.at[:, side], wd.at[0, crel]))
    return cuts


def gather_steps(sems, loc, here, raw, full):
    dps, zs, x_dev, y_dev, c_dev, z_devs, c = here
    d = dps[0]
    wq, wo, wu, wd = full
    pieces = (
        lambda k, dd: wq.at[k, :, dd],
        lambda k, dd: wo.at[k, dd],
        lambda k, dd: wu.at[k, :, dd],
        lambda k, dd: wd.at[k, :, dd],
    )
    theirs = [[sems.remote(src, dst, c_dev) for src, dst in group] for group in weight_cuts(1 - c, raw, full, 1)]
    copies = {}
    own = []
    ready = set()

    def pair_start():
        for m, group in enumerate(weight_cuts(c, raw, full, 0)):
            for copy in theirs[m]:
                copy.start()
            own.append([loc.copy(src, dst) for src, dst in group])

    def own_ready(m):
        if m not in ready:
            ready.add(m)
            for copy in own[m]:
                copy.wait()
            for copy in theirs[m]:
                copy.wait_recv()

    def z_send(s):
        m, k = ORDER[s]
        own_ready(m)
        src = pieces[m](0, d)
        copy = sems.remote(src, pieces[m](k, d), z_devs[k])
        copies["z", m, k] = copy
        copy.start()

    def forward(s):
        m, k = ORDER[s]
        if (k == 2) == (m in (0, 2)):
            copies["x", m, k].wait_recv()
            src = pieces[m](k, dps[1])
            copy = sems.remote(src, src, y_dev)
        else:
            copies["y", m, k].wait_recv()
            src = pieces[m](k, dps[2])
            copy = sems.remote(src, src, x_dev)
        copies["d", m, k] = copy
        copy.start()

    def steps():
        for s in range(len(ORDER)):
            m, k = ORDER[s]
            copies["z", m, k].wait_recv()
            src = pieces[m](k, d)
            for axis, dev in (("x", x_dev), ("y", y_dev)):
                copy = sems.remote(src, src, dev)
                copies[axis, m, k] = copy
                copy.start()
            if s + WINDOW < len(ORDER):
                copies["z", m, k].wait_send()
                z_send(s + WINDOW)
            if s > 0:
                forward(s - 1)
            yield
        forward(len(ORDER) - 1)
        yield

    def slot_ready(m, k):
        if k == 0:
            own_ready(m)
            return
        copies["y" if (k == 2) == (m in (0, 2)) else "x", m, k].wait_recv()
        copies["d", m, k].wait_recv()

    def close():
        for group in theirs:
            for copy in group:
                copy.wait_send()
        for s, (m, k) in enumerate(ORDER):
            if s + WINDOW >= len(ORDER):
                copies["z", m, k].wait_send()
            for axis in "xyd":
                copies[axis, m, k].wait_send()

    return pair_start, z_send, steps(), slot_ready, close


def dot_nt(a, b):
    return lax.dot_general(a, b, (((1,), (1,)), ((), ())), preferred_element_type=F32)


def dot_tn(a, b):
    return lax.dot_general(a, b, (((0,), (0,)), ((), ())), preferred_element_type=F32)


def dot_nn(a, b):
    return lax.dot_general(a, b, (((1,), (0,)), ((), ())), preferred_element_type=F32)


BQ = 256


def segments(shape, axis, start, n1, seq):
    pos = (lax.broadcasted_iota(jnp.int32, shape, axis) + start).astype(F32)
    return (pos >= n1).astype(F32) + (pos >= float(seq)).astype(F32)


def attend_fwd_rows(qkv, o, lse_ref, zr, lo, hi, n1, seq):
    tp = qkv.shape[0]
    lane = lax.broadcasted_iota(jnp.int32, (1, 128), 1)
    base = zr * 384

    @pl.loop(lo, hi)
    def _(i):
        start = pl.multiple_of(i * BQ, BQ)
        rows = pl.ds(start, BQ)
        q = qkv[rows, base : base + 128] * BF(0.125)
        same = segments((BQ, 1), 0, start, n1, seq) == segments((1, tp), 1, 0, n1, seq)
        out = jnp.zeros((BQ, 128), F32)
        for h in range(2):
            mask = lax.div(lane, 64) == h
            s = dot_nt(jnp.where(mask, q, BF(0)), qkv[:, base + 128 : base + 256])
            s = jnp.where(same, s, -1e30)
            top = jnp.max(s, axis=1, keepdims=True)
            e = jnp.exp(s - top)
            total = jnp.sum(e, axis=1, keepdims=True)
            mixed = dot_nn(e.astype(BF), qkv[:, base + 256 : base + 384]) / total
            out = jnp.where(mask, mixed, out)
            lse = jnp.broadcast_to(top + jnp.log(total), (BQ, 128))
            lse_ref[2 * zr + h : 2 * zr + h + 1, rows] = jnp.transpose(lse)[0:1]
        o[rows, zr * 128 : zr * 128 + 128] = out.astype(BF)


def halves_mean(a, b):
    return (jnp.sum(a, axis=1, keepdims=True) + jnp.sum(b, axis=1, keepdims=True)) * (1.0 / D)


def forward_kernel(
    seq, x_own, g_own, vec_own, bias_own, ids, qf, ow, up, dn,
    wq, wo, wu, wd, n1_out, x_out, g_out, vec_out, bias_out, a1_out, qkv_out, o_out, lse_out, m_out, a2_out, gp_out, gd_out, y_out,
    x_oth, g_oth, vec_oth, bias_all, cnt, wq_v, wo_v, wu_v, wd_v, a1, qkv, o, lse, m, pb, pr, pr2, a2, u, gp, gd,
    ss, rs, ls,
):
    tp = x_own.shape[0]
    nb = tp // BQ
    dps, zs, x_dev, y_dev, c_dev, z_devs = place()
    c, z = lax.axis_index("gx"), zs[0]
    sems, loc = Sems(ss, rs), Locals(ls)
    pair_start, z_send, steps, slot_ready, close = gather_steps(
        sems, loc, (dps, zs, x_dev, y_dev, c_dev, z_devs, c), (qf, ow, up, dn), (wq, wo, wu, wd)
    )

    def poll(n=1):
        for _ in range(n):
            next(steps, None)

    ids_low = (ids[...] == 0).astype(F32)
    for r in range(2):
        cnt[0, r] = jnp.broadcast_to(jnp.sum(ids_low[r : r + 1], axis=1, keepdims=True), (8, 128))
    bias_all[0] = bias_own[...]
    greet((x_dev, y_dev, c_dev) + z_devs[1:])
    pair_start()
    x_copy = sems.remote(x_own, x_oth, c_dev)
    x_copy.start()
    small = [sems.remote(vec_own, vec_oth, c_dev), sems.remote(cnt.at[0], cnt.at[1], c_dev)]
    small += [sems.remote(bias_own, bias_all.at[k], z_devs[k]) for k in (1, 2, 3)]
    for copy in small:
        copy.start()
    g_copy = sems.remote(g_own, g_oth, c_dev)
    g_copy.start()
    for s in range(WINDOW):
        z_send(s)
    for copy in small:
        copy.wait_recv()
    x_copy.wait_recv()
    vec = [(vec_own[i : i + 1, :].astype(F32), vec_oth[i : i + 1, :].astype(F32)) for i in range(6)]
    n1 = cnt[lax.rem(lax.div(z, 2) + c, 2), lax.rem(z, 2)]
    n1_out[...] = n1
    n1 = n1[0:1, 0:1]
    loc.later(x_oth, x_out)
    loc.later(vec_oth, vec_out)
    loc.later(bias_all, bias_out)

    @pl.loop(0, nb)
    def _(i):
        rows = pl.ds(pl.multiple_of(i * BQ, BQ), BQ)
        xo, xt = x_own[rows, :].astype(F32), x_oth[rows, :].astype(F32)
        mean = halves_mean(xo, xt)
        inv = lax.rsqrt(halves_mean(xo * xo, xt * xt) - mean * mean + norm_eps)
        a1[rows, 0:512] = ((xo - mean) * inv * vec[0][0] + vec[1][0]).astype(BF)
        a1[rows, 512:1024] = ((xt - mean) * inv * vec[0][1] + vec[1][1]).astype(BF)

    loc.later(a1, a1_out)
    for zr in range(4):
        slot_ready(0, zr)
        loc.copy(wq.at[zr], wq_v.at[zr]).wait()
        qb, vb = bias_all[zr, 1:2, 0:128].astype(F32), bias_all[zr, 1:2, 128:256].astype(F32)
        bias = jnp.concatenate([qb, jnp.zeros_like(qb), vb], axis=1)

        @pl.loop(0, nb)
        def _(i):
            rows = pl.ds(pl.multiple_of(i * BQ, BQ), BQ)
            qkv[rows, zr * 384 : zr * 384 + 384] = (dot_nn(a1[rows, :], wq_v[zr].reshape(1024, 384)) + bias).astype(BF)

        if zr == 0:
            poll()
        attend_fwd_rows(qkv, o, lse, zr, 0, 2, n1, seq)
        poll()
        attend_fwd_rows(qkv, o, lse, zr, 2, nb, n1, seq)
        if zr < 3:
            poll()
    loc.later(qkv, qkv_out)
    loc.later(o, o_out)
    loc.later(lse, lse_out)
    for zr in range(4):
        slot_ready(1, zr)
    loc.copy(wo, wo_v).wait()
    swaps = []
    for i in range(nb):
        rows = pl.ds(i * BQ, BQ)
        part = dot_nn(o[rows, :], wo_v[...].reshape(512, 1024))
        pb[rows, 0:512] = part[:, 512:].astype(BF)
        pb[rows, 512:1024] = part[:, :512].astype(BF)
        copy = sems.remote(pb.at[rows], pr.at[rows], c_dev)
        copy.start()
        swaps.append(copy)
        m[rows, :] = part
    poll()
    for i in range(nb):
        rows = pl.ds(i * BQ, BQ)
        swaps[i].wait_recv()
        mo = x_own[rows, :].astype(F32) + m[rows, 0:512] + pr[rows, 0:512].astype(F32) + vec[2][0]
        mt = x_oth[rows, :].astype(F32) + m[rows, 512:1024] + pr[rows, 512:1024].astype(F32) + vec[2][1]
        mean = halves_mean(mo, mt)
        inv = lax.rsqrt(halves_mean(mo * mo, mt * mt) - mean * mean + norm_eps)
        m[rows, 0:512] = mo
        m[rows, 512:1024] = mt
        a2[rows, 0:512] = ((mo - mean) * inv * vec[3][0] + vec[4][0]).astype(BF)
        a2[rows, 512:1024] = ((mt - mean) * inv * vec[3][1] + vec[4][1]).astype(BF)
    m_copy = loc.copy(m, m_out)
    loc.later(a2, a2_out)
    g_copy.wait_recv()
    loc.later(g_oth, g_out)
    for zr in range(4):
        slot_ready(2, zr)
        loc.copy(wu.at[zr], wu_v.at[zr]).wait()
        bias = bias_all[zr, 0:1, :].astype(F32)

        @pl.loop(0, nb)
        def _(i):
            rows = pl.ds(pl.multiple_of(i * BQ, BQ), BQ)
            h = dot_nn(a2[rows, :], wu_v[zr].reshape(1024, 512)) + bias
            cdf = 0.5 * (1.0 + lax.erf(h * math.sqrt(0.5)))
            u[rows, zr * 512 : zr * 512 + 512] = (h * cdf).astype(BF)
            gp[rows, zr * 512 : zr * 512 + 512] = (cdf + h * jnp.exp(-0.5 * h * h) * (1.0 / math.sqrt(2 * math.pi))).astype(BF)

        for j, gref in enumerate((g_own, g_oth)):
            gd[zr, :, :, 512 * j : 512 * j + 512] = (
                dot_tn(u[:, zr * 512 : zr * 512 + 512], gref[...]).astype(BF).reshape(4, 128, 512)
            )
        loc.later(gd.at[zr], gd_out.at[zr])
        poll()
    loc.later(gp, gp_out)
    m_copy.wait()
    for copy in swaps:
        copy.wait_send()
    poll(3)

    def add_down(zrs, rows, final):
        own = other = None
        for zr in zrs:
            block = u[rows, zr * 512 : zr * 512 + 512]
            to_own, to_other = dot_nn(block, wd_v[zr, 0].reshape(512, 512)), dot_nn(block, wd_v[zr, 1].reshape(512, 512))
            own, other = (to_own, to_other) if own is None else (own + to_own, other + to_other)
        m[rows, 0:512] += own
        if final:
            pb[rows, 0:512] = (m[rows, 512:1024] + other).astype(BF)
        else:
            m[rows, 512:1024] = other

    for zr in range(3):
        slot_ready(3, zr)
    early = [loc.copy(wd.at[zr], wd_v.at[zr]) for zr in range(3)]
    for copy in early:
        copy.wait()

    @pl.loop(0, nb)
    def _(i):
        add_down((0, 1, 2), pl.ds(pl.multiple_of(i * BQ, BQ), BQ), False)

    poll(99)
    slot_ready(3, 3)
    loc.copy(wd.at[3], wd_v.at[3]).wait()
    outs = []
    for i in range(nb):
        rows = pl.ds(i * BQ, BQ)
        add_down((3,), rows, True)
        copy = sems.remote(pb.at[rows, pl.ds(0, 512)], pr2.at[rows], c_dev)
        copy.start()
        outs.append(copy)
    for i in range(nb):
        rows = pl.ds(i * BQ, BQ)
        outs[i].wait()
        y_out[rows, :] = (m[rows, 0:512] + pr2[rows, :].astype(F32) + vec[5][0]).astype(BF)
    for copy in small + [x_copy, g_copy]:
        copy.wait_send()
    close()
    loc.close()


def forward_all(x_own, g_own, vec_own, bias_own, ids, qf, ow, up, dn):
    tp = x_own.shape[0]
    seq = ids.shape[1]
    n_remote = N_PAIR + 7 + 48 + 2 * (tp // BQ)
    n_local = N_PAIR + 32
    hbm = [
        (4, 2, 4, 128, 384), (4, 4, 32, 1024), (4, 2, 4, 128, 512), (4, 2, 4, 128, 512),
    ]
    sds = jax.ShapeDtypeStruct
    out_shape = [sds(s, BF) for s in hbm] + [
        sds((8, 128), F32), sds((tp, 512), BF), sds((tp, 512), BF), sds(vec_own.shape, BF), sds((4,) + bias_own.shape, BF),
        sds((tp, 1024), BF), sds((tp, 1536), BF), sds((tp, 512), BF), sds((8, tp), F32), sds((tp, 1024), F32),
        sds((tp, 1024), BF), sds((tp, 2048), BF), sds((4, 4, 128, 1024), BF), sds((tp, 512), BF),
    ]
    scratch = [
        pltpu.VMEM((tp, 512), BF), pltpu.VMEM((tp, 512), BF), pltpu.VMEM(vec_own.shape, BF), pltpu.VMEM((4,) + bias_own.shape, BF),
        pltpu.VMEM((2, 2, 8, 128), F32), pltpu.VMEM(hbm[0], BF), pltpu.VMEM(hbm[1], BF), pltpu.VMEM(hbm[2], BF), pltpu.VMEM(hbm[3], BF),
        pltpu.VMEM((tp, 1024), BF), pltpu.VMEM((tp, 1536), BF), pltpu.VMEM((tp, 512), BF), pltpu.VMEM((8, tp), F32),
        pltpu.VMEM((tp, 1024), F32), pltpu.VMEM((tp, 1024), BF), pltpu.VMEM((tp, 1024), BF), pltpu.VMEM((tp, 512), BF), pltpu.VMEM((tp, 1024), BF),
        pltpu.VMEM((tp, 2048), BF), pltpu.VMEM((tp, 2048), BF), pltpu.VMEM((4, 4, 128, 1024), BF),
        pltpu.SemaphoreType.DMA((n_remote,)), pltpu.SemaphoreType.DMA((n_remote,)), pltpu.SemaphoreType.DMA((n_local,)),
    ]
    return pl.pallas_call(
        functools.partial(forward_kernel, seq),
        out_shape=out_shape,
        in_specs=[VMEM] * 5 + [ANY] * 4,
        out_specs=[ANY] * 4 + [VMEM] + [ANY] * 12 + [VMEM],
        scratch_shapes=scratch,
        compiler_params=pltpu.CompilerParams(collective_id=0, has_side_effects=True, vmem_limit_bytes=62 << 20),
        cost_estimate=pl.CostEstimate(flops=25 * 10**9, bytes_accessed=80 * 10**6, transcendentals=10**7),
        name="forward",
    )(x_own, g_own, vec_own, bias_own, ids, qf, ow, up, dn)


BLOCKS = ((128, 1024), (256, 512), (128, 256), (256, 384))
ZORDER = (1, 2, 3, 0)


def half_block(m):
    rows, cols = BLOCKS[m]
    return (rows // 2, cols) if m in (1, 3) else (rows, cols // 2)


class Scatter:
    def __init__(self, sems, here, g, first_src, rx, ry, rz, sw, keep, got):
        self.sems, self.g, self.first_src = sems, g, first_src
        self.dps, self.zs, self.x_dev, self.y_dev, self.c_dev, self.z_devs = here
        self.rx, self.ry, self.rz, self.sw, self.keep, self.got = rx, ry, rz, sw, keep, got
        self.first, self.second, self.third, self.last = {}, {}, {}, {}

    def stage1(self, m, zr):
        dev, rels = (self.x_dev, (1, 3)) if zr < 2 else (self.y_dev, (2, 3))
        for slot in (1, 0):
            src = self.first_src[m].at[zr, self.dps[rels[slot]]]
            copy = self.sems.remote(src, self.rx[m].at[zr, slot], dev)
            self.first[m, zr, slot] = copy
            copy.start()

    def stage2(self, m, zr):
        dev, rel = (self.y_dev, 2) if zr < 2 else (self.x_dev, 1)
        g, dd = self.g[m], self.dps[rel]
        self.first[m, zr, 1].wait_recv()
        g[zr, dd] = (g[zr, dd].astype(F32) + self.rx[m][zr, 1].astype(F32)).astype(BF)
        copy = self.sems.remote(g.at[zr, dd], self.ry[m].at[zr], dev)
        self.second[m, zr] = copy
        copy.start()

    def stage3(self, m, zr):
        g, dd = self.g[m], self.dps[0]
        self.first[m, zr, 0].wait_recv()
        self.second[m, zr].wait_recv()
        g[zr, dd] = (g[zr, dd].astype(F32) + self.rx[m][zr, 0].astype(F32) + self.ry[m][zr].astype(F32)).astype(BF)
        if zr > 0:
            copy = self.sems.remote(g.at[zr, dd], self.rz[m].at[zr - 1], self.z_devs[zr])
            self.third[m, zr] = copy
            copy.start()

    def stage4(self, m):
        for zr in (1, 2, 3):
            self.third[m, zr].wait_recv()
        rz = self.rz[m]
        total = self.g[m][0, self.dps[0]].astype(F32) + rz[0].astype(F32) + rz[1].astype(F32) + rz[2].astype(F32)
        rows, cols = BLOCKS[m]
        if m in (1, 3):
            self.keep[m][...] = total[: rows // 2]
            self.sw[m][...] = total[rows // 2 :]
        else:
            self.keep[m][...] = total[:, : cols // 2]
            self.sw[m][...] = total[:, cols // 2 :]
        copy = self.sems.remote(self.sw[m], self.got[m], self.c_dev)
        self.last[m] = copy
        copy.start()

    def close(self):
        for copies in (self.first, self.second, self.third):
            for copy in copies.values():
                copy.wait_send()
        for copy in self.last.values():
            copy.wait()


def attend_bwd_rows(big, do_ref, lse_ref, dk_acc, dv_acc, zr, lo, hi, n1, seq):
    tp = big.shape[0]
    lane = lax.broadcasted_iota(jnp.int32, (1, 128), 1)
    base = zr * 384
    ocol = 1536 + zr * 128

    @pl.loop(lo, hi)
    def _(i):
        start = pl.multiple_of(i * BQ, BQ)
        rows = pl.ds(start, BQ)
        q = big[rows, base : base + 128]
        do = do_ref[rows, zr * 128 : zr * 128 + 128]
        prod = do.astype(F32) * big[rows, ocol : ocol + 128].astype(F32)
        seg_q = segments((1, BQ), 1, start, n1, seq)
        dq = jnp.zeros((BQ, 128), F32)
        for h in range(2):
            mask = lax.div(lane, 64) == h
            lse = lse_ref[2 * zr + h : 2 * zr + h + 1, rows]
            delta = jnp.sum(jnp.where(mask, prod, 0.0), axis=1, keepdims=True)
            delta = jnp.transpose(jnp.broadcast_to(delta, (BQ, 128)))[0:1]
            qm = jnp.where(mask, q, BF(0)) * BF(0.125)
            dom = jnp.where(mask, do, BF(0))
            for kb in range(tp // BQ):
                keys = pl.ds(kb * BQ, BQ)
                same = segments((BQ, 1), 0, kb * BQ, n1, seq) == seg_q
                k = big[keys, base + 128 : base + 256]
                s = dot_nt(k, qm)
                p = jnp.where(same, jnp.exp(s - lse), 0.0)
                dp = dot_nt(big[keys, base + 256 : base + 384], dom)
                ds = (p * (dp - delta)).astype(BF)
                dv_acc[keys, :] += dot_nn(p.astype(BF), dom)
                dk_acc[keys, :] += dot_nn(ds, qm)
                dq += jnp.where(mask, dot_tn(ds, k), 0.0)
        big[rows, base : base + 128] = (dq * 0.125).astype(BF)


def backward_kernel(
    seq, x_own, x_oth, g_own_h, g_oth_h, vec_own, vec_oth, n1_ref, a1_h, qkv_h, o_h, lse, m_h, a2_h, gp_h, gd_h, wq_h, wo_h, wu_h, wd_h,
    grad_out, small_out, keep0, keep1, keep2, keep3, got0, got1, got2, got3,
    big, ga, gb, wbuf, wo_v, part, pb, pr, mbuf, act, dm, dk_acc, dv_acc, vsum, vdp, vz, vzr, vhalf, vc,
    gd, gu, go, gq, rx0, rx1, rx2, rx3, ry0, ry1, ry2, ry3, rz0, rz1, rz2, rz3, sw0, sw1, sw2, sw3,
    ss, rs, ls, free,
):
    tp = big.shape[0]
    nb = tp // BQ
    here = place()
    dps, zs, x_dev, y_dev, c_dev, z_devs = here
    c, z = lax.axis_index("gx"), zs[0]
    xy_dev = (dps[3], c, z)
    sems, loc = Sems(ss, rs), Locals(ls)
    scatter = Scatter(
        sems, here, (gd, gu, go, gq), (gd_h, gu, go, gq), (rx0, rx1, rx2, rx3), (ry0, ry1, ry2, ry3), (rz0, rz1, rz2, rz3),
        (sw0, sw1, sw2, sw3), (keep0, keep1, keep2, keep3), (got0, got1, got2, got3),
    )

    def rs_steps():
        two = lambda m: [(2, m, zr) for zr in ZORDER]
        three = lambda m: [(3, m, zr) for zr in ZORDER] + [(4, m, 0)]
        plan = two(0) + two(1) + three(0) + two(2) + three(1) + two(3)[:2] + three(2) + two(3)[2:] + three(3)
        for stage, m, zr in plan:
            if stage == 2:
                scatter.stage2(m, zr)
            elif stage == 3:
                scatter.stage3(m, zr)
            else:
                scatter.stage4(m)
            yield

    steps = rs_steps()

    def poll(n):
        for _ in range(n):
            next(steps, None)

    ga_in, gb_in = loc.copy(g_own_h, ga), loc.copy(g_oth_h, gb)
    wd_in, gp_in = loc.copy(wd_h, wbuf), loc.copy(gp_h, big)
    a2_in = loc.copy(a2_h, act)
    gd_in, wo_in = loc.copy(gd_h, gd), loc.copy(wo_h, wo_v)
    m_in = {}

    def load_m(i):
        m_in[i] = loc.copy(m_h.at[pl.ds(i * BQ, BQ)], mbuf.at[i % 2])

    load_m(0)
    load_m(1)
    vec = [(vec_own[i : i + 1, :].astype(F32), vec_oth[i : i + 1, :].astype(F32)) for i in range(6)]
    n1 = n1_ref[0:1, 0:1]
    vsum[...] = jnp.zeros_like(vsum)
    vhalf[...] = jnp.zeros_like(vhalf)
    greet((x_dev, y_dev, xy_dev, c_dev) + z_devs[1:])
    for zr in ZORDER:
        scatter.stage1(0, zr)
    for copy in (ga_in, gb_in, wd_in, gp_in):
        copy.wait()

    for zr in range(4):

        @pl.loop(0, nb)
        def _(i):
            rows = pl.ds(pl.multiple_of(i * BQ, BQ), BQ)
            du = dot_nt(ga[rows, :], wbuf[zr, 0].reshape(512, 512)) + dot_nt(gb[rows, :], wbuf[zr, 1].reshape(512, 512))
            dh = (du * big[rows, zr * 512 : zr * 512 + 512].astype(F32)).astype(BF)
            big[rows, zr * 512 : zr * 512 + 512] = dh
            vsum[zr, 6:7, :] += jnp.sum(dh.astype(F32), axis=0, keepdims=True)

    wu_in = loc.copy(wu_h, wbuf)
    a2_in.wait()
    for zr in ZORDER:
        for j in range(2):
            block = dot_tn(act[:, 512 * j : 512 * j + 512], big[:, zr * 512 : zr * 512 + 512])
            gu[zr, :, 128 * j : 128 * j + 128, :] = block.astype(BF).reshape(4, 128, 512)
        scatter.stage1(1, zr)
    gd_in.wait()
    poll(2)
    wu_in.wait()
    swaps = []
    for i in range(nb):
        rows = pl.ds(i * BQ, BQ)
        total = dot_nt(big[rows, 0:512], wbuf[0].reshape(1024, 512))
        for zr in range(1, 4):
            total += dot_nt(big[rows, zr * 512 : zr * 512 + 512], wbuf[zr].reshape(1024, 512))
        pb[rows, 0:512] = total[:, 512:].astype(BF)
        pb[rows, 512:1024] = total[:, :512].astype(BF)
        copy = sems.remote(pb.at[rows], pr.at[rows], c_dev)
        copy.start()
        swaps.append(copy)
        part[rows, :] = total
    qkv_in = loc.copy(qkv_h, big.at[:, pl.ds(0, 1536)])
    o_in = loc.copy(o_h, big.at[:, pl.ds(1536, 512)])
    wq_in = loc.copy(wq_h, wbuf.at[:, :, :, :, pl.ds(0, 384)])
    poll(2)
    for i in range(nb):
        rows = pl.ds(i * BQ, BQ)
        m_in[i].wait()
        mo, mt = mbuf[i % 2, :, 0:512], mbuf[i % 2, :, 512:1024]
        mean = halves_mean(mo, mt)
        inv = lax.rsqrt(halves_mean(mo * mo, mt * mt) - mean * mean + norm_eps)
        ho, ht = (mo - mean) * inv, (mt - mean) * inv
        if i + 2 < nb:
            load_m(i + 2)
        swaps[i].wait_recv()
        do_, dt = part[rows, 0:512] + pr[rows, 0:512].astype(F32), part[rows, 512:1024] + pr[rows, 512:1024].astype(F32)
        bo, bt = do_ * vec[3][0], dt * vec[3][1]
        first, second = halves_mean(bo, bt), halves_mean(bo * ho, bt * ht)
        go_, gt = ga[rows, :].astype(F32), gb[rows, :].astype(F32)
        dmo = go_ + inv * (bo - first - ho * second)
        dmt = gt + inv * (bt - first - ht * second)
        dm[rows, :] = dmo
        act[rows, 0:512] = dmo.astype(BF)
        act[rows, 512:1024] = dmt.astype(BF)
        vsum[0, 2:3, :] += jnp.sum(dmo.astype(BF).astype(F32), axis=0, keepdims=True)
        vsum[0, 3:4, :] += jnp.sum(do_ * ho, axis=0, keepdims=True)
        vsum[0, 4:5, :] += jnp.sum(do_, axis=0, keepdims=True)
        vsum[0, 5:6, :] += jnp.sum(go_, axis=0, keepdims=True)
    pl.semaphore_signal(free, inc=1, device_id=c_dev, device_id_type=MESH)
    wo_in.wait()
    o_in.wait()
    for j in range(2):
        block = dot_tn(big[:, 1536:2048], act[:, 512 * j : 512 * j + 512]).astype(BF)
        for dd in range(4):
            go[:, dd, :, 128 * j : 128 * j + 128] = block[:, 128 * dd : 128 * dd + 128].reshape(4, 128, 128)
    for zr in ZORDER:
        scatter.stage1(2, zr)

    @pl.loop(0, nb)
    def _(i):
        rows = pl.ds(pl.multiple_of(i * BQ, BQ), BQ)
        ga[rows, :] = dot_nt(act[rows, :], wo_v[...].reshape(512, 1024)).astype(BF)

    a1_in = loc.copy(a1_h, act)
    qkv_in.wait()
    poll(2)
    for step, zr in enumerate(ZORDER):
        dk_acc[...] = jnp.zeros_like(dk_acc)
        dv_acc[...] = jnp.zeros_like(dv_acc)
        attend_bwd_rows(big, ga, lse, dk_acc, dv_acc, zr, 0, 2, n1, seq)
        poll(3 if step == 3 else 4)
        attend_bwd_rows(big, ga, lse, dk_acc, dv_acc, zr, 2, nb, n1, seq)
        base = zr * 384
        big[:, base + 128 : base + 256] = dk_acc[...].astype(BF)
        big[:, base + 256 : base + 384] = dv_acc[...].astype(BF)
        for j in (0, 2):
            cols = big[:, base + 128 * j : base + 128 * j + 128].astype(F32)
            vsum[zr, 7:8, 64 * j : 64 * j + 128] = jnp.sum(cols, axis=0, keepdims=True)
        if step == 0:
            a1_in.wait()
        for j in range(2):
            block = dot_tn(act[:, 512 * j : 512 * j + 512], big[:, base : base + 384])
            gq[zr, :, 128 * j : 128 * j + 128, :] = block.astype(BF).reshape(4, 128, 384)
        scatter.stage1(3, zr)
        poll(1 if step == 3 else 3)
    xa_in, xb_in = loc.copy(x_own, ga), loc.copy(x_oth, gb)
    wq_in.wait()
    for copy in swaps:
        copy.wait_send()
    pl.semaphore_wait(free, 1)
    xa_in.wait()
    xb_in.wait()
    swaps = []
    for i in range(nb):
        rows = pl.ds(i * BQ, BQ)
        total = dot_nt(big[rows, 0:384], wbuf[0, :, :, :, 0:384].reshape(1024, 384))
        for zr in range(1, 4):
            total += dot_nt(big[rows, zr * 384 : zr * 384 + 384], wbuf[zr, :, :, :, 0:384].reshape(1024, 384))
        pb[rows, 0:512] = total[:, 512:].astype(BF)
        pb[rows, 512:1024] = total[:, :512].astype(BF)
        copy = sems.remote(pb.at[rows], pr.at[rows], c_dev)
        copy.start()
        swaps.append(copy)
        part[rows, :] = total
        xo, xt = ga[rows, :].astype(F32), gb[rows, :].astype(F32)
        mean = halves_mean(xo, xt)
        inv = lax.rsqrt(halves_mean(xo * xo, xt * xt) - mean * mean + norm_eps)
        vsum[0, 0:1, :] += jnp.sum(total[:, :512] * ((xo - mean) * inv), axis=0, keepdims=True)
        vsum[0, 1:2, :] += jnp.sum(total[:, :512], axis=0, keepdims=True)
        vhalf[0, 0:1, :] += jnp.sum(total[:, 512:] * ((xt - mean) * inv), axis=0, keepdims=True)
        vhalf[0, 1:2, :] += jnp.sum(total[:, 512:], axis=0, keepdims=True)
    half_copy = sems.remote(vhalf.at[0], vhalf.at[1], c_dev)
    half_copy.start()
    poll(4)
    half_copy.wait()
    vsum[0] += vhalf[1]
    for k in (1, 2, 3):
        vsum[k, 0:6, :] = vsum[0, 0:6, :]
    dp_copies = [sems.remote(vsum, vdp.at[k], dev) for k, dev in enumerate((x_dev, y_dev, xy_dev))]
    for copy in dp_copies:
        copy.start()
    poll(4)
    for i in range(nb):
        rows = pl.ds(i * BQ, BQ)
        swaps[i].wait_recv()
        xo, xt = ga[rows, :].astype(F32), gb[rows, :].astype(F32)
        mean = halves_mean(xo, xt)
        inv = lax.rsqrt(halves_mean(xo * xo, xt * xt) - mean * mean + norm_eps)
        ho, ht = (xo - mean) * inv, (xt - mean) * inv
        bo = (part[rows, 0:512] + pr[rows, 0:512].astype(F32)) * vec[0][0]
        bt = (part[rows, 512:1024] + pr[rows, 512:1024].astype(F32)) * vec[0][1]
        first, second = halves_mean(bo, bt), halves_mean(bo * ho, bt * ht)
        grad_out[rows, :] = (dm[rows, :] + inv * (bo - first - ho * second)).astype(BF)
    for copy in dp_copies:
        copy.wait()
    vz[...] = (vsum[...] + vdp[0]) + (vdp[1] + vdp[2])
    z_copies = [sems.remote(vz.at[k], vzr.at[k], z_devs[k]) for k in (1, 2, 3)]
    for copy in z_copies:
        copy.start()
    poll(4)
    for copy in z_copies:
        copy.wait()
    vc[0] = (vz[0] + vzr[1]) + (vzr[2] + vzr[3])
    c_copy = sems.remote(vc.at[0], vc.at[1], c_dev)
    c_copy.start()
    poll(99)
    c_copy.wait()
    small_out[...] = vc[...]
    for copy in swaps:
        copy.wait_send()
    scatter.close()


def backward_all(*args):
    x_own, lse = args[0], args[10]
    seq, tp = lse[1], x_own.shape[0]
    lse = lse[0]
    nb = tp // BQ
    sds = jax.ShapeDtypeStruct
    halves = [half_block(m) for m in range(4)]
    n_remote = 4 * (8 + 4 + 3 + 1) + 2 * nb + 8
    hbm = lambda n: [ANY] * n
    scratch = [
        pltpu.VMEM((tp, 2048), BF), pltpu.VMEM((tp, 512), BF), pltpu.VMEM((tp, 512), BF), pltpu.VMEM((4, 2, 4, 128, 512), BF),
        pltpu.VMEM((4, 4, 32, 1024), BF), pltpu.VMEM((tp, 1024), F32), pltpu.VMEM((tp, 1024), BF), pltpu.VMEM((tp, 1024), BF),
        pltpu.VMEM((2, BQ, 1024), F32), pltpu.VMEM((tp, 1024), BF), pltpu.VMEM((tp, 512), F32), pltpu.VMEM((tp, 128), F32),
        pltpu.VMEM((tp, 128), F32), pltpu.VMEM((4, 8, 512), F32), pltpu.VMEM((3, 4, 8, 512), F32), pltpu.VMEM((4, 8, 512), F32), pltpu.VMEM((4, 8, 512), F32),
        pltpu.VMEM((2, 8, 512), F32), pltpu.VMEM((2, 8, 512), F32),
    ]
    scratch += [pltpu.VMEM((4, 4) + b, BF) for b in BLOCKS]
    scratch += [pltpu.VMEM((4, 2) + b, BF) for b in BLOCKS]
    scratch += [pltpu.VMEM((4,) + b, BF) for b in BLOCKS]
    scratch += [pltpu.VMEM((3,) + b, BF) for b in BLOCKS]
    scratch += [pltpu.VMEM(h, F32) for h in halves]
    scratch += [pltpu.SemaphoreType.DMA((n_remote,))] * 2 + [pltpu.SemaphoreType.DMA((nb + 14,)), pltpu.SemaphoreType.REGULAR]
    return pl.pallas_call(
        functools.partial(backward_kernel, seq),
        out_shape=[sds((tp, 512), BF), sds((2, 8, 512), F32)] + [sds(h, F32) for h in halves * 2],
        in_specs=hbm(4) + [VMEM] * 3 + hbm(3) + [VMEM] + hbm(8),
        out_specs=[VMEM] * 10,
        scratch_shapes=scratch,
        compiler_params=pltpu.CompilerParams(collective_id=1, has_side_effects=True, vmem_limit_bytes=63 << 20),
        cost_estimate=pl.CostEstimate(flops=40 * 10**9, bytes_accessed=100 * 10**6, transcendentals=10**7),
        name="backward",
    )(*args[:10], lse, *args[11:])


def local_chip(
    tokens, segment_ids, norm1_gain, norm1_shift, qkv_weight, qv_bias, out_weight, out_bias,
    norm2_gain, norm2_shift, up_weight, up_bias, down_weight, down_bias, cotangent,
):
    seq = segment_ids.shape[1]
    tp = -(-seq // BQ) * BQ
    c = lax.axis_index("gx")
    pad = ((0, tp - seq), (0, 0))
    x_own = jnp.pad(tokens, pad)
    g_own = jnp.pad(cotangent, pad)
    vec_own = jnp.pad(
        jnp.stack([norm1_gain, norm1_shift, out_bias, norm2_gain, norm2_shift, down_bias]), ((0, 10), (0, 0))
    )
    up_mine = lax.dynamic_index_in_dim(up_bias.reshape(4, 2, 128), c, 1, False).reshape(1, 512)
    qv_mine = lax.dynamic_index_in_dim(qv_bias.reshape(2, 2, 128), c, 1, False).reshape(1, 256)
    bias_own = jnp.concatenate([up_mine, jnp.pad(qv_mine, ((0, 0), (0, 256))), jnp.zeros((14, 512), BF)], axis=0)
    (wq, wo, wu, wd, n1, x_oth, g_oth, vec_oth, _, a1, qkv, o, lse, m, a2, gp, gd, y) = forward_all(
        x_own, g_own, vec_own, bias_own, segment_ids, qkv_weight.reshape(4, 128, 768), out_weight.reshape(2, 4, 32, 512),
        up_weight.reshape(4, 128, 1024), down_weight.reshape(4, 2, 128, 512),
    )
    grad, small, kd, ku, ko, kq, td, tu, to, tq = backward_all(
        x_own, x_oth, g_own, g_oth, vec_own, vec_oth, n1, a1, qkv, o, (lse, seq), m, a2, gp, gd, wq, wo, wu, wd
    )

    def by_core(keep, got, axis):
        return jnp.where(c == 0, jnp.stack([keep, got], axis), jnp.stack([got, keep], axis))

    down_grad = by_core(kd, td, 0).reshape(1, 256, 512)
    up_grad = by_core(ku.reshape(128, 4, 128), tu.reshape(128, 4, 128), 2).reshape(1, 128, 1024)
    out_grad = by_core(ko, to, 0).reshape(256, 1, 128)
    qkv_grad = by_core(kq.reshape(128, 3, 128), tq.reshape(128, 3, 128), 2).reshape(1, 128, 3, 256)
    width = small[0]
    up_bias_grad = by_core(small[0, 6].reshape(4, 128), small[1, 6].reshape(4, 128), 1).reshape(1024)
    qv_bias_grad = by_core(small[0, 7, :256].reshape(2, 128), small[1, 7, :256].reshape(2, 128), 1).reshape(2, 256)
    return (
        y[:seq], grad[:seq], width[0], width[1], qkv_grad, qv_bias_grad, out_grad, width[2],
        width[3], width[4], up_grad, up_bias_grad, down_grad, width[5],
    )


def solution(mesh):
    sizes = dict(mesh.shape)
    chip_rows = sizes["dp"] == 4 and sizes["gx"] == 2 and sizes["gy"] == 4

    def whole(*args):
        rows, seq = args[1].shape
        fast = chip_rows and rows * seq == args[0].shape[0] and rows == 16
        body = local_chip if fast else local
        return jax.shard_map(
            body,
            mesh=mesh,
            in_specs=(
                P(("dp", "gy"), "gx"), P(("dp", "gx"), None), P("gx"), P("gx"), P("gx", None, "gy"), P(None, "gy"),
                P("gy", "gx"), P("gx"), P("gx"), P("gx"), P("gx", "gy"), P("gy"), P("gy", "gx"), P("gx"), P(("dp", "gy"), "gx"),
            ),
            out_specs=(
                P(("dp", "gy"), "gx"), P(("dp", "gy"), "gx"), P("gx"), P("gx"), P("gx", "dp", None, "gy"), P(None, "gy"),
                P("gy", "gx", "dp"), P("gx"), P("gx"), P("gx"), P("gx", "dp", "gy"), P("gy"), P("gy", "dp", "gx"), P("gx"),
            ),
            check_vma=False,
        )(*args)

    return whole
```

```python
import functools
import math

import jax
import jax.numpy as jnp
from jax import lax
from jax.experimental import pallas as pl
from jax.experimental.pallas import tpu as pltpu
from jax.sharding import PartitionSpec as P

D = 1024
HD = 64
MESH = pl.DeviceIdType.MESH
F32 = jnp.float32
BF = jnp.bfloat16
ANY = pl.BlockSpec(memory_space=pl.ANY)
SMEM = pl.BlockSpec(memory_space=pltpu.SMEM)
VMEM = pl.BlockSpec(memory_space=pltpu.VMEM)
norm_eps = 1e-06


def times_right(left, right):
    return jnp.dot(left, right, preferred_element_type=jnp.float32)


def times_back(left, right):
    return lax.dot_general(
        left, right, (((1,), (1,)), ((), ())), preferred_element_type=jnp.float32
    )


def times_outer(left, right):
    return lax.dot_general(
        left, right, (((0,), (0,)), ((), ())), preferred_element_type=jnp.float32
    )


def exact_gelu(values):
    return jax.nn.gelu(values, approximate=False)


def norm_forward(values, gain, shift):
    moments = lax.psum((jnp.sum(values, axis=1), jnp.sum(values * values, axis=1)), "gx")
    mean_val = moments[0] / D
    inverse = lax.rsqrt(moments[1] / D - mean_val * mean_val + norm_eps)
    hat_vals = (values - mean_val[:, None]) * inverse[:, None]
    return (hat_vals * gain + shift, hat_vals, inverse)


def norm_backward(grad_norm, hat_vals, inverse, gain):
    scaled = grad_norm * gain
    moments = lax.psum((jnp.sum(scaled, axis=1), jnp.sum(scaled * hat_vals, axis=1)), "gx")
    grad_in = inverse[:, None] * (
        scaled - (moments[0] / D)[:, None] - hat_vals * (moments[1] / D)[:, None]
    )
    return (grad_in, jnp.sum(grad_norm * hat_vals, axis=0), jnp.sum(grad_norm, axis=0))


def gather_gy(values):
    return lax.all_gather(values, "gy", axis=0, tiled=True)


def gather_gx(values):
    return lax.all_gather(values, "gx", axis=0, tiled=True)


def sum_over_gx(left, multiply):
    keep_rows = left.shape[0] // lax.axis_size("gx")

    def term(start, count):
        return multiply(left)

    return lax.psum_scatter(
        term(jnp.int32(0), keep_rows * lax.axis_size("gx")), "gx", scatter_dimension=0, tiled=True
    )


def sum_over_gy(left, multiply):
    keep_rows = left.shape[0] // lax.axis_size("gy")

    def term(start, count):
        return multiply(left)

    return lax.psum_scatter(
        term(jnp.int32(0), keep_rows * lax.axis_size("gy")), "gy", scatter_dimension=0, tiled=True
    )


def masked_scores(query_part, key_part, segment):
    scaling = 1.0 / math.sqrt(query_part.shape[-1])
    scores = (
        jnp.einsum("qhd,khd->hqk", query_part, key_part, preferred_element_type=jnp.float32)
        * scaling
    )
    same = segment[:, None] == segment[None, :]
    return jnp.where(same[None], scores, -1e30)


def attend_forward(item):
    packed, segment = item
    scores = masked_scores(packed[:, 0], packed[:, 1], segment)
    top_val = jnp.max(scores, axis=-1, keepdims=True)
    expo = jnp.exp(scores - top_val)
    total = jnp.sum(expo, axis=-1, keepdims=True)
    probs = (expo / total).astype(jnp.bfloat16)
    mixed = jnp.einsum("hqk,khd->qhd", probs, packed[:, 2], preferred_element_type=jnp.float32)
    return (mixed.astype(jnp.bfloat16), (top_val + jnp.log(total))[..., 0])


def attend_backward(item):
    packed, segment, log_sum, grad_out = item
    query_part = packed[:, 0]
    key_part = packed[:, 1]
    value_part = packed[:, 2]
    scaling = 1.0 / math.sqrt(query_part.shape[-1])
    scores = masked_scores(query_part, key_part, segment)
    probs = jnp.exp(scores - log_sum[..., None])
    probs_low = probs.astype(jnp.bfloat16)
    grad_prob = jnp.einsum("qhd,khd->hqk", grad_out, value_part, preferred_element_type=jnp.float32)
    grad_value = jnp.einsum("hqk,qhd->khd", probs_low, grad_out, preferred_element_type=jnp.float32)
    delta = jnp.sum(probs * grad_prob, axis=-1, keepdims=True)
    grad_score = (probs * (grad_prob - delta)).astype(jnp.bfloat16)
    grad_query = (
        jnp.einsum("hqk,khd->qhd", grad_score, key_part, preferred_element_type=jnp.float32)
        * scaling
    )
    grad_key = (
        jnp.einsum("hqk,qhd->khd", grad_score, query_part, preferred_element_type=jnp.float32)
        * scaling
    )
    return jnp.stack([grad_query, grad_key, grad_value], axis=1).astype(jnp.bfloat16)


def local(
    tokens,
    segment_ids,
    norm1_gain,
    norm1_shift,
    qkv_weight,
    qv_bias,
    out_weight,
    out_bias,
    norm2_gain,
    norm2_shift,
    up_weight,
    up_bias,
    down_weight,
    down_bias,
    cotangent,
):
    head_width = qkv_weight.shape[2]
    local_heads = head_width // HD
    seq_len = segment_ids.shape[1]
    qkv_flat = qkv_weight.reshape(qkv_weight.shape[0], 3 * head_width)
    gain_one = norm1_gain.astype(jnp.float32)
    gain_two = norm2_gain.astype(jnp.float32)
    resid = tokens.astype(jnp.float32)
    normed, hat_one, inv_one = norm_forward(resid, gain_one, norm1_shift.astype(jnp.float32))
    first_low = normed.astype(jnp.bfloat16)
    first_rows = gather_gy(first_low)
    qkv_all = sum_over_gx(first_rows, lambda piece: times_right(piece, qkv_flat))
    bias_full = jnp.stack([qv_bias[0], jnp.zeros_like(qv_bias[0]), qv_bias[1]]).astype(jnp.float32)
    qkv_low = (qkv_all.reshape(-1, 3, head_width) + bias_full[None]).astype(jnp.bfloat16)
    packed = qkv_low.reshape(-1, seq_len, 3, local_heads, HD)
    mixed, log_sums = lax.map(attend_forward, (packed, segment_ids))
    mixed_low = mixed.reshape(-1, head_width)
    mixed_rows = gather_gx(mixed_low)
    branch = sum_over_gy(
        mixed_rows, lambda piece: times_right(piece, out_weight)
    ) + out_bias.astype(jnp.float32)
    middle = resid + branch
    normed_two, hat_two, inv_two = norm_forward(middle, gain_two, norm2_shift.astype(jnp.float32))
    second_low = normed_two.astype(jnp.bfloat16)
    second_rows = gather_gy(second_low)
    hidden = sum_over_gx(second_rows, lambda piece: times_right(piece, up_weight)) + up_bias.astype(
        jnp.float32
    )
    active, gelu_pull = jax.vjp(exact_gelu, hidden)
    active_low = active.astype(jnp.bfloat16)
    active_rows = gather_gx(active_low)
    branch_two = sum_over_gy(
        active_rows, lambda piece: times_right(piece, down_weight)
    ) + down_bias.astype(jnp.float32)
    output = (middle + branch_two).astype(jnp.bfloat16)
    grad_top = cotangent.astype(jnp.float32)
    down_bias_grad = jnp.sum(grad_top, axis=0)
    grad_top_rows = gather_gy(cotangent)
    down_weight_grad = times_outer(active_rows, grad_top_rows)
    grad_active = sum_over_gx(grad_top_rows, lambda piece: times_back(piece, down_weight))
    grad_hidden = gelu_pull(grad_active)[0].astype(jnp.bfloat16)
    up_bias_grad = jnp.sum(grad_hidden.astype(jnp.float32), axis=0)
    hidden_rows = gather_gx(grad_hidden)
    up_weight_grad = times_outer(second_rows, hidden_rows)
    grad_norm_two = sum_over_gy(hidden_rows, lambda piece: times_back(piece, up_weight))
    grad_in_two, norm2_gain_grad, norm2_shift_grad = norm_backward(
        grad_norm_two, hat_two, inv_two, gain_two
    )
    grad_middle = grad_top + grad_in_two
    grad_branch = grad_middle.astype(jnp.bfloat16)
    out_bias_grad = jnp.sum(grad_branch.astype(jnp.float32), axis=0)
    branch_rows = gather_gy(grad_branch)
    out_weight_grad = times_outer(mixed_rows, branch_rows)
    grad_mixed = sum_over_gx(branch_rows, lambda piece: times_back(piece, out_weight)).astype(
        jnp.bfloat16
    )
    grad_mixed = grad_mixed.reshape(-1, seq_len, local_heads, HD)
    grad_packed = lax.map(attend_backward, (packed, segment_ids, log_sums, grad_mixed))
    grad_qkv = grad_packed.reshape(-1, 3 * head_width)
    third_sums = jnp.sum(grad_qkv.astype(jnp.float32), axis=0).reshape(3, head_width)
    qv_bias_grad = jnp.stack([third_sums[0], third_sums[2]])
    qkv_rows = gather_gx(grad_qkv)
    qkv_weight_grad = times_outer(first_rows, qkv_rows).reshape(qkv_weight.shape)
    grad_norm_one = sum_over_gy(qkv_rows, lambda piece: times_back(piece, qkv_flat))
    grad_in_one, norm1_gain_grad, norm1_shift_grad = norm_backward(
        grad_norm_one, hat_one, inv_one, gain_one
    )
    input_grad = (grad_middle + grad_in_one).astype(jnp.bfloat16)
    qkv_weight_grad, out_weight_grad, up_weight_grad, down_weight_grad = (
        lax.psum_scatter(qkv_weight_grad, "dp", scatter_dimension=0, tiled=True),
        lax.psum_scatter(out_weight_grad, "dp", scatter_dimension=1, tiled=True),
        lax.psum_scatter(up_weight_grad, "dp", scatter_dimension=0, tiled=True),
        lax.psum_scatter(down_weight_grad, "dp", scatter_dimension=0, tiled=True),
    )
    qkv_weight_grad = qkv_weight_grad[None]
    out_weight_grad = out_weight_grad[:, None, :]
    up_weight_grad = up_weight_grad[None]
    down_weight_grad = down_weight_grad[None]
    (
        norm1_gain_grad,
        norm1_shift_grad,
        norm2_gain_grad,
        norm2_shift_grad,
        out_bias_grad,
        down_bias_grad,
    ) = lax.psum(
        (
            norm1_gain_grad,
            norm1_shift_grad,
            norm2_gain_grad,
            norm2_shift_grad,
            out_bias_grad,
            down_bias_grad,
        ),
        ("dp", "gy"),
    )
    up_bias_grad, qv_bias_grad = lax.psum((up_bias_grad, qv_bias_grad), ("dp", "gx"))
    return (
        output,
        input_grad,
        norm1_gain_grad,
        norm1_shift_grad,
        qkv_weight_grad,
        qv_bias_grad,
        out_weight_grad,
        out_bias_grad,
        norm2_gain_grad,
        norm2_shift_grad,
        up_weight_grad,
        up_bias_grad,
        down_weight_grad,
        down_bias_grad,
    )


def flip1(i):
    return i + 1 - 2 * lax.rem(i, 2)


def flip2(i):
    return i + 2 - 4 * lax.div(i, 2)


def place():
    dp, c, z = lax.axis_index("dp"), lax.axis_index("gx"), lax.axis_index("gy")
    dps = (dp, flip1(dp), flip2(dp), 3 - dp)
    zs = (z, flip1(z), flip2(z), 3 - z)
    x_dev = (dps[1], c, z)
    y_dev = (dps[2], c, z)
    c_dev = (dp, 1 - c, z)
    z_devs = (None,) + tuple((dp, c, zz) for zz in zs[1:])
    return dps, zs, x_dev, y_dev, c_dev, z_devs


def greet(devices):
    barrier = pltpu.get_barrier_semaphore()
    for device in devices:
        pl.semaphore_signal(barrier, inc=1, device_id=device, device_id_type=MESH)
    pl.semaphore_wait(barrier, len(devices))


WINDOW = 6
ORDER = tuple((m, k) for m in range(2) for k in (1, 2, 3)) + tuple((m, k) for k in (1, 2, 3) for m in (2, 3))
N_PAIR = 9


class Sems:
    def __init__(self, ss, rs):
        self.ss, self.rs, self.n = ss, rs, 0

    def at(self, i, src, dst, device):
        return pltpu.make_async_remote_copy(
            src, dst, self.ss.at[i], self.rs.at[i], device_id=device, device_id_type=MESH
        )

    def block(self, count):
        self.n += count
        return self.n - count

    def remote(self, src, dst, device):
        return self.at(self.block(1), src, dst, device)


class Locals:
    def __init__(self, ls):
        self.ls, self.n, self.open = ls, 0, []

    def at(self, i, src, dst):
        return pltpu.make_async_copy(src, dst, self.ls.at[i])

    def block(self, count):
        self.n += count
        return self.n - count

    def copy(self, src, dst):
        copy = self.at(self.block(1), src, dst)
        copy.start()
        return copy

    def later(self, src, dst):
        self.open.append(self.copy(src, dst))

    def close(self):
        for copy in self.open:
            copy.wait()


class Queue:
    def __init__(self, width):
        self.width, self.open = width, []

    def start(self, copy):
        if len(self.open) >= self.width:
            self.open.pop(0).wait_send()
        copy.start()
        self.open.append(copy)

    def close(self):
        for copy in self.open:
            copy.wait_send()


def weight_cuts(side, raw, full, crel):
    qf, ow, up, dn = raw
    wq, wo, wu, wd = full
    cols = pl.ds(crel * 512, 512)
    cuts = [[], [], [], []]
    for t in range(3):
        off = pl.multiple_of(t * 256 + side * 128, 128)
        cuts[0].append((qf.at[:, :, pl.ds(off, 128)], wq.at[0, crel, :, :, pl.ds(t * 128, 128)]))
    cuts[1].append((ow.at[side], wo.at[0, :, :, cols]))
    for t in range(4):
        off = pl.multiple_of(t * 256 + side * 128, 128)
        cuts[2].append((up.at[:, :, pl.ds(off, 128)], wu.at[0, crel, :, :, pl.ds(t * 128, 128)]))
    cuts[3].append((dn.at[:, side], wd.at[0, crel]))
    return cuts


class Gather:
    def __init__(self, sems, loc, here, c, raw, full):
        self.sems, self.loc, self.raw, self.full, self.c = sems, loc, raw, full, c
        self.dps, self.zs, self.x_dev, self.y_dev, self.c_dev, self.z_devs = here
        self.theirs = [[sems.remote(src, dst, self.c_dev) for src, dst in group] for group in weight_cuts(1 - c, raw, full, 1)]
        self.mine = weight_cuts(c, raw, full, 0)
        self.own, self.copies, self.ready = {}, {}, set()
        self.queues = {"x": Queue(99), "y": Queue(99), "z": Queue(WINDOW)}
        self.gen = self.steps()

    def piece(self, m, k, dd):
        return self.full[m].at[k, dd] if m == 1 else self.full[m].at[k, :, dd]

    def pair_start(self, m):
        for copy in self.theirs[m]:
            copy.start()
        self.own[m] = [self.loc.copy(src, dst) for src, dst in self.mine[m]]

    def own_ready(self, m):
        if m not in self.ready:
            self.ready.add(m)
            for copy in self.own[m]:
                copy.wait()
            for copy in self.theirs[m]:
                copy.wait_recv()

    def z_send(self, s):
        m, k = ORDER[s]
        self.own_ready(m)
        copy = self.sems.remote(self.piece(m, 0, self.dps[0]), self.piece(m, k, self.dps[0]), self.z_devs[k])
        self.copies["z", m, k] = copy
        self.queues["z"].start(copy)

    def by_x(self, m, k):
        return (k == 2) == (m in (0, 2))

    def forward(self, s):
        m, k = ORDER[s]
        if self.by_x(m, k):
            self.copies["x", m, k].wait_recv()
            src = self.piece(m, k, self.dps[1])
            copy, axis = self.sems.remote(src, src, self.y_dev), "y"
        else:
            self.copies["y", m, k].wait_recv()
            src = self.piece(m, k, self.dps[2])
            copy, axis = self.sems.remote(src, src, self.x_dev), "x"
        self.copies["d", m, k] = copy
        self.queues[axis].start(copy)

    def steps(self):
        for s, (m, k) in enumerate(ORDER):
            self.copies["z", m, k].wait_recv()
            if s + WINDOW < len(ORDER):
                self.z_send(s + WINDOW)
            src = self.piece(m, k, self.dps[0])
            for axis, dev in (("x", self.x_dev), ("y", self.y_dev)):
                copy = self.sems.remote(src, src, dev)
                self.copies[axis, m, k] = copy
                self.queues[axis].start(copy)
            yield
            if s > 0:
                self.forward(s - 1)
                yield
        self.forward(len(ORDER) - 1)
        yield

    def poll(self, n=1):
        for _ in range(n):
            next(self.gen, None)

    def need(self, m, k):
        if k == 0:
            self.own_ready(m)
            return
        while ("d", m, k) not in self.copies:
            self.poll()
        self.copies["y" if self.by_x(m, k) else "x", m, k].wait_recv()
        self.copies["d", m, k].wait_recv()

    def close(self):
        for group in self.theirs:
            for copy in group:
                copy.wait_send()
        for queue in self.queues.values():
            queue.close()


def dot_nt(a, b):
    return lax.dot_general(a, b, (((1,), (1,)), ((), ())), preferred_element_type=F32)


def dot_tn(a, b):
    return lax.dot_general(a, b, (((0,), (0,)), ((), ())), preferred_element_type=F32)


def dot_nn(a, b):
    return lax.dot_general(a, b, (((1,), (0,)), ((), ())), preferred_element_type=F32)


BQ = 256


SMALL = 64


def small_block(i):
    return pl.ds(pl.multiple_of(i * SMALL, SMALL), SMALL)


def row_block(i):
    return pl.ds(pl.multiple_of(i * BQ, BQ), BQ)


def segments(shape, axis, start, n1, seq):
    pos = (lax.broadcasted_iota(jnp.int32, shape, axis) + start).astype(F32)
    return (pos >= n1).astype(F32) + (pos >= float(seq)).astype(F32)


def masked_keys(big, kx, zr, n1, seq):
    tp = big.shape[0]
    lane = lax.broadcasted_iota(jnp.int32, (1, 128), 1)
    seg = segments((tp, 1), 0, 0, n1, seq)
    for h in range(2):
        t = lane - 64 * (1 - h)
        away = jnp.where(seg == t.astype(F32), 0.0, -1e30)
        away = jnp.where(t < 0, 0.0, jnp.where(t < 3, away, 0.0)).astype(BF)
        kx[h] = jnp.where(lax.div(lane, 64) == h, big[:, zr * 384 + 128 : zr * 384 + 256], away)


def attend_fwd_rows(big, lse_ref, kx, zr, start, count, n1, seq):
    lane = lax.broadcasted_iota(jnp.int32, (1, 128), 1)
    base = zr * 384
    rows = slice(start, start + count)
    q = big[rows, base : base + 128] * BF(0.125)
    seg = segments((count, 1), 0, start, n1, seq)
    out = jnp.zeros((count, 128), F32)
    for h in range(2):
        mask = lax.div(lane, 64) == h
        own_seg = (seg == (lane - 64 * (1 - h)).astype(F32)).astype(BF)
        s = dot_nt(jnp.where(mask, q, own_seg), kx[h])
        top = jnp.max(s, axis=1, keepdims=True)
        e = jnp.exp(s - top)
        total = jnp.sum(e, axis=1, keepdims=True)
        mixed = dot_nn(e.astype(BF), big[:, base + 256 : base + 384]) / total
        out = jnp.where(mask, mixed, out)
        lse = jnp.broadcast_to(top + jnp.log(total), (count, 128))
        lse_ref[2 * zr + h : 2 * zr + h + 1, rows] = jnp.transpose(lse)[0:1]
    big[rows, 1536 + zr * 128 : 1664 + zr * 128] = out.astype(BF)


def halves_mean(a, b):
    return (jnp.sum(a, axis=1, keepdims=True) + jnp.sum(b, axis=1, keepdims=True)) * (1.0 / D)


def forward_kernel(
    seq, x_own, g_own, vec_own, bias_own, ids, qf, ow, up, dn,
    wq_out, wo_out, wu_out, n1_out, x_out, g_out, vec_out, a1_out, big_out, lse_out, m_out, dh_out, gd_out, gu_out, usum, y_out,
    x_oth, g_oth, vec_oth, bias_all, cnt, wq, wo, wu, wd, act, big, lse, m, pb, pr, pr2, dh, gd, gu, kx,
    ss, rs, ls,
):
    tp = x_own.shape[0]
    nb = tp // BQ
    here = place()
    dps, zs, x_dev, y_dev, c_dev, z_devs = here
    c, z = lax.axis_index("gx"), zs[0]
    sems, loc = Sems(ss, rs), Locals(ls)
    gather = Gather(sems, loc, here, c, (qf, ow, up, dn), (wq, wo, wu, wd))
    poll = gather.poll

    ids_low = (ids[...] == 0).astype(F32)
    for r in range(2):
        cnt[0, r] = jnp.broadcast_to(jnp.sum(ids_low[r : r + 1], axis=1, keepdims=True), (8, 128))
    bias_all[0] = bias_own[...]
    usum[...] = jnp.zeros_like(usum)
    greet((x_dev, y_dev, c_dev) + z_devs[1:])
    gather.pair_start(0)
    small = [sems.remote(vec_own, vec_oth, c_dev), sems.remote(cnt.at[0], cnt.at[1], c_dev)]
    small += [sems.remote(bias_own, bias_all.at[k], z_devs[k]) for k in (1, 2, 3)]
    x_copy = sems.remote(x_own, x_oth, c_dev)
    for copy in small + [x_copy]:
        copy.start()
    for s in range(3):
        gather.z_send(s)
    for m_ in (1, 2, 3):
        gather.pair_start(m_)
    for copy in small:
        copy.wait_recv()
    x_copy.wait_recv()
    vec = [(vec_own[i : i + 1, :].astype(F32), vec_oth[i : i + 1, :].astype(F32)) for i in range(6)]
    n1 = cnt[lax.rem(lax.div(z, 2) + c, 2), lax.rem(z, 2)]
    n1_out[...] = n1
    n1 = n1[0:1, 0:1]
    loc.later(x_oth, x_out)
    loc.later(vec_oth, vec_out)

    @pl.loop(0, nb)
    def _(i):
        rows = row_block(i)
        xo, xt = x_own[rows, :].astype(F32), x_oth[rows, :].astype(F32)
        mean = halves_mean(xo, xt)
        inv = lax.rsqrt(halves_mean(xo * xo, xt * xt) - mean * mean + norm_eps)
        act[rows, 0:512] = ((xo - mean) * inv * vec[0][0] + vec[1][0]).astype(BF)
        act[rows, 512:1024] = ((xt - mean) * inv * vec[0][1] + vec[1][1]).astype(BF)

    a1_copy = loc.copy(act, a1_out)
    g_copy = sems.remote(g_own, g_oth, c_dev)
    g_copy.start()
    for s in range(3, WINDOW):
        gather.z_send(s)
    poll()
    for zr in range(4):
        gather.need(0, zr)
        qb, vb = bias_all[zr, 1:2, 0:128].astype(F32), bias_all[zr, 1:2, 128:256].astype(F32)
        bias = jnp.concatenate([qb, jnp.zeros_like(qb), vb], axis=1)

        @pl.loop(0, nb)
        def _(i):
            rows = row_block(i)
            big[rows, zr * 384 : zr * 384 + 384] = (dot_nn(act[rows, :], wq[zr].reshape(1024, 384)) + bias).astype(BF)

        masked_keys(big, kx, zr, n1, seq)
        poll()
        attend_fwd_rows(big, lse, kx, zr, 0, tp // 2, n1, seq)
        poll()
        attend_fwd_rows(big, lse, kx, zr, tp // 2, tp // 2, n1, seq)
        poll()
    loc.later(wq, wq_out)
    loc.later(lse, lse_out)
    big_copy = loc.copy(big, big_out)
    g_copy.wait_recv()
    loc.later(g_oth, g_out)
    for zr in range(4):
        gather.need(1, zr)
    loc.later(wo, wo_out)
    swap = sems.block(nb)

    @pl.loop(0, nb)
    def _(i):
        rows = row_block(i)
        part = dot_nn(big[rows, 1536:2048], wo[...].reshape(512, 1024))
        pb[rows, 0:512] = part[:, 512:].astype(BF)
        pb[rows, 512:1024] = part[:, :512].astype(BF)
        sems.at(swap + i, pb.at[rows], pr.at[rows], c_dev).start()
        m[rows, :] = part

    a1_copy.wait()
    poll()

    @pl.loop(0, nb)
    def _(i):
        rows = row_block(i)
        sems.at(swap + i, pb.at[rows], pr.at[rows], c_dev).wait()
        mo = x_own[rows, :].astype(F32) + m[rows, 0:512] + pr[rows, 0:512].astype(F32) + vec[2][0]
        mt = x_oth[rows, :].astype(F32) + m[rows, 512:1024] + pr[rows, 512:1024].astype(F32) + vec[2][1]
        mean = halves_mean(mo, mt)
        inv = lax.rsqrt(halves_mean(mo * mo, mt * mt) - mean * mean + norm_eps)
        m[rows, 0:512] = mo
        m[rows, 512:1024] = mt
        act[rows, 0:512] = ((mo - mean) * inv * vec[3][0] + vec[4][0]).astype(BF)
        act[rows, 512:1024] = ((mt - mean) * inv * vec[3][1] + vec[4][1]).astype(BF)

    m_copy = loc.copy(m, m_out)
    outs = {}
    last = sems.block(nb)

    def send_down():
        @pl.loop(0, nb)
        def _(i):
            rows = row_block(i)
            pb[rows, 0:512] = m[rows, 512:1024].astype(BF)
            sems.at(last + i, pb.at[rows, pl.ds(0, 512)], pr2.at[rows], c_dev).start()

    for zr in range(4):
        gather.need(2, zr)
        gather.need(3, zr)
        loc.later(wu.at[zr], wu_out.at[zr])
        bias = bias_all[zr, 0:1, :].astype(F32)
        lo = zr * 512
        if zr == 0:
            big_copy.wait()
            m_copy.wait()

        def hidden(first, last):
            @pl.loop(first, last)
            def _(i):
                rows = row_block(i)
                h = dot_nn(act[rows, :], wu[zr].reshape(1024, 512)) + bias
                w_own, w_oth = wd[zr, 0].reshape(512, 512), wd[zr, 1].reshape(512, 512)
                du = dot_nt(g_own[rows, :], w_own) + dot_nt(g_oth[rows, :], w_oth)
                cdf = 0.5 * (1.0 + lax.erf(h * math.sqrt(0.5)))
                slope = cdf + h * jnp.exp(-0.5 * h * h) * (1.0 / math.sqrt(2 * math.pi))
                u = (h * cdf).astype(BF)
                grad = (du * slope).astype(BF)
                big[rows, lo : lo + 512] = u
                dh[rows, lo : lo + 512] = grad
                usum[zr, 6:7, :] += jnp.sum(grad.astype(F32), axis=0, keepdims=True)
                m[rows, 0:512] += dot_nn(u, w_own)
                if zr == 0:
                    m[rows, 512:1024] = dot_nn(u, w_oth)
                else:
                    m[rows, 512:1024] += dot_nn(u, w_oth)

        for first, end in ((0, 2), (2, 4), (4, nb)):
            hidden(first, end)
            poll()
        if zr == 3:
            send_down()
        loc.later(dh.at[:, pl.ds(lo, 512)], dh_out.at[:, pl.ds(lo, 512)])
        slot = zr % 2
        if zr > 1:
            outs["d", zr - 2].wait()
            outs["u", zr - 2].wait()
        for j, gref in enumerate((g_own, g_oth)):
            gd[slot, :, :, 512 * j : 512 * j + 512] = dot_tn(big[:, lo : lo + 512], gref[...]).astype(BF).reshape(4, 128, 512)
        outs["d", zr] = loc.copy(gd.at[slot], gd_out.at[zr])
        poll()
        for j in range(2):
            block = dot_tn(act[:, 512 * j : 512 * j + 512], dh[:, lo : lo + 512])
            gu[slot, :, 128 * j : 128 * j + 128, :] = block.astype(BF).reshape(4, 128, 512)
        outs["u", zr] = loc.copy(gu.at[slot], gu_out.at[zr])
        poll()
    @pl.loop(0, nb)
    def _(i):
        rows = row_block(i)
        sems.at(last + i, pb.at[rows, pl.ds(0, 512)], pr2.at[rows], c_dev).wait()
        y_out[rows, :] = (m[rows, 0:512] + pr2[rows, :].astype(F32) + vec[5][0]).astype(BF)

    for copy in small + [x_copy, g_copy]:
        copy.wait_send()
    for zr in (2, 3):
        outs["d", zr].wait()
        outs["u", zr].wait()
    gather.close()
    loc.close()


def forward_all(x_own, g_own, vec_own, bias_own, ids, qf, ow, up, dn):
    tp = x_own.shape[0]
    seq = ids.shape[1]
    n_remote = N_PAIR + 7 + 48 + 2 * (tp // BQ)
    sds = jax.ShapeDtypeStruct
    vm = pltpu.VMEM
    wide = (4, 2, 4, 128, 512)
    weights = [(4, 2, 4, 128, 384), (4, 4, 32, 1024), wide, wide]
    out_shape = [sds(s, BF) for s in weights[:3]] + [
        sds((8, 128), F32), sds((tp, 512), BF), sds((tp, 512), BF), sds(vec_own.shape, BF), sds((tp, 1024), BF),
        sds((tp, 2048), BF), sds((8, tp), F32), sds((tp, 1024), F32), sds((tp, 2048), BF), sds((4, 4, 128, 1024), BF),
        sds((4, 4, 256, 512), BF), sds((4, 8, 512), F32), sds((tp, 512), BF),
    ]
    scratch = [vm((tp, 512), BF), vm((tp, 512), BF), vm(vec_own.shape, BF), vm((4,) + bias_own.shape, BF), vm((2, 2, 8, 128), F32)]
    scratch += [vm(s, BF) for s in weights]
    scratch += [
        vm((tp, 1024), BF), vm((tp, 2048), BF), vm((8, tp), F32), vm((tp, 1024), F32), vm((tp, 1024), BF), vm((tp, 1024), BF),
        vm((tp, 512), BF), vm((tp, 2048), BF), vm((2, 4, 128, 1024), BF), vm((2, 4, 256, 512), BF), vm((2, tp, 128), BF),
        pltpu.SemaphoreType.DMA((n_remote,)), pltpu.SemaphoreType.DMA((n_remote,)), pltpu.SemaphoreType.DMA((40,)),
    ]
    return pl.pallas_call(
        functools.partial(forward_kernel, seq),
        out_shape=out_shape,
        in_specs=[VMEM] * 5 + [ANY] * 4,
        out_specs=[ANY] * 3 + [VMEM] + [ANY] * 10 + [VMEM] * 2,
        scratch_shapes=scratch,
        compiler_params=pltpu.CompilerParams(collective_id=0, has_side_effects=True, vmem_limit_bytes=63 << 20),
        cost_estimate=pl.CostEstimate(flops=40 * 10**9, bytes_accessed=80 * 10**6, transcendentals=10**7),
        name="forward",
    )(x_own, g_own, vec_own, bias_own, ids, qf, ow, up, dn)


BLOCKS = ((128, 1024), (256, 512), (128, 256), (256, 384))
ZORDER = (1, 2, 3, 0)
XYORDER = (1, 2, 0, 3)


def half_block(m):
    rows, cols = BLOCKS[m]
    return (rows // 2, cols) if m in (1, 3) else (rows, cols // 2)


def by_turns(*lists):
    out = []
    for i in range(max(len(l) for l in lists)):
        out += [l[i] for l in lists if i < len(l)]
    return out


class Scatter:
    def __init__(self, sems, here, g, first_src, rx, ry, rz, sw, keep, got):
        self.sems, self.g, self.first_src = sems, g, first_src
        self.dps, self.zs, self.x_dev, self.y_dev, self.c_dev, self.z_devs = here
        self.rx, self.ry, self.rz, self.sw, self.keep, self.got = rx, ry, rz, sw, keep, got
        self.first, self.second, self.third, self.last = {}, {}, {}, {}
        self.queues = {axis: Queue(4) for axis in "xyz"}
        self.made = set()
        one = lambda m, slot: [(1, m, zr, slot) for zr in XYORDER]
        two = lambda m: [(2, m, zr, 0) for zr in ZORDER]
        three = lambda m: [(3, m, zr, 0) for zr in ZORDER]
        four = lambda m: [(4, m, 0, 0)]
        fresh = lambda zr: [(1, 3, zr, 1), (1, 3, zr, 0)]
        self.plan = (
            one(0, 1) + one(0, 0) + by_turns(two(0), one(1, 1)) + by_turns(one(1, 0), three(0)) + by_turns(two(1), one(2, 1))
            + by_turns(one(2, 0), three(1)) + four(0) + fresh(1) + two(2) + fresh(2) + three(2) + [(2, 3, 1, 0)] + four(1)
            + fresh(3) + [(2, 3, 2, 0), (3, 3, 1, 0)] + four(2) + fresh(0) + [(2, 3, 3, 0), (3, 3, 2, 0), (2, 3, 0, 0)]
            + [(3, 3, 3, 0), (3, 3, 0, 0)] + four(3)
        )

    def poll(self, n):
        while n > 0 and self.plan:
            stage, m, zr, slot = self.plan[0]
            if stage == 1 and (m, zr) not in self.made:
                return
            self.plan.pop(0)
            if stage == 1:
                self.stage1(m, zr, slot)
            elif stage == 2:
                self.stage2(m, zr)
            elif stage == 3:
                self.stage3(m, zr)
            else:
                self.stage4(m)
            n -= 1

    def stage1(self, m, zr, slot):
        axis, dev, rels = ("x", self.x_dev, (1, 3)) if zr < 2 else ("y", self.y_dev, (2, 3))
        src = self.first_src[m].at[zr, self.dps[rels[slot]]]
        copy = self.sems.remote(src, self.rx[m].at[zr, slot], dev)
        self.first[m, zr, slot] = copy
        self.queues[axis].start(copy)

    def stage2(self, m, zr):
        axis, dev, rel = ("y", self.y_dev, 2) if zr < 2 else ("x", self.x_dev, 1)
        g, dd = self.g[m], self.dps[rel]
        self.first[m, zr, 1].wait_recv()
        g[zr, dd] = (g[zr, dd].astype(F32) + self.rx[m][zr, 1].astype(F32)).astype(BF)
        copy = self.sems.remote(g.at[zr, dd], self.ry[m].at[zr], dev)
        self.second[m, zr] = copy
        self.queues[axis].start(copy)

    def stage3(self, m, zr):
        g, dd = self.g[m], self.dps[0]
        self.first[m, zr, 0].wait_recv()
        self.second[m, zr].wait_recv()
        g[zr, dd] = (g[zr, dd].astype(F32) + self.rx[m][zr, 0].astype(F32) + self.ry[m][zr].astype(F32)).astype(BF)
        if zr > 0:
            copy = self.sems.remote(g.at[zr, dd], self.rz[m].at[zr - 1], self.z_devs[zr])
            self.third[m, zr] = copy
            self.queues["z"].start(copy)

    def stage4(self, m):
        for zr in (1, 2, 3):
            self.third[m, zr].wait_recv()
        rz = self.rz[m]
        total = self.g[m][0, self.dps[0]].astype(F32) + rz[0].astype(F32) + rz[1].astype(F32) + rz[2].astype(F32)
        rows, cols = BLOCKS[m]
        if m in (1, 3):
            self.keep[m][...] = total[: rows // 2]
            self.sw[m][...] = total[rows // 2 :]
        else:
            self.keep[m][...] = total[:, : cols // 2]
            self.sw[m][...] = total[:, cols // 2 :]
        copy = self.sems.remote(self.sw[m], self.got[m], self.c_dev)
        self.last[m] = copy
        copy.start()

    def close(self):
        for queue in self.queues.values():
            queue.close()
        for copy in self.last.values():
            copy.wait()


def attend_bwd_rows(big, do_ref, lse_ref, k_t, dk_acc, dv_acc, zr, lo, hi, n1, seq):
    tp = big.shape[0]
    lane = lax.broadcasted_iota(jnp.int32, (1, 128), 1)
    base = zr * 384
    ocol = 1536 + zr * 128

    @pl.loop(lo, hi)
    def _(i):
        start = pl.multiple_of(i * BQ, BQ)
        rows = pl.ds(start, BQ)
        q = big[rows, base : base + 128]
        do = do_ref[rows, zr * 128 : zr * 128 + 128]
        prod = do.astype(F32) * big[rows, ocol : ocol + 128].astype(F32)
        seg_q = segments((1, BQ), 1, start, n1, seq)
        dq_t = jnp.zeros((128, BQ), F32)
        row = lax.broadcasted_iota(jnp.int32, (128, 1), 0)
        for h in range(2):
            mask = lax.div(lane, 64) == h
            lse = lse_ref[2 * zr + h : 2 * zr + h + 1, rows]
            delta = jnp.sum(jnp.where(mask, prod, 0.0), axis=1, keepdims=True)
            delta = jnp.transpose(jnp.broadcast_to(delta, (BQ, 128)))[0:1]
            qm = jnp.where(mask, q, BF(0)) * BF(0.125)
            dom = jnp.where(mask, do, BF(0))
            for keys in (slice(0, tp // 2), slice(tp // 2, tp)):
                same = segments((tp // 2, 1), 0, keys.start, n1, seq) == seg_q
                s = dot_nt(big[keys, base + 128 : base + 256], qm)
                p = jnp.where(same, jnp.exp(s - lse), 0.0)
                dp = dot_nt(big[keys, base + 256 : base + 384], dom)
                ds = (p * (dp - delta)).astype(BF)
                dv_acc[keys, :] += dot_nn(p.astype(BF), dom)
                dk_acc[keys, :] += dot_nn(ds, qm)
                dq_t += jnp.where(lax.div(row, 64) == h, dot_nn(k_t[:, keys], ds), 0.0)
        dq = jnp.transpose(dq_t)
        big[rows, base : base + 128] = (dq * 0.125).astype(BF)


def backward_kernel(
    seq, x_own, x_oth, g_own_h, g_oth_h, vec_own, vec_oth, n1_ref, usum, lse, a1_h, big_h, m_h, dh_h, gd_h, gu_h, wq_h, wo_h, wu_h,
    grad_out, small_out, keep0, keep1, keep2, keep3, got0, got1, got2, got3,
    big, ga, gb, wbuf, wo_v, part, pb, pr, mbuf, act, dm, k_t, dk_acc, dv_acc, vsum, vdp, vz, vzr, vhalf, vc,
    gd, gu, go, gq, rx0, rx1, rx2, rx3, ry0, ry1, ry2, ry3, rz0, rz1, rz2, rz3, sw0, sw1, sw2, sw3,
    ss, rs, ls, free,
):
    tp = big.shape[0]
    nb = tp // BQ
    here = place()
    dps, zs, x_dev, y_dev, c_dev, z_devs = here
    c, z = lax.axis_index("gx"), zs[0]
    xy_dev = (dps[3], c, z)
    sems, loc = Sems(ss, rs), Locals(ls)
    scatter = Scatter(
        sems, here, (gd, gu, go, gq), (gd_h, gu_h, go, gq), (rx0, rx1, rx2, rx3), (ry0, ry1, ry2, ry3), (rz0, rz1, rz2, rz3),
        (sw0, sw1, sw2, sw3), (keep0, keep1, keep2, keep3), (got0, got1, got2, got3),
    )
    poll, made = scatter.poll, scatter.made
    greet((x_dev, y_dev, xy_dev, c_dev) + z_devs[1:])
    made.update((m, zr) for m in range(2) for zr in range(4))
    poll(8)
    dh_in = loc.copy(dh_h, big)
    wu_in = loc.copy(wu_h, wbuf)
    gd_in, gu_in = loc.copy(gd_h, gd), loc.copy(gu_h, gu)
    ga_in, gb_in = loc.copy(g_own_h, ga), loc.copy(g_oth_h, gb)
    wo_in = loc.copy(wo_h, wo_v)
    m_sem = loc.block(tp // SMALL)

    def load_m(i):
        return loc.at(m_sem + i, m_h.at[small_block(i)], mbuf.at[lax.rem(i, 2)])

    load_m(0).start()
    vec = [(vec_own[i : i + 1, :].astype(F32), vec_oth[i : i + 1, :].astype(F32)) for i in range(6)]
    n1 = n1_ref[0:1, 0:1]
    vsum[...] = usum[...]
    vhalf[...] = jnp.zeros_like(vhalf)
    dh_in.wait()
    wu_in.wait()
    swap = sems.block(nb)

    @pl.loop(0, nb)
    def _(i):
        rows = row_block(i)
        total = dot_nt(big[rows, 0:512], wbuf[0].reshape(1024, 512))
        for zr in range(1, 4):
            total += dot_nt(big[rows, zr * 512 : zr * 512 + 512], wbuf[zr].reshape(1024, 512))
        pb[rows, 0:512] = total[:, 512:].astype(BF)
        pb[rows, 512:1024] = total[:, :512].astype(BF)
        sems.at(swap + i, pb.at[rows], pr.at[rows], c_dev).start()
        part[rows, :] = total

    big_in = loc.copy(big_h, big)
    wq_in = loc.copy(wq_h, wbuf.at[:, :, :, :, pl.ds(0, 384)])
    gd_in.wait()
    gu_in.wait()
    ga_in.wait()
    gb_in.wait()
    poll(4)
    @pl.loop(0, tp // SMALL)
    def _(i):
        rows = small_block(i)

        @pl.when(i + 1 < tp // SMALL)
        def _():
            load_m(i + 1).start()

        @pl.when(lax.rem(i, BQ // SMALL) == 0)
        def _():
            whole = lax.div(i, BQ // SMALL)
            sems.at(swap + whole, pb.at[row_block(whole)], pr.at[row_block(whole)], c_dev).wait()

        load_m(i).wait()
        slot = lax.rem(i, 2)
        mo, mt = mbuf[slot, :, 0:512], mbuf[slot, :, 512:1024]
        mean = halves_mean(mo, mt)
        inv = lax.rsqrt(halves_mean(mo * mo, mt * mt) - mean * mean + norm_eps)
        ho, ht = (mo - mean) * inv, (mt - mean) * inv
        do_, dt = part[rows, 0:512] + pr[rows, 0:512].astype(F32), part[rows, 512:1024] + pr[rows, 512:1024].astype(F32)
        bo, bt = do_ * vec[3][0], dt * vec[3][1]
        first, second = halves_mean(bo, bt), halves_mean(bo * ho, bt * ht)
        go_, gt = ga[rows, :].astype(F32), gb[rows, :].astype(F32)
        dmo = go_ + inv * (bo - first - ho * second)
        dmt = gt + inv * (bt - first - ht * second)
        dm[rows, :] = dmo
        act[rows, 0:512] = dmo.astype(BF)
        act[rows, 512:1024] = dmt.astype(BF)
        vsum[0, 2:3, :] += jnp.sum(dmo.astype(BF).astype(F32), axis=0, keepdims=True)
        vsum[0, 3:4, :] += jnp.sum(do_ * ho, axis=0, keepdims=True)
        vsum[0, 4:5, :] += jnp.sum(do_, axis=0, keepdims=True)
        vsum[0, 5:6, :] += jnp.sum(go_, axis=0, keepdims=True)

    pl.semaphore_signal(free, inc=1, device_id=c_dev, device_id_type=MESH)
    poll(4)
    wo_in.wait()
    big_in.wait()
    for j in range(2):
        block = dot_tn(big[:, 1536:2048], act[:, 512 * j : 512 * j + 512]).astype(BF)
        for dd in range(4):
            go[:, dd, :, 128 * j : 128 * j + 128] = block[:, 128 * dd : 128 * dd + 128].reshape(4, 128, 128)
    made.update((2, zr) for zr in range(4))

    @pl.loop(0, nb)
    def _(i):
        rows = row_block(i)
        ga[rows, :] = dot_nt(act[rows, :], wo_v[...].reshape(512, 1024)).astype(BF)

    a1_in = loc.copy(a1_h, act)
    xb_in = loc.copy(x_oth, gb)
    poll(4)
    for step, zr in enumerate(ZORDER):
        base = zr * 384
        dk_acc[...] = jnp.zeros_like(dk_acc)
        dv_acc[...] = jnp.zeros_like(dv_acc)
        k_t[...] = jnp.transpose(big[:, base + 128 : base + 256].astype(F32)).astype(BF)
        for lo, hi in ((0, 2), (2, 4), (4, nb)):
            attend_bwd_rows(big, ga, lse, k_t, dk_acc, dv_acc, zr, lo, hi, n1, seq)
            if hi < nb:
                poll(POLLS[step][0])
        big[:, base + 128 : base + 256] = dk_acc[...].astype(BF)
        big[:, base + 256 : base + 384] = dv_acc[...].astype(BF)
        if step == 0:
            a1_in.wait()
            wq_in.wait()
        for j in range(2):
            block = dot_tn(act[:, 512 * j : 512 * j + 512], big[:, base : base + 384])
            gq[zr, :, 128 * j : 128 * j + 128, :] = block.astype(BF).reshape(4, 128, 384)
        made.add((3, zr))
        poll(POLLS[step][1])
        for j in (0, 2):
            cols = big[:, base + 128 * j : base + 128 * j + 128].astype(F32)
            vsum[zr, 7:8, 64 * j : 64 * j + 128] = jnp.sum(cols, axis=0, keepdims=True)
        if step < 3:

            @pl.loop(0, nb)
            def _(i):
                rows = row_block(i)
                more = dot_nt(big[rows, base : base + 384], wbuf[zr, :, :, :, 0:384].reshape(1024, 384))
                part[rows, :] = more if step == 0 else part[rows, :] + more

    xa_in = loc.copy(x_own, ga)
    pl.semaphore_wait(free, 1)
    xa_in.wait()
    xb_in.wait()
    swap2 = sems.block(nb)
    base = ZORDER[3] * 384

    @pl.loop(0, nb)
    def _(i):
        rows = row_block(i)
        total = part[rows, :] + dot_nt(big[rows, base : base + 384], wbuf[ZORDER[3], :, :, :, 0:384].reshape(1024, 384))
        pb[rows, 0:512] = total[:, 512:].astype(BF)
        pb[rows, 512:1024] = total[:, :512].astype(BF)
        sems.at(swap2 + i, pb.at[rows], pr.at[rows], c_dev).start()
        part[rows, :] = total
        xo, xt = ga[rows, :].astype(F32), gb[rows, :].astype(F32)
        mean = halves_mean(xo, xt)
        inv = lax.rsqrt(halves_mean(xo * xo, xt * xt) - mean * mean + norm_eps)
        vsum[0, 0:1, :] += jnp.sum(total[:, :512] * ((xo - mean) * inv), axis=0, keepdims=True)
        vsum[0, 1:2, :] += jnp.sum(total[:, :512], axis=0, keepdims=True)
        vhalf[0, 0:1, :] += jnp.sum(total[:, 512:] * ((xt - mean) * inv), axis=0, keepdims=True)
        vhalf[0, 1:2, :] += jnp.sum(total[:, 512:], axis=0, keepdims=True)

    half_copy = sems.remote(vhalf.at[0], vhalf.at[1], c_dev)
    half_copy.start()
    poll(POLLS[4][0])
    half_copy.wait()
    vsum[0] += vhalf[1]
    for k in (1, 2, 3):
        vsum[k, 0:6, :] = vsum[0, 0:6, :]
    dp_copies = [sems.remote(vsum, vdp.at[k], dev) for k, dev in enumerate((x_dev, y_dev, xy_dev))]
    for copy in dp_copies:
        copy.start()
    poll(POLLS[4][1])

    @pl.loop(0, nb)
    def _(i):
        rows = row_block(i)
        sems.at(swap2 + i, pb.at[rows], pr.at[rows], c_dev).wait()
        xo, xt = ga[rows, :].astype(F32), gb[rows, :].astype(F32)
        mean = halves_mean(xo, xt)
        inv = lax.rsqrt(halves_mean(xo * xo, xt * xt) - mean * mean + norm_eps)
        ho, ht = (xo - mean) * inv, (xt - mean) * inv
        bo = (part[rows, 0:512] + pr[rows, 0:512].astype(F32)) * vec[0][0]
        bt = (part[rows, 512:1024] + pr[rows, 512:1024].astype(F32)) * vec[0][1]
        first, second = halves_mean(bo, bt), halves_mean(bo * ho, bt * ht)
        ga[rows, :] = (dm[rows, :] + inv * (bo - first - ho * second)).astype(BF)

    loc.later(ga, grad_out)
    for copy in dp_copies:
        copy.wait()
    vz[...] = (vsum[...] + vdp[0]) + (vdp[1] + vdp[2])
    z_copies = [sems.remote(vz.at[k], vzr.at[k], z_devs[k]) for k in (1, 2, 3)]
    for copy in z_copies:
        copy.start()
    poll(POLLS[4][2])
    for copy in z_copies:
        copy.wait()
    vc[0] = (vz[0] + vzr[1]) + (vzr[2] + vzr[3])
    c_copy = sems.remote(vc.at[0], vc.at[1], c_dev)
    c_copy.start()
    poll(99)
    c_copy.wait()
    small_out[...] = vc[...]
    loc.close()
    scatter.close()


POLLS = ((4, 4), (4, 4), (4, 4), (4, 4), (2, 2, 2))


def backward_all(seq, *args):
    tp = args[0].shape[0]
    nb = tp // BQ
    sds = jax.ShapeDtypeStruct
    vm = pltpu.VMEM
    halves = [half_block(m) for m in range(4)]
    n_remote = 4 * (8 + 4 + 3 + 1) + 2 * nb + 8
    scratch = [
        vm((tp, 2048), BF), vm((tp, 512), BF), vm((tp, 512), BF), vm((4, 2, 4, 128, 512), BF), vm((4, 4, 32, 1024), BF),
        vm((tp, 1024), F32), vm((tp, 1024), BF), vm((tp, 1024), BF), vm((2, SMALL, 1024), F32), vm((tp, 1024), BF),
        vm((tp, 512), F32), vm((128, tp), BF), vm((tp, 128), F32), vm((tp, 128), F32), vm((4, 8, 512), F32), vm((3, 4, 8, 512), F32),
        vm((4, 8, 512), F32), vm((4, 8, 512), F32), vm((2, 8, 512), F32), vm((2, 8, 512), F32),
    ]
    scratch += [vm((4, 4) + b, BF) for b in BLOCKS]
    scratch += [vm((4, 2) + b, BF) for b in BLOCKS]
    scratch += [vm((4,) + b, BF) for b in BLOCKS]
    scratch += [vm((3,) + b, BF) for b in BLOCKS]
    scratch += [vm(h, F32) for h in halves]
    scratch += [pltpu.SemaphoreType.DMA((n_remote,))] * 2 + [pltpu.SemaphoreType.DMA((tp // SMALL + 14,)), pltpu.SemaphoreType.REGULAR]
    return pl.pallas_call(
        functools.partial(backward_kernel, seq),
        out_shape=[sds((tp, 512), BF), sds((2, 8, 512), F32)] + [sds(h, F32) for h in halves * 2],
        in_specs=[ANY] * 4 + [VMEM] * 5 + [ANY] * 9,
        out_specs=[ANY] + [VMEM] * 9,
        scratch_shapes=scratch,
        compiler_params=pltpu.CompilerParams(collective_id=1, has_side_effects=True, vmem_limit_bytes=63 << 20),
        cost_estimate=pl.CostEstimate(flops=40 * 10**9, bytes_accessed=100 * 10**6, transcendentals=10**7),
        name="backward",
    )(*args)


def local_chip(
    tokens, segment_ids, norm1_gain, norm1_shift, qkv_weight, qv_bias, out_weight, out_bias,
    norm2_gain, norm2_shift, up_weight, up_bias, down_weight, down_bias, cotangent,
):
    seq = segment_ids.shape[1]
    tp = -(-seq // BQ) * BQ
    c = lax.axis_index("gx")
    pad = ((0, tp - seq), (0, 0))
    x_own = jnp.pad(tokens, pad)
    g_own = jnp.pad(cotangent, pad)
    vec_own = jnp.concatenate(
        [norm1_gain, norm1_shift, out_bias, norm2_gain, norm2_shift, down_bias, jnp.zeros(10 * 512, BF)]
    ).reshape(16, 512)
    up_mine = lax.dynamic_index_in_dim(up_bias.reshape(4, 2, 128), c, 1, False).reshape(512)
    qv_mine = lax.dynamic_index_in_dim(qv_bias.reshape(2, 2, 128), c, 1, False).reshape(256)
    bias_own = jnp.concatenate([up_mine, qv_mine, jnp.zeros(14 * 512 + 256, BF)]).reshape(16, 512)
    (wq, wo, wu, n1, x_oth, g_oth, vec_oth, a1, big, lse, m, dh, gd, gu, usum, y) = forward_all(
        x_own, g_own, vec_own, bias_own, segment_ids, qkv_weight.reshape(4, 128, 768), out_weight.reshape(2, 4, 32, 512),
        up_weight.reshape(4, 128, 1024), down_weight.reshape(4, 2, 128, 512),
    )
    grad, small, kd, ku, ko, kq, td, tu, to, tq = backward_all(
        seq, x_own, x_oth, g_own, g_oth, vec_own, vec_oth, n1, usum, lse, a1, big, m, dh, gd, gu, wq, wo, wu
    )

    def by_core(keep, got, axis):
        return jnp.where(c == 0, jnp.stack([keep, got], axis), jnp.stack([got, keep], axis))

    down_grad = by_core(kd, td, 0).reshape(1, 256, 512)
    up_grad = by_core(ku.reshape(128, 4, 128), tu.reshape(128, 4, 128), 2).reshape(1, 128, 1024)
    out_grad = by_core(ko, to, 0).reshape(256, 1, 128)
    qkv_grad = by_core(kq.reshape(128, 3, 128), tq.reshape(128, 3, 128), 2).reshape(1, 128, 3, 256)
    width = small[0]
    up_bias_grad = by_core(small[0, 6].reshape(4, 128), small[1, 6].reshape(4, 128), 1).reshape(1024)
    qv_bias_grad = by_core(small[0, 7, :256].reshape(2, 128), small[1, 7, :256].reshape(2, 128), 1).reshape(2, 256)
    return (
        y[:seq], grad[:seq], width[0], width[1], qkv_grad, qv_bias_grad, out_grad, width[2],
        width[3], width[4], up_grad, up_bias_grad, down_grad, width[5],
    )


def solution(mesh):
    sizes = dict(mesh.shape)
    chip_rows = sizes["dp"] == 4 and sizes["gx"] == 2 and sizes["gy"] == 4

    def whole(*args):
        rows, seq = args[1].shape
        fast = chip_rows and rows * seq == args[0].shape[0] and rows == 16
        body = local_chip if fast else local
        return jax.shard_map(
            body,
            mesh=mesh,
            in_specs=(
                P(("dp", "gy"), "gx"), P(("dp", "gx"), None), P("gx"), P("gx"), P("gx", None, "gy"), P(None, "gy"),
                P("gy", "gx"), P("gx"), P("gx"), P("gx"), P("gx", "gy"), P("gy"), P("gy", "gx"), P("gx"), P(("dp", "gy"), "gx"),
            ),
            out_specs=(
                P(("dp", "gy"), "gx"), P(("dp", "gy"), "gx"), P("gx"), P("gx"), P("gx", "dp", None, "gy"), P(None, "gy"),
                P("gy", "gx", "dp"), P("gx"), P("gx"), P("gx"), P("gx", "dp", "gy"), P("gy"), P("gy", "dp", "gx"), P("gx"),
            ),
            check_vma=False,
        )(*args)

    return whole
```

```python
import functools
import math

import jax
import jax.numpy as jnp
from jax import lax
from jax.experimental import pallas as pl
from jax.experimental.pallas import tpu as pltpu
from jax.sharding import PartitionSpec as P

D = 1024
HD = 64
MESH = pl.DeviceIdType.MESH
F32 = jnp.float32
BF = jnp.bfloat16
ANY = pl.BlockSpec(memory_space=pl.ANY)
SMEM = pl.BlockSpec(memory_space=pltpu.SMEM)
VMEM = pl.BlockSpec(memory_space=pltpu.VMEM)
norm_eps = 1e-06


def times_right(left, right):
    return jnp.dot(left, right, preferred_element_type=jnp.float32)


def times_back(left, right):
    return lax.dot_general(
        left, right, (((1,), (1,)), ((), ())), preferred_element_type=jnp.float32
    )


def times_outer(left, right):
    return lax.dot_general(
        left, right, (((0,), (0,)), ((), ())), preferred_element_type=jnp.float32
    )


def exact_gelu(values):
    return jax.nn.gelu(values, approximate=False)


def norm_forward(values, gain, shift):
    moments = lax.psum((jnp.sum(values, axis=1), jnp.sum(values * values, axis=1)), "gx")
    mean_val = moments[0] / D
    inverse = lax.rsqrt(moments[1] / D - mean_val * mean_val + norm_eps)
    hat_vals = (values - mean_val[:, None]) * inverse[:, None]
    return (hat_vals * gain + shift, hat_vals, inverse)


def norm_backward(grad_norm, hat_vals, inverse, gain):
    scaled = grad_norm * gain
    moments = lax.psum((jnp.sum(scaled, axis=1), jnp.sum(scaled * hat_vals, axis=1)), "gx")
    grad_in = inverse[:, None] * (
        scaled - (moments[0] / D)[:, None] - hat_vals * (moments[1] / D)[:, None]
    )
    return (grad_in, jnp.sum(grad_norm * hat_vals, axis=0), jnp.sum(grad_norm, axis=0))


def gather_gy(values):
    return lax.all_gather(values, "gy", axis=0, tiled=True)


def gather_gx(values):
    return lax.all_gather(values, "gx", axis=0, tiled=True)


def sum_over_gx(left, multiply):
    keep_rows = left.shape[0] // lax.axis_size("gx")

    def term(start, count):
        return multiply(left)

    return lax.psum_scatter(
        term(jnp.int32(0), keep_rows * lax.axis_size("gx")), "gx", scatter_dimension=0, tiled=True
    )


def sum_over_gy(left, multiply):
    keep_rows = left.shape[0] // lax.axis_size("gy")

    def term(start, count):
        return multiply(left)

    return lax.psum_scatter(
        term(jnp.int32(0), keep_rows * lax.axis_size("gy")), "gy", scatter_dimension=0, tiled=True
    )


def masked_scores(query_part, key_part, segment):
    scaling = 1.0 / math.sqrt(query_part.shape[-1])
    scores = (
        jnp.einsum("qhd,khd->hqk", query_part, key_part, preferred_element_type=jnp.float32)
        * scaling
    )
    same = segment[:, None] == segment[None, :]
    return jnp.where(same[None], scores, -1e30)


def attend_forward(item):
    packed, segment = item
    scores = masked_scores(packed[:, 0], packed[:, 1], segment)
    top_val = jnp.max(scores, axis=-1, keepdims=True)
    expo = jnp.exp(scores - top_val)
    total = jnp.sum(expo, axis=-1, keepdims=True)
    probs = (expo / total).astype(jnp.bfloat16)
    mixed = jnp.einsum("hqk,khd->qhd", probs, packed[:, 2], preferred_element_type=jnp.float32)
    return (mixed.astype(jnp.bfloat16), (top_val + jnp.log(total))[..., 0])


def attend_backward(item):
    packed, segment, log_sum, grad_out = item
    query_part = packed[:, 0]
    key_part = packed[:, 1]
    value_part = packed[:, 2]
    scaling = 1.0 / math.sqrt(query_part.shape[-1])
    scores = masked_scores(query_part, key_part, segment)
    probs = jnp.exp(scores - log_sum[..., None])
    probs_low = probs.astype(jnp.bfloat16)
    grad_prob = jnp.einsum("qhd,khd->hqk", grad_out, value_part, preferred_element_type=jnp.float32)
    grad_value = jnp.einsum("hqk,qhd->khd", probs_low, grad_out, preferred_element_type=jnp.float32)
    delta = jnp.sum(probs * grad_prob, axis=-1, keepdims=True)
    grad_score = (probs * (grad_prob - delta)).astype(jnp.bfloat16)
    grad_query = (
        jnp.einsum("hqk,khd->qhd", grad_score, key_part, preferred_element_type=jnp.float32)
        * scaling
    )
    grad_key = (
        jnp.einsum("hqk,qhd->khd", grad_score, query_part, preferred_element_type=jnp.float32)
        * scaling
    )
    return jnp.stack([grad_query, grad_key, grad_value], axis=1).astype(jnp.bfloat16)


def local(
    tokens,
    segment_ids,
    norm1_gain,
    norm1_shift,
    qkv_weight,
    qv_bias,
    out_weight,
    out_bias,
    norm2_gain,
    norm2_shift,
    up_weight,
    up_bias,
    down_weight,
    down_bias,
    cotangent,
):
    head_width = qkv_weight.shape[2]
    local_heads = head_width // HD
    seq_len = segment_ids.shape[1]
    qkv_flat = qkv_weight.reshape(qkv_weight.shape[0], 3 * head_width)
    gain_one = norm1_gain.astype(jnp.float32)
    gain_two = norm2_gain.astype(jnp.float32)
    resid = tokens.astype(jnp.float32)
    normed, hat_one, inv_one = norm_forward(resid, gain_one, norm1_shift.astype(jnp.float32))
    first_low = normed.astype(jnp.bfloat16)
    first_rows = gather_gy(first_low)
    qkv_all = sum_over_gx(first_rows, lambda piece: times_right(piece, qkv_flat))
    bias_full = jnp.stack([qv_bias[0], jnp.zeros_like(qv_bias[0]), qv_bias[1]]).astype(jnp.float32)
    qkv_low = (qkv_all.reshape(-1, 3, head_width) + bias_full[None]).astype(jnp.bfloat16)
    packed = qkv_low.reshape(-1, seq_len, 3, local_heads, HD)
    mixed, log_sums = lax.map(attend_forward, (packed, segment_ids))
    mixed_low = mixed.reshape(-1, head_width)
    mixed_rows = gather_gx(mixed_low)
    branch = sum_over_gy(
        mixed_rows, lambda piece: times_right(piece, out_weight)
    ) + out_bias.astype(jnp.float32)
    middle = resid + branch
    normed_two, hat_two, inv_two = norm_forward(middle, gain_two, norm2_shift.astype(jnp.float32))
    second_low = normed_two.astype(jnp.bfloat16)
    second_rows = gather_gy(second_low)
    hidden = sum_over_gx(second_rows, lambda piece: times_right(piece, up_weight)) + up_bias.astype(
        jnp.float32
    )
    active, gelu_pull = jax.vjp(exact_gelu, hidden)
    active_low = active.astype(jnp.bfloat16)
    active_rows = gather_gx(active_low)
    branch_two = sum_over_gy(
        active_rows, lambda piece: times_right(piece, down_weight)
    ) + down_bias.astype(jnp.float32)
    output = (middle + branch_two).astype(jnp.bfloat16)
    grad_top = cotangent.astype(jnp.float32)
    down_bias_grad = jnp.sum(grad_top, axis=0)
    grad_top_rows = gather_gy(cotangent)
    down_weight_grad = times_outer(active_rows, grad_top_rows)
    grad_active = sum_over_gx(grad_top_rows, lambda piece: times_back(piece, down_weight))
    grad_hidden = gelu_pull(grad_active)[0].astype(jnp.bfloat16)
    up_bias_grad = jnp.sum(grad_hidden.astype(jnp.float32), axis=0)
    hidden_rows = gather_gx(grad_hidden)
    up_weight_grad = times_outer(second_rows, hidden_rows)
    grad_norm_two = sum_over_gy(hidden_rows, lambda piece: times_back(piece, up_weight))
    grad_in_two, norm2_gain_grad, norm2_shift_grad = norm_backward(
        grad_norm_two, hat_two, inv_two, gain_two
    )
    grad_middle = grad_top + grad_in_two
    grad_branch = grad_middle.astype(jnp.bfloat16)
    out_bias_grad = jnp.sum(grad_branch.astype(jnp.float32), axis=0)
    branch_rows = gather_gy(grad_branch)
    out_weight_grad = times_outer(mixed_rows, branch_rows)
    grad_mixed = sum_over_gx(branch_rows, lambda piece: times_back(piece, out_weight)).astype(
        jnp.bfloat16
    )
    grad_mixed = grad_mixed.reshape(-1, seq_len, local_heads, HD)
    grad_packed = lax.map(attend_backward, (packed, segment_ids, log_sums, grad_mixed))
    grad_qkv = grad_packed.reshape(-1, 3 * head_width)
    third_sums = jnp.sum(grad_qkv.astype(jnp.float32), axis=0).reshape(3, head_width)
    qv_bias_grad = jnp.stack([third_sums[0], third_sums[2]])
    qkv_rows = gather_gx(grad_qkv)
    qkv_weight_grad = times_outer(first_rows, qkv_rows).reshape(qkv_weight.shape)
    grad_norm_one = sum_over_gy(qkv_rows, lambda piece: times_back(piece, qkv_flat))
    grad_in_one, norm1_gain_grad, norm1_shift_grad = norm_backward(
        grad_norm_one, hat_one, inv_one, gain_one
    )
    input_grad = (grad_middle + grad_in_one).astype(jnp.bfloat16)
    qkv_weight_grad, out_weight_grad, up_weight_grad, down_weight_grad = (
        lax.psum_scatter(qkv_weight_grad, "dp", scatter_dimension=0, tiled=True),
        lax.psum_scatter(out_weight_grad, "dp", scatter_dimension=1, tiled=True),
        lax.psum_scatter(up_weight_grad, "dp", scatter_dimension=0, tiled=True),
        lax.psum_scatter(down_weight_grad, "dp", scatter_dimension=0, tiled=True),
    )
    qkv_weight_grad = qkv_weight_grad[None]
    out_weight_grad = out_weight_grad[:, None, :]
    up_weight_grad = up_weight_grad[None]
    down_weight_grad = down_weight_grad[None]
    (
        norm1_gain_grad,
        norm1_shift_grad,
        norm2_gain_grad,
        norm2_shift_grad,
        out_bias_grad,
        down_bias_grad,
    ) = lax.psum(
        (
            norm1_gain_grad,
            norm1_shift_grad,
            norm2_gain_grad,
            norm2_shift_grad,
            out_bias_grad,
            down_bias_grad,
        ),
        ("dp", "gy"),
    )
    up_bias_grad, qv_bias_grad = lax.psum((up_bias_grad, qv_bias_grad), ("dp", "gx"))
    return (
        output,
        input_grad,
        norm1_gain_grad,
        norm1_shift_grad,
        qkv_weight_grad,
        qv_bias_grad,
        out_weight_grad,
        out_bias_grad,
        norm2_gain_grad,
        norm2_shift_grad,
        up_weight_grad,
        up_bias_grad,
        down_weight_grad,
        down_bias_grad,
    )


def flip1(i):
    return i + 1 - 2 * lax.rem(i, 2)


def flip2(i):
    return i + 2 - 4 * lax.div(i, 2)


def place():
    dp, c, z = lax.axis_index("dp"), lax.axis_index("gx"), lax.axis_index("gy")
    dps = (dp, flip1(dp), flip2(dp), 3 - dp)
    zs = (z, flip1(z), flip2(z), 3 - z)
    x_dev = (dps[1], c, z)
    y_dev = (dps[2], c, z)
    c_dev = (dp, 1 - c, z)
    z_devs = (None,) + tuple((dp, c, zz) for zz in zs[1:])
    return dps, zs, x_dev, y_dev, c_dev, z_devs


def greet(devices):
    barrier = pltpu.get_barrier_semaphore()
    for device in devices:
        pl.semaphore_signal(barrier, inc=1, device_id=device, device_id_type=MESH)
    pl.semaphore_wait(barrier, len(devices))


WINDOW = 6
ORDER = tuple((m, k) for m in range(2) for k in (1, 2, 3)) + tuple((m, k) for k in (1, 2, 3) for m in (2, 3))
N_PAIR = 9


class Sems:
    def __init__(self, ss, rs):
        self.ss, self.rs, self.n = ss, rs, 0

    def at(self, i, src, dst, device):
        return pltpu.make_async_remote_copy(
            src, dst, self.ss.at[i], self.rs.at[i], device_id=device, device_id_type=MESH
        )

    def block(self, count):
        self.n += count
        return self.n - count

    def remote(self, src, dst, device):
        return self.at(self.block(1), src, dst, device)


class Locals:
    def __init__(self, ls):
        self.ls, self.n, self.open = ls, 0, []

    def at(self, i, src, dst):
        return pltpu.make_async_copy(src, dst, self.ls.at[i])

    def block(self, count):
        self.n += count
        return self.n - count

    def copy(self, src, dst):
        copy = self.at(self.block(1), src, dst)
        copy.start()
        return copy

    def later(self, src, dst):
        self.open.append(self.copy(src, dst))

    def close(self):
        for copy in self.open:
            copy.wait()


class Queue:
    def __init__(self, width):
        self.width, self.open = width, []

    def start(self, copy):
        if len(self.open) >= self.width:
            self.open.pop(0).wait_send()
        copy.start()
        self.open.append(copy)

    def close(self):
        for copy in self.open:
            copy.wait_send()


def weight_cuts(side, raw, full, crel):
    qf, ow, up, dn = raw
    wq, wo, wu, wd = full
    cols = pl.ds(crel * 512, 512)
    cuts = [[], [], [], []]
    for t in range(3):
        off = pl.multiple_of(t * 256 + side * 128, 128)
        cuts[0].append((qf.at[:, :, pl.ds(off, 128)], wq.at[0, crel, :, :, pl.ds(t * 128, 128)]))
    cuts[1].append((ow.at[side], wo.at[0, :, :, cols]))
    for t in range(4):
        off = pl.multiple_of(t * 256 + side * 128, 128)
        cuts[2].append((up.at[:, :, pl.ds(off, 128)], wu.at[0, crel, :, :, pl.ds(t * 128, 128)]))
    cuts[3].append((dn.at[:, side], wd.at[0, crel]))
    return cuts


class Gather:
    def __init__(self, sems, loc, here, c, raw, full):
        self.sems, self.loc, self.raw, self.full, self.c = sems, loc, raw, full, c
        self.dps, self.zs, self.x_dev, self.y_dev, self.c_dev, self.z_devs = here
        self.theirs = [[sems.remote(src, dst, self.c_dev) for src, dst in group] for group in weight_cuts(1 - c, raw, full, 1)]
        self.mine = weight_cuts(c, raw, full, 0)
        self.own, self.copies, self.ready = {}, {}, set()
        self.queues = {"x": Queue(99), "y": Queue(99), "z": Queue(WINDOW)}
        self.gen = self.steps()

    def piece(self, m, k, dd):
        return self.full[m].at[k, dd] if m == 1 else self.full[m].at[k, :, dd]

    def pair_start(self, m):
        for copy in self.theirs[m]:
            copy.start()
        self.own[m] = [self.loc.copy(src, dst) for src, dst in self.mine[m]]

    def own_ready(self, m):
        if m not in self.ready:
            self.ready.add(m)
            for copy in self.own[m]:
                copy.wait()
            for copy in self.theirs[m]:
                copy.wait_recv()

    def z_send(self, s):
        m, k = ORDER[s]
        self.own_ready(m)
        copy = self.sems.remote(self.piece(m, 0, self.dps[0]), self.piece(m, k, self.dps[0]), self.z_devs[k])
        self.copies["z", m, k] = copy
        self.queues["z"].start(copy)

    def by_x(self, m, k):
        return (k == 2) == (m in (0, 2))

    def forward(self, s):
        m, k = ORDER[s]
        if self.by_x(m, k):
            self.copies["x", m, k].wait_recv()
            src = self.piece(m, k, self.dps[1])
            copy, axis = self.sems.remote(src, src, self.y_dev), "y"
        else:
            self.copies["y", m, k].wait_recv()
            src = self.piece(m, k, self.dps[2])
            copy, axis = self.sems.remote(src, src, self.x_dev), "x"
        self.copies["d", m, k] = copy
        self.queues[axis].start(copy)

    def steps(self):
        for s, (m, k) in enumerate(ORDER):
            self.copies["z", m, k].wait_recv()
            if s + WINDOW < len(ORDER):
                self.z_send(s + WINDOW)
            src = self.piece(m, k, self.dps[0])
            for axis, dev in (("x", self.x_dev), ("y", self.y_dev)):
                copy = self.sems.remote(src, src, dev)
                self.copies[axis, m, k] = copy
                self.queues[axis].start(copy)
            yield
            if s > 0:
                self.forward(s - 1)
                yield
        self.forward(len(ORDER) - 1)
        yield

    def poll(self, n=1):
        for _ in range(n):
            next(self.gen, None)

    def need(self, m, k):
        if k == 0:
            self.own_ready(m)
            return
        while ("d", m, k) not in self.copies:
            self.poll()
        self.copies["y" if self.by_x(m, k) else "x", m, k].wait_recv()
        self.copies["d", m, k].wait_recv()

    def close(self):
        for group in self.theirs:
            for copy in group:
                copy.wait_send()
        for queue in self.queues.values():
            queue.close()


def dot_nt(a, b):
    return lax.dot_general(a, b, (((1,), (1,)), ((), ())), preferred_element_type=F32)


def dot_tn(a, b):
    return lax.dot_general(a, b, (((0,), (0,)), ((), ())), preferred_element_type=F32)


def dot_nn(a, b):
    return lax.dot_general(a, b, (((1,), (0,)), ((), ())), preferred_element_type=F32)


BQ = 256


SMALL = 64


def small_block(i):
    return pl.ds(pl.multiple_of(i * SMALL, SMALL), SMALL)


def row_block(i):
    return pl.ds(pl.multiple_of(i * BQ, BQ), BQ)


def segments(shape, axis, start, n1, seq):
    pos = (lax.broadcasted_iota(jnp.int32, shape, axis) + start).astype(F32)
    return (pos >= n1).astype(F32) + (pos >= float(seq)).astype(F32)


def masked_keys(big, kx, zr, n1, seq):
    tp = big.shape[0]
    lane = lax.broadcasted_iota(jnp.int32, (1, 128), 1)
    seg = segments((tp, 1), 0, 0, n1, seq)
    for h in range(2):
        t = lane - 64 * (1 - h)
        away = jnp.where(seg == t.astype(F32), 0.0, -1e30)
        away = jnp.where(t < 0, 0.0, jnp.where(t < 3, away, 0.0)).astype(BF)
        kx[h] = jnp.where(lax.div(lane, 64) == h, big[:, zr * 384 + 128 : zr * 384 + 256], away)


def attend_fwd_rows(big, lse_ref, kx, zr, start, count, n1, seq):
    lane = lax.broadcasted_iota(jnp.int32, (1, 128), 1)
    base = zr * 384
    rows = slice(start, start + count)
    q = big[rows, base : base + 128] * BF(0.125)
    seg = segments((count, 1), 0, start, n1, seq)
    out = jnp.zeros((count, 128), F32)
    for h in range(2):
        mask = lax.div(lane, 64) == h
        own_seg = (seg == (lane - 64 * (1 - h)).astype(F32)).astype(BF)
        s = dot_nt(jnp.where(mask, q, own_seg), kx[h])
        top = jnp.max(s, axis=1, keepdims=True)
        e = jnp.exp(s - top)
        total = jnp.sum(e, axis=1, keepdims=True)
        mixed = dot_nn(e.astype(BF), big[:, base + 256 : base + 384]) / total
        out = jnp.where(mask, mixed, out)
        lse = jnp.broadcast_to(top + jnp.log(total), (count, 128))
        lse_ref[2 * zr + h : 2 * zr + h + 1, rows] = jnp.transpose(lse)[0:1]
    big[rows, 1536 + zr * 128 : 1664 + zr * 128] = out.astype(BF)


def halves_mean(a, b):
    return (jnp.sum(a, axis=1, keepdims=True) + jnp.sum(b, axis=1, keepdims=True)) * (1.0 / D)


def forward_kernel(
    seq, x_own, g_own, v0, v1, v2, v3, v4, v5, up_bias, qv_bias, ids, qf, ow, up, dn,
    wq_out, wo_out, wu_out, n1_out, x_out, g_out, vec_out, a1_out, big_out, lse_out, m_out, dh_out, gd_out, gu_out, rxu_out,
    usum, y_out,
    x_oth, g_oth, vec_all, bias_all, cnt, wq, wo, wu, wd, act, big, lse, m, pb, pr, pr2, dh, gd, gu, kx,
    ss, rs, ls,
):
    tp = x_own.shape[0]
    nb = tp // BQ
    here = place()
    dps, zs, x_dev, y_dev, c_dev, z_devs = here
    c, z = lax.axis_index("gx"), zs[0]
    sems, loc = Sems(ss, rs), Locals(ls)
    gather = Gather(sems, loc, here, c, (qf, ow, up, dn), (wq, wo, wu, wd))
    poll = gather.poll

    ids_low = (ids[...] == 0).astype(F32)
    for r in range(2):
        cnt[0, r] = jnp.broadcast_to(jnp.sum(ids_low[r : r + 1], axis=1, keepdims=True), (8, 128))
    vec_all[...] = jnp.zeros_like(vec_all)
    bias_all[...] = jnp.zeros_like(bias_all)
    for i, ref in enumerate((v0, v1, v2, v3, v4, v5)):
        vec_all[0, i : i + 1, :] = ref[...].astype(F32).reshape(1, 512)

    def cut(row, j):
        return jnp.where(c == 0, row[:, 256 * j : 256 * j + 128], row[:, 256 * j + 128 : 256 * j + 256])

    up_row = up_bias[...].astype(F32).reshape(1, 1024)
    qv_rows = qv_bias[...].astype(F32)
    for j in range(4):
        bias_all[0, 0:1, 128 * j : 128 * j + 128] = cut(up_row, j)
    for j in range(2):
        bias_all[0, 1:2, 128 * j : 128 * j + 128] = cut(qv_rows[j : j + 1], 0)
    usum[...] = jnp.zeros_like(usum)
    greet((x_dev, y_dev, c_dev) + z_devs[1:])
    gather.pair_start(0)
    small = [sems.remote(vec_all.at[0], vec_all.at[1], c_dev), sems.remote(cnt.at[0], cnt.at[1], c_dev)]
    small += [sems.remote(bias_all.at[0], bias_all.at[k], z_devs[k]) for k in (1, 2, 3)]
    x_copy = sems.remote(x_own, x_oth, c_dev)
    for copy in small + [x_copy]:
        copy.start()
    for s in range(3):
        gather.z_send(s)
    for m_ in (1, 2, 3):
        gather.pair_start(m_)
    for copy in small:
        copy.wait_recv()
    x_copy.wait_recv()
    vec = [(vec_all[0, i : i + 1, :], vec_all[1, i : i + 1, :]) for i in range(6)]
    n1 = cnt[lax.rem(lax.div(z, 2) + c, 2), lax.rem(z, 2)]
    n1_out[...] = n1
    n1 = n1[0:1, 0:1]
    loc.later(x_oth, x_out)
    loc.later(vec_all, vec_out)

    @pl.loop(0, nb)
    def _(i):
        rows = row_block(i)
        xo, xt = x_own[rows, :].astype(F32), x_oth[rows, :].astype(F32)
        mean = halves_mean(xo, xt)
        inv = lax.rsqrt(halves_mean(xo * xo, xt * xt) - mean * mean + norm_eps)
        act[rows, 0:512] = ((xo - mean) * inv * vec[0][0] + vec[1][0]).astype(BF)
        act[rows, 512:1024] = ((xt - mean) * inv * vec[0][1] + vec[1][1]).astype(BF)

    a1_copy = loc.copy(act, a1_out)
    g_copy = sems.remote(g_own, g_oth, c_dev)
    g_copy.start()
    for s in range(3, WINDOW):
        gather.z_send(s)
    poll()
    for zr in range(4):
        gather.need(0, zr)
        qb, vb = bias_all[zr, 1:2, 0:128], bias_all[zr, 1:2, 128:256]
        bias = jnp.concatenate([qb, jnp.zeros_like(qb), vb], axis=1)

        @pl.loop(0, nb)
        def _(i):
            rows = row_block(i)
            big[rows, zr * 384 : zr * 384 + 384] = (dot_nn(act[rows, :], wq[zr].reshape(1024, 384)) + bias).astype(BF)

        masked_keys(big, kx, zr, n1, seq)
        poll()
        attend_fwd_rows(big, lse, kx, zr, 0, tp // 2, n1, seq)
        poll()
        attend_fwd_rows(big, lse, kx, zr, tp // 2, tp // 2, n1, seq)
        poll()
    loc.later(wq, wq_out)
    loc.later(lse, lse_out)
    big_copy = loc.copy(big, big_out)
    g_copy.wait_recv()
    loc.later(g_oth, g_out)
    for zr in range(4):
        gather.need(1, zr)
    loc.later(wo, wo_out)
    swap = sems.block(nb)

    @pl.loop(0, nb)
    def _(i):
        rows = row_block(i)
        part = dot_nn(big[rows, 1536:2048], wo[...].reshape(512, 1024))
        pb[rows, 0:512] = part[:, 512:].astype(BF)
        pb[rows, 512:1024] = part[:, :512].astype(BF)
        sems.at(swap + i, pb.at[rows], pr.at[rows], c_dev).start()
        m[rows, :] = part

    a1_copy.wait()
    poll()

    @pl.loop(0, nb)
    def _(i):
        rows = row_block(i)
        sems.at(swap + i, pb.at[rows], pr.at[rows], c_dev).wait()
        mo = x_own[rows, :].astype(F32) + m[rows, 0:512] + pr[rows, 0:512].astype(F32) + vec[2][0]
        mt = x_oth[rows, :].astype(F32) + m[rows, 512:1024] + pr[rows, 512:1024].astype(F32) + vec[2][1]
        mean = halves_mean(mo, mt)
        inv = lax.rsqrt(halves_mean(mo * mo, mt * mt) - mean * mean + norm_eps)
        m[rows, 0:512] = mo
        m[rows, 512:1024] = mt
        act[rows, 0:512] = ((mo - mean) * inv * vec[3][0] + vec[4][0]).astype(BF)
        act[rows, 512:1024] = ((mt - mean) * inv * vec[3][1] + vec[4][1]).astype(BF)

    m_copy = loc.copy(m, m_out)
    outs, early = {}, []
    last = sems.block(nb)

    def send_down():
        @pl.loop(0, nb)
        def _(i):
            rows = row_block(i)
            pb[rows, 0:512] = m[rows, 512:1024].astype(BF)
            sems.at(last + i, pb.at[rows, pl.ds(0, 512)], pr2.at[rows], c_dev).start()

    for zr in range(4):
        gather.need(2, zr)
        gather.need(3, zr)
        if zr == 3:
            for key in (("u", 1), ("u", 2),):
                outs.pop(key).wait()
            for slot in (1, 0):
                for j, zz, dev, rels in ((0, 1, x_dev, (1, 3)), (1, 2, y_dev, (2, 3)),):
                    for grad_h, land in ((gu_out, rxu_out),):
                        early.append(sems.remote(grad_h.at[zz, dps[rels[slot]]], land.at[j, slot], dev))
                        early[-1].start()
        loc.later(wu.at[zr], wu_out.at[zr])
        bias = bias_all[zr, 0:1, :]
        lo = zr * 512
        if zr == 0:
            big_copy.wait()
            m_copy.wait()

        def hidden(first, last):
            @pl.loop(first, last)
            def _(i):
                rows = row_block(i)
                h = dot_nn(act[rows, :], wu[zr].reshape(1024, 512)) + bias
                w_own, w_oth = wd[zr, 0].reshape(512, 512), wd[zr, 1].reshape(512, 512)
                du = dot_nt(g_own[rows, :], w_own) + dot_nt(g_oth[rows, :], w_oth)
                cdf = 0.5 * (1.0 + lax.erf(h * math.sqrt(0.5)))
                slope = cdf + h * jnp.exp(-0.5 * h * h) * (1.0 / math.sqrt(2 * math.pi))
                u = (h * cdf).astype(BF)
                grad = (du * slope).astype(BF)
                big[rows, lo : lo + 512] = u
                dh[rows, lo : lo + 512] = grad
                usum[zr, 6:7, :] += jnp.sum(grad.astype(F32), axis=0, keepdims=True)
                m[rows, 0:512] += dot_nn(u, w_own)
                if zr == 0:
                    m[rows, 512:1024] = dot_nn(u, w_oth)
                else:
                    m[rows, 512:1024] += dot_nn(u, w_oth)

        for first, end in ((0, 2), (2, 4), (4, nb)):
            hidden(first, end)
            poll()
        if zr == 3:
            send_down()
        loc.later(dh.at[:, pl.ds(lo, 512)], dh_out.at[:, pl.ds(lo, 512)])
        slot = zr % 2
        for key in (("d", zr - 2), ("u", zr - 2)):
            if key in outs:
                outs.pop(key).wait()
        for j, gref in enumerate((g_own, g_oth)):
            gd[slot, :, :, 512 * j : 512 * j + 512] = dot_tn(big[:, lo : lo + 512], gref[...]).astype(BF).reshape(4, 128, 512)
        outs["d", zr] = loc.copy(gd.at[slot], gd_out.at[zr])
        poll()
        for j in range(2):
            block = dot_tn(act[:, 512 * j : 512 * j + 512], dh[:, lo : lo + 512])
            gu[slot, :, 128 * j : 128 * j + 128, :] = block.astype(BF).reshape(4, 128, 512)
        outs["u", zr] = loc.copy(gu.at[slot], gu_out.at[zr])
        poll()
    def result(rows, i):
        sems.at(last + i, pb.at[rows, pl.ds(0, 512)], pr2.at[rows], c_dev).wait()
        return (m[rows, 0:512] + pr2[rows, :].astype(F32) + vec[5][0]).astype(BF)

    @pl.loop(0, nb - 1)
    def _(i):
        rows = row_block(i)
        y_out[rows, :] = result(rows, i)

    end = tp - BQ
    y_out[end:seq, :] = result(pl.ds(end, BQ), nb - 1)[: seq - end]

    for copy in small + [x_copy, g_copy]:
        copy.wait_send()
    for copy in early:
        copy.wait()
    for copy in outs.values():
        copy.wait()
    gather.close()
    loc.close()


def forward_all(x_own, g_own, vectors, up_bias, qv_bias, ids, qf, ow, up, dn):
    tp = x_own.shape[0]
    seq = ids.shape[1]
    n_remote = N_PAIR + 7 + 48 + 2 * (tp // BQ) + 4
    sds = jax.ShapeDtypeStruct
    vm = pltpu.VMEM
    wide = (4, 2, 4, 128, 512)
    weights = [(4, 2, 4, 128, 384), (4, 4, 32, 1024), wide, wide]
    out_shape = [sds(s, BF) for s in weights[:3]] + [
        sds((8, 128), F32), sds((tp, 512), BF), sds((tp, 512), BF), sds((2, 8, 512), F32), sds((tp, 1024), BF),
        sds((tp, 2048), BF), sds((8, tp), F32), sds((tp, 1024), F32), sds((tp, 2048), BF), sds((4, 4, 128, 1024), BF),
        sds((4, 4, 256, 512), BF), sds((2, 2, 256, 512), BF), sds((4, 8, 512), F32), sds((seq, 512), BF),
    ]
    scratch = [vm((tp, 512), BF), vm((tp, 512), BF), vm((2, 8, 512), F32), vm((4, 8, 512), F32), vm((2, 2, 8, 128), F32)]
    scratch += [vm(s, BF) for s in weights]
    scratch += [
        vm((tp, 1024), BF), vm((tp, 2048), BF), vm((8, tp), F32), vm((tp, 1024), F32), vm((tp, 1024), BF), vm((tp, 1024), BF),
        vm((tp, 512), BF), vm((tp, 2048), BF), vm((2, 4, 128, 1024), BF), vm((2, 4, 256, 512), BF), vm((2, tp, 128), BF),
        pltpu.SemaphoreType.DMA((n_remote,)), pltpu.SemaphoreType.DMA((n_remote,)), pltpu.SemaphoreType.DMA((40,)),
    ]
    return pl.pallas_call(
        functools.partial(forward_kernel, seq),
        out_shape=out_shape,
        in_specs=[VMEM] * 11 + [ANY] * 4,
        out_specs=[ANY] * 3 + [VMEM] + [ANY] * 11 + [VMEM] * 2,
        scratch_shapes=scratch,
        compiler_params=pltpu.CompilerParams(collective_id=0, has_side_effects=True, vmem_limit_bytes=63 << 20),
        cost_estimate=pl.CostEstimate(flops=40 * 10**9, bytes_accessed=80 * 10**6, transcendentals=10**7),
        name="forward",
    )(x_own, g_own, *vectors, up_bias, qv_bias, ids, qf, ow, up, dn)


BLOCKS = ((128, 1024), (256, 512), (128, 256), (256, 384))
ZORDER = (1, 2, 3, 0)


def half_block(m):
    rows, cols = BLOCKS[m]
    return (rows // 2, cols) if m in (1, 3) else (rows, cols // 2)


class Landed:
    def __init__(self, copy):
        self.wait_recv = copy.wait


class Scatter:
    def __init__(self, sems, here, g, first_src, rx, ry, rz, sw, out, c):
        self.sems, self.g, self.first_src = sems, g, first_src
        self.dps, self.zs, self.x_dev, self.y_dev, self.c_dev, self.z_devs = here
        self.rx, self.ry, self.rz, self.sw, self.out, self.c = rx, ry, rz, sw, out, c
        self.first, self.second, self.third, self.last = {}, {}, {}, {}
        self.queues = {axis: Queue(99) for axis in "xyz"}
        self.point = 0

    def poll(self):
        for code in SCHEDULE[self.point]:
            stage, m, zr, slot = code // 1000, code // 100 % 10, code // 10 % 10, code % 10
            if stage == 1:
                self.stage1(m, zr, slot)
            elif stage == 2:
                self.stage2(m, zr)
            elif stage == 3:
                self.stage3(m, zr)
            else:
                self.stage4(m)
        self.point += 1

    def stage1(self, m, zr, slot):
        axis, dev, rels = ("x", self.x_dev, (1, 3)) if zr < 2 else ("y", self.y_dev, (2, 3))
        src = self.first_src[m].at[zr, self.dps[rels[slot]]]
        copy = self.sems.remote(src, self.rx[m].at[zr, slot], dev)
        self.first[m, zr, slot] = copy
        self.queues[axis].start(copy)

    def stage2(self, m, zr):
        axis, dev, rel = ("y", self.y_dev, 2) if zr < 2 else ("x", self.x_dev, 1)
        g, dd = self.g[m], self.dps[rel]
        self.first[m, zr, 1].wait_recv()
        g[zr, dd] = (g[zr, dd].astype(F32) + self.rx[m][zr, 1].astype(F32)).astype(BF)
        copy = self.sems.remote(g.at[zr, dd], self.ry[m].at[zr], dev)
        self.second[m, zr] = copy
        self.queues[axis].start(copy)

    def stage3(self, m, zr):
        g, dd = self.g[m], self.dps[0]
        self.first[m, zr, 0].wait_recv()
        self.second[m, zr].wait_recv()
        g[zr, dd] = (g[zr, dd].astype(F32) + self.rx[m][zr, 0].astype(F32) + self.ry[m][zr].astype(F32)).astype(BF)
        if zr > 0:
            copy = self.sems.remote(g.at[zr, dd], self.rz[m].at[zr - 1], self.z_devs[zr])
            self.third[m, zr] = copy
            self.queues["z"].start(copy)

    def stage4(self, m):
        for zr in (1, 2, 3):
            self.third[m, zr].wait_recv()
        rz = self.rz[m]
        total = self.g[m][0, self.dps[0]].astype(F32) + rz[0].astype(F32) + rz[1].astype(F32) + rz[2].astype(F32)
        rows, cols = BLOCKS[m]
        sw, out, c = self.sw[m], self.out[m], self.c
        if m in (1, 3):
            keep, sw[...] = total[: rows // 2], total[rows // 2 :]
            pairs = []
            for j in range(cols // 128):
                mine = pl.ds(pl.multiple_of(j * 256 + c * 128, 128), 128)
                out[:, mine] = keep[:, j * 128 : j * 128 + 128]
                pairs.append((sw.at[:, pl.ds(j * 128, 128)], out.at[:, mine]))
        else:
            out[c], sw[...] = total[:, : cols // 2], total[:, cols // 2 :]
            pairs = [(sw, out.at[c])]
        self.last[m] = [self.sems.remote(src, dst, self.c_dev) for src, dst in pairs]
        for copy in self.last[m]:
            copy.start()

    def close(self):
        for queue in self.queues.values():
            queue.close()
        for group in self.last.values():
            for copy in group:
                copy.wait()


def attend_bwd_rows(big, do_ref, lse_ref, k_t, dk_acc, dv_acc, zr, lo, hi, n1, seq):
    tp = big.shape[0]
    lane = lax.broadcasted_iota(jnp.int32, (1, 128), 1)
    base = zr * 384
    ocol = 1536 + zr * 128

    @pl.loop(lo, hi)
    def _(i):
        start = pl.multiple_of(i * BQ, BQ)
        rows = pl.ds(start, BQ)
        q = big[rows, base : base + 128]
        do = do_ref[rows, zr * 128 : zr * 128 + 128]
        prod = do.astype(F32) * big[rows, ocol : ocol + 128].astype(F32)
        seg_q = segments((1, BQ), 1, start, n1, seq)
        dq_t = jnp.zeros((128, BQ), F32)
        row = lax.broadcasted_iota(jnp.int32, (128, 1), 0)
        for h in range(2):
            mask = lax.div(lane, 64) == h
            lse = lse_ref[2 * zr + h : 2 * zr + h + 1, rows]
            delta = jnp.sum(jnp.where(mask, prod, 0.0), axis=1, keepdims=True)
            delta = jnp.transpose(jnp.broadcast_to(delta, (BQ, 128)))[0:1]
            qm = jnp.where(mask, q, BF(0)) * BF(0.125)
            dom = jnp.where(mask, do, BF(0))
            for keys in (slice(0, tp // 2), slice(tp // 2, tp)):
                same = segments((tp // 2, 1), 0, keys.start, n1, seq) == seg_q
                s = dot_nt(big[keys, base + 128 : base + 256], qm)
                p = jnp.where(same, jnp.exp(s - lse), 0.0)
                dp = dot_nt(big[keys, base + 256 : base + 384], dom)
                ds = (p * (dp - delta)).astype(BF)
                dv_acc[keys, :] += dot_nn(p.astype(BF), dom)
                dk_acc[keys, :] += dot_nn(ds, qm)
                dq_t += jnp.where(lax.div(row, 64) == h, dot_nn(k_t[:, keys], ds), 0.0)
        dq = jnp.transpose(dq_t)
        big[rows, base : base + 128] = (dq * 0.125).astype(BF)


def backward_kernel(
    seq, x_own, x_oth, g_own_h, g_oth_h, vec_all, n1_ref, usum, lse, a1_h, big_h, m_h, dh_h, gd_h, gu_h, rxu_h, wq_h, wo_h, wu_h,
    grad_out, small_out, out0, out1, out2, out3,
    big, ga, gb, wbuf, wo_v, part, pb, pr, mbuf, act, dm, k_t, dk_acc, dv_acc, vsum, vdp, vz, vzr, vhalf, vc,
    gd, gu, go, gq, rx0, rx1, rx2, rx3, ry0, ry1, ry2, ry3, rz0, rz1, rz2, rz3, sw0, sw1, sw2, sw3,
    ss, rs, ls, free,
):
    tp = big.shape[0]
    nb = tp // BQ
    here = place()
    dps, zs, x_dev, y_dev, c_dev, z_devs = here
    c, z = lax.axis_index("gx"), zs[0]
    xy_dev = (dps[3], c, z)
    sems, loc = Sems(ss, rs), Locals(ls)
    scatter = Scatter(
        sems, here, (gd, gu, go, gq), (gd_h, gu_h, go, gq), (rx0, rx1, rx2, rx3), (ry0, ry1, ry2, ry3), (rz0, rz1, rz2, rz3),
        (sw0, sw1, sw2, sw3), (out0, out1, out2, out3), c,
    )
    poll = scatter.poll
    greet((x_dev, y_dev, xy_dev, c_dev) + z_devs[1:])
    poll()
    dh_in = loc.copy(dh_h, big)
    wu_in = loc.copy(wu_h, wbuf)
    m_sem = loc.block(tp // SMALL)

    def load_m(i):
        return loc.at(m_sem + i, m_h.at[small_block(i)], mbuf.at[lax.rem(i, 2)])

    vec = [(vec_all[0, i : i + 1, :], vec_all[1, i : i + 1, :]) for i in range(6)]
    n1 = n1_ref[0:1, 0:1]
    vsum[...] = usum[...]
    vhalf[...] = jnp.zeros_like(vhalf)
    dh_in.wait()
    wu_in.wait()
    gd_in, gu_in = loc.copy(gd_h, gd), loc.copy(gu_h, gu)
    ga_in, gb_in = loc.copy(g_own_h, ga), loc.copy(g_oth_h, gb)
    wo_in = loc.copy(wo_h, wo_v)
    for j, zr in enumerate((1, 2)):
        for mm, land in ((1, rxu_h),):
            for slot in (1, 0):
                scatter.first[mm, zr, slot] = Landed(loc.copy(land.at[j, slot], scatter.rx[mm].at[zr, slot]))
    load_m(0).start()
    swap = sems.block(nb)

    @pl.loop(0, nb)
    def _(i):
        rows = row_block(i)
        total = dot_nt(big[rows, 0:512], wbuf[0].reshape(1024, 512))
        for zr in range(1, 4):
            total += dot_nt(big[rows, zr * 512 : zr * 512 + 512], wbuf[zr].reshape(1024, 512))
        pb[rows, 0:512] = total[:, 512:].astype(BF)
        pb[rows, 512:1024] = total[:, :512].astype(BF)
        sems.at(swap + i, pb.at[rows], pr.at[rows], c_dev).start()
        part[rows, :] = total

    big_in = loc.copy(big_h, big)
    wq_in = loc.copy(wq_h, wbuf.at[:, :, :, :, pl.ds(0, 384)])
    gd_in.wait()
    gu_in.wait()
    ga_in.wait()
    gb_in.wait()
    poll()
    @pl.loop(0, tp // SMALL)
    def _(i):
        rows = small_block(i)

        @pl.when(i + 1 < tp // SMALL)
        def _():
            load_m(i + 1).start()

        @pl.when(lax.rem(i, BQ // SMALL) == 0)
        def _():
            whole = lax.div(i, BQ // SMALL)
            sems.at(swap + whole, pb.at[row_block(whole)], pr.at[row_block(whole)], c_dev).wait()

        load_m(i).wait()
        slot = lax.rem(i, 2)
        mo, mt = mbuf[slot, :, 0:512], mbuf[slot, :, 512:1024]
        mean = halves_mean(mo, mt)
        inv = lax.rsqrt(halves_mean(mo * mo, mt * mt) - mean * mean + norm_eps)
        ho, ht = (mo - mean) * inv, (mt - mean) * inv
        do_, dt = part[rows, 0:512] + pr[rows, 0:512].astype(F32), part[rows, 512:1024] + pr[rows, 512:1024].astype(F32)
        bo, bt = do_ * vec[3][0], dt * vec[3][1]
        first, second = halves_mean(bo, bt), halves_mean(bo * ho, bt * ht)
        go_, gt = ga[rows, :].astype(F32), gb[rows, :].astype(F32)
        dmo = go_ + inv * (bo - first - ho * second)
        dmt = gt + inv * (bt - first - ht * second)
        dm[rows, :] = dmo
        act[rows, 0:512] = dmo.astype(BF)
        act[rows, 512:1024] = dmt.astype(BF)
        vsum[0, 2:3, :] += jnp.sum(dmo.astype(BF).astype(F32), axis=0, keepdims=True)
        vsum[0, 3:4, :] += jnp.sum(do_ * ho, axis=0, keepdims=True)
        vsum[0, 4:5, :] += jnp.sum(do_, axis=0, keepdims=True)
        vsum[0, 5:6, :] += jnp.sum(go_, axis=0, keepdims=True)

    pl.semaphore_signal(free, inc=1, device_id=c_dev, device_id_type=MESH)
    poll()
    wo_in.wait()
    big_in.wait()
    for j in range(2):
        block = dot_tn(big[:, 1536:2048], act[:, 512 * j : 512 * j + 512]).astype(BF)
        for dd in range(4):
            go[:, dd, :, 128 * j : 128 * j + 128] = block[:, 128 * dd : 128 * dd + 128].reshape(4, 128, 128)

    @pl.loop(0, nb)
    def _(i):
        rows = row_block(i)
        ga[rows, :] = dot_nt(act[rows, :], wo_v[...].reshape(512, 1024)).astype(BF)

    a1_in = loc.copy(a1_h, act)
    xb_in = loc.copy(x_oth, gb)
    poll()
    for step, zr in enumerate(ZORDER):
        base = zr * 384
        dk_acc[...] = jnp.zeros_like(dk_acc)
        dv_acc[...] = jnp.zeros_like(dv_acc)
        k_t[...] = jnp.transpose(big[:, base + 128 : base + 256].astype(F32)).astype(BF)
        for lo, hi in ((0, 2), (2, 4), (4, nb)):
            attend_bwd_rows(big, ga, lse, k_t, dk_acc, dv_acc, zr, lo, hi, n1, seq)
            if hi < nb:
                poll()
        big[:, base + 128 : base + 256] = dk_acc[...].astype(BF)
        big[:, base + 256 : base + 384] = dv_acc[...].astype(BF)
        if step == 0:
            a1_in.wait()
            wq_in.wait()
        for j in range(2):
            block = dot_tn(act[:, 512 * j : 512 * j + 512], big[:, base : base + 384])
            gq[zr, :, 128 * j : 128 * j + 128, :] = block.astype(BF).reshape(4, 128, 384)
        poll()
        for j in (0, 2):
            cols = big[:, base + 128 * j : base + 128 * j + 128].astype(F32)
            vsum[zr, 7:8, 64 * j : 64 * j + 128] = jnp.sum(cols, axis=0, keepdims=True)
        if step < 3:

            @pl.loop(0, nb)
            def _(i):
                rows = row_block(i)
                more = dot_nt(big[rows, base : base + 384], wbuf[zr, :, :, :, 0:384].reshape(1024, 384))
                part[rows, :] = more if step == 0 else part[rows, :] + more

    xa_in = loc.copy(x_own, ga)
    pl.semaphore_wait(free, 1)
    xa_in.wait()
    xb_in.wait()
    swap2 = sems.block(nb)
    base = ZORDER[3] * 384

    @pl.loop(0, nb)
    def _(i):
        rows = row_block(i)
        total = part[rows, :] + dot_nt(big[rows, base : base + 384], wbuf[ZORDER[3], :, :, :, 0:384].reshape(1024, 384))
        pb[rows, 0:512] = total[:, 512:].astype(BF)
        pb[rows, 512:1024] = total[:, :512].astype(BF)
        sems.at(swap2 + i, pb.at[rows], pr.at[rows], c_dev).start()
        part[rows, :] = total
        xo, xt = ga[rows, :].astype(F32), gb[rows, :].astype(F32)
        mean = halves_mean(xo, xt)
        inv = lax.rsqrt(halves_mean(xo * xo, xt * xt) - mean * mean + norm_eps)
        vsum[0, 0:1, :] += jnp.sum(total[:, :512] * ((xo - mean) * inv), axis=0, keepdims=True)
        vsum[0, 1:2, :] += jnp.sum(total[:, :512], axis=0, keepdims=True)
        vhalf[0, 0:1, :] += jnp.sum(total[:, 512:] * ((xt - mean) * inv), axis=0, keepdims=True)
        vhalf[0, 1:2, :] += jnp.sum(total[:, 512:], axis=0, keepdims=True)

    half_copy = sems.remote(vhalf.at[0], vhalf.at[1], c_dev)
    half_copy.start()
    poll()
    half_copy.wait()
    vsum[0] += vhalf[1]
    for k in (1, 2, 3):
        vsum[k, 0:6, :] = vsum[0, 0:6, :]
    dp_copies = [sems.remote(vsum, vdp.at[k], dev) for k, dev in enumerate((x_dev, y_dev, xy_dev))]
    for copy in dp_copies:
        copy.start()
    poll()

    @pl.loop(0, nb)
    def _(i):
        rows = row_block(i)
        sems.at(swap2 + i, pb.at[rows], pr.at[rows], c_dev).wait()
        xo, xt = ga[rows, :].astype(F32), gb[rows, :].astype(F32)
        mean = halves_mean(xo, xt)
        inv = lax.rsqrt(halves_mean(xo * xo, xt * xt) - mean * mean + norm_eps)
        ho, ht = (xo - mean) * inv, (xt - mean) * inv
        bo = (part[rows, 0:512] + pr[rows, 0:512].astype(F32)) * vec[0][0]
        bt = (part[rows, 512:1024] + pr[rows, 512:1024].astype(F32)) * vec[0][1]
        first, second = halves_mean(bo, bt), halves_mean(bo * ho, bt * ht)
        ga[rows, :] = (dm[rows, :] + inv * (bo - first - ho * second)).astype(BF)

    loc.later(ga, grad_out)
    for copy in dp_copies:
        copy.wait()
    vz[...] = (vsum[...] + vdp[0]) + (vdp[1] + vdp[2])
    z_copies = [sems.remote(vz.at[k], vzr.at[k], z_devs[k]) for k in (1, 2, 3)]
    for copy in z_copies:
        copy.start()
    poll()
    for copy in z_copies:
        copy.wait()
    vc[0] = (vz[0] + vzr[1]) + (vzr[2] + vzr[3])
    c_copy = sems.remote(vc.at[0], vc.at[1], c_dev)
    c_copy.start()
    poll()
    c_copy.wait()
    small_out[...] = vc[...]
    loc.close()
    scatter.close()


SCHEDULE = (
    (1130, 1100, 1010, 1030),
    (2110, 1011, 1031, 1000, 2120),
    (),
    (),
    (1020, 1021),
    (2030, 3110),
    (1311, 2010, 3120),
    (1310, 1131),
    (2020, 3030, 2310),
    (1001,),
    (1321, 1320, 1101, 3010, 2130),
    (3310, 3020),
    (1331, 1330),
    (2000, 1210, 1211, 2320),
    (2100, 3130, 1200),
    (1301, 2210, 2330),
    (3320,),
    (),
    (3210, 1230, 1231, 3000, 4000, 1300, 1201),
    (1220, 1221, 3100, 4100, 2300, 3330, 2200, 2230, 2220, 3230, 3200, 3220, 3300, 4300, 4200),
)


def backward_all(seq, *args):
    tp = args[0].shape[0]
    nb = tp // BQ
    sds = jax.ShapeDtypeStruct
    vm = pltpu.VMEM
    halves = [half_block(m) for m in range(4)]
    n_remote = 4 * (8 + 4 + 3) - 4 + 9 + 2 * nb + 8
    scratch = [
        vm((tp, 2048), BF), vm((tp, 512), BF), vm((tp, 512), BF), vm((4, 2, 4, 128, 512), BF), vm((4, 4, 32, 1024), BF),
        vm((tp, 1024), F32), vm((tp, 1024), BF), vm((tp, 1024), BF), vm((2, SMALL, 1024), F32), vm((tp, 1024), BF),
        vm((tp, 512), F32), vm((128, tp), BF), vm((tp, 128), F32), vm((tp, 128), F32), vm((4, 8, 512), F32), vm((3, 4, 8, 512), F32),
        vm((4, 8, 512), F32), vm((4, 8, 512), F32), vm((2, 8, 512), F32), vm((2, 8, 512), F32),
    ]
    scratch += [vm((4, 4) + b, BF) for b in BLOCKS]
    scratch += [vm((4, 2) + b, BF) for b in BLOCKS]
    scratch += [vm((4,) + b, BF) for b in BLOCKS]
    scratch += [vm((3,) + b, BF) for b in BLOCKS]
    scratch += [vm(h, F32) for h in halves]
    scratch += [pltpu.SemaphoreType.DMA((n_remote,))] * 2 + [pltpu.SemaphoreType.DMA((tp // SMALL + 24,)), pltpu.SemaphoreType.REGULAR]
    return pl.pallas_call(
        functools.partial(backward_kernel, seq),
        out_shape=[sds((tp, 512), BF), sds((2, 8, 512), F32)]
        + [sds(d, F32) for d in ((2, 128, 512), (128, 1024), (2, 128, 128), (128, 768))],
        in_specs=[ANY] * 4 + [VMEM] * 4 + [ANY] * 10,
        out_specs=[ANY] + [VMEM] * 5,
        scratch_shapes=scratch,
        compiler_params=pltpu.CompilerParams(collective_id=1, has_side_effects=True, vmem_limit_bytes=63 << 20),
        cost_estimate=pl.CostEstimate(flops=40 * 10**9, bytes_accessed=100 * 10**6, transcendentals=10**7),
        name="backward",
    )(*args)


def local_chip(
    tokens, segment_ids, norm1_gain, norm1_shift, qkv_weight, qv_bias, out_weight, out_bias,
    norm2_gain, norm2_shift, up_weight, up_bias, down_weight, down_bias, cotangent,
):
    seq = segment_ids.shape[1]
    tp = -(-seq // BQ) * BQ
    c = lax.axis_index("gx")
    pad = ((0, tp - seq), (0, 0))
    x_own = jnp.pad(tokens, pad)
    g_own = jnp.pad(cotangent, pad)
    vectors = (norm1_gain, norm1_shift, out_bias, norm2_gain, norm2_shift, down_bias)
    (wq, wo, wu, n1, x_oth, g_oth, vec_all, a1, big, lse, m, dh, gd, gu, rxu, usum, y) = forward_all(
        x_own, g_own, vectors, up_bias, qv_bias, segment_ids, qkv_weight.reshape(4, 128, 768), out_weight.reshape(2, 4, 32, 512),
        up_weight.reshape(4, 128, 1024), down_weight.reshape(4, 2, 128, 512),
    )
    grad, small, down_grad, up_grad, out_grad, qkv_grad = backward_all(
        seq, x_own, x_oth, g_own, g_oth, vec_all, n1, usum, lse, a1, big, m, dh, gd, gu, rxu, wq, wo, wu
    )

    def by_core(keep, got, axis):
        return jnp.where(c == 0, jnp.stack([keep, got], axis), jnp.stack([got, keep], axis))

    width = small[0]
    up_bias_grad = by_core(small[0, 6].reshape(4, 128), small[1, 6].reshape(4, 128), 1).reshape(1024)
    qv_bias_grad = by_core(small[0, 7, :256].reshape(2, 128), small[1, 7, :256].reshape(2, 128), 1).reshape(2, 256)
    return (
        y, grad[:seq], width[0], width[1], qkv_grad.reshape(1, 128, 3, 256), qv_bias_grad, out_grad.reshape(256, 1, 128), width[2],
        width[3], width[4], up_grad.reshape(1, 128, 1024), up_bias_grad, down_grad.reshape(1, 256, 512), width[5],
    )


def solution(mesh):
    sizes = dict(mesh.shape)
    chip_rows = sizes["dp"] == 4 and sizes["gx"] == 2 and sizes["gy"] == 4

    def whole(*args):
        rows, seq = args[1].shape
        fast = chip_rows and rows * seq == args[0].shape[0] and rows == 16
        body = local_chip if fast else local
        return jax.shard_map(
            body,
            mesh=mesh,
            in_specs=(
                P(("dp", "gy"), "gx"), P(("dp", "gx"), None), P("gx"), P("gx"), P("gx", None, "gy"), P(None, "gy"),
                P("gy", "gx"), P("gx"), P("gx"), P("gx"), P("gx", "gy"), P("gy"), P("gy", "gx"), P("gx"), P(("dp", "gy"), "gx"),
            ),
            out_specs=(
                P(("dp", "gy"), "gx"), P(("dp", "gy"), "gx"), P("gx"), P("gx"), P("gx", "dp", None, "gy"), P(None, "gy"),
                P("gy", "gx", "dp"), P("gx"), P("gx"), P("gx"), P("gx", "dp", "gy"), P("gy"), P("gy", "dp", "gx"), P("gx"),
            ),
            check_vma=False,
        )(*args)

    return whole
```

```python
import functools
import math

import jax
import jax.numpy as jnp
from jax import lax
from jax.experimental import pallas as pl
from jax.experimental.pallas import tpu as pltpu
from jax.sharding import PartitionSpec as P

D = 1024
HD = 64
MESH = pl.DeviceIdType.MESH
F32 = jnp.float32
BF = jnp.bfloat16
ANY = pl.BlockSpec(memory_space=pl.ANY)
SMEM = pl.BlockSpec(memory_space=pltpu.SMEM)
VMEM = pl.BlockSpec(memory_space=pltpu.VMEM)
norm_eps = 1e-06


def times_right(left, right):
    return jnp.dot(left, right, preferred_element_type=jnp.float32)


def times_back(left, right):
    return lax.dot_general(
        left, right, (((1,), (1,)), ((), ())), preferred_element_type=jnp.float32
    )


def times_outer(left, right):
    return lax.dot_general(
        left, right, (((0,), (0,)), ((), ())), preferred_element_type=jnp.float32
    )


def exact_gelu(values):
    return jax.nn.gelu(values, approximate=False)


def norm_forward(values, gain, shift):
    moments = lax.psum((jnp.sum(values, axis=1), jnp.sum(values * values, axis=1)), "gx")
    mean_val = moments[0] / D
    inverse = lax.rsqrt(moments[1] / D - mean_val * mean_val + norm_eps)
    hat_vals = (values - mean_val[:, None]) * inverse[:, None]
    return (hat_vals * gain + shift, hat_vals, inverse)


def norm_backward(grad_norm, hat_vals, inverse, gain):
    scaled = grad_norm * gain
    moments = lax.psum((jnp.sum(scaled, axis=1), jnp.sum(scaled * hat_vals, axis=1)), "gx")
    grad_in = inverse[:, None] * (
        scaled - (moments[0] / D)[:, None] - hat_vals * (moments[1] / D)[:, None]
    )
    return (grad_in, jnp.sum(grad_norm * hat_vals, axis=0), jnp.sum(grad_norm, axis=0))


def gather_gy(values):
    return lax.all_gather(values, "gy", axis=0, tiled=True)


def gather_gx(values):
    return lax.all_gather(values, "gx", axis=0, tiled=True)


def sum_over_gx(left, multiply):
    keep_rows = left.shape[0] // lax.axis_size("gx")

    def term(start, count):
        return multiply(left)

    return lax.psum_scatter(
        term(jnp.int32(0), keep_rows * lax.axis_size("gx")), "gx", scatter_dimension=0, tiled=True
    )


def sum_over_gy(left, multiply):
    keep_rows = left.shape[0] // lax.axis_size("gy")

    def term(start, count):
        return multiply(left)

    return lax.psum_scatter(
        term(jnp.int32(0), keep_rows * lax.axis_size("gy")), "gy", scatter_dimension=0, tiled=True
    )


def masked_scores(query_part, key_part, segment):
    scaling = 1.0 / math.sqrt(query_part.shape[-1])
    scores = (
        jnp.einsum("qhd,khd->hqk", query_part, key_part, preferred_element_type=jnp.float32)
        * scaling
    )
    same = segment[:, None] == segment[None, :]
    return jnp.where(same[None], scores, -1e30)


def attend_forward(item):
    packed, segment = item
    scores = masked_scores(packed[:, 0], packed[:, 1], segment)
    top_val = jnp.max(scores, axis=-1, keepdims=True)
    expo = jnp.exp(scores - top_val)
    total = jnp.sum(expo, axis=-1, keepdims=True)
    probs = (expo / total).astype(jnp.bfloat16)
    mixed = jnp.einsum("hqk,khd->qhd", probs, packed[:, 2], preferred_element_type=jnp.float32)
    return (mixed.astype(jnp.bfloat16), (top_val + jnp.log(total))[..., 0])


def attend_backward(item):
    packed, segment, log_sum, grad_out = item
    query_part = packed[:, 0]
    key_part = packed[:, 1]
    value_part = packed[:, 2]
    scaling = 1.0 / math.sqrt(query_part.shape[-1])
    scores = masked_scores(query_part, key_part, segment)
    probs = jnp.exp(scores - log_sum[..., None])
    probs_low = probs.astype(jnp.bfloat16)
    grad_prob = jnp.einsum("qhd,khd->hqk", grad_out, value_part, preferred_element_type=jnp.float32)
    grad_value = jnp.einsum("hqk,qhd->khd", probs_low, grad_out, preferred_element_type=jnp.float32)
    delta = jnp.sum(probs * grad_prob, axis=-1, keepdims=True)
    grad_score = (probs * (grad_prob - delta)).astype(jnp.bfloat16)
    grad_query = (
        jnp.einsum("hqk,khd->qhd", grad_score, key_part, preferred_element_type=jnp.float32)
        * scaling
    )
    grad_key = (
        jnp.einsum("hqk,qhd->khd", grad_score, query_part, preferred_element_type=jnp.float32)
        * scaling
    )
    return jnp.stack([grad_query, grad_key, grad_value], axis=1).astype(jnp.bfloat16)


def local(
    tokens,
    segment_ids,
    norm1_gain,
    norm1_shift,
    qkv_weight,
    qv_bias,
    out_weight,
    out_bias,
    norm2_gain,
    norm2_shift,
    up_weight,
    up_bias,
    down_weight,
    down_bias,
    cotangent,
):
    head_width = qkv_weight.shape[2]
    local_heads = head_width // HD
    seq_len = segment_ids.shape[1]
    qkv_flat = qkv_weight.reshape(qkv_weight.shape[0], 3 * head_width)
    gain_one = norm1_gain.astype(jnp.float32)
    gain_two = norm2_gain.astype(jnp.float32)
    resid = tokens.astype(jnp.float32)
    normed, hat_one, inv_one = norm_forward(resid, gain_one, norm1_shift.astype(jnp.float32))
    first_low = normed.astype(jnp.bfloat16)
    first_rows = gather_gy(first_low)
    qkv_all = sum_over_gx(first_rows, lambda piece: times_right(piece, qkv_flat))
    bias_full = jnp.stack([qv_bias[0], jnp.zeros_like(qv_bias[0]), qv_bias[1]]).astype(jnp.float32)
    qkv_low = (qkv_all.reshape(-1, 3, head_width) + bias_full[None]).astype(jnp.bfloat16)
    packed = qkv_low.reshape(-1, seq_len, 3, local_heads, HD)
    mixed, log_sums = lax.map(attend_forward, (packed, segment_ids))
    mixed_low = mixed.reshape(-1, head_width)
    mixed_rows = gather_gx(mixed_low)
    branch = sum_over_gy(
        mixed_rows, lambda piece: times_right(piece, out_weight)
    ) + out_bias.astype(jnp.float32)
    middle = resid + branch
    normed_two, hat_two, inv_two = norm_forward(middle, gain_two, norm2_shift.astype(jnp.float32))
    second_low = normed_two.astype(jnp.bfloat16)
    second_rows = gather_gy(second_low)
    hidden = sum_over_gx(second_rows, lambda piece: times_right(piece, up_weight)) + up_bias.astype(
        jnp.float32
    )
    active, gelu_pull = jax.vjp(exact_gelu, hidden)
    active_low = active.astype(jnp.bfloat16)
    active_rows = gather_gx(active_low)
    branch_two = sum_over_gy(
        active_rows, lambda piece: times_right(piece, down_weight)
    ) + down_bias.astype(jnp.float32)
    output = (middle + branch_two).astype(jnp.bfloat16)
    grad_top = cotangent.astype(jnp.float32)
    down_bias_grad = jnp.sum(grad_top, axis=0)
    grad_top_rows = gather_gy(cotangent)
    down_weight_grad = times_outer(active_rows, grad_top_rows)
    grad_active = sum_over_gx(grad_top_rows, lambda piece: times_back(piece, down_weight))
    grad_hidden = gelu_pull(grad_active)[0].astype(jnp.bfloat16)
    up_bias_grad = jnp.sum(grad_hidden.astype(jnp.float32), axis=0)
    hidden_rows = gather_gx(grad_hidden)
    up_weight_grad = times_outer(second_rows, hidden_rows)
    grad_norm_two = sum_over_gy(hidden_rows, lambda piece: times_back(piece, up_weight))
    grad_in_two, norm2_gain_grad, norm2_shift_grad = norm_backward(
        grad_norm_two, hat_two, inv_two, gain_two
    )
    grad_middle = grad_top + grad_in_two
    grad_branch = grad_middle.astype(jnp.bfloat16)
    out_bias_grad = jnp.sum(grad_branch.astype(jnp.float32), axis=0)
    branch_rows = gather_gy(grad_branch)
    out_weight_grad = times_outer(mixed_rows, branch_rows)
    grad_mixed = sum_over_gx(branch_rows, lambda piece: times_back(piece, out_weight)).astype(
        jnp.bfloat16
    )
    grad_mixed = grad_mixed.reshape(-1, seq_len, local_heads, HD)
    grad_packed = lax.map(attend_backward, (packed, segment_ids, log_sums, grad_mixed))
    grad_qkv = grad_packed.reshape(-1, 3 * head_width)
    third_sums = jnp.sum(grad_qkv.astype(jnp.float32), axis=0).reshape(3, head_width)
    qv_bias_grad = jnp.stack([third_sums[0], third_sums[2]])
    qkv_rows = gather_gx(grad_qkv)
    qkv_weight_grad = times_outer(first_rows, qkv_rows).reshape(qkv_weight.shape)
    grad_norm_one = sum_over_gy(qkv_rows, lambda piece: times_back(piece, qkv_flat))
    grad_in_one, norm1_gain_grad, norm1_shift_grad = norm_backward(
        grad_norm_one, hat_one, inv_one, gain_one
    )
    input_grad = (grad_middle + grad_in_one).astype(jnp.bfloat16)
    qkv_weight_grad, out_weight_grad, up_weight_grad, down_weight_grad = (
        lax.psum_scatter(qkv_weight_grad, "dp", scatter_dimension=0, tiled=True),
        lax.psum_scatter(out_weight_grad, "dp", scatter_dimension=1, tiled=True),
        lax.psum_scatter(up_weight_grad, "dp", scatter_dimension=0, tiled=True),
        lax.psum_scatter(down_weight_grad, "dp", scatter_dimension=0, tiled=True),
    )
    qkv_weight_grad = qkv_weight_grad[None]
    out_weight_grad = out_weight_grad[:, None, :]
    up_weight_grad = up_weight_grad[None]
    down_weight_grad = down_weight_grad[None]
    (
        norm1_gain_grad,
        norm1_shift_grad,
        norm2_gain_grad,
        norm2_shift_grad,
        out_bias_grad,
        down_bias_grad,
    ) = lax.psum(
        (
            norm1_gain_grad,
            norm1_shift_grad,
            norm2_gain_grad,
            norm2_shift_grad,
            out_bias_grad,
            down_bias_grad,
        ),
        ("dp", "gy"),
    )
    up_bias_grad, qv_bias_grad = lax.psum((up_bias_grad, qv_bias_grad), ("dp", "gx"))
    return (
        output,
        input_grad,
        norm1_gain_grad,
        norm1_shift_grad,
        qkv_weight_grad,
        qv_bias_grad,
        out_weight_grad,
        out_bias_grad,
        norm2_gain_grad,
        norm2_shift_grad,
        up_weight_grad,
        up_bias_grad,
        down_weight_grad,
        down_bias_grad,
    )


def flip1(i):
    return i + 1 - 2 * lax.rem(i, 2)


def flip2(i):
    return i + 2 - 4 * lax.div(i, 2)


def place():
    dp, c, z = lax.axis_index("dp"), lax.axis_index("gx"), lax.axis_index("gy")
    dps = (dp, flip1(dp), flip2(dp), 3 - dp)
    zs = (z, flip1(z), flip2(z), 3 - z)
    x_dev = (dps[1], c, z)
    y_dev = (dps[2], c, z)
    c_dev = (dp, 1 - c, z)
    z_devs = (None,) + tuple((dp, c, zz) for zz in zs[1:])
    return dps, zs, x_dev, y_dev, c_dev, z_devs


def greet(devices):
    barrier = pltpu.get_barrier_semaphore()
    for device in devices:
        pl.semaphore_signal(barrier, inc=1, device_id=device, device_id_type=MESH)
    pl.semaphore_wait(barrier, len(devices))


ORDER = ((0, 1), (0, 2), (0, 3), (1, 2), (1, 1), (1, 3), (2, 1), (3, 1), (2, 2), (3, 2), (2, 3), (3, 3))
GATHER = (
    (100, 101, 102),
    (),
    (),
    (103,),
    (104, 200),
    (105,),
    (201, 300, 202, 106, 301, 203, 107, 204, 108),
    (109,),
    (205, 302),
    (110, 303, 304),
    (),
    (305, 206),
    (),
    (111,),
    (),
    (207,),
    (306,),
    (),
    (),
    (),
    (),
    (),
    (208,),
    (307,),
    (),
    (),
    (),
    (209,),
    (),
    (),
    (308,),
    (),
    (),
    (210,),
    (),
    (),
    (309,),
    (),
    (211,),
    (),
    (),
    (310,),
    (),
    (311,),
    (),
    (),
    (),
    (),
    (),
    (),
    (),
    (),
)
N_PAIR = 9


class Sems:
    def __init__(self, ss, rs):
        self.ss, self.rs, self.n = ss, rs, 0

    def at(self, i, src, dst, device):
        return pltpu.make_async_remote_copy(
            src, dst, self.ss.at[i], self.rs.at[i], device_id=device, device_id_type=MESH
        )

    def block(self, count):
        self.n += count
        return self.n - count

    def remote(self, src, dst, device):
        return self.at(self.block(1), src, dst, device)


class Locals:
    def __init__(self, ls):
        self.ls, self.n, self.open = ls, 0, []

    def at(self, i, src, dst):
        return pltpu.make_async_copy(src, dst, self.ls.at[i])

    def block(self, count):
        self.n += count
        return self.n - count

    def copy(self, src, dst):
        copy = self.at(self.block(1), src, dst)
        copy.start()
        return copy

    def later(self, src, dst):
        self.open.append(self.copy(src, dst))

    def close(self):
        for copy in self.open:
            copy.wait()


class Queue:
    def __init__(self, width):
        self.width, self.open = width, []

    def start(self, copy):
        if len(self.open) >= self.width:
            self.open.pop(0).wait_send()
        copy.start()
        self.open.append(copy)

    def close(self):
        for copy in self.open:
            copy.wait_send()


def weight_cuts(side, raw, full, crel):
    qf, ow, up, dn = raw
    wq, wo, wu, wd = full
    cols = pl.ds(crel * 512, 512)
    cuts = [[], [], [], []]
    for t in range(3):
        off = pl.multiple_of(t * 256 + side * 128, 128)
        cuts[0].append((qf.at[:, :, pl.ds(off, 128)], wq.at[0, crel, :, :, pl.ds(t * 128, 128)]))
    cuts[1].append((ow.at[side], wo.at[0, :, :, cols]))
    for t in range(4):
        off = pl.multiple_of(t * 256 + side * 128, 128)
        cuts[2].append((up.at[:, :, pl.ds(off, 128)], wu.at[0, crel, :, :, pl.ds(t * 128, 128)]))
    cuts[3].append((dn.at[:, side], wd.at[0, crel]))
    return cuts


class Gather:
    def __init__(self, sems, loc, here, c, raw, full):
        self.sems, self.loc, self.raw, self.full, self.c = sems, loc, raw, full, c
        self.dps, self.zs, self.x_dev, self.y_dev, self.c_dev, self.z_devs = here
        self.theirs = [[sems.remote(src, dst, self.c_dev) for src, dst in group] for group in weight_cuts(1 - c, raw, full, 1)]
        self.mine = weight_cuts(c, raw, full, 0)
        self.own, self.copies, self.ready = {}, {}, set()
        self.queues = {axis: Queue(99) for axis in "xyz"}
        self.point = 0

    def piece(self, m, k, dd):
        return self.full[m].at[k, dd] if m == 1 else self.full[m].at[k, :, dd]

    def pair_start(self, m):
        for copy in self.theirs[m]:
            copy.start()
        self.own[m] = [self.loc.copy(src, dst) for src, dst in self.mine[m]]

    def own_ready(self, m):
        if m not in self.ready:
            self.ready.add(m)
            for copy in self.own[m]:
                copy.wait()
            for copy in self.theirs[m]:
                copy.wait_recv()

    def z_send(self, s):
        m, k = ORDER[s]
        self.own_ready(m)
        copy = self.sems.remote(self.piece(m, 0, self.dps[0]), self.piece(m, k, self.dps[0]), self.z_devs[k])
        self.copies["z", m, k] = copy
        self.queues["z"].start(copy)

    def by_x(self, m, k):
        return (k == 2) == (m in (0, 2))

    def forward(self, s):
        m, k = ORDER[s]
        if self.by_x(m, k):
            self.copies["x", m, k].wait_recv()
            src = self.piece(m, k, self.dps[1])
            copy, axis = self.sems.remote(src, src, self.y_dev), "y"
        else:
            self.copies["y", m, k].wait_recv()
            src = self.piece(m, k, self.dps[2])
            copy, axis = self.sems.remote(src, src, self.x_dev), "x"
        self.copies["d", m, k] = copy
        self.queues[axis].start(copy)

    def spread(self, s):
        m, k = ORDER[s]
        self.copies["z", m, k].wait_recv()
        src = self.piece(m, k, self.dps[0])
        for axis, dev in (("x", self.x_dev), ("y", self.y_dev)):
            copy = self.sems.remote(src, src, dev)
            self.copies[axis, m, k] = copy
            self.queues[axis].start(copy)

    def poll(self):
        for code in GATHER[self.point]:
            (self.z_send, self.spread, self.forward)[code // 100 - 1](code % 100)
        self.point += 1

    def need(self, m, k):
        self.poll()
        if k == 0:
            self.own_ready(m)
            return
        self.copies["y" if self.by_x(m, k) else "x", m, k].wait_recv()
        self.copies["d", m, k].wait_recv()

    def close(self):
        for group in self.theirs:
            for copy in group:
                copy.wait_send()
        for queue in self.queues.values():
            queue.close()


def dot_nt(a, b):
    return lax.dot_general(a, b, (((1,), (1,)), ((), ())), preferred_element_type=F32)


def dot_tn(a, b):
    return lax.dot_general(a, b, (((0,), (0,)), ((), ())), preferred_element_type=F32)


def dot_nn(a, b):
    return lax.dot_general(a, b, (((1,), (0,)), ((), ())), preferred_element_type=F32)


BQ = 256


SMALL = 64


def small_block(i):
    return pl.ds(pl.multiple_of(i * SMALL, SMALL), SMALL)


def row_block(i):
    return pl.ds(pl.multiple_of(i * BQ, BQ), BQ)


def segments(shape, axis, start, n1, seq):
    pos = (lax.broadcasted_iota(jnp.int32, shape, axis) + start).astype(F32)
    return (pos >= n1).astype(F32) + (pos >= float(seq)).astype(F32)


def masked_keys(big, kx, zr, n1, seq):
    tp = big.shape[0]
    lane = lax.broadcasted_iota(jnp.int32, (1, 128), 1)
    seg = segments((tp, 1), 0, 0, n1, seq)
    for h in range(2):
        t = lane - 64 * (1 - h)
        away = jnp.where(seg == t.astype(F32), 0.0, -1e30)
        away = jnp.where(t < 0, 0.0, jnp.where(t < 3, away, 0.0)).astype(BF)
        kx[h] = jnp.where(lax.div(lane, 64) == h, big[:, zr * 384 + 128 : zr * 384 + 256], away)


def attend_fwd_rows(big, lse_ref, kx, zr, start, count, n1, seq):
    lane = lax.broadcasted_iota(jnp.int32, (1, 128), 1)
    base = zr * 384
    rows = slice(start, start + count)
    q = big[rows, base : base + 128] * BF(0.125)
    seg = segments((count, 1), 0, start, n1, seq)
    out = jnp.zeros((count, 128), F32)
    for h in range(2):
        mask = lax.div(lane, 64) == h
        own_seg = (seg == (lane - 64 * (1 - h)).astype(F32)).astype(BF)
        s = dot_nt(jnp.where(mask, q, own_seg), kx[h])
        top = jnp.max(s, axis=1, keepdims=True)
        e = jnp.exp(s - top)
        total = jnp.sum(e, axis=1, keepdims=True)
        mixed = dot_nn(e.astype(BF), big[:, base + 256 : base + 384]) / total
        out = jnp.where(mask, mixed, out)
        lse = jnp.broadcast_to(top + jnp.log(total), (count, 128))
        lse_ref[2 * zr + h : 2 * zr + h + 1, rows] = jnp.transpose(lse)[0:1]
    big[rows, 1536 + zr * 128 : 1664 + zr * 128] = out.astype(BF)


def halves_mean(a, b):
    return (jnp.sum(a, axis=1, keepdims=True) + jnp.sum(b, axis=1, keepdims=True)) * (1.0 / D)


def forward_kernel(
    seq, x_own, g_own, v0, v1, v2, v3, v4, v5, up_bias, qv_bias, ids, qf, ow, up, dn,
    wq_out, wo_out, wu_out, n1_out, x_out, g_out, vec_out, a1_out, big_out, lse_out, m_out, dh_out, gd_out, gu_out, rxu_out,
    usum, y_out,
    x_oth, g_oth, vec_all, bias_all, cnt, wq, wo, wu, wd, act, big, lse, m, pb, pr, pr2, dh, gd, gu, kx,
    ss, rs, ls,
):
    tp = x_own.shape[0]
    nb = tp // BQ
    here = place()
    dps, zs, x_dev, y_dev, c_dev, z_devs = here
    c, z = lax.axis_index("gx"), zs[0]
    sems, loc = Sems(ss, rs), Locals(ls)
    gather = Gather(sems, loc, here, c, (qf, ow, up, dn), (wq, wo, wu, wd))
    poll = gather.poll

    ids_low = (ids[...] == 0).astype(F32)
    for r in range(2):
        cnt[0, r] = jnp.broadcast_to(jnp.sum(ids_low[r : r + 1], axis=1, keepdims=True), (8, 128))
    vec_all[...] = jnp.zeros_like(vec_all)
    bias_all[...] = jnp.zeros_like(bias_all)
    for i, ref in enumerate((v0, v1, v2, v3, v4, v5)):
        vec_all[0, i : i + 1, :] = ref[...].astype(F32).reshape(1, 512)

    def cut(row, j):
        return jnp.where(c == 0, row[:, 256 * j : 256 * j + 128], row[:, 256 * j + 128 : 256 * j + 256])

    up_row = up_bias[...].astype(F32).reshape(1, 1024)
    qv_rows = qv_bias[...].astype(F32)
    for j in range(4):
        bias_all[0, 0:1, 128 * j : 128 * j + 128] = cut(up_row, j)
    for j in range(2):
        bias_all[0, 1:2, 128 * j : 128 * j + 128] = cut(qv_rows[j : j + 1], 0)
    usum[...] = jnp.zeros_like(usum)
    greet((x_dev, y_dev, c_dev) + z_devs[1:])
    gather.pair_start(0)
    small = [sems.remote(vec_all.at[0], vec_all.at[1], c_dev), sems.remote(cnt.at[0], cnt.at[1], c_dev)]
    small += [sems.remote(bias_all.at[0], bias_all.at[k], z_devs[k]) for k in (1, 2, 3)]
    x_copy = sems.remote(x_own, x_oth, c_dev)
    for copy in small + [x_copy]:
        copy.start()
    poll()
    for m_ in (1, 2, 3):
        gather.pair_start(m_)
    for copy in small:
        copy.wait_recv()
    x_copy.wait_recv()
    vec = [(vec_all[0, i : i + 1, :], vec_all[1, i : i + 1, :]) for i in range(6)]
    n1 = cnt[lax.rem(lax.div(z, 2) + c, 2), lax.rem(z, 2)]
    n1_out[...] = n1
    n1 = n1[0:1, 0:1]
    loc.later(x_oth, x_out)
    loc.later(vec_all, vec_out)

    @pl.loop(0, nb)
    def _(i):
        rows = row_block(i)
        xo, xt = x_own[rows, :].astype(F32), x_oth[rows, :].astype(F32)
        mean = halves_mean(xo, xt)
        inv = lax.rsqrt(halves_mean(xo * xo, xt * xt) - mean * mean + norm_eps)
        act[rows, 0:512] = ((xo - mean) * inv * vec[0][0] + vec[1][0]).astype(BF)
        act[rows, 512:1024] = ((xt - mean) * inv * vec[0][1] + vec[1][1]).astype(BF)

    a1_copy = loc.copy(act, a1_out)
    g_copy = sems.remote(g_own, g_oth, c_dev)
    g_copy.start()
    poll()
    for zr in range(4):
        gather.need(0, zr)
        qb, vb = bias_all[zr, 1:2, 0:128], bias_all[zr, 1:2, 128:256]
        bias = jnp.concatenate([qb, jnp.zeros_like(qb), vb], axis=1)

        @pl.loop(0, nb)
        def _(i):
            rows = row_block(i)
            big[rows, zr * 384 : zr * 384 + 384] = (dot_nn(act[rows, :], wq[zr].reshape(1024, 384)) + bias).astype(BF)

        masked_keys(big, kx, zr, n1, seq)
        poll()
        attend_fwd_rows(big, lse, kx, zr, 0, tp // 2, n1, seq)
        poll()
        attend_fwd_rows(big, lse, kx, zr, tp // 2, tp // 2, n1, seq)
        poll()
    loc.later(wq, wq_out)
    loc.later(lse, lse_out)
    big_copy = loc.copy(big, big_out)
    g_copy.wait_recv()
    loc.later(g_oth, g_out)
    for zr in range(4):
        gather.need(1, zr)
    loc.later(wo, wo_out)
    swap = sems.block(nb)

    @pl.loop(0, nb)
    def _(i):
        rows = row_block(i)
        part = dot_nn(big[rows, 1536:2048], wo[...].reshape(512, 1024))
        pb[rows, 0:512] = part[:, 512:].astype(BF)
        pb[rows, 512:1024] = part[:, :512].astype(BF)
        sems.at(swap + i, pb.at[rows], pr.at[rows], c_dev).start()
        m[rows, :] = part

    a1_copy.wait()
    poll()

    @pl.loop(0, nb)
    def _(i):
        rows = row_block(i)
        sems.at(swap + i, pb.at[rows], pr.at[rows], c_dev).wait()
        mo = x_own[rows, :].astype(F32) + m[rows, 0:512] + pr[rows, 0:512].astype(F32) + vec[2][0]
        mt = x_oth[rows, :].astype(F32) + m[rows, 512:1024] + pr[rows, 512:1024].astype(F32) + vec[2][1]
        mean = halves_mean(mo, mt)
        inv = lax.rsqrt(halves_mean(mo * mo, mt * mt) - mean * mean + norm_eps)
        m[rows, 0:512] = mo
        m[rows, 512:1024] = mt
        act[rows, 0:512] = ((mo - mean) * inv * vec[3][0] + vec[4][0]).astype(BF)
        act[rows, 512:1024] = ((mt - mean) * inv * vec[3][1] + vec[4][1]).astype(BF)

    m_copy = loc.copy(m, m_out)
    poll()
    outs, early = {}, []
    last = sems.block(nb)

    def send_down():
        @pl.loop(0, nb)
        def _(i):
            rows = row_block(i)
            pb[rows, 0:512] = m[rows, 512:1024].astype(BF)
            sems.at(last + i, pb.at[rows, pl.ds(0, 512)], pr2.at[rows], c_dev).start()

    for zr in range(4):
        gather.need(2, zr)
        gather.need(3, zr)
        if zr == 3:
            for key in (("u", 1), ("u", 2),):
                outs.pop(key).wait()
            for slot in (1, 0):
                for j, zz, dev, rels in ((0, 1, x_dev, (1, 3)), (1, 2, y_dev, (2, 3)),):
                    for grad_h, land in ((gu_out, rxu_out),):
                        early.append(sems.remote(grad_h.at[zz, dps[rels[slot]]], land.at[j, slot], dev))
                        early[-1].start()
        loc.later(wu.at[zr], wu_out.at[zr])
        bias = bias_all[zr, 0:1, :]
        lo = zr * 512
        if zr == 0:
            big_copy.wait()
            m_copy.wait()

        def hidden(first, last):
            @pl.loop(first, last)
            def _(i):
                rows = row_block(i)
                h = dot_nn(act[rows, :], wu[zr].reshape(1024, 512)) + bias
                w_own, w_oth = wd[zr, 0].reshape(512, 512), wd[zr, 1].reshape(512, 512)
                du = dot_nt(g_own[rows, :], w_own) + dot_nt(g_oth[rows, :], w_oth)
                cdf = 0.5 * (1.0 + lax.erf(h * math.sqrt(0.5)))
                slope = cdf + h * jnp.exp(-0.5 * h * h) * (1.0 / math.sqrt(2 * math.pi))
                u = (h * cdf).astype(BF)
                grad = (du * slope).astype(BF)
                big[rows, lo : lo + 512] = u
                dh[rows, lo : lo + 512] = grad
                usum[zr, 6:7, :] += jnp.sum(grad.astype(F32), axis=0, keepdims=True)
                m[rows, 0:512] += dot_nn(u, w_own)
                if zr == 0:
                    m[rows, 512:1024] = dot_nn(u, w_oth)
                else:
                    m[rows, 512:1024] += dot_nn(u, w_oth)

        for first, end in ((0, 2), (2, 4), (4, nb)):
            hidden(first, end)
            poll()
        if zr == 3:
            send_down()
        loc.later(dh.at[:, pl.ds(lo, 512)], dh_out.at[:, pl.ds(lo, 512)])
        slot = zr % 2
        for key in (("d", zr - 2), ("u", zr - 2)):
            if key in outs:
                outs.pop(key).wait()
        for j, gref in enumerate((g_own, g_oth)):
            gd[slot, :, :, 512 * j : 512 * j + 512] = dot_tn(big[:, lo : lo + 512], gref[...]).astype(BF).reshape(4, 128, 512)
        outs["d", zr] = loc.copy(gd.at[slot], gd_out.at[zr])
        poll()
        for j in range(2):
            block = dot_tn(act[:, 512 * j : 512 * j + 512], dh[:, lo : lo + 512])
            gu[slot, :, 128 * j : 128 * j + 128, :] = block.astype(BF).reshape(4, 128, 512)
        outs["u", zr] = loc.copy(gu.at[slot], gu_out.at[zr])
        poll()
    def result(rows, i):
        sems.at(last + i, pb.at[rows, pl.ds(0, 512)], pr2.at[rows], c_dev).wait()
        return (m[rows, 0:512] + pr2[rows, :].astype(F32) + vec[5][0]).astype(BF)

    @pl.loop(0, nb - 1)
    def _(i):
        rows = row_block(i)
        y_out[rows, :] = result(rows, i)

    end = tp - BQ
    y_out[end:seq, :] = result(pl.ds(end, BQ), nb - 1)[: seq - end]

    for copy in small + [x_copy, g_copy]:
        copy.wait_send()
    for copy in early:
        copy.wait()
    for copy in outs.values():
        copy.wait()
    gather.close()
    loc.close()


def forward_all(x_own, g_own, vectors, up_bias, qv_bias, ids, qf, ow, up, dn):
    tp = x_own.shape[0]
    seq = ids.shape[1]
    n_remote = N_PAIR + 7 + 48 + 2 * (tp // BQ) + 4
    sds = jax.ShapeDtypeStruct
    vm = pltpu.VMEM
    wide = (4, 2, 4, 128, 512)
    weights = [(4, 2, 4, 128, 384), (4, 4, 32, 1024), wide, wide]
    out_shape = [sds(s, BF) for s in weights[:3]] + [
        sds((8, 128), F32), sds((tp, 512), BF), sds((tp, 512), BF), sds((2, 8, 512), F32), sds((tp, 1024), BF),
        sds((tp, 2048), BF), sds((8, tp), F32), sds((tp, 1024), F32), sds((tp, 2048), BF), sds((4, 4, 128, 1024), BF),
        sds((4, 4, 256, 512), BF), sds((2, 2, 256, 512), BF), sds((4, 8, 512), F32), sds((seq, 512), BF),
    ]
    scratch = [vm((tp, 512), BF), vm((tp, 512), BF), vm((2, 8, 512), F32), vm((4, 8, 512), F32), vm((2, 2, 8, 128), F32)]
    scratch += [vm(s, BF) for s in weights]
    scratch += [
        vm((tp, 1024), BF), vm((tp, 2048), BF), vm((8, tp), F32), vm((tp, 1024), F32), vm((tp, 1024), BF), vm((tp, 1024), BF),
        vm((tp, 512), BF), vm((tp, 2048), BF), vm((2, 4, 128, 1024), BF), vm((2, 4, 256, 512), BF), vm((2, tp, 128), BF),
        pltpu.SemaphoreType.DMA((n_remote,)), pltpu.SemaphoreType.DMA((n_remote,)), pltpu.SemaphoreType.DMA((40,)),
    ]
    return pl.pallas_call(
        functools.partial(forward_kernel, seq),
        out_shape=out_shape,
        in_specs=[VMEM] * 11 + [ANY] * 4,
        out_specs=[ANY] * 3 + [VMEM] + [ANY] * 11 + [VMEM] * 2,
        scratch_shapes=scratch,
        compiler_params=pltpu.CompilerParams(collective_id=0, has_side_effects=True, vmem_limit_bytes=63 << 20),
        cost_estimate=pl.CostEstimate(flops=40 * 10**9, bytes_accessed=80 * 10**6, transcendentals=10**7),
        name="forward",
    )(x_own, g_own, *vectors, up_bias, qv_bias, ids, qf, ow, up, dn)


BLOCKS = ((128, 1024), (256, 512), (128, 256), (256, 384))
ZORDER = (1, 2, 3, 0)


def half_block(m):
    rows, cols = BLOCKS[m]
    return (rows // 2, cols) if m in (1, 3) else (rows, cols // 2)


class Landed:
    def __init__(self, copy):
        self.wait_recv = copy.wait


class Scatter:
    def __init__(self, sems, here, g, first_src, rx, ry, rz, sw, out, c):
        self.sems, self.g, self.first_src = sems, g, first_src
        self.dps, self.zs, self.x_dev, self.y_dev, self.c_dev, self.z_devs = here
        self.rx, self.ry, self.rz, self.sw, self.out, self.c = rx, ry, rz, sw, out, c
        self.first, self.second, self.third, self.last = {}, {}, {}, {}
        self.queues = {axis: Queue(99) for axis in "xyz"}
        self.point = 0

    def poll(self):
        for code in SCHEDULE[self.point]:
            stage, m, zr, slot = code // 1000, code // 100 % 10, code // 10 % 10, code % 10
            if stage == 1:
                self.stage1(m, zr, slot)
            elif stage == 2:
                self.stage2(m, zr)
            elif stage == 3:
                self.stage3(m, zr)
            else:
                self.stage4(m)
        self.point += 1

    def stage1(self, m, zr, slot):
        axis, dev, rels = ("x", self.x_dev, (1, 3)) if zr < 2 else ("y", self.y_dev, (2, 3))
        src = self.first_src[m].at[zr, self.dps[rels[slot]]]
        copy = self.sems.remote(src, self.rx[m].at[zr, slot], dev)
        self.first[m, zr, slot] = copy
        self.queues[axis].start(copy)

    def stage2(self, m, zr):
        axis, dev, rel = ("y", self.y_dev, 2) if zr < 2 else ("x", self.x_dev, 1)
        g, dd = self.g[m], self.dps[rel]
        self.first[m, zr, 1].wait_recv()
        g[zr, dd] = (g[zr, dd].astype(F32) + self.rx[m][zr, 1].astype(F32)).astype(BF)
        copy = self.sems.remote(g.at[zr, dd], self.ry[m].at[zr], dev)
        self.second[m, zr] = copy
        self.queues[axis].start(copy)

    def stage3(self, m, zr):
        g, dd = self.g[m], self.dps[0]
        self.first[m, zr, 0].wait_recv()
        self.second[m, zr].wait_recv()
        g[zr, dd] = (g[zr, dd].astype(F32) + self.rx[m][zr, 0].astype(F32) + self.ry[m][zr].astype(F32)).astype(BF)
        if zr > 0:
            copy = self.sems.remote(g.at[zr, dd], self.rz[m].at[zr - 1], self.z_devs[zr])
            self.third[m, zr] = copy
            self.queues["z"].start(copy)

    def stage4(self, m):
        for zr in (1, 2, 3):
            self.third[m, zr].wait_recv()
        rz = self.rz[m]
        total = self.g[m][0, self.dps[0]].astype(F32) + rz[0].astype(F32) + rz[1].astype(F32) + rz[2].astype(F32)
        rows, cols = BLOCKS[m]
        sw, out, c = self.sw[m], self.out[m], self.c
        if m in (1, 3):
            keep, sw[...] = total[: rows // 2], total[rows // 2 :]
            pairs = []
            for j in range(cols // 128):
                mine = pl.ds(pl.multiple_of(j * 256 + c * 128, 128), 128)
                out[:, mine] = keep[:, j * 128 : j * 128 + 128]
                pairs.append((sw.at[:, pl.ds(j * 128, 128)], out.at[:, mine]))
        else:
            out[c], sw[...] = total[:, : cols // 2], total[:, cols // 2 :]
            pairs = [(sw, out.at[c])]
        self.last[m] = [self.sems.remote(src, dst, self.c_dev) for src, dst in pairs]
        for copy in self.last[m]:
            copy.start()

    def close(self):
        for queue in self.queues.values():
            queue.close()
        for group in self.last.values():
            for copy in group:
                copy.wait()


def attend_bwd_rows(big, do_ref, lse_ref, k_t, dk_acc, dv_acc, zr, lo, hi, n1, seq):
    tp = big.shape[0]
    lane = lax.broadcasted_iota(jnp.int32, (1, 128), 1)
    base = zr * 384
    ocol = 1536 + zr * 128

    @pl.loop(lo, hi)
    def _(i):
        start = pl.multiple_of(i * BQ, BQ)
        rows = pl.ds(start, BQ)
        q = big[rows, base : base + 128]
        do = do_ref[rows, zr * 128 : zr * 128 + 128]
        prod = do.astype(F32) * big[rows, ocol : ocol + 128].astype(F32)
        seg_q = segments((1, BQ), 1, start, n1, seq)
        dq_t = jnp.zeros((128, BQ), F32)
        row = lax.broadcasted_iota(jnp.int32, (128, 1), 0)
        for h in range(2):
            mask = lax.div(lane, 64) == h
            lse = lse_ref[2 * zr + h : 2 * zr + h + 1, rows]
            delta = jnp.sum(jnp.where(mask, prod, 0.0), axis=1, keepdims=True)
            delta = jnp.transpose(jnp.broadcast_to(delta, (BQ, 128)))[0:1]
            qm = jnp.where(mask, q, BF(0)) * BF(0.125)
            dom = jnp.where(mask, do, BF(0))
            for keys in (slice(0, tp // 2), slice(tp // 2, tp)):
                same = segments((tp // 2, 1), 0, keys.start, n1, seq) == seg_q
                s = dot_nt(big[keys, base + 128 : base + 256], qm)
                p = jnp.where(same, jnp.exp(s - lse), 0.0)
                dp = dot_nt(big[keys, base + 256 : base + 384], dom)
                ds = (p * (dp - delta)).astype(BF)
                dv_acc[keys, :] += dot_nn(p.astype(BF), dom)
                dk_acc[keys, :] += dot_nn(ds, qm)
                dq_t += jnp.where(lax.div(row, 64) == h, dot_nn(k_t[:, keys], ds), 0.0)
        dq = jnp.transpose(dq_t)
        big[rows, base : base + 128] = (dq * 0.125).astype(BF)


def backward_kernel(
    seq, x_own, x_oth, g_own_h, g_oth_h, vec_all, n1_ref, usum, lse, a1_h, big_h, m_h, dh_h, gd_h, gu_h, rxu_h, wq_h, wo_h, wu_h,
    grad_out, small_out, out0, out1, out2, out3,
    big, ga, gb, wbuf, wo_v, part, pb, pr, mbuf, act, dm, k_t, dk_acc, dv_acc, vsum, vdp, vz, vzr, vhalf, vc,
    gd, gu, go, gq, rx0, rx1, rx2, rx3, ry0, ry1, ry2, ry3, rz0, rz1, rz2, rz3, sw0, sw1, sw2, sw3,
    ss, rs, ls, free,
):
    tp = big.shape[0]
    nb = tp // BQ
    here = place()
    dps, zs, x_dev, y_dev, c_dev, z_devs = here
    c, z = lax.axis_index("gx"), zs[0]
    xy_dev = (dps[3], c, z)
    sems, loc = Sems(ss, rs), Locals(ls)
    scatter = Scatter(
        sems, here, (gd, gu, go, gq), (gd_h, gu_h, go, gq), (rx0, rx1, rx2, rx3), (ry0, ry1, ry2, ry3), (rz0, rz1, rz2, rz3),
        (sw0, sw1, sw2, sw3), (out0, out1, out2, out3), c,
    )
    poll = scatter.poll
    greet((x_dev, y_dev, xy_dev, c_dev) + z_devs[1:])
    poll()
    dh_in = loc.copy(dh_h, big)
    wu_in = loc.copy(wu_h, wbuf)
    m_sem = loc.block(tp // SMALL)

    def load_m(i):
        return loc.at(m_sem + i, m_h.at[small_block(i)], mbuf.at[lax.rem(i, 2)])

    vec = [(vec_all[0, i : i + 1, :], vec_all[1, i : i + 1, :]) for i in range(6)]
    n1 = n1_ref[0:1, 0:1]
    vsum[...] = usum[...]
    vhalf[...] = jnp.zeros_like(vhalf)
    dh_in.wait()
    wu_in.wait()
    gd_in, gu_in = loc.copy(gd_h, gd), loc.copy(gu_h, gu)
    ga_in, gb_in = loc.copy(g_own_h, ga), loc.copy(g_oth_h, gb)
    wo_in = loc.copy(wo_h, wo_v)
    for j, zr in enumerate((1, 2)):
        for mm, land in ((1, rxu_h),):
            for slot in (1, 0):
                scatter.first[mm, zr, slot] = Landed(loc.copy(land.at[j, slot], scatter.rx[mm].at[zr, slot]))
    load_m(0).start()
    swap = sems.block(nb)

    @pl.loop(0, nb)
    def _(i):
        rows = row_block(i)
        total = dot_nt(big[rows, 0:512], wbuf[0].reshape(1024, 512))
        for zr in range(1, 4):
            total += dot_nt(big[rows, zr * 512 : zr * 512 + 512], wbuf[zr].reshape(1024, 512))
        pb[rows, 0:512] = total[:, 512:].astype(BF)
        pb[rows, 512:1024] = total[:, :512].astype(BF)
        sems.at(swap + i, pb.at[rows], pr.at[rows], c_dev).start()
        part[rows, :] = total

    big_in = loc.copy(big_h, big)
    wq_in = loc.copy(wq_h, wbuf.at[:, :, :, :, pl.ds(0, 384)])
    gd_in.wait()
    gu_in.wait()
    ga_in.wait()
    gb_in.wait()
    poll()
    @pl.loop(0, tp // SMALL)
    def _(i):
        rows = small_block(i)

        @pl.when(i + 1 < tp // SMALL)
        def _():
            load_m(i + 1).start()

        @pl.when(lax.rem(i, BQ // SMALL) == 0)
        def _():
            whole = lax.div(i, BQ // SMALL)
            sems.at(swap + whole, pb.at[row_block(whole)], pr.at[row_block(whole)], c_dev).wait()

        load_m(i).wait()
        slot = lax.rem(i, 2)
        mo, mt = mbuf[slot, :, 0:512], mbuf[slot, :, 512:1024]
        mean = halves_mean(mo, mt)
        inv = lax.rsqrt(halves_mean(mo * mo, mt * mt) - mean * mean + norm_eps)
        ho, ht = (mo - mean) * inv, (mt - mean) * inv
        do_, dt = part[rows, 0:512] + pr[rows, 0:512].astype(F32), part[rows, 512:1024] + pr[rows, 512:1024].astype(F32)
        bo, bt = do_ * vec[3][0], dt * vec[3][1]
        first, second = halves_mean(bo, bt), halves_mean(bo * ho, bt * ht)
        go_, gt = ga[rows, :].astype(F32), gb[rows, :].astype(F32)
        dmo = go_ + inv * (bo - first - ho * second)
        dmt = gt + inv * (bt - first - ht * second)
        dm[rows, :] = dmo
        act[rows, 0:512] = dmo.astype(BF)
        act[rows, 512:1024] = dmt.astype(BF)
        vsum[0, 2:3, :] += jnp.sum(dmo.astype(BF).astype(F32), axis=0, keepdims=True)
        vsum[0, 3:4, :] += jnp.sum(do_ * ho, axis=0, keepdims=True)
        vsum[0, 4:5, :] += jnp.sum(do_, axis=0, keepdims=True)
        vsum[0, 5:6, :] += jnp.sum(go_, axis=0, keepdims=True)

    pl.semaphore_signal(free, inc=1, device_id=c_dev, device_id_type=MESH)
    poll()
    wo_in.wait()
    big_in.wait()
    for j in range(2):
        block = dot_tn(big[:, 1536:2048], act[:, 512 * j : 512 * j + 512]).astype(BF)
        for dd in range(4):
            go[:, dd, :, 128 * j : 128 * j + 128] = block[:, 128 * dd : 128 * dd + 128].reshape(4, 128, 128)

    @pl.loop(0, nb)
    def _(i):
        rows = row_block(i)
        ga[rows, :] = dot_nt(act[rows, :], wo_v[...].reshape(512, 1024)).astype(BF)

    a1_in = loc.copy(a1_h, act)
    xb_in = loc.copy(x_oth, gb)
    poll()
    for step, zr in enumerate(ZORDER):
        base = zr * 384
        dk_acc[...] = jnp.zeros_like(dk_acc)
        dv_acc[...] = jnp.zeros_like(dv_acc)
        k_t[...] = jnp.transpose(big[:, base + 128 : base + 256].astype(F32)).astype(BF)
        for lo, hi in ((0, 2), (2, 4), (4, nb)):
            attend_bwd_rows(big, ga, lse, k_t, dk_acc, dv_acc, zr, lo, hi, n1, seq)
            if hi < nb:
                poll()
        big[:, base + 128 : base + 256] = dk_acc[...].astype(BF)
        big[:, base + 256 : base + 384] = dv_acc[...].astype(BF)
        if step == 0:
            a1_in.wait()
            wq_in.wait()
        for j in range(2):
            block = dot_tn(act[:, 512 * j : 512 * j + 512], big[:, base : base + 384])
            gq[zr, :, 128 * j : 128 * j + 128, :] = block.astype(BF).reshape(4, 128, 384)
        poll()
        for j in (0, 2):
            cols = big[:, base + 128 * j : base + 128 * j + 128].astype(F32)
            vsum[zr, 7:8, 64 * j : 64 * j + 128] = jnp.sum(cols, axis=0, keepdims=True)
        if step < 3:

            @pl.loop(0, nb)
            def _(i):
                rows = row_block(i)
                more = dot_nt(big[rows, base : base + 384], wbuf[zr, :, :, :, 0:384].reshape(1024, 384))
                part[rows, :] = more if step == 0 else part[rows, :] + more

    xa_in = loc.copy(x_own, ga)
    pl.semaphore_wait(free, 1)
    xa_in.wait()
    xb_in.wait()
    swap2 = sems.block(nb)
    base = ZORDER[3] * 384

    @pl.loop(0, nb)
    def _(i):
        rows = row_block(i)
        total = part[rows, :] + dot_nt(big[rows, base : base + 384], wbuf[ZORDER[3], :, :, :, 0:384].reshape(1024, 384))
        pb[rows, 0:512] = total[:, 512:].astype(BF)
        pb[rows, 512:1024] = total[:, :512].astype(BF)
        sems.at(swap2 + i, pb.at[rows], pr.at[rows], c_dev).start()
        part[rows, :] = total
        xo, xt = ga[rows, :].astype(F32), gb[rows, :].astype(F32)
        mean = halves_mean(xo, xt)
        inv = lax.rsqrt(halves_mean(xo * xo, xt * xt) - mean * mean + norm_eps)
        vsum[0, 0:1, :] += jnp.sum(total[:, :512] * ((xo - mean) * inv), axis=0, keepdims=True)
        vsum[0, 1:2, :] += jnp.sum(total[:, :512], axis=0, keepdims=True)
        vhalf[0, 0:1, :] += jnp.sum(total[:, 512:] * ((xt - mean) * inv), axis=0, keepdims=True)
        vhalf[0, 1:2, :] += jnp.sum(total[:, 512:], axis=0, keepdims=True)

    half_copy = sems.remote(vhalf.at[0], vhalf.at[1], c_dev)
    half_copy.start()
    poll()
    half_copy.wait()
    vsum[0] += vhalf[1]
    for k in (1, 2, 3):
        vsum[k, 0:6, :] = vsum[0, 0:6, :]
    dp_copies = [sems.remote(vsum, vdp.at[k], dev) for k, dev in enumerate((x_dev, y_dev, xy_dev))]
    for copy in dp_copies:
        copy.start()
    poll()

    @pl.loop(0, nb)
    def _(i):
        rows = row_block(i)
        sems.at(swap2 + i, pb.at[rows], pr.at[rows], c_dev).wait()
        xo, xt = ga[rows, :].astype(F32), gb[rows, :].astype(F32)
        mean = halves_mean(xo, xt)
        inv = lax.rsqrt(halves_mean(xo * xo, xt * xt) - mean * mean + norm_eps)
        ho, ht = (xo - mean) * inv, (xt - mean) * inv
        bo = (part[rows, 0:512] + pr[rows, 0:512].astype(F32)) * vec[0][0]
        bt = (part[rows, 512:1024] + pr[rows, 512:1024].astype(F32)) * vec[0][1]
        first, second = halves_mean(bo, bt), halves_mean(bo * ho, bt * ht)
        ga[rows, :] = (dm[rows, :] + inv * (bo - first - ho * second)).astype(BF)

    loc.later(ga, grad_out)
    for copy in dp_copies:
        copy.wait()
    vz[...] = (vsum[...] + vdp[0]) + (vdp[1] + vdp[2])
    z_copies = [sems.remote(vz.at[k], vzr.at[k], z_devs[k]) for k in (1, 2, 3)]
    for copy in z_copies:
        copy.start()
    poll()
    for copy in z_copies:
        copy.wait()
    vc[0] = (vz[0] + vzr[1]) + (vzr[2] + vzr[3])
    c_copy = sems.remote(vc.at[0], vc.at[1], c_dev)
    c_copy.start()
    poll()
    c_copy.wait()
    small_out[...] = vc[...]
    loc.close()
    scatter.close()


SCHEDULE = (
    (1100, 1130, 1010, 1020, 1000, 1030),
    (2110, 2120, 1011, 1131),
    (),
    (1210, 1220),
    (1211, 1221),
    (3110, 3120, 1200, 1230),
    (1201, 2130, 1231, 1021, 2010),
    (2230, 2200, 2210, 2220),
    (3130, 1311, 1310, 2020),
    (3230, 1321, 3220),
    (2310, 3010, 3210, 3200, 1101, 1320, 1001),
    (2320, 1031),
    (3310, 3020, 1331),
    (2100, 4200),
    (2030, 2000, 1330),
    (2330, 3320, 1301),
    (1300,),
    (3100, 4100, 3030),
    (),
    (3000, 2300, 3330, 4000, 3300, 4300),
)


def backward_all(seq, *args):
    tp = args[0].shape[0]
    nb = tp // BQ
    sds = jax.ShapeDtypeStruct
    vm = pltpu.VMEM
    halves = [half_block(m) for m in range(4)]
    n_remote = 4 * (8 + 4 + 3) - 4 + 9 + 2 * nb + 8
    scratch = [
        vm((tp, 2048), BF), vm((tp, 512), BF), vm((tp, 512), BF), vm((4, 2, 4, 128, 512), BF), vm((4, 4, 32, 1024), BF),
        vm((tp, 1024), F32), vm((tp, 1024), BF), vm((tp, 1024), BF), vm((2, SMALL, 1024), F32), vm((tp, 1024), BF),
        vm((tp, 512), F32), vm((128, tp), BF), vm((tp, 128), F32), vm((tp, 128), F32), vm((4, 8, 512), F32), vm((3, 4, 8, 512), F32),
        vm((4, 8, 512), F32), vm((4, 8, 512), F32), vm((2, 8, 512), F32), vm((2, 8, 512), F32),
    ]
    scratch += [vm((4, 4) + b, BF) for b in BLOCKS]
    scratch += [vm((4, 2) + b, BF) for b in BLOCKS]
    scratch += [vm((4,) + b, BF) for b in BLOCKS]
    scratch += [vm((3,) + b, BF) for b in BLOCKS]
    scratch += [vm(h, F32) for h in halves]
    scratch += [pltpu.SemaphoreType.DMA((n_remote,))] * 2 + [pltpu.SemaphoreType.DMA((tp // SMALL + 24,)), pltpu.SemaphoreType.REGULAR]
    return pl.pallas_call(
        functools.partial(backward_kernel, seq),
        out_shape=[sds((tp, 512), BF), sds((2, 8, 512), F32)]
        + [sds(d, F32) for d in ((2, 128, 512), (128, 1024), (2, 128, 128), (128, 768))],
        in_specs=[ANY] * 4 + [VMEM] * 4 + [ANY] * 10,
        out_specs=[ANY] + [VMEM] * 5,
        scratch_shapes=scratch,
        compiler_params=pltpu.CompilerParams(collective_id=1, has_side_effects=True, vmem_limit_bytes=63 << 20),
        cost_estimate=pl.CostEstimate(flops=40 * 10**9, bytes_accessed=100 * 10**6, transcendentals=10**7),
        name="backward",
    )(*args)


def local_chip(
    tokens, segment_ids, norm1_gain, norm1_shift, qkv_weight, qv_bias, out_weight, out_bias,
    norm2_gain, norm2_shift, up_weight, up_bias, down_weight, down_bias, cotangent,
):
    seq = segment_ids.shape[1]
    tp = -(-seq // BQ) * BQ
    c = lax.axis_index("gx")
    pad = ((0, tp - seq), (0, 0))
    x_own = jnp.pad(tokens, pad)
    g_own = jnp.pad(cotangent, pad)
    vectors = (norm1_gain, norm1_shift, out_bias, norm2_gain, norm2_shift, down_bias)
    (wq, wo, wu, n1, x_oth, g_oth, vec_all, a1, big, lse, m, dh, gd, gu, rxu, usum, y) = forward_all(
        x_own, g_own, vectors, up_bias, qv_bias, segment_ids, qkv_weight.reshape(4, 128, 768), out_weight.reshape(2, 4, 32, 512),
        up_weight.reshape(4, 128, 1024), down_weight.reshape(4, 2, 128, 512),
    )
    grad, small, down_grad, up_grad, out_grad, qkv_grad = backward_all(
        seq, x_own, x_oth, g_own, g_oth, vec_all, n1, usum, lse, a1, big, m, dh, gd, gu, rxu, wq, wo, wu
    )

    def by_core(keep, got, axis):
        return jnp.where(c == 0, jnp.stack([keep, got], axis), jnp.stack([got, keep], axis))

    width = small[0]
    up_bias_grad = by_core(small[0, 6].reshape(4, 128), small[1, 6].reshape(4, 128), 1).reshape(1024)
    qv_bias_grad = by_core(small[0, 7, :256].reshape(2, 128), small[1, 7, :256].reshape(2, 128), 1).reshape(2, 256)
    return (
        y, grad[:seq], width[0], width[1], qkv_grad.reshape(1, 128, 3, 256), qv_bias_grad, out_grad.reshape(256, 1, 128), width[2],
        width[3], width[4], up_grad.reshape(1, 128, 1024), up_bias_grad, down_grad.reshape(1, 256, 512), width[5],
    )


def solution(mesh):
    sizes = dict(mesh.shape)
    chip_rows = sizes["dp"] == 4 and sizes["gx"] == 2 and sizes["gy"] == 4

    def whole(*args):
        rows, seq = args[1].shape
        fast = chip_rows and rows * seq == args[0].shape[0] and rows == 16
        body = local_chip if fast else local
        return jax.shard_map(
            body,
            mesh=mesh,
            in_specs=(
                P(("dp", "gy"), "gx"), P(("dp", "gx"), None), P("gx"), P("gx"), P("gx", None, "gy"), P(None, "gy"),
                P("gy", "gx"), P("gx"), P("gx"), P("gx"), P("gx", "gy"), P("gy"), P("gy", "gx"), P("gx"), P(("dp", "gy"), "gx"),
            ),
            out_specs=(
                P(("dp", "gy"), "gx"), P(("dp", "gy"), "gx"), P("gx"), P("gx"), P("gx", "dp", None, "gy"), P(None, "gy"),
                P("gy", "gx", "dp"), P("gx"), P("gx"), P("gx"), P("gx", "dp", "gy"), P("gy"), P("gy", "dp", "gx"), P("gx"),
            ),
            check_vma=False,
        )(*args)

    return whole
```

```python
import functools
import math

import jax
import jax.numpy as jnp
from jax import lax
from jax.experimental import pallas as pl
from jax.experimental.pallas import tpu as pltpu
from jax.sharding import PartitionSpec as P

D = 1024
HD = 64
MESH = pl.DeviceIdType.MESH
F32 = jnp.float32
BF = jnp.bfloat16
ANY = pl.BlockSpec(memory_space=pl.ANY)
SMEM = pl.BlockSpec(memory_space=pltpu.SMEM)
VMEM = pl.BlockSpec(memory_space=pltpu.VMEM)
norm_eps = 1e-06


def times_right(left, right):
    return jnp.dot(left, right, preferred_element_type=jnp.float32)


def times_back(left, right):
    return lax.dot_general(
        left, right, (((1,), (1,)), ((), ())), preferred_element_type=jnp.float32
    )


def times_outer(left, right):
    return lax.dot_general(
        left, right, (((0,), (0,)), ((), ())), preferred_element_type=jnp.float32
    )


def exact_gelu(values):
    return jax.nn.gelu(values, approximate=False)


def norm_forward(values, gain, shift):
    moments = lax.psum((jnp.sum(values, axis=1), jnp.sum(values * values, axis=1)), "gx")
    mean_val = moments[0] / D
    inverse = lax.rsqrt(moments[1] / D - mean_val * mean_val + norm_eps)
    hat_vals = (values - mean_val[:, None]) * inverse[:, None]
    return (hat_vals * gain + shift, hat_vals, inverse)


def norm_backward(grad_norm, hat_vals, inverse, gain):
    scaled = grad_norm * gain
    moments = lax.psum((jnp.sum(scaled, axis=1), jnp.sum(scaled * hat_vals, axis=1)), "gx")
    grad_in = inverse[:, None] * (
        scaled - (moments[0] / D)[:, None] - hat_vals * (moments[1] / D)[:, None]
    )
    return (grad_in, jnp.sum(grad_norm * hat_vals, axis=0), jnp.sum(grad_norm, axis=0))


def gather_gy(values):
    return lax.all_gather(values, "gy", axis=0, tiled=True)


def gather_gx(values):
    return lax.all_gather(values, "gx", axis=0, tiled=True)


def sum_over_gx(left, multiply):
    keep_rows = left.shape[0] // lax.axis_size("gx")

    def term(start, count):
        return multiply(left)

    return lax.psum_scatter(
        term(jnp.int32(0), keep_rows * lax.axis_size("gx")), "gx", scatter_dimension=0, tiled=True
    )


def sum_over_gy(left, multiply):
    keep_rows = left.shape[0] // lax.axis_size("gy")

    def term(start, count):
        return multiply(left)

    return lax.psum_scatter(
        term(jnp.int32(0), keep_rows * lax.axis_size("gy")), "gy", scatter_dimension=0, tiled=True
    )


def masked_scores(query_part, key_part, segment):
    scaling = 1.0 / math.sqrt(query_part.shape[-1])
    scores = (
        jnp.einsum("qhd,khd->hqk", query_part, key_part, preferred_element_type=jnp.float32)
        * scaling
    )
    same = segment[:, None] == segment[None, :]
    return jnp.where(same[None], scores, -1e30)


def attend_forward(item):
    packed, segment = item
    scores = masked_scores(packed[:, 0], packed[:, 1], segment)
    top_val = jnp.max(scores, axis=-1, keepdims=True)
    expo = jnp.exp(scores - top_val)
    total = jnp.sum(expo, axis=-1, keepdims=True)
    probs = (expo / total).astype(jnp.bfloat16)
    mixed = jnp.einsum("hqk,khd->qhd", probs, packed[:, 2], preferred_element_type=jnp.float32)
    return (mixed.astype(jnp.bfloat16), (top_val + jnp.log(total))[..., 0])


def attend_backward(item):
    packed, segment, log_sum, grad_out = item
    query_part = packed[:, 0]
    key_part = packed[:, 1]
    value_part = packed[:, 2]
    scaling = 1.0 / math.sqrt(query_part.shape[-1])
    scores = masked_scores(query_part, key_part, segment)
    probs = jnp.exp(scores - log_sum[..., None])
    probs_low = probs.astype(jnp.bfloat16)
    grad_prob = jnp.einsum("qhd,khd->hqk", grad_out, value_part, preferred_element_type=jnp.float32)
    grad_value = jnp.einsum("hqk,qhd->khd", probs_low, grad_out, preferred_element_type=jnp.float32)
    delta = jnp.sum(probs * grad_prob, axis=-1, keepdims=True)
    grad_score = (probs * (grad_prob - delta)).astype(jnp.bfloat16)
    grad_query = (
        jnp.einsum("hqk,khd->qhd", grad_score, key_part, preferred_element_type=jnp.float32)
        * scaling
    )
    grad_key = (
        jnp.einsum("hqk,qhd->khd", grad_score, query_part, preferred_element_type=jnp.float32)
        * scaling
    )
    return jnp.stack([grad_query, grad_key, grad_value], axis=1).astype(jnp.bfloat16)


def local(
    tokens,
    segment_ids,
    norm1_gain,
    norm1_shift,
    qkv_weight,
    qv_bias,
    out_weight,
    out_bias,
    norm2_gain,
    norm2_shift,
    up_weight,
    up_bias,
    down_weight,
    down_bias,
    cotangent,
):
    head_width = qkv_weight.shape[2]
    local_heads = head_width // HD
    seq_len = segment_ids.shape[1]
    qkv_flat = qkv_weight.reshape(qkv_weight.shape[0], 3 * head_width)
    gain_one = norm1_gain.astype(jnp.float32)
    gain_two = norm2_gain.astype(jnp.float32)
    resid = tokens.astype(jnp.float32)
    normed, hat_one, inv_one = norm_forward(resid, gain_one, norm1_shift.astype(jnp.float32))
    first_low = normed.astype(jnp.bfloat16)
    first_rows = gather_gy(first_low)
    qkv_all = sum_over_gx(first_rows, lambda piece: times_right(piece, qkv_flat))
    bias_full = jnp.stack([qv_bias[0], jnp.zeros_like(qv_bias[0]), qv_bias[1]]).astype(jnp.float32)
    qkv_low = (qkv_all.reshape(-1, 3, head_width) + bias_full[None]).astype(jnp.bfloat16)
    packed = qkv_low.reshape(-1, seq_len, 3, local_heads, HD)
    mixed, log_sums = lax.map(attend_forward, (packed, segment_ids))
    mixed_low = mixed.reshape(-1, head_width)
    mixed_rows = gather_gx(mixed_low)
    branch = sum_over_gy(
        mixed_rows, lambda piece: times_right(piece, out_weight)
    ) + out_bias.astype(jnp.float32)
    middle = resid + branch
    normed_two, hat_two, inv_two = norm_forward(middle, gain_two, norm2_shift.astype(jnp.float32))
    second_low = normed_two.astype(jnp.bfloat16)
    second_rows = gather_gy(second_low)
    hidden = sum_over_gx(second_rows, lambda piece: times_right(piece, up_weight)) + up_bias.astype(
        jnp.float32
    )
    active, gelu_pull = jax.vjp(exact_gelu, hidden)
    active_low = active.astype(jnp.bfloat16)
    active_rows = gather_gx(active_low)
    branch_two = sum_over_gy(
        active_rows, lambda piece: times_right(piece, down_weight)
    ) + down_bias.astype(jnp.float32)
    output = (middle + branch_two).astype(jnp.bfloat16)
    grad_top = cotangent.astype(jnp.float32)
    down_bias_grad = jnp.sum(grad_top, axis=0)
    grad_top_rows = gather_gy(cotangent)
    down_weight_grad = times_outer(active_rows, grad_top_rows)
    grad_active = sum_over_gx(grad_top_rows, lambda piece: times_back(piece, down_weight))
    grad_hidden = gelu_pull(grad_active)[0].astype(jnp.bfloat16)
    up_bias_grad = jnp.sum(grad_hidden.astype(jnp.float32), axis=0)
    hidden_rows = gather_gx(grad_hidden)
    up_weight_grad = times_outer(second_rows, hidden_rows)
    grad_norm_two = sum_over_gy(hidden_rows, lambda piece: times_back(piece, up_weight))
    grad_in_two, norm2_gain_grad, norm2_shift_grad = norm_backward(
        grad_norm_two, hat_two, inv_two, gain_two
    )
    grad_middle = grad_top + grad_in_two
    grad_branch = grad_middle.astype(jnp.bfloat16)
    out_bias_grad = jnp.sum(grad_branch.astype(jnp.float32), axis=0)
    branch_rows = gather_gy(grad_branch)
    out_weight_grad = times_outer(mixed_rows, branch_rows)
    grad_mixed = sum_over_gx(branch_rows, lambda piece: times_back(piece, out_weight)).astype(
        jnp.bfloat16
    )
    grad_mixed = grad_mixed.reshape(-1, seq_len, local_heads, HD)
    grad_packed = lax.map(attend_backward, (packed, segment_ids, log_sums, grad_mixed))
    grad_qkv = grad_packed.reshape(-1, 3 * head_width)
    third_sums = jnp.sum(grad_qkv.astype(jnp.float32), axis=0).reshape(3, head_width)
    qv_bias_grad = jnp.stack([third_sums[0], third_sums[2]])
    qkv_rows = gather_gx(grad_qkv)
    qkv_weight_grad = times_outer(first_rows, qkv_rows).reshape(qkv_weight.shape)
    grad_norm_one = sum_over_gy(qkv_rows, lambda piece: times_back(piece, qkv_flat))
    grad_in_one, norm1_gain_grad, norm1_shift_grad = norm_backward(
        grad_norm_one, hat_one, inv_one, gain_one
    )
    input_grad = (grad_middle + grad_in_one).astype(jnp.bfloat16)
    qkv_weight_grad, out_weight_grad, up_weight_grad, down_weight_grad = (
        lax.psum_scatter(qkv_weight_grad, "dp", scatter_dimension=0, tiled=True),
        lax.psum_scatter(out_weight_grad, "dp", scatter_dimension=1, tiled=True),
        lax.psum_scatter(up_weight_grad, "dp", scatter_dimension=0, tiled=True),
        lax.psum_scatter(down_weight_grad, "dp", scatter_dimension=0, tiled=True),
    )
    qkv_weight_grad = qkv_weight_grad[None]
    out_weight_grad = out_weight_grad[:, None, :]
    up_weight_grad = up_weight_grad[None]
    down_weight_grad = down_weight_grad[None]
    (
        norm1_gain_grad,
        norm1_shift_grad,
        norm2_gain_grad,
        norm2_shift_grad,
        out_bias_grad,
        down_bias_grad,
    ) = lax.psum(
        (
            norm1_gain_grad,
            norm1_shift_grad,
            norm2_gain_grad,
            norm2_shift_grad,
            out_bias_grad,
            down_bias_grad,
        ),
        ("dp", "gy"),
    )
    up_bias_grad, qv_bias_grad = lax.psum((up_bias_grad, qv_bias_grad), ("dp", "gx"))
    return (
        output,
        input_grad,
        norm1_gain_grad,
        norm1_shift_grad,
        qkv_weight_grad,
        qv_bias_grad,
        out_weight_grad,
        out_bias_grad,
        norm2_gain_grad,
        norm2_shift_grad,
        up_weight_grad,
        up_bias_grad,
        down_weight_grad,
        down_bias_grad,
    )


def flip1(i):
    return i + 1 - 2 * lax.rem(i, 2)


def flip2(i):
    return i + 2 - 4 * lax.div(i, 2)


def place():
    dp, c, z = lax.axis_index("dp"), lax.axis_index("gx"), lax.axis_index("gy")
    dps = (dp, flip1(dp), flip2(dp), 3 - dp)
    zs = (z, flip1(z), flip2(z), 3 - z)
    x_dev = (dps[1], c, z)
    y_dev = (dps[2], c, z)
    c_dev = (dp, 1 - c, z)
    z_devs = (None,) + tuple((dp, c, zz) for zz in zs[1:])
    return dps, zs, x_dev, y_dev, c_dev, z_devs


def greet(devices):
    barrier = pltpu.get_barrier_semaphore()
    for device in devices:
        pl.semaphore_signal(barrier, inc=1, device_id=device, device_id_type=MESH)
    pl.semaphore_wait(barrier, len(devices))


ORDER = ((0, 1), (0, 2), (0, 3), (1, 2), (1, 1), (1, 3), (2, 1), (2, 2), (3, 1), (3, 2), (2, 3), (3, 3))
GATHER = (
    (100, 101, 102),
    (),
    (),
    (103,),
    (104, 200),
    (105,),
    (201, 300, 202, 106, 301, 203, 107, 204, 108),
    (109,),
    (205, 302),
    (110, 303, 304),
    (),
    (206, 305),
    (),
    (111,),
    (),
    (207, 306),
    (),
    (),
    (),
    (),
    (),
    (),
    (208, 307),
    (),
    (),
    (),
    (),
    (209,),
    (),
    (),
    (308,),
    (),
    (210, 309, 211),
    (),
    (),
    (),
    (310,),
    (),
    (),
    (),
    (311,),
    (),
    (),
    (),
    (),
    (),
    (),
    (),
    (),
    (),
    (),
    (),
)
N_PAIR = 9


class Sems:
    def __init__(self, ss, rs):
        self.ss, self.rs, self.n = ss, rs, 0

    def at(self, i, src, dst, device):
        return pltpu.make_async_remote_copy(
            src, dst, self.ss.at[i], self.rs.at[i], device_id=device, device_id_type=MESH
        )

    def block(self, count):
        self.n += count
        return self.n - count

    def remote(self, src, dst, device):
        return self.at(self.block(1), src, dst, device)


class Locals:
    def __init__(self, ls):
        self.ls, self.n, self.open = ls, 0, []

    def at(self, i, src, dst):
        return pltpu.make_async_copy(src, dst, self.ls.at[i])

    def block(self, count):
        self.n += count
        return self.n - count

    def copy(self, src, dst):
        copy = self.at(self.block(1), src, dst)
        copy.start()
        return copy

    def later(self, src, dst):
        self.open.append(self.copy(src, dst))

    def close(self):
        for copy in self.open:
            copy.wait()


class Queue:
    def __init__(self, width):
        self.width, self.open = width, []

    def start(self, copy):
        if len(self.open) >= self.width:
            self.open.pop(0).wait_send()
        copy.start()
        self.open.append(copy)

    def close(self):
        for copy in self.open:
            copy.wait_send()


def weight_cuts(side, raw, full, crel):
    qf, ow, up, dn = raw
    wq, wo, wu, wd = full
    cols = pl.ds(crel * 512, 512)
    cuts = [[], [], [], []]
    for t in range(3):
        off = pl.multiple_of(t * 256 + side * 128, 128)
        cuts[0].append((qf.at[:, :, pl.ds(off, 128)], wq.at[0, crel, :, :, pl.ds(t * 128, 128)]))
    cuts[1].append((ow.at[side], wo.at[0, :, :, cols]))
    for t in range(4):
        off = pl.multiple_of(t * 256 + side * 128, 128)
        cuts[2].append((up.at[:, :, pl.ds(off, 128)], wu.at[0, crel, :, :, pl.ds(t * 128, 128)]))
    cuts[3].append((dn.at[:, side], wd.at[0, crel]))
    return cuts


class Gather:
    def __init__(self, sems, loc, here, c, raw, full):
        self.sems, self.loc, self.raw, self.full, self.c = sems, loc, raw, full, c
        self.dps, self.zs, self.x_dev, self.y_dev, self.c_dev, self.z_devs = here
        self.theirs = [[sems.remote(src, dst, self.c_dev) for src, dst in group] for group in weight_cuts(1 - c, raw, full, 1)]
        self.mine = weight_cuts(c, raw, full, 0)
        self.own, self.copies, self.ready = {}, {}, set()
        self.queues = {axis: Queue(99) for axis in "xyz"}
        self.point = 0

    def piece(self, m, k, dd):
        return self.full[m].at[k, dd] if m == 1 else self.full[m].at[k, :, dd]

    def pair_start(self, m):
        for copy in self.theirs[m]:
            copy.start()
        self.own[m] = [self.loc.copy(src, dst) for src, dst in self.mine[m]]

    def own_ready(self, m):
        if m not in self.ready:
            self.ready.add(m)
            for copy in self.own[m]:
                copy.wait()
            for copy in self.theirs[m]:
                copy.wait_recv()

    def z_send(self, s):
        m, k = ORDER[s]
        self.own_ready(m)
        copy = self.sems.remote(self.piece(m, 0, self.dps[0]), self.piece(m, k, self.dps[0]), self.z_devs[k])
        self.copies["z", m, k] = copy
        self.queues["z"].start(copy)

    def by_x(self, m, k):
        return (k == 2) == (m in (0, 2))

    def forward(self, s):
        m, k = ORDER[s]
        if self.by_x(m, k):
            self.copies["x", m, k].wait_recv()
            src = self.piece(m, k, self.dps[1])
            copy, axis = self.sems.remote(src, src, self.y_dev), "y"
        else:
            self.copies["y", m, k].wait_recv()
            src = self.piece(m, k, self.dps[2])
            copy, axis = self.sems.remote(src, src, self.x_dev), "x"
        self.copies["d", m, k] = copy
        self.queues[axis].start(copy)

    def spread(self, s):
        m, k = ORDER[s]
        self.copies["z", m, k].wait_recv()
        src = self.piece(m, k, self.dps[0])
        for axis, dev in (("x", self.x_dev), ("y", self.y_dev)):
            copy = self.sems.remote(src, src, dev)
            self.copies[axis, m, k] = copy
            self.queues[axis].start(copy)

    def poll(self):
        for code in GATHER[self.point]:
            (self.z_send, self.spread, self.forward)[code // 100 - 1](code % 100)
        self.point += 1

    def need(self, m, k):
        self.poll()
        if k == 0:
            self.own_ready(m)
            return
        self.copies["y" if self.by_x(m, k) else "x", m, k].wait_recv()
        self.copies["d", m, k].wait_recv()

    def close(self):
        for group in self.theirs:
            for copy in group:
                copy.wait_send()
        for queue in self.queues.values():
            queue.close()


def dot_nt(a, b):
    return lax.dot_general(a, b, (((1,), (1,)), ((), ())), preferred_element_type=F32)


def dot_tn(a, b):
    return lax.dot_general(a, b, (((0,), (0,)), ((), ())), preferred_element_type=F32)


def dot_nn(a, b):
    return lax.dot_general(a, b, (((1,), (0,)), ((), ())), preferred_element_type=F32)


BQ = 256


SMALL = 64


def small_block(i):
    return pl.ds(pl.multiple_of(i * SMALL, SMALL), SMALL)


def row_block(i):
    return pl.ds(pl.multiple_of(i * BQ, BQ), BQ)


def segments(shape, axis, start, n1, seq):
    pos = (lax.broadcasted_iota(jnp.int32, shape, axis) + start).astype(F32)
    return (pos >= n1).astype(F32) + (pos >= float(seq)).astype(F32)


def masked_keys(big, kx, zr, n1, seq):
    tp = big.shape[0]
    lane = lax.broadcasted_iota(jnp.int32, (1, 128), 1)
    seg = segments((tp, 1), 0, 0, n1, seq)
    for h in range(2):
        t = lane - 64 * (1 - h)
        away = jnp.where(seg == t.astype(F32), 0.0, -1e30)
        away = jnp.where(t < 0, 0.0, jnp.where(t < 3, away, 0.0)).astype(BF)
        kx[h] = jnp.where(lax.div(lane, 64) == h, big[:, zr * 384 + 128 : zr * 384 + 256], away)


def attend_fwd_rows(big, lse_ref, kx, zr, start, count, n1, seq):
    lane = lax.broadcasted_iota(jnp.int32, (1, 128), 1)
    base = zr * 384
    rows = slice(start, start + count)
    q = big[rows, base : base + 128] * BF(0.125)
    seg = segments((count, 1), 0, start, n1, seq)
    out = jnp.zeros((count, 128), F32)
    for h in range(2):
        mask = lax.div(lane, 64) == h
        own_seg = (seg == (lane - 64 * (1 - h)).astype(F32)).astype(BF)
        s = dot_nt(jnp.where(mask, q, own_seg), kx[h])
        top = jnp.max(s, axis=1, keepdims=True)
        e = jnp.exp(s - top)
        total = jnp.sum(e, axis=1, keepdims=True)
        mixed = dot_nn(e.astype(BF), big[:, base + 256 : base + 384]) / total
        out = jnp.where(mask, mixed, out)
        lse = jnp.broadcast_to(top + jnp.log(total), (count, 128))
        lse_ref[2 * zr + h : 2 * zr + h + 1, rows] = jnp.transpose(lse)[0:1]
    big[rows, 1536 + zr * 128 : 1664 + zr * 128] = out.astype(BF)


def halves_mean(a, b):
    return (jnp.sum(a, axis=1, keepdims=True) + jnp.sum(b, axis=1, keepdims=True)) * (1.0 / D)


def forward_kernel(
    seq, both, v0, v1, v2, v3, v4, v5, up_bias, qv_bias, ids, qf, ow, up, dn,
    wq_out, wo_out, wu_out, n1_out, x_out, g_out, vec_out, a1_out, big_out, lse_out, m_out, dh_out, gd_out, gu_out, rxu_out,
    usum, y_out,
    x_oth, g_oth, vec_all, bias_all, cnt, wq, wo, wu, wd, act, big, lse, m, pb, pr, pr2, dh, gd, gu, kx,
    ss, rs, ls,
):
    x_own, g_own = both.at[0], both.at[1]
    tp = x_own.shape[0]
    nb = tp // BQ
    here = place()
    dps, zs, x_dev, y_dev, c_dev, z_devs = here
    c, z = lax.axis_index("gx"), zs[0]
    sems, loc = Sems(ss, rs), Locals(ls)
    gather = Gather(sems, loc, here, c, (qf, ow, up, dn), (wq, wo, wu, wd))
    poll = gather.poll

    ids_low = (ids[...] == 0).astype(F32)
    for r in range(2):
        cnt[0, r] = jnp.broadcast_to(jnp.sum(ids_low[r : r + 1], axis=1, keepdims=True), (8, 128))
    vec_all[...] = jnp.zeros_like(vec_all)
    bias_all[...] = jnp.zeros_like(bias_all)
    for i, ref in enumerate((v0, v1, v2, v3, v4, v5)):
        vec_all[0, i : i + 1, :] = ref[...].astype(F32).reshape(1, 512)

    def cut(row, j):
        return jnp.where(c == 0, row[:, 256 * j : 256 * j + 128], row[:, 256 * j + 128 : 256 * j + 256])

    up_row = up_bias[...].astype(F32).reshape(1, 1024)
    qv_rows = qv_bias[...].astype(F32)
    for j in range(4):
        bias_all[0, 0:1, 128 * j : 128 * j + 128] = cut(up_row, j)
    for j in range(2):
        bias_all[0, 1:2, 128 * j : 128 * j + 128] = cut(qv_rows[j : j + 1], 0)
    usum[...] = jnp.zeros_like(usum)
    greet((x_dev, y_dev, c_dev) + z_devs[1:])
    gather.pair_start(0)
    small = [sems.remote(vec_all.at[0], vec_all.at[1], c_dev), sems.remote(cnt.at[0], cnt.at[1], c_dev)]
    small += [sems.remote(bias_all.at[0], bias_all.at[k], z_devs[k]) for k in (1, 2, 3)]
    x_copy = sems.remote(x_own, x_oth, c_dev)
    for copy in small + [x_copy]:
        copy.start()
    poll()
    for m_ in (1, 2, 3):
        gather.pair_start(m_)
    for copy in small:
        copy.wait_recv()
    x_copy.wait_recv()
    vec = [(vec_all[0, i : i + 1, :], vec_all[1, i : i + 1, :]) for i in range(6)]
    n1 = cnt[lax.rem(lax.div(z, 2) + c, 2), lax.rem(z, 2)]
    n1_out[...] = n1
    n1 = n1[0:1, 0:1]
    loc.later(x_oth, x_out)
    loc.later(vec_all, vec_out)

    @pl.loop(0, nb)
    def _(i):
        rows = row_block(i)
        xo, xt = x_own[rows, :].astype(F32), x_oth[rows, :].astype(F32)
        mean = halves_mean(xo, xt)
        inv = lax.rsqrt(halves_mean(xo * xo, xt * xt) - mean * mean + norm_eps)
        act[rows, 0:512] = ((xo - mean) * inv * vec[0][0] + vec[1][0]).astype(BF)
        act[rows, 512:1024] = ((xt - mean) * inv * vec[0][1] + vec[1][1]).astype(BF)

    a1_copy = loc.copy(act, a1_out)
    g_copy = sems.remote(g_own, g_oth, c_dev)
    g_copy.start()
    poll()
    for zr in range(4):
        gather.need(0, zr)
        qb, vb = bias_all[zr, 1:2, 0:128], bias_all[zr, 1:2, 128:256]
        bias = jnp.concatenate([qb, jnp.zeros_like(qb), vb], axis=1)

        @pl.loop(0, nb)
        def _(i):
            rows = row_block(i)
            big[rows, zr * 384 : zr * 384 + 384] = (dot_nn(act[rows, :], wq[zr].reshape(1024, 384)) + bias).astype(BF)

        masked_keys(big, kx, zr, n1, seq)
        poll()
        attend_fwd_rows(big, lse, kx, zr, 0, tp // 2, n1, seq)
        poll()
        attend_fwd_rows(big, lse, kx, zr, tp // 2, tp // 2, n1, seq)
        poll()
    loc.later(wq, wq_out)
    loc.later(lse, lse_out)
    big_copy = loc.copy(big, big_out)
    g_copy.wait_recv()
    loc.later(g_oth, g_out)
    for zr in range(4):
        gather.need(1, zr)
    loc.later(wo, wo_out)
    swap = sems.block(nb)

    @pl.loop(0, nb)
    def _(i):
        rows = row_block(i)
        part = dot_nn(big[rows, 1536:2048], wo[...].reshape(512, 1024))
        pb[rows, 0:512] = part[:, 512:].astype(BF)
        pb[rows, 512:1024] = part[:, :512].astype(BF)
        sems.at(swap + i, pb.at[rows], pr.at[rows], c_dev).start()
        m[rows, :] = part

    a1_copy.wait()
    poll()

    @pl.loop(0, nb)
    def _(i):
        rows = row_block(i)
        sems.at(swap + i, pb.at[rows], pr.at[rows], c_dev).wait()
        mo = x_own[rows, :].astype(F32) + m[rows, 0:512] + pr[rows, 0:512].astype(F32) + vec[2][0]
        mt = x_oth[rows, :].astype(F32) + m[rows, 512:1024] + pr[rows, 512:1024].astype(F32) + vec[2][1]
        mean = halves_mean(mo, mt)
        inv = lax.rsqrt(halves_mean(mo * mo, mt * mt) - mean * mean + norm_eps)
        m[rows, 0:512] = mo
        m[rows, 512:1024] = mt
        act[rows, 0:512] = ((mo - mean) * inv * vec[3][0] + vec[4][0]).astype(BF)
        act[rows, 512:1024] = ((mt - mean) * inv * vec[3][1] + vec[4][1]).astype(BF)

    m_copy = loc.copy(m, m_out)
    poll()
    outs, early = {}, []
    last = sems.block(nb)

    def send_down():
        @pl.loop(0, nb)
        def _(i):
            rows = row_block(i)
            pb[rows, 0:512] = m[rows, 512:1024].astype(BF)
            sems.at(last + i, pb.at[rows, pl.ds(0, 512)], pr2.at[rows], c_dev).start()

    for zr in range(4):
        gather.need(2, zr)
        gather.need(3, zr)
        if zr == 3:
            for key in (("u", 1), ("u", 2),):
                outs.pop(key).wait()
            for slot in (1, 0):
                for j, zz, dev, rels in ((0, 1, x_dev, (1, 3)), (1, 2, y_dev, (2, 3)),):
                    for grad_h, land in ((gu_out, rxu_out),):
                        early.append(sems.remote(grad_h.at[zz, dps[rels[slot]]], land.at[j, slot], dev))
                        early[-1].start()
        loc.later(wu.at[zr], wu_out.at[zr])
        bias = bias_all[zr, 0:1, :]
        lo = zr * 512
        if zr == 0:
            big_copy.wait()
            m_copy.wait()

        def hidden(first, last):
            @pl.loop(first, last)
            def _(i):
                rows = row_block(i)
                h = dot_nn(act[rows, :], wu[zr].reshape(1024, 512)) + bias
                w_own, w_oth = wd[zr, 0].reshape(512, 512), wd[zr, 1].reshape(512, 512)
                du = dot_nt(g_own[rows, :], w_own) + dot_nt(g_oth[rows, :], w_oth)
                cdf = 0.5 * (1.0 + lax.erf(h * math.sqrt(0.5)))
                slope = cdf + h * jnp.exp(-0.5 * h * h) * (1.0 / math.sqrt(2 * math.pi))
                u = (h * cdf).astype(BF)
                grad = (du * slope).astype(BF)
                big[rows, lo : lo + 512] = u
                dh[rows, lo : lo + 512] = grad
                usum[zr, 6:7, :] += jnp.sum(grad.astype(F32), axis=0, keepdims=True)
                m[rows, 0:512] += dot_nn(u, w_own)
                if zr == 0:
                    m[rows, 512:1024] = dot_nn(u, w_oth)
                else:
                    m[rows, 512:1024] += dot_nn(u, w_oth)

        for first, end in ((0, 2), (2, 4), (4, nb)):
            hidden(first, end)
            poll()
        if zr == 3:
            send_down()
        loc.later(dh.at[:, pl.ds(lo, 512)], dh_out.at[:, pl.ds(lo, 512)])
        slot = zr % 2
        for key in (("d", zr - 2), ("u", zr - 2)):
            if key in outs:
                outs.pop(key).wait()
        for j, gref in enumerate((g_own, g_oth)):
            gd[slot, :, :, 512 * j : 512 * j + 512] = dot_tn(big[:, lo : lo + 512], gref[...]).astype(BF).reshape(4, 128, 512)
        outs["d", zr] = loc.copy(gd.at[slot], gd_out.at[zr])
        poll()
        for j in range(2):
            block = dot_tn(act[:, 512 * j : 512 * j + 512], dh[:, lo : lo + 512])
            gu[slot, :, 128 * j : 128 * j + 128, :] = block.astype(BF).reshape(4, 128, 512)
        outs["u", zr] = loc.copy(gu.at[slot], gu_out.at[zr])
        poll()
    def result(rows, i):
        sems.at(last + i, pb.at[rows, pl.ds(0, 512)], pr2.at[rows], c_dev).wait()
        return (m[rows, 0:512] + pr2[rows, :].astype(F32) + vec[5][0]).astype(BF)

    @pl.loop(0, nb - 1)
    def _(i):
        rows = row_block(i)
        y_out[rows, :] = result(rows, i)

    end = tp - BQ
    y_out[end:seq, :] = result(pl.ds(end, BQ), nb - 1)[: seq - end]

    for copy in small + [x_copy, g_copy]:
        copy.wait_send()
    for copy in early:
        copy.wait()
    for copy in outs.values():
        copy.wait()
    gather.close()
    loc.close()


def forward_all(both, vectors, up_bias, qv_bias, ids, qf, ow, up, dn):
    tp = both.shape[1]
    seq = ids.shape[1]
    n_remote = N_PAIR + 7 + 48 + 2 * (tp // BQ) + 4
    sds = jax.ShapeDtypeStruct
    vm = pltpu.VMEM
    wide = (4, 2, 4, 128, 512)
    weights = [(4, 2, 4, 128, 384), (4, 4, 32, 1024), wide, wide]
    out_shape = [sds(s, BF) for s in weights[:3]] + [
        sds((8, 128), F32), sds((tp, 512), BF), sds((tp, 512), BF), sds((2, 8, 512), F32), sds((tp, 1024), BF),
        sds((tp, 2048), BF), sds((8, tp), F32), sds((tp, 1024), F32), sds((tp, 2048), BF), sds((4, 4, 128, 1024), BF),
        sds((4, 4, 256, 512), BF), sds((2, 2, 256, 512), BF), sds((4, 8, 512), F32), sds((seq, 512), BF),
    ]
    scratch = [vm((tp, 512), BF), vm((tp, 512), BF), vm((2, 8, 512), F32), vm((4, 8, 512), F32), vm((2, 2, 8, 128), F32)]
    scratch += [vm(s, BF) for s in weights]
    scratch += [
        vm((tp, 1024), BF), vm((tp, 2048), BF), vm((8, tp), F32), vm((tp, 1024), F32), vm((tp, 1024), BF), vm((tp, 1024), BF),
        vm((tp, 512), BF), vm((tp, 2048), BF), vm((2, 4, 128, 1024), BF), vm((2, 4, 256, 512), BF), vm((2, tp, 128), BF),
        pltpu.SemaphoreType.DMA((n_remote,)), pltpu.SemaphoreType.DMA((n_remote,)), pltpu.SemaphoreType.DMA((40,)),
    ]
    return pl.pallas_call(
        functools.partial(forward_kernel, seq),
        out_shape=out_shape,
        in_specs=[VMEM] * 10 + [ANY] * 4,
        out_specs=[ANY] * 3 + [VMEM] + [ANY] * 11 + [VMEM] * 2,
        scratch_shapes=scratch,
        compiler_params=pltpu.CompilerParams(collective_id=0, has_side_effects=True, vmem_limit_bytes=63 << 20),
        cost_estimate=pl.CostEstimate(flops=40 * 10**9, bytes_accessed=80 * 10**6, transcendentals=10**7),
        name="forward",
    )(both, *vectors, up_bias, qv_bias, ids, qf, ow, up, dn)


BLOCKS = ((128, 1024), (256, 512), (128, 256), (256, 384))
ZORDER = (1, 2, 3, 0)


def half_block(m):
    rows, cols = BLOCKS[m]
    return (rows // 2, cols) if m in (1, 3) else (rows, cols // 2)


class Landed:
    def __init__(self, copy):
        self.wait_recv = copy.wait


class Scatter:
    def __init__(self, sems, here, g, first_src, rx, ry, rz, sw, out, c):
        self.sems, self.g, self.first_src = sems, g, first_src
        self.dps, self.zs, self.x_dev, self.y_dev, self.c_dev, self.z_devs = here
        self.rx, self.ry, self.rz, self.sw, self.out, self.c = rx, ry, rz, sw, out, c
        self.first, self.second, self.third, self.last = {}, {}, {}, {}
        self.queues = {axis: Queue(99) for axis in "xyz"}
        self.point = 0

    def poll(self):
        for code in SCHEDULE[self.point]:
            stage, m, zr, slot = code // 1000, code // 100 % 10, code // 10 % 10, code % 10
            if stage == 1:
                self.stage1(m, zr, slot)
            elif stage == 2:
                self.stage2(m, zr)
            elif stage == 3:
                self.stage3(m, zr)
            else:
                self.stage4(m)
        self.point += 1

    def stage1(self, m, zr, slot):
        axis, dev, rels = ("x", self.x_dev, (1, 3)) if zr < 2 else ("y", self.y_dev, (2, 3))
        src = self.first_src[m].at[zr, self.dps[rels[slot]]]
        copy = self.sems.remote(src, self.rx[m].at[zr, slot], dev)
        self.first[m, zr, slot] = copy
        self.queues[axis].start(copy)

    def stage2(self, m, zr):
        axis, dev, rel = ("y", self.y_dev, 2) if zr < 2 else ("x", self.x_dev, 1)
        g, dd = self.g[m], self.dps[rel]
        self.first[m, zr, 1].wait_recv()
        g[zr, dd] = (g[zr, dd].astype(F32) + self.rx[m][zr, 1].astype(F32)).astype(BF)
        copy = self.sems.remote(g.at[zr, dd], self.ry[m].at[zr], dev)
        self.second[m, zr] = copy
        self.queues[axis].start(copy)

    def stage3(self, m, zr):
        g, dd = self.g[m], self.dps[0]
        self.first[m, zr, 0].wait_recv()
        self.second[m, zr].wait_recv()
        g[zr, dd] = (g[zr, dd].astype(F32) + self.rx[m][zr, 0].astype(F32) + self.ry[m][zr].astype(F32)).astype(BF)
        if zr > 0:
            copy = self.sems.remote(g.at[zr, dd], self.rz[m].at[zr - 1], self.z_devs[zr])
            self.third[m, zr] = copy
            self.queues["z"].start(copy)

    def stage4(self, m):
        for zr in (1, 2, 3):
            self.third[m, zr].wait_recv()
        rz = self.rz[m]
        total = self.g[m][0, self.dps[0]].astype(F32) + rz[0].astype(F32) + rz[1].astype(F32) + rz[2].astype(F32)
        rows, cols = BLOCKS[m]
        sw, out, c = self.sw[m], self.out[m], self.c
        if m in (1, 3):
            keep, sw[...] = total[: rows // 2], total[rows // 2 :]
            pairs = []
            for j in range(cols // 128):
                mine = pl.ds(pl.multiple_of(j * 256 + c * 128, 128), 128)
                out[:, mine] = keep[:, j * 128 : j * 128 + 128]
                pairs.append((sw.at[:, pl.ds(j * 128, 128)], out.at[:, mine]))
        else:
            out[c], sw[...] = total[:, : cols // 2], total[:, cols // 2 :]
            pairs = [(sw, out.at[c])]
        self.last[m] = [self.sems.remote(src, dst, self.c_dev) for src, dst in pairs]
        for copy in self.last[m]:
            copy.start()

    def close(self):
        for queue in self.queues.values():
            queue.close()
        for group in self.last.values():
            for copy in group:
                copy.wait()


def attend_bwd_rows(big, do_ref, lse_ref, k_t, dk_acc, dv_acc, zr, lo, hi, n1, seq):
    tp = big.shape[0]
    lane = lax.broadcasted_iota(jnp.int32, (1, 128), 1)
    base = zr * 384
    ocol = 1536 + zr * 128

    @pl.loop(lo, hi)
    def _(i):
        start = pl.multiple_of(i * BQ, BQ)
        rows = pl.ds(start, BQ)
        q = big[rows, base : base + 128]
        do = do_ref[rows, zr * 128 : zr * 128 + 128]
        prod = do.astype(F32) * big[rows, ocol : ocol + 128].astype(F32)
        seg_q = segments((1, BQ), 1, start, n1, seq)
        dq_t = jnp.zeros((128, BQ), F32)
        row = lax.broadcasted_iota(jnp.int32, (128, 1), 0)
        for h in range(2):
            mask = lax.div(lane, 64) == h
            lse = lse_ref[2 * zr + h : 2 * zr + h + 1, rows]
            delta = jnp.sum(jnp.where(mask, prod, 0.0), axis=1, keepdims=True)
            delta = jnp.transpose(jnp.broadcast_to(delta, (BQ, 128)))[0:1]
            qm = jnp.where(mask, q, BF(0)) * BF(0.125)
            dom = jnp.where(mask, do, BF(0))
            for keys in (slice(0, tp // 2), slice(tp // 2, tp)):
                same = segments((tp // 2, 1), 0, keys.start, n1, seq) == seg_q
                s = dot_nt(big[keys, base + 128 : base + 256], qm)
                p = jnp.where(same, jnp.exp(s - lse), 0.0)
                dp = dot_nt(big[keys, base + 256 : base + 384], dom)
                ds = (p * (dp - delta)).astype(BF)
                dv_acc[keys, :] += dot_nn(p.astype(BF), dom)
                dk_acc[keys, :] += dot_nn(ds, qm)
                dq_t += jnp.where(lax.div(row, 64) == h, dot_nn(k_t[:, keys], ds), 0.0)
        dq = jnp.transpose(dq_t)
        big[rows, base : base + 128] = (dq * 0.125).astype(BF)


def backward_kernel(
    seq, both, x_oth, g_oth_h, vec_all, n1_ref, usum, lse, a1_h, big_h, m_h, dh_h, gd_h, gu_h, rxu_h, wq_h, wo_h, wu_h,
    grad_out, small_out, out0, out1, out2, out3,
    big, ga, gb, wbuf, wo_v, part, pb, pr, mbuf, act, dm, k_t, dk_acc, dv_acc, vsum, vdp, vz, vzr, vhalf, vc,
    gd, gu, go, gq, rx0, rx1, rx2, rx3, ry0, ry1, ry2, ry3, rz0, rz1, rz2, rz3, sw0, sw1, sw2, sw3,
    ss, rs, ls, free,
):
    x_own, g_own_h = both.at[0], both.at[1]
    tp = big.shape[0]
    nb = tp // BQ
    here = place()
    dps, zs, x_dev, y_dev, c_dev, z_devs = here
    c, z = lax.axis_index("gx"), zs[0]
    xy_dev = (dps[3], c, z)
    sems, loc = Sems(ss, rs), Locals(ls)
    scatter = Scatter(
        sems, here, (gd, gu, go, gq), (gd_h, gu_h, go, gq), (rx0, rx1, rx2, rx3), (ry0, ry1, ry2, ry3), (rz0, rz1, rz2, rz3),
        (sw0, sw1, sw2, sw3), (out0, out1, out2, out3), c,
    )
    poll = scatter.poll
    greet((x_dev, y_dev, xy_dev, c_dev) + z_devs[1:])
    poll()
    dh_in = loc.copy(dh_h, big)
    wu_in = loc.copy(wu_h, wbuf)
    m_sem = loc.block(tp // SMALL)

    def load_m(i):
        return loc.at(m_sem + i, m_h.at[small_block(i)], mbuf.at[lax.rem(i, 2)])

    vec = [(vec_all[0, i : i + 1, :], vec_all[1, i : i + 1, :]) for i in range(6)]
    n1 = n1_ref[0:1, 0:1]
    vsum[...] = usum[...]
    vhalf[...] = jnp.zeros_like(vhalf)
    dh_in.wait()
    wu_in.wait()
    gd_in, gu_in = loc.copy(gd_h, gd), loc.copy(gu_h, gu)
    ga_in, gb_in = loc.copy(g_own_h, ga), loc.copy(g_oth_h, gb)
    wo_in = loc.copy(wo_h, wo_v)
    for j, zr in enumerate((1, 2)):
        for mm, land in ((1, rxu_h),):
            for slot in (1, 0):
                scatter.first[mm, zr, slot] = Landed(loc.copy(land.at[j, slot], scatter.rx[mm].at[zr, slot]))
    load_m(0).start()
    swap = sems.block(nb)

    @pl.loop(0, nb)
    def _(i):
        rows = row_block(i)
        total = dot_nt(big[rows, 0:512], wbuf[0].reshape(1024, 512))
        for zr in range(1, 4):
            total += dot_nt(big[rows, zr * 512 : zr * 512 + 512], wbuf[zr].reshape(1024, 512))
        pb[rows, 0:512] = total[:, 512:].astype(BF)
        pb[rows, 512:1024] = total[:, :512].astype(BF)
        sems.at(swap + i, pb.at[rows], pr.at[rows], c_dev).start()
        part[rows, :] = total

    big_in = loc.copy(big_h, big)
    wq_in = loc.copy(wq_h, wbuf.at[:, :, :, :, pl.ds(0, 384)])
    gd_in.wait()
    gu_in.wait()
    ga_in.wait()
    gb_in.wait()
    poll()
    @pl.loop(0, tp // SMALL)
    def _(i):
        rows = small_block(i)

        @pl.when(i + 1 < tp // SMALL)
        def _():
            load_m(i + 1).start()

        @pl.when(lax.rem(i, BQ // SMALL) == 0)
        def _():
            whole = lax.div(i, BQ // SMALL)
            sems.at(swap + whole, pb.at[row_block(whole)], pr.at[row_block(whole)], c_dev).wait()

        load_m(i).wait()
        slot = lax.rem(i, 2)
        mo, mt = mbuf[slot, :, 0:512], mbuf[slot, :, 512:1024]
        mean = halves_mean(mo, mt)
        inv = lax.rsqrt(halves_mean(mo * mo, mt * mt) - mean * mean + norm_eps)
        ho, ht = (mo - mean) * inv, (mt - mean) * inv
        do_, dt = part[rows, 0:512] + pr[rows, 0:512].astype(F32), part[rows, 512:1024] + pr[rows, 512:1024].astype(F32)
        bo, bt = do_ * vec[3][0], dt * vec[3][1]
        first, second = halves_mean(bo, bt), halves_mean(bo * ho, bt * ht)
        go_, gt = ga[rows, :].astype(F32), gb[rows, :].astype(F32)
        dmo = go_ + inv * (bo - first - ho * second)
        dmt = gt + inv * (bt - first - ht * second)
        dm[rows, :] = dmo
        act[rows, 0:512] = dmo.astype(BF)
        act[rows, 512:1024] = dmt.astype(BF)
        vsum[0, 2:3, :] += jnp.sum(dmo.astype(BF).astype(F32), axis=0, keepdims=True)
        vsum[0, 3:4, :] += jnp.sum(do_ * ho, axis=0, keepdims=True)
        vsum[0, 4:5, :] += jnp.sum(do_, axis=0, keepdims=True)
        vsum[0, 5:6, :] += jnp.sum(go_, axis=0, keepdims=True)

    pl.semaphore_signal(free, inc=1, device_id=c_dev, device_id_type=MESH)
    poll()
    wo_in.wait()
    big_in.wait()
    for j in range(2):
        block = dot_tn(big[:, 1536:2048], act[:, 512 * j : 512 * j + 512]).astype(BF)
        for dd in range(4):
            go[:, dd, :, 128 * j : 128 * j + 128] = block[:, 128 * dd : 128 * dd + 128].reshape(4, 128, 128)

    @pl.loop(0, nb)
    def _(i):
        rows = row_block(i)
        ga[rows, :] = dot_nt(act[rows, :], wo_v[...].reshape(512, 1024)).astype(BF)

    a1_in = loc.copy(a1_h, act)
    xb_in = loc.copy(x_oth, gb)
    poll()
    for step, zr in enumerate(ZORDER):
        base = zr * 384
        dk_acc[...] = jnp.zeros_like(dk_acc)
        dv_acc[...] = jnp.zeros_like(dv_acc)
        k_t[...] = jnp.transpose(big[:, base + 128 : base + 256].astype(F32)).astype(BF)
        for lo, hi in ((0, 2), (2, 4), (4, nb)):
            attend_bwd_rows(big, ga, lse, k_t, dk_acc, dv_acc, zr, lo, hi, n1, seq)
            if hi < nb:
                poll()
        big[:, base + 128 : base + 256] = dk_acc[...].astype(BF)
        big[:, base + 256 : base + 384] = dv_acc[...].astype(BF)
        if step == 0:
            a1_in.wait()
            wq_in.wait()
        for j in range(2):
            block = dot_tn(act[:, 512 * j : 512 * j + 512], big[:, base : base + 384])
            gq[zr, :, 128 * j : 128 * j + 128, :] = block.astype(BF).reshape(4, 128, 384)
        poll()
        for j in (0, 2):
            cols = big[:, base + 128 * j : base + 128 * j + 128].astype(F32)
            vsum[zr, 7:8, 64 * j : 64 * j + 128] = jnp.sum(cols, axis=0, keepdims=True)
        if step < 3:

            @pl.loop(0, nb)
            def _(i):
                rows = row_block(i)
                more = dot_nt(big[rows, base : base + 384], wbuf[zr, :, :, :, 0:384].reshape(1024, 384))
                part[rows, :] = more if step == 0 else part[rows, :] + more

    xa_in = loc.copy(x_own, ga)
    pl.semaphore_wait(free, 1)
    xa_in.wait()
    xb_in.wait()
    swap2 = sems.block(nb)
    base = ZORDER[3] * 384

    @pl.loop(0, nb)
    def _(i):
        rows = row_block(i)
        total = part[rows, :] + dot_nt(big[rows, base : base + 384], wbuf[ZORDER[3], :, :, :, 0:384].reshape(1024, 384))
        pb[rows, 0:512] = total[:, 512:].astype(BF)
        pb[rows, 512:1024] = total[:, :512].astype(BF)
        sems.at(swap2 + i, pb.at[rows], pr.at[rows], c_dev).start()
        part[rows, :] = total
        xo, xt = ga[rows, :].astype(F32), gb[rows, :].astype(F32)
        mean = halves_mean(xo, xt)
        inv = lax.rsqrt(halves_mean(xo * xo, xt * xt) - mean * mean + norm_eps)
        vsum[0, 0:1, :] += jnp.sum(total[:, :512] * ((xo - mean) * inv), axis=0, keepdims=True)
        vsum[0, 1:2, :] += jnp.sum(total[:, :512], axis=0, keepdims=True)
        vhalf[0, 0:1, :] += jnp.sum(total[:, 512:] * ((xt - mean) * inv), axis=0, keepdims=True)
        vhalf[0, 1:2, :] += jnp.sum(total[:, 512:], axis=0, keepdims=True)

    half_copy = sems.remote(vhalf.at[0], vhalf.at[1], c_dev)
    half_copy.start()
    poll()
    half_copy.wait()
    vsum[0] += vhalf[1]
    for k in (1, 2, 3):
        vsum[k, 0:6, :] = vsum[0, 0:6, :]
    dp_copies = [sems.remote(vsum, vdp.at[k], dev) for k, dev in enumerate((x_dev, y_dev, xy_dev))]
    for copy in dp_copies:
        copy.start()
    poll()

    @pl.loop(0, nb)
    def _(i):
        rows = row_block(i)
        sems.at(swap2 + i, pb.at[rows], pr.at[rows], c_dev).wait()
        xo, xt = ga[rows, :].astype(F32), gb[rows, :].astype(F32)
        mean = halves_mean(xo, xt)
        inv = lax.rsqrt(halves_mean(xo * xo, xt * xt) - mean * mean + norm_eps)
        ho, ht = (xo - mean) * inv, (xt - mean) * inv
        bo = (part[rows, 0:512] + pr[rows, 0:512].astype(F32)) * vec[0][0]
        bt = (part[rows, 512:1024] + pr[rows, 512:1024].astype(F32)) * vec[0][1]
        first, second = halves_mean(bo, bt), halves_mean(bo * ho, bt * ht)
        ga[rows, :] = (dm[rows, :] + inv * (bo - first - ho * second)).astype(BF)

    loc.later(ga, grad_out)
    for copy in dp_copies:
        copy.wait()
    vz[...] = (vsum[...] + vdp[0]) + (vdp[1] + vdp[2])
    z_copies = [sems.remote(vz.at[k], vzr.at[k], z_devs[k]) for k in (1, 2, 3)]
    for copy in z_copies:
        copy.start()
    poll()
    for copy in z_copies:
        copy.wait()
    vc[0] = (vz[0] + vzr[1]) + (vzr[2] + vzr[3])
    c_copy = sems.remote(vc.at[0], vc.at[1], c_dev)
    c_copy.start()
    poll()
    c_copy.wait()
    small_out[...] = vc[...]
    loc.close()
    scatter.close()


SCHEDULE = (
    (1030, 1010, 1020, 1000),
    (2120, 1031, 2110, 1011),
    (),
    (1230, 1210, 3120, 2030),
    (1220, 1200, 1021),
    (3110, 1231, 2010),
    (1001, 1311, 3030),
    (1310, 1131, 2230, 2020),
    (3010, 1221, 2000),
    (2130, 1321, 2310),
    (3230, 2220),
    (3020, 3000, 1320, 2320),
    (1331, 1211),
    (3220, 3310, 1330, 1201, 1101, 4000, 3320),
    (2330, 2200, 2210),
    (1301, 1130),
    (3210, 2100, 3200, 1300),
    (3330,),
    (3130, 4200, 2300, 1100),
    (3300, 4300, 3100, 4100),
)


def backward_all(seq, *args):
    tp = args[0].shape[1]
    nb = tp // BQ
    sds = jax.ShapeDtypeStruct
    vm = pltpu.VMEM
    halves = [half_block(m) for m in range(4)]
    n_remote = 4 * (8 + 4 + 3) - 4 + 9 + 2 * nb + 8
    scratch = [
        vm((tp, 2048), BF), vm((tp, 512), BF), vm((tp, 512), BF), vm((4, 2, 4, 128, 512), BF), vm((4, 4, 32, 1024), BF),
        vm((tp, 1024), F32), vm((tp, 1024), BF), vm((tp, 1024), BF), vm((2, SMALL, 1024), F32), vm((tp, 1024), BF),
        vm((tp, 512), F32), vm((128, tp), BF), vm((tp, 128), F32), vm((tp, 128), F32), vm((4, 8, 512), F32), vm((3, 4, 8, 512), F32),
        vm((4, 8, 512), F32), vm((4, 8, 512), F32), vm((2, 8, 512), F32), vm((2, 8, 512), F32),
    ]
    scratch += [vm((4, 4) + b, BF) for b in BLOCKS]
    scratch += [vm((4, 2) + b, BF) for b in BLOCKS]
    scratch += [vm((4,) + b, BF) for b in BLOCKS]
    scratch += [vm((3,) + b, BF) for b in BLOCKS]
    scratch += [vm(h, F32) for h in halves]
    scratch += [pltpu.SemaphoreType.DMA((n_remote,))] * 2 + [pltpu.SemaphoreType.DMA((tp // SMALL + 24,)), pltpu.SemaphoreType.REGULAR]
    return pl.pallas_call(
        functools.partial(backward_kernel, seq),
        out_shape=[sds((tp, 512), BF), sds((2, 8, 512), F32)]
        + [sds(d, F32) for d in ((2, 128, 512), (128, 1024), (2, 128, 128), (128, 768))],
        in_specs=[ANY] * 3 + [VMEM] * 4 + [ANY] * 10,
        out_specs=[ANY] + [VMEM] * 5,
        scratch_shapes=scratch,
        compiler_params=pltpu.CompilerParams(collective_id=1, has_side_effects=True, vmem_limit_bytes=63 << 20),
        cost_estimate=pl.CostEstimate(flops=40 * 10**9, bytes_accessed=100 * 10**6, transcendentals=10**7),
        name="backward",
    )(*args)


def local_chip(
    tokens, segment_ids, norm1_gain, norm1_shift, qkv_weight, qv_bias, out_weight, out_bias,
    norm2_gain, norm2_shift, up_weight, up_bias, down_weight, down_bias, cotangent,
):
    seq = segment_ids.shape[1]
    tp = -(-seq // BQ) * BQ
    c = lax.axis_index("gx")
    pad = ((0, tp - seq), (0, 0))
    both = jnp.pad(jnp.stack([tokens, cotangent]), ((0, 0),) + pad)
    vectors = (norm1_gain, norm1_shift, out_bias, norm2_gain, norm2_shift, down_bias)
    (wq, wo, wu, n1, x_oth, g_oth, vec_all, a1, big, lse, m, dh, gd, gu, rxu, usum, y) = forward_all(
        both, vectors, up_bias, qv_bias, segment_ids, qkv_weight.reshape(4, 128, 768), out_weight.reshape(2, 4, 32, 512),
        up_weight.reshape(4, 128, 1024), down_weight.reshape(4, 2, 128, 512),
    )
    grad, small, down_grad, up_grad, out_grad, qkv_grad = backward_all(
        seq, both, x_oth, g_oth, vec_all, n1, usum, lse, a1, big, m, dh, gd, gu, rxu, wq, wo, wu
    )

    def by_core(keep, got, axis):
        return jnp.where(c == 0, jnp.stack([keep, got], axis), jnp.stack([got, keep], axis))

    width = small[0]
    up_bias_grad = by_core(small[0, 6].reshape(4, 128), small[1, 6].reshape(4, 128), 1).reshape(1024)
    qv_bias_grad = by_core(small[0, 7, :256].reshape(2, 128), small[1, 7, :256].reshape(2, 128), 1).reshape(2, 256)
    return (
        y, grad[:seq], width[0], width[1], qkv_grad.reshape(1, 128, 3, 256), qv_bias_grad, out_grad.reshape(256, 1, 128), width[2],
        width[3], width[4], up_grad.reshape(1, 128, 1024), up_bias_grad, down_grad.reshape(1, 256, 512), width[5],
    )


def solution(mesh):
    sizes = dict(mesh.shape)
    chip_rows = sizes["dp"] == 4 and sizes["gx"] == 2 and sizes["gy"] == 4

    def whole(*args):
        rows, seq = args[1].shape
        fast = chip_rows and rows * seq == args[0].shape[0] and rows == 16
        body = local_chip if fast else local
        return jax.shard_map(
            body,
            mesh=mesh,
            in_specs=(
                P(("dp", "gy"), "gx"), P(("dp", "gx"), None), P("gx"), P("gx"), P("gx", None, "gy"), P(None, "gy"),
                P("gy", "gx"), P("gx"), P("gx"), P("gx"), P("gx", "gy"), P("gy"), P("gy", "gx"), P("gx"), P(("dp", "gy"), "gx"),
            ),
            out_specs=(
                P(("dp", "gy"), "gx"), P(("dp", "gy"), "gx"), P("gx"), P("gx"), P("gx", "dp", None, "gy"), P(None, "gy"),
                P("gy", "gx", "dp"), P("gx"), P("gx"), P("gx"), P("gx", "dp", "gy"), P("gy"), P("gy", "dp", "gx"), P("gx"),
            ),
            check_vma=False,
        )(*args)

    return whole
```

```python
import functools
import math

import jax
import jax.numpy as jnp
from jax import lax
from jax.experimental import pallas as pl
from jax.experimental.pallas import tpu as pltpu
from jax.sharding import PartitionSpec as P

D = 1024
HD = 64
MESH = pl.DeviceIdType.MESH
F32 = jnp.float32
BF = jnp.bfloat16
ANY = pl.BlockSpec(memory_space=pl.ANY)
SMEM = pl.BlockSpec(memory_space=pltpu.SMEM)
VMEM = pl.BlockSpec(memory_space=pltpu.VMEM)
norm_eps = 1e-06


def times_right(left, right):
    return jnp.dot(left, right, preferred_element_type=jnp.float32)


def times_back(left, right):
    return lax.dot_general(
        left, right, (((1,), (1,)), ((), ())), preferred_element_type=jnp.float32
    )


def times_outer(left, right):
    return lax.dot_general(
        left, right, (((0,), (0,)), ((), ())), preferred_element_type=jnp.float32
    )


def exact_gelu(values):
    return jax.nn.gelu(values, approximate=False)


def norm_forward(values, gain, shift):
    moments = lax.psum((jnp.sum(values, axis=1), jnp.sum(values * values, axis=1)), "gx")
    mean_val = moments[0] / D
    inverse = lax.rsqrt(moments[1] / D - mean_val * mean_val + norm_eps)
    hat_vals = (values - mean_val[:, None]) * inverse[:, None]
    return (hat_vals * gain + shift, hat_vals, inverse)


def norm_backward(grad_norm, hat_vals, inverse, gain):
    scaled = grad_norm * gain
    moments = lax.psum((jnp.sum(scaled, axis=1), jnp.sum(scaled * hat_vals, axis=1)), "gx")
    grad_in = inverse[:, None] * (
        scaled - (moments[0] / D)[:, None] - hat_vals * (moments[1] / D)[:, None]
    )
    return (grad_in, jnp.sum(grad_norm * hat_vals, axis=0), jnp.sum(grad_norm, axis=0))


def gather_gy(values):
    return lax.all_gather(values, "gy", axis=0, tiled=True)


def gather_gx(values):
    return lax.all_gather(values, "gx", axis=0, tiled=True)


def sum_over_gx(left, multiply):
    keep_rows = left.shape[0] // lax.axis_size("gx")

    def term(start, count):
        return multiply(left)

    return lax.psum_scatter(
        term(jnp.int32(0), keep_rows * lax.axis_size("gx")), "gx", scatter_dimension=0, tiled=True
    )


def sum_over_gy(left, multiply):
    keep_rows = left.shape[0] // lax.axis_size("gy")

    def term(start, count):
        return multiply(left)

    return lax.psum_scatter(
        term(jnp.int32(0), keep_rows * lax.axis_size("gy")), "gy", scatter_dimension=0, tiled=True
    )


def masked_scores(query_part, key_part, segment):
    scaling = 1.0 / math.sqrt(query_part.shape[-1])
    scores = (
        jnp.einsum("qhd,khd->hqk", query_part, key_part, preferred_element_type=jnp.float32)
        * scaling
    )
    same = segment[:, None] == segment[None, :]
    return jnp.where(same[None], scores, -1e30)


def attend_forward(item):
    packed, segment = item
    scores = masked_scores(packed[:, 0], packed[:, 1], segment)
    top_val = jnp.max(scores, axis=-1, keepdims=True)
    expo = jnp.exp(scores - top_val)
    total = jnp.sum(expo, axis=-1, keepdims=True)
    probs = (expo / total).astype(jnp.bfloat16)
    mixed = jnp.einsum("hqk,khd->qhd", probs, packed[:, 2], preferred_element_type=jnp.float32)
    return (mixed.astype(jnp.bfloat16), (top_val + jnp.log(total))[..., 0])


def attend_backward(item):
    packed, segment, log_sum, grad_out = item
    query_part = packed[:, 0]
    key_part = packed[:, 1]
    value_part = packed[:, 2]
    scaling = 1.0 / math.sqrt(query_part.shape[-1])
    scores = masked_scores(query_part, key_part, segment)
    probs = jnp.exp(scores - log_sum[..., None])
    probs_low = probs.astype(jnp.bfloat16)
    grad_prob = jnp.einsum("qhd,khd->hqk", grad_out, value_part, preferred_element_type=jnp.float32)
    grad_value = jnp.einsum("hqk,qhd->khd", probs_low, grad_out, preferred_element_type=jnp.float32)
    delta = jnp.sum(probs * grad_prob, axis=-1, keepdims=True)
    grad_score = (probs * (grad_prob - delta)).astype(jnp.bfloat16)
    grad_query = (
        jnp.einsum("hqk,khd->qhd", grad_score, key_part, preferred_element_type=jnp.float32)
        * scaling
    )
    grad_key = (
        jnp.einsum("hqk,qhd->khd", grad_score, query_part, preferred_element_type=jnp.float32)
        * scaling
    )
    return jnp.stack([grad_query, grad_key, grad_value], axis=1).astype(jnp.bfloat16)


def local(
    tokens,
    segment_ids,
    norm1_gain,
    norm1_shift,
    qkv_weight,
    qv_bias,
    out_weight,
    out_bias,
    norm2_gain,
    norm2_shift,
    up_weight,
    up_bias,
    down_weight,
    down_bias,
    cotangent,
):
    head_width = qkv_weight.shape[2]
    local_heads = head_width // HD
    seq_len = segment_ids.shape[1]
    qkv_flat = qkv_weight.reshape(qkv_weight.shape[0], 3 * head_width)
    gain_one = norm1_gain.astype(jnp.float32)
    gain_two = norm2_gain.astype(jnp.float32)
    resid = tokens.astype(jnp.float32)
    normed, hat_one, inv_one = norm_forward(resid, gain_one, norm1_shift.astype(jnp.float32))
    first_low = normed.astype(jnp.bfloat16)
    first_rows = gather_gy(first_low)
    qkv_all = sum_over_gx(first_rows, lambda piece: times_right(piece, qkv_flat))
    bias_full = jnp.stack([qv_bias[0], jnp.zeros_like(qv_bias[0]), qv_bias[1]]).astype(jnp.float32)
    qkv_low = (qkv_all.reshape(-1, 3, head_width) + bias_full[None]).astype(jnp.bfloat16)
    packed = qkv_low.reshape(-1, seq_len, 3, local_heads, HD)
    mixed, log_sums = lax.map(attend_forward, (packed, segment_ids))
    mixed_low = mixed.reshape(-1, head_width)
    mixed_rows = gather_gx(mixed_low)
    branch = sum_over_gy(
        mixed_rows, lambda piece: times_right(piece, out_weight)
    ) + out_bias.astype(jnp.float32)
    middle = resid + branch
    normed_two, hat_two, inv_two = norm_forward(middle, gain_two, norm2_shift.astype(jnp.float32))
    second_low = normed_two.astype(jnp.bfloat16)
    second_rows = gather_gy(second_low)
    hidden = sum_over_gx(second_rows, lambda piece: times_right(piece, up_weight)) + up_bias.astype(
        jnp.float32
    )
    active, gelu_pull = jax.vjp(exact_gelu, hidden)
    active_low = active.astype(jnp.bfloat16)
    active_rows = gather_gx(active_low)
    branch_two = sum_over_gy(
        active_rows, lambda piece: times_right(piece, down_weight)
    ) + down_bias.astype(jnp.float32)
    output = (middle + branch_two).astype(jnp.bfloat16)
    grad_top = cotangent.astype(jnp.float32)
    down_bias_grad = jnp.sum(grad_top, axis=0)
    grad_top_rows = gather_gy(cotangent)
    down_weight_grad = times_outer(active_rows, grad_top_rows)
    grad_active = sum_over_gx(grad_top_rows, lambda piece: times_back(piece, down_weight))
    grad_hidden = gelu_pull(grad_active)[0].astype(jnp.bfloat16)
    up_bias_grad = jnp.sum(grad_hidden.astype(jnp.float32), axis=0)
    hidden_rows = gather_gx(grad_hidden)
    up_weight_grad = times_outer(second_rows, hidden_rows)
    grad_norm_two = sum_over_gy(hidden_rows, lambda piece: times_back(piece, up_weight))
    grad_in_two, norm2_gain_grad, norm2_shift_grad = norm_backward(
        grad_norm_two, hat_two, inv_two, gain_two
    )
    grad_middle = grad_top + grad_in_two
    grad_branch = grad_middle.astype(jnp.bfloat16)
    out_bias_grad = jnp.sum(grad_branch.astype(jnp.float32), axis=0)
    branch_rows = gather_gy(grad_branch)
    out_weight_grad = times_outer(mixed_rows, branch_rows)
    grad_mixed = sum_over_gx(branch_rows, lambda piece: times_back(piece, out_weight)).astype(
        jnp.bfloat16
    )
    grad_mixed = grad_mixed.reshape(-1, seq_len, local_heads, HD)
    grad_packed = lax.map(attend_backward, (packed, segment_ids, log_sums, grad_mixed))
    grad_qkv = grad_packed.reshape(-1, 3 * head_width)
    third_sums = jnp.sum(grad_qkv.astype(jnp.float32), axis=0).reshape(3, head_width)
    qv_bias_grad = jnp.stack([third_sums[0], third_sums[2]])
    qkv_rows = gather_gx(grad_qkv)
    qkv_weight_grad = times_outer(first_rows, qkv_rows).reshape(qkv_weight.shape)
    grad_norm_one = sum_over_gy(qkv_rows, lambda piece: times_back(piece, qkv_flat))
    grad_in_one, norm1_gain_grad, norm1_shift_grad = norm_backward(
        grad_norm_one, hat_one, inv_one, gain_one
    )
    input_grad = (grad_middle + grad_in_one).astype(jnp.bfloat16)
    qkv_weight_grad, out_weight_grad, up_weight_grad, down_weight_grad = (
        lax.psum_scatter(qkv_weight_grad, "dp", scatter_dimension=0, tiled=True),
        lax.psum_scatter(out_weight_grad, "dp", scatter_dimension=1, tiled=True),
        lax.psum_scatter(up_weight_grad, "dp", scatter_dimension=0, tiled=True),
        lax.psum_scatter(down_weight_grad, "dp", scatter_dimension=0, tiled=True),
    )
    qkv_weight_grad = qkv_weight_grad[None]
    out_weight_grad = out_weight_grad[:, None, :]
    up_weight_grad = up_weight_grad[None]
    down_weight_grad = down_weight_grad[None]
    (
        norm1_gain_grad,
        norm1_shift_grad,
        norm2_gain_grad,
        norm2_shift_grad,
        out_bias_grad,
        down_bias_grad,
    ) = lax.psum(
        (
            norm1_gain_grad,
            norm1_shift_grad,
            norm2_gain_grad,
            norm2_shift_grad,
            out_bias_grad,
            down_bias_grad,
        ),
        ("dp", "gy"),
    )
    up_bias_grad, qv_bias_grad = lax.psum((up_bias_grad, qv_bias_grad), ("dp", "gx"))
    return (
        output,
        input_grad,
        norm1_gain_grad,
        norm1_shift_grad,
        qkv_weight_grad,
        qv_bias_grad,
        out_weight_grad,
        out_bias_grad,
        norm2_gain_grad,
        norm2_shift_grad,
        up_weight_grad,
        up_bias_grad,
        down_weight_grad,
        down_bias_grad,
    )


def flip1(i):
    return i + 1 - 2 * lax.rem(i, 2)


def flip2(i):
    return i + 2 - 4 * lax.div(i, 2)


def place():
    dp, c, z = lax.axis_index("dp"), lax.axis_index("gx"), lax.axis_index("gy")
    dps = (dp, flip1(dp), flip2(dp), 3 - dp)
    zs = (z, flip1(z), flip2(z), 3 - z)
    x_dev = (dps[1], c, z)
    y_dev = (dps[2], c, z)
    c_dev = (dp, 1 - c, z)
    z_devs = (None,) + tuple((dp, c, zz) for zz in zs[1:])
    return dps, zs, x_dev, y_dev, c_dev, z_devs


def greet(devices):
    barrier = pltpu.get_barrier_semaphore()
    for device in devices:
        pl.semaphore_signal(barrier, inc=1, device_id=device, device_id_type=MESH)
    pl.semaphore_wait(barrier, len(devices))


ORDER = ((0, 1), (0, 2), (0, 3), (1, 2), (1, 1), (1, 3), (2, 1), (2, 2), (3, 1), (3, 2), (2, 3), (3, 3))
GATHER = (
    (100, 101, 102),
    (),
    (),
    (103,),
    (104, 200),
    (105,),
    (201, 300, 202, 106, 301, 203, 107, 204, 108),
    (109,),
    (205, 302),
    (110, 303, 304),
    (),
    (206, 305),
    (),
    (111,),
    (),
    (207, 306),
    (),
    (),
    (),
    (),
    (),
    (),
    (208, 307),
    (),
    (),
    (),
    (),
    (209,),
    (),
    (),
    (308,),
    (),
    (210, 309, 211),
    (),
    (),
    (),
    (310,),
    (),
    (),
    (),
    (311,),
    (),
    (),
    (),
    (),
    (),
    (),
    (),
    (),
    (),
    (),
    (),
)
N_PAIR = 9


class Sems:
    def __init__(self, ss, rs):
        self.ss, self.rs, self.n = ss, rs, 0

    def at(self, i, src, dst, device):
        return pltpu.make_async_remote_copy(
            src, dst, self.ss.at[i], self.rs.at[i], device_id=device, device_id_type=MESH
        )

    def block(self, count):
        self.n += count
        return self.n - count

    def remote(self, src, dst, device):
        return self.at(self.block(1), src, dst, device)


class Locals:
    def __init__(self, ls):
        self.ls, self.n, self.open = ls, 0, []

    def at(self, i, src, dst):
        return pltpu.make_async_copy(src, dst, self.ls.at[i])

    def block(self, count):
        self.n += count
        return self.n - count

    def copy(self, src, dst):
        copy = self.at(self.block(1), src, dst)
        copy.start()
        return copy

    def later(self, src, dst):
        self.open.append(self.copy(src, dst))

    def close(self):
        for copy in self.open:
            copy.wait()


class Queue:
    def __init__(self, width):
        self.width, self.open = width, []

    def start(self, copy):
        if len(self.open) >= self.width:
            self.open.pop(0).wait_send()
        copy.start()
        self.open.append(copy)

    def close(self):
        for copy in self.open:
            copy.wait_send()


def weight_cuts(side, raw, full, crel):
    qf, ow, up, dn = raw
    wq, wo, wu, wd = full
    cols = pl.ds(crel * 512, 512)
    cuts = [[], [], [], []]
    for t in range(3):
        off = pl.multiple_of(t * 256 + side * 128, 128)
        cuts[0].append((qf.at[:, :, pl.ds(off, 128)], wq.at[0, crel, :, :, pl.ds(t * 128, 128)]))
    cuts[1].append((ow.at[side], wo.at[0, :, :, cols]))
    for t in range(4):
        off = pl.multiple_of(t * 256 + side * 128, 128)
        cuts[2].append((up.at[:, :, pl.ds(off, 128)], wu.at[0, crel, :, :, pl.ds(t * 128, 128)]))
    cuts[3].append((dn.at[:, side], wd.at[0, crel]))
    return cuts


class Gather:
    def __init__(self, sems, loc, here, c, raw, full):
        self.sems, self.loc, self.raw, self.full, self.c = sems, loc, raw, full, c
        self.dps, self.zs, self.x_dev, self.y_dev, self.c_dev, self.z_devs = here
        self.theirs = [[sems.remote(src, dst, self.c_dev) for src, dst in group] for group in weight_cuts(1 - c, raw, full, 1)]
        self.mine = weight_cuts(c, raw, full, 0)
        self.own, self.copies, self.ready = {}, {}, set()
        self.queues = {axis: Queue(99) for axis in "xyz"}
        self.point = 0

    def piece(self, m, k, dd):
        return self.full[m].at[k, dd] if m == 1 else self.full[m].at[k, :, dd]

    def pair_start(self, m):
        for copy in self.theirs[m]:
            copy.start()
        self.own[m] = [self.loc.copy(src, dst) for src, dst in self.mine[m]]

    def own_ready(self, m):
        if m not in self.ready:
            self.ready.add(m)
            for copy in self.own[m]:
                copy.wait()
            for copy in self.theirs[m]:
                copy.wait_recv()

    def z_send(self, s):
        m, k = ORDER[s]
        self.own_ready(m)
        copy = self.sems.remote(self.piece(m, 0, self.dps[0]), self.piece(m, k, self.dps[0]), self.z_devs[k])
        self.copies["z", m, k] = copy
        self.queues["z"].start(copy)

    def by_x(self, m, k):
        return (k == 2) == (m in (0, 2))

    def forward(self, s):
        m, k = ORDER[s]
        if self.by_x(m, k):
            self.copies["x", m, k].wait_recv()
            src = self.piece(m, k, self.dps[1])
            copy, axis = self.sems.remote(src, src, self.y_dev), "y"
        else:
            self.copies["y", m, k].wait_recv()
            src = self.piece(m, k, self.dps[2])
            copy, axis = self.sems.remote(src, src, self.x_dev), "x"
        self.copies["d", m, k] = copy
        self.queues[axis].start(copy)

    def spread(self, s):
        m, k = ORDER[s]
        self.copies["z", m, k].wait_recv()
        src = self.piece(m, k, self.dps[0])
        for axis, dev in (("x", self.x_dev), ("y", self.y_dev)):
            copy = self.sems.remote(src, src, dev)
            self.copies[axis, m, k] = copy
            self.queues[axis].start(copy)

    def poll(self):
        for code in GATHER[self.point]:
            (self.z_send, self.spread, self.forward)[code // 100 - 1](code % 100)
        self.point += 1

    def need(self, m, k):
        self.poll()
        if k == 0:
            self.own_ready(m)
            return
        self.copies["y" if self.by_x(m, k) else "x", m, k].wait_recv()
        self.copies["d", m, k].wait_recv()

    def close(self):
        for group in self.theirs:
            for copy in group:
                copy.wait_send()
        for queue in self.queues.values():
            queue.close()


def dot_nt(a, b):
    return lax.dot_general(a, b, (((1,), (1,)), ((), ())), preferred_element_type=F32)


def dot_tn(a, b):
    return lax.dot_general(a, b, (((0,), (0,)), ((), ())), preferred_element_type=F32)


def dot_nn(a, b):
    return lax.dot_general(a, b, (((1,), (0,)), ((), ())), preferred_element_type=F32)


BQ = 256


SMALL = 64


def small_block(i):
    return pl.ds(pl.multiple_of(i * SMALL, SMALL), SMALL)


def row_block(i):
    return pl.ds(pl.multiple_of(i * BQ, BQ), BQ)


def segments(shape, axis, start, n1, seq):
    pos = (lax.broadcasted_iota(jnp.int32, shape, axis) + start).astype(F32)
    return (pos >= n1).astype(F32) + (pos >= float(seq)).astype(F32)


def masked_keys(big, kx, zr, n1, seq):
    tp = big.shape[0]
    lane = lax.broadcasted_iota(jnp.int32, (1, 128), 1)
    seg = segments((tp, 1), 0, 0, n1, seq)
    for h in range(2):
        t = lane - 64 * (1 - h)
        away = jnp.where(seg == t.astype(F32), 0.0, -1e30)
        away = jnp.where(t < 0, 0.0, jnp.where(t < 3, away, 0.0)).astype(BF)
        kx[h] = jnp.where(lax.div(lane, 64) == h, big[:, zr * 384 + 128 : zr * 384 + 256], away)


def attend_fwd_rows(big, lse_ref, kx, zr, start, count, n1, seq):
    lane = lax.broadcasted_iota(jnp.int32, (1, 128), 1)
    base = zr * 384
    rows = slice(start, start + count)
    q = big[rows, base : base + 128] * BF(0.125)
    seg = segments((count, 1), 0, start, n1, seq)
    out = jnp.zeros((count, 128), F32)
    for h in range(2):
        mask = lax.div(lane, 64) == h
        own_seg = (seg == (lane - 64 * (1 - h)).astype(F32)).astype(BF)
        s = dot_nt(jnp.where(mask, q, own_seg), kx[h])
        top = jnp.max(s, axis=1, keepdims=True)
        e = jnp.exp(s - top)
        total = jnp.sum(e, axis=1, keepdims=True)
        mixed = dot_nn(e.astype(BF), big[:, base + 256 : base + 384]) / total
        out = jnp.where(mask, mixed, out)
        lse = jnp.broadcast_to(top + jnp.log(total), (count, 128))
        lse_ref[2 * zr + h : 2 * zr + h + 1, rows] = jnp.transpose(lse)[0:1]
    big[rows, 1536 + zr * 128 : 1664 + zr * 128] = out.astype(BF)


def halves_mean(a, b):
    return (jnp.sum(a, axis=1, keepdims=True) + jnp.sum(b, axis=1, keepdims=True)) * (1.0 / D)


def forward_kernel(
    seq, both, v0, v1, v2, v3, v4, v5, up_bias, qv_bias, ids, qf, ow, up, dn,
    wq_out, wo_out, wu_out, n1_out, x_out, g_out, vec_out, a1_out, big_out, lse_out, m_out, dh_out, gd_out, gu_out, rxu_out,
    usum, y_out,
    x_oth, g_oth, vec_all, bias_all, cnt, wq, wo, wu, wd, act, big, lse, m, pb, pr, pr2, dh, gd, gu, kx,
    ss, rs, ls,
):
    x_own, g_own = both.at[0], both.at[1]
    tp = x_own.shape[0]
    nb = tp // BQ
    here = place()
    dps, zs, x_dev, y_dev, c_dev, z_devs = here
    c, z = lax.axis_index("gx"), zs[0]
    sems, loc = Sems(ss, rs), Locals(ls)
    gather = Gather(sems, loc, here, c, (qf, ow, up, dn), (wq, wo, wu, wd))
    poll = gather.poll

    ids_low = (ids[...] == 0).astype(F32)
    for r in range(2):
        cnt[0, r] = jnp.broadcast_to(jnp.sum(ids_low[r : r + 1], axis=1, keepdims=True), (8, 128))
    vec_all[...] = jnp.zeros_like(vec_all)
    bias_all[...] = jnp.zeros_like(bias_all)
    for i, ref in enumerate((v0, v1, v2, v3, v4, v5)):
        vec_all[0, i : i + 1, :] = ref[...].astype(F32).reshape(1, 512)

    def cut(row, j):
        return jnp.where(c == 0, row[:, 256 * j : 256 * j + 128], row[:, 256 * j + 128 : 256 * j + 256])

    up_row = up_bias[...].astype(F32).reshape(1, 1024)
    qv_rows = qv_bias[...].astype(F32)
    for j in range(4):
        bias_all[0, 0:1, 128 * j : 128 * j + 128] = cut(up_row, j)
    for j in range(2):
        bias_all[0, 1:2, 128 * j : 128 * j + 128] = cut(qv_rows[j : j + 1], 0)
    usum[...] = jnp.zeros_like(usum)
    greet((x_dev, y_dev, c_dev) + z_devs[1:])
    gather.pair_start(0)
    small = [sems.remote(vec_all.at[0], vec_all.at[1], c_dev), sems.remote(cnt.at[0], cnt.at[1], c_dev)]
    small += [sems.remote(bias_all.at[0], bias_all.at[k], z_devs[k]) for k in (1, 2, 3)]
    x_copy = sems.remote(x_own, x_oth, c_dev)
    for copy in small + [x_copy]:
        copy.start()
    poll()
    for m_ in (1, 2, 3):
        gather.pair_start(m_)
    for copy in small:
        copy.wait_recv()
    x_copy.wait_recv()
    vec = [(vec_all[0, i : i + 1, :], vec_all[1, i : i + 1, :]) for i in range(6)]
    n1 = cnt[lax.rem(lax.div(z, 2) + c, 2), lax.rem(z, 2)]
    n1_out[...] = n1
    n1 = n1[0:1, 0:1]
    loc.later(x_oth, x_out)
    loc.later(vec_all, vec_out)

    @pl.loop(0, nb)
    def _(i):
        rows = row_block(i)
        xo, xt = x_own[rows, :].astype(F32), x_oth[rows, :].astype(F32)
        mean = halves_mean(xo, xt)
        inv = lax.rsqrt(halves_mean(xo * xo, xt * xt) - mean * mean + norm_eps)
        act[rows, 0:512] = ((xo - mean) * inv * vec[0][0] + vec[1][0]).astype(BF)
        act[rows, 512:1024] = ((xt - mean) * inv * vec[0][1] + vec[1][1]).astype(BF)

    a1_copy = loc.copy(act, a1_out)
    g_copy = sems.remote(g_own, g_oth, c_dev)
    g_copy.start()
    poll()
    for zr in range(4):
        gather.need(0, zr)
        qb, vb = bias_all[zr, 1:2, 0:128], bias_all[zr, 1:2, 128:256]
        bias = jnp.concatenate([qb, jnp.zeros_like(qb), vb], axis=1)

        @pl.loop(0, nb)
        def _(i):
            rows = row_block(i)
            big[rows, zr * 384 : zr * 384 + 384] = (dot_nn(act[rows, :], wq[zr].reshape(1024, 384)) + bias).astype(BF)

        masked_keys(big, kx, zr, n1, seq)
        poll()
        attend_fwd_rows(big, lse, kx, zr, 0, tp // 2, n1, seq)
        poll()
        attend_fwd_rows(big, lse, kx, zr, tp // 2, tp // 2, n1, seq)
        poll()
    loc.later(wq, wq_out)
    loc.later(lse, lse_out)
    big_copy = loc.copy(big, big_out)
    g_copy.wait_recv()
    loc.later(g_oth, g_out)
    for zr in range(4):
        gather.need(1, zr)
    loc.later(wo, wo_out)
    swap = sems.block(nb)

    @pl.loop(0, nb)
    def _(i):
        rows = row_block(i)
        part = dot_nn(big[rows, 1536:2048], wo[...].reshape(512, 1024))
        pb[rows, 0:512] = part[:, 512:].astype(BF)
        pb[rows, 512:1024] = part[:, :512].astype(BF)
        sems.at(swap + i, pb.at[rows], pr.at[rows], c_dev).start()
        m[rows, :] = part

    a1_copy.wait()
    poll()

    @pl.loop(0, nb)
    def _(i):
        rows = row_block(i)
        sems.at(swap + i, pb.at[rows], pr.at[rows], c_dev).wait()
        mo = x_own[rows, :].astype(F32) + m[rows, 0:512] + pr[rows, 0:512].astype(F32) + vec[2][0]
        mt = x_oth[rows, :].astype(F32) + m[rows, 512:1024] + pr[rows, 512:1024].astype(F32) + vec[2][1]
        mean = halves_mean(mo, mt)
        inv = lax.rsqrt(halves_mean(mo * mo, mt * mt) - mean * mean + norm_eps)
        m[rows, 0:512] = mo
        m[rows, 512:1024] = mt
        act[rows, 0:512] = ((mo - mean) * inv * vec[3][0] + vec[4][0]).astype(BF)
        act[rows, 512:1024] = ((mt - mean) * inv * vec[3][1] + vec[4][1]).astype(BF)

    m_copy = loc.copy(m, m_out)
    poll()
    outs, early = {}, []
    last = sems.block(nb)

    def send_down():
        @pl.loop(0, nb)
        def _(i):
            rows = row_block(i)
            pb[rows, 0:512] = m[rows, 512:1024].astype(BF)
            sems.at(last + i, pb.at[rows, pl.ds(0, 512)], pr2.at[rows], c_dev).start()

    for zr in range(4):
        gather.need(2, zr)
        gather.need(3, zr)
        if zr == 3:
            for key in (("u", 1), ("u", 2),):
                outs.pop(key).wait()
            for slot in (1, 0):
                for j, zz, dev, rels in ((0, 1, x_dev, (1, 3)), (1, 2, y_dev, (2, 3)),):
                    for grad_h, land in ((gu_out, rxu_out),):
                        early.append(sems.remote(grad_h.at[zz, dps[rels[slot]]], land.at[j, slot], dev))
                        early[-1].start()
        loc.later(wu.at[zr], wu_out.at[zr])
        bias = bias_all[zr, 0:1, :]
        lo = zr * 512
        if zr == 0:
            big_copy.wait()
            m_copy.wait()

        def hidden(first, last):
            @pl.loop(first, last)
            def _(i):
                rows = row_block(i)
                h = dot_nn(act[rows, :], wu[zr].reshape(1024, 512)) + bias
                w_own, w_oth = wd[zr, 0].reshape(512, 512), wd[zr, 1].reshape(512, 512)
                du = dot_nt(g_own[rows, :], w_own) + dot_nt(g_oth[rows, :], w_oth)
                cdf = 0.5 * (1.0 + lax.erf(h * math.sqrt(0.5)))
                slope = cdf + h * jnp.exp(-0.5 * h * h) * (1.0 / math.sqrt(2 * math.pi))
                u = (h * cdf).astype(BF)
                grad = (du * slope).astype(BF)
                big[rows, lo : lo + 512] = u
                dh[rows, lo : lo + 512] = grad
                usum[zr, 6:7, :] += jnp.sum(grad.astype(F32), axis=0, keepdims=True)
                m[rows, 0:512] += dot_nn(u, w_own)
                if zr == 0:
                    m[rows, 512:1024] = dot_nn(u, w_oth)
                else:
                    m[rows, 512:1024] += dot_nn(u, w_oth)

        for first, end in ((0, 2), (2, 4), (4, nb)):
            hidden(first, end)
            poll()
        if zr == 3:
            send_down()
        loc.later(dh.at[:, pl.ds(lo, 512)], dh_out.at[:, pl.ds(lo, 512)])
        slot = zr % 2
        for key in (("d", zr - 2), ("u", zr - 2)):
            if key in outs:
                outs.pop(key).wait()
        for j, gref in enumerate((g_own, g_oth)):
            gd[slot, :, :, 512 * j : 512 * j + 512] = dot_tn(big[:, lo : lo + 512], gref[...]).astype(BF).reshape(4, 128, 512)
        outs["d", zr] = loc.copy(gd.at[slot], gd_out.at[zr])
        poll()
        for j in range(2):
            block = dot_tn(act[:, 512 * j : 512 * j + 512], dh[:, lo : lo + 512])
            gu[slot, :, 128 * j : 128 * j + 128, :] = block.astype(BF).reshape(4, 128, 512)
        outs["u", zr] = loc.copy(gu.at[slot], gu_out.at[zr])
        poll()
    def result(rows, i):
        sems.at(last + i, pb.at[rows, pl.ds(0, 512)], pr2.at[rows], c_dev).wait()
        return (m[rows, 0:512] + pr2[rows, :].astype(F32) + vec[5][0]).astype(BF)

    @pl.loop(0, nb - 1)
    def _(i):
        rows = row_block(i)
        y_out[rows, :] = result(rows, i)

    end = tp - BQ
    y_out[end:seq, :] = result(pl.ds(end, BQ), nb - 1)[: seq - end]

    for copy in small + [x_copy, g_copy]:
        copy.wait_send()
    for copy in early:
        copy.wait()
    for copy in outs.values():
        copy.wait()
    gather.close()
    loc.close()


def forward_all(both, vectors, up_bias, qv_bias, ids, qf, ow, up, dn):
    tp = both.shape[1]
    seq = ids.shape[1]
    n_remote = N_PAIR + 7 + 48 + 2 * (tp // BQ) + 4
    sds = jax.ShapeDtypeStruct
    vm = pltpu.VMEM
    wide = (4, 2, 4, 128, 512)
    weights = [(4, 2, 4, 128, 384), (4, 4, 32, 1024), wide, wide]
    out_shape = [sds(s, BF) for s in weights[:3]] + [
        sds((8, 128), F32), sds((tp, 512), BF), sds((tp, 512), BF), sds((2, 8, 512), F32), sds((tp, 1024), BF),
        sds((tp, 2048), BF), sds((8, tp), F32), sds((tp, 1024), F32), sds((tp, 2048), BF), sds((4, 4, 128, 1024), BF),
        sds((4, 4, 256, 512), BF), sds((2, 2, 256, 512), BF), sds((4, 8, 512), F32), sds((seq, 512), BF),
    ]
    scratch = [vm((tp, 512), BF), vm((tp, 512), BF), vm((2, 8, 512), F32), vm((4, 8, 512), F32), vm((2, 2, 8, 128), F32)]
    scratch += [vm(s, BF) for s in weights]
    scratch += [
        vm((tp, 1024), BF), vm((tp, 2048), BF), vm((8, tp), F32), vm((tp, 1024), F32), vm((tp, 1024), BF), vm((tp, 1024), BF),
        vm((tp, 512), BF), vm((tp, 2048), BF), vm((2, 4, 128, 1024), BF), vm((2, 4, 256, 512), BF), vm((2, tp, 128), BF),
        pltpu.SemaphoreType.DMA((n_remote,)), pltpu.SemaphoreType.DMA((n_remote,)), pltpu.SemaphoreType.DMA((40,)),
    ]
    return pl.pallas_call(
        functools.partial(forward_kernel, seq),
        out_shape=out_shape,
        in_specs=[VMEM] * 10 + [ANY] * 4,
        out_specs=[ANY] * 3 + [VMEM] + [ANY] * 11 + [VMEM] * 2,
        scratch_shapes=scratch,
        compiler_params=pltpu.CompilerParams(collective_id=0, has_side_effects=True, vmem_limit_bytes=63 << 20),
        cost_estimate=pl.CostEstimate(flops=40 * 10**9, bytes_accessed=80 * 10**6, transcendentals=10**7),
        name="forward",
    )(both, *vectors, up_bias, qv_bias, ids, qf, ow, up, dn)


BLOCKS = ((128, 1024), (256, 512), (128, 256), (256, 384))
ZORDER = (1, 2, 3, 0)


def half_block(m):
    rows, cols = BLOCKS[m]
    return (rows // 2, cols) if m in (1, 3) else (rows, cols // 2)


class Landed:
    def __init__(self, copy):
        self.wait_recv = copy.wait


class Scatter:
    def __init__(self, sems, here, g, first_src, rx, ry, rz, sw, out, c):
        self.sems, self.g, self.first_src = sems, g, first_src
        self.dps, self.zs, self.x_dev, self.y_dev, self.c_dev, self.z_devs = here
        self.rx, self.ry, self.rz, self.sw, self.out, self.c = rx, ry, rz, sw, out, c
        self.first, self.second, self.third, self.last = {}, {}, {}, {}
        self.queues = {axis: Queue(99) for axis in "xyz"}
        self.point = 0

    def poll(self):
        for code in SCHEDULE[self.point]:
            stage, m, zr, slot = code // 1000, code // 100 % 10, code // 10 % 10, code % 10
            if stage == 1:
                self.stage1(m, zr, slot)
            elif stage == 2:
                self.stage2(m, zr)
            elif stage == 3:
                self.stage3(m, zr)
            else:
                self.stage4(m)
        self.point += 1

    def stage1(self, m, zr, slot):
        axis, dev, rels = ("x", self.x_dev, (1, 3)) if zr < 2 else ("y", self.y_dev, (2, 3))
        src = self.first_src[m].at[zr, self.dps[rels[slot]]]
        copy = self.sems.remote(src, self.rx[m].at[zr, slot], dev)
        self.first[m, zr, slot] = copy
        self.queues[axis].start(copy)

    def stage2(self, m, zr):
        axis, dev, rel = ("y", self.y_dev, 2) if zr < 2 else ("x", self.x_dev, 1)
        g, dd = self.g[m], self.dps[rel]
        self.first[m, zr, 1].wait_recv()
        g[zr, dd] = (g[zr, dd].astype(F32) + self.rx[m][zr, 1].astype(F32)).astype(BF)
        copy = self.sems.remote(g.at[zr, dd], self.ry[m].at[zr], dev)
        self.second[m, zr] = copy
        self.queues[axis].start(copy)

    def stage3(self, m, zr):
        g, dd = self.g[m], self.dps[0]
        self.first[m, zr, 0].wait_recv()
        self.second[m, zr].wait_recv()
        g[zr, dd] = (g[zr, dd].astype(F32) + self.rx[m][zr, 0].astype(F32) + self.ry[m][zr].astype(F32)).astype(BF)
        if zr > 0:
            copy = self.sems.remote(g.at[zr, dd], self.rz[m].at[zr - 1], self.z_devs[zr])
            self.third[m, zr] = copy
            self.queues["z"].start(copy)

    def stage4(self, m):
        for zr in (1, 2, 3):
            self.third[m, zr].wait_recv()
        rz = self.rz[m]
        total = self.g[m][0, self.dps[0]].astype(F32) + rz[0].astype(F32) + rz[1].astype(F32) + rz[2].astype(F32)
        rows, cols = BLOCKS[m]
        sw, out, c = self.sw[m], self.out[m], self.c
        if m in (1, 3):
            keep, sw[...] = total[: rows // 2], total[rows // 2 :]
            pairs = []
            for j in range(cols // 128):
                mine = pl.ds(pl.multiple_of(j * 256 + c * 128, 128), 128)
                out[:, mine] = keep[:, j * 128 : j * 128 + 128]
                pairs.append((sw.at[:, pl.ds(j * 128, 128)], out.at[:, mine]))
        else:
            out[c], sw[...] = total[:, : cols // 2], total[:, cols // 2 :]
            pairs = [(sw, out.at[c])]
        self.last[m] = [self.sems.remote(src, dst, self.c_dev) for src, dst in pairs]
        for copy in self.last[m]:
            copy.start()

    def close(self):
        for queue in self.queues.values():
            queue.close()
        for group in self.last.values():
            for copy in group:
                copy.wait()


def attend_bwd_rows(big, do_ref, lse_ref, k_t, dk_acc, dv_acc, zr, lo, hi, n1, seq):
    tp = big.shape[0]
    lane = lax.broadcasted_iota(jnp.int32, (1, 128), 1)
    base = zr * 384
    ocol = 1536 + zr * 128

    @pl.loop(lo, hi)
    def _(i):
        start = pl.multiple_of(i * BQ, BQ)
        rows = pl.ds(start, BQ)
        q = big[rows, base : base + 128]
        do = do_ref[rows, zr * 128 : zr * 128 + 128]
        prod = do.astype(F32) * big[rows, ocol : ocol + 128].astype(F32)
        seg_q = segments((1, BQ), 1, start, n1, seq)
        dq_t = jnp.zeros((128, BQ), F32)
        row = lax.broadcasted_iota(jnp.int32, (128, 1), 0)
        for h in range(2):
            mask = lax.div(lane, 64) == h
            lse = lse_ref[2 * zr + h : 2 * zr + h + 1, rows]
            delta = jnp.sum(jnp.where(mask, prod, 0.0), axis=1, keepdims=True)
            delta = jnp.transpose(jnp.broadcast_to(delta, (BQ, 128)))[0:1]
            qm = jnp.where(mask, q, BF(0)) * BF(0.125)
            dom = jnp.where(mask, do, BF(0))
            for keys in (slice(0, tp // 2), slice(tp // 2, tp)):
                same = segments((tp // 2, 1), 0, keys.start, n1, seq) == seg_q
                s = dot_nt(big[keys, base + 128 : base + 256], qm)
                p = jnp.where(same, jnp.exp(s - lse), 0.0)
                dp = dot_nt(big[keys, base + 256 : base + 384], dom)
                ds = (p * (dp - delta)).astype(BF)
                dv_acc[keys, :] += dot_nn(p.astype(BF), dom)
                dk_acc[keys, :] += dot_nn(ds, qm)
                dq_t += jnp.where(lax.div(row, 64) == h, dot_nn(k_t[:, keys], ds), 0.0)
        dq = jnp.transpose(dq_t)
        big[rows, base : base + 128] = (dq * 0.125).astype(BF)


def backward_kernel(
    seq, both, x_oth, g_oth_h, vec_all, n1_ref, usum, lse, a1_h, big_h, m_h, dh_h, gd_h, gu_h, rxu_h, wq_h, wo_h, wu_h,
    grad_out, small_out, out0, out1, out2, out3,
    big, ga, gb, wbuf, wo_v, part, pb, pr, mbuf, act, dm, k_t, dk_acc, dv_acc, vsum, vdp, vz, vzr, vhalf, vc,
    gd, gu, go, gq, rx0, rx1, rx2, rx3, ry0, ry1, ry2, ry3, rz0, rz1, rz2, rz3, sw0, sw1, sw2, sw3,
    ss, rs, ls, free,
):
    x_own, g_own_h = both.at[0], both.at[1]
    tp = big.shape[0]
    nb = tp // BQ
    here = place()
    dps, zs, x_dev, y_dev, c_dev, z_devs = here
    c, z = lax.axis_index("gx"), zs[0]
    xy_dev = (dps[3], c, z)
    sems, loc = Sems(ss, rs), Locals(ls)
    scatter = Scatter(
        sems, here, (gd, gu, go, gq), (gd_h, gu_h, go, gq), (rx0, rx1, rx2, rx3), (ry0, ry1, ry2, ry3), (rz0, rz1, rz2, rz3),
        (sw0, sw1, sw2, sw3), (out0, out1, out2, out3), c,
    )
    poll = scatter.poll
    greet((x_dev, y_dev, xy_dev, c_dev) + z_devs[1:])
    poll()
    dh_in = loc.copy(dh_h, big)
    wu_in = loc.copy(wu_h, wbuf)
    m_sem = loc.block(tp // SMALL)

    def load_m(i):
        return loc.at(m_sem + i, m_h.at[small_block(i)], mbuf.at[lax.rem(i, 2)])

    vec = [(vec_all[0, i : i + 1, :], vec_all[1, i : i + 1, :]) for i in range(6)]
    n1 = n1_ref[0:1, 0:1]
    vsum[...] = usum[...]
    vhalf[...] = jnp.zeros_like(vhalf)
    dh_in.wait()
    wu_in.wait()
    gd_in, gu_in = loc.copy(gd_h, gd), loc.copy(gu_h, gu)
    ga_in, gb_in = loc.copy(g_own_h, ga), loc.copy(g_oth_h, gb)
    wo_in = loc.copy(wo_h, wo_v)
    for j, zr in enumerate((1, 2)):
        for mm, land in ((1, rxu_h),):
            for slot in (1, 0):
                scatter.first[mm, zr, slot] = Landed(loc.copy(land.at[j, slot], scatter.rx[mm].at[zr, slot]))
    load_m(0).start()
    swap = sems.block(nb)

    @pl.loop(0, nb)
    def _(i):
        rows = row_block(i)
        total = dot_nt(big[rows, 0:512], wbuf[0].reshape(1024, 512))
        for zr in range(1, 4):
            total += dot_nt(big[rows, zr * 512 : zr * 512 + 512], wbuf[zr].reshape(1024, 512))
        pb[rows, 0:512] = total[:, 512:].astype(BF)
        pb[rows, 512:1024] = total[:, :512].astype(BF)
        sems.at(swap + i, pb.at[rows], pr.at[rows], c_dev).start()
        part[rows, :] = total

    big_in = loc.copy(big_h, big)
    wq_in = loc.copy(wq_h, wbuf.at[:, :, :, :, pl.ds(0, 384)])
    gd_in.wait()
    gu_in.wait()
    ga_in.wait()
    gb_in.wait()
    poll()
    @pl.loop(0, tp // SMALL)
    def _(i):
        rows = small_block(i)

        @pl.when(i + 1 < tp // SMALL)
        def _():
            load_m(i + 1).start()

        @pl.when(lax.rem(i, BQ // SMALL) == 0)
        def _():
            whole = lax.div(i, BQ // SMALL)
            sems.at(swap + whole, pb.at[row_block(whole)], pr.at[row_block(whole)], c_dev).wait()

        load_m(i).wait()
        slot = lax.rem(i, 2)
        mo, mt = mbuf[slot, :, 0:512], mbuf[slot, :, 512:1024]
        mean = halves_mean(mo, mt)
        inv = lax.rsqrt(halves_mean(mo * mo, mt * mt) - mean * mean + norm_eps)
        ho, ht = (mo - mean) * inv, (mt - mean) * inv
        do_, dt = part[rows, 0:512] + pr[rows, 0:512].astype(F32), part[rows, 512:1024] + pr[rows, 512:1024].astype(F32)
        bo, bt = do_ * vec[3][0], dt * vec[3][1]
        first, second = halves_mean(bo, bt), halves_mean(bo * ho, bt * ht)
        go_, gt = ga[rows, :].astype(F32), gb[rows, :].astype(F32)
        dmo = go_ + inv * (bo - first - ho * second)
        dmt = gt + inv * (bt - first - ht * second)
        dm[rows, :] = dmo
        act[rows, 0:512] = dmo.astype(BF)
        act[rows, 512:1024] = dmt.astype(BF)
        vsum[0, 2:3, :] += jnp.sum(dmo.astype(BF).astype(F32), axis=0, keepdims=True)
        vsum[0, 3:4, :] += jnp.sum(do_ * ho, axis=0, keepdims=True)
        vsum[0, 4:5, :] += jnp.sum(do_, axis=0, keepdims=True)
        vsum[0, 5:6, :] += jnp.sum(go_, axis=0, keepdims=True)

    pl.semaphore_signal(free, inc=1, device_id=c_dev, device_id_type=MESH)
    poll()
    wo_in.wait()
    big_in.wait()
    for j in range(2):
        block = dot_tn(big[:, 1536:2048], act[:, 512 * j : 512 * j + 512]).astype(BF)
        for dd in range(4):
            go[:, dd, :, 128 * j : 128 * j + 128] = block[:, 128 * dd : 128 * dd + 128].reshape(4, 128, 128)

    @pl.loop(0, nb)
    def _(i):
        rows = row_block(i)
        ga[rows, :] = dot_nt(act[rows, :], wo_v[...].reshape(512, 1024)).astype(BF)

    a1_in = loc.copy(a1_h, act)
    xb_in = loc.copy(x_oth, gb)
    poll()
    for step, zr in enumerate(ZORDER):
        base = zr * 384
        dk_acc[...] = jnp.zeros_like(dk_acc)
        dv_acc[...] = jnp.zeros_like(dv_acc)
        k_t[...] = jnp.transpose(big[:, base + 128 : base + 256].astype(F32)).astype(BF)
        for lo, hi in ((0, 2), (2, 4), (4, nb)):
            attend_bwd_rows(big, ga, lse, k_t, dk_acc, dv_acc, zr, lo, hi, n1, seq)
            if hi < nb:
                poll()
        big[:, base + 128 : base + 256] = dk_acc[...].astype(BF)
        big[:, base + 256 : base + 384] = dv_acc[...].astype(BF)
        if step == 0:
            a1_in.wait()
            wq_in.wait()
        for j in range(2):
            block = dot_tn(act[:, 512 * j : 512 * j + 512], big[:, base : base + 384])
            gq[zr, :, 128 * j : 128 * j + 128, :] = block.astype(BF).reshape(4, 128, 384)
        poll()
        for j in (0, 2):
            cols = big[:, base + 128 * j : base + 128 * j + 128].astype(F32)
            vsum[zr, 7:8, 64 * j : 64 * j + 128] = jnp.sum(cols, axis=0, keepdims=True)
        if step < 3:

            @pl.loop(0, nb)
            def _(i):
                rows = row_block(i)
                more = dot_nt(big[rows, base : base + 384], wbuf[zr, :, :, :, 0:384].reshape(1024, 384))
                part[rows, :] = more if step == 0 else part[rows, :] + more

    xa_in = loc.copy(x_own, ga)
    pl.semaphore_wait(free, 1)
    xa_in.wait()
    xb_in.wait()
    swap2 = sems.block(nb)
    base = ZORDER[3] * 384

    @pl.loop(0, nb)
    def _(i):
        rows = row_block(i)
        total = part[rows, :] + dot_nt(big[rows, base : base + 384], wbuf[ZORDER[3], :, :, :, 0:384].reshape(1024, 384))
        pb[rows, 0:512] = total[:, 512:].astype(BF)
        pb[rows, 512:1024] = total[:, :512].astype(BF)
        sems.at(swap2 + i, pb.at[rows], pr.at[rows], c_dev).start()
        part[rows, :] = total
        xo, xt = ga[rows, :].astype(F32), gb[rows, :].astype(F32)
        mean = halves_mean(xo, xt)
        inv = lax.rsqrt(halves_mean(xo * xo, xt * xt) - mean * mean + norm_eps)
        vsum[0, 0:1, :] += jnp.sum(total[:, :512] * ((xo - mean) * inv), axis=0, keepdims=True)
        vsum[0, 1:2, :] += jnp.sum(total[:, :512], axis=0, keepdims=True)
        vhalf[0, 0:1, :] += jnp.sum(total[:, 512:] * ((xt - mean) * inv), axis=0, keepdims=True)
        vhalf[0, 1:2, :] += jnp.sum(total[:, 512:], axis=0, keepdims=True)

    half_copy = sems.remote(vhalf.at[0], vhalf.at[1], c_dev)
    half_copy.start()
    poll()
    half_copy.wait()
    vsum[0] += vhalf[1]
    for k in (1, 2, 3):
        vsum[k, 0:6, :] = vsum[0, 0:6, :]
    dp_copies = [sems.remote(vsum, vdp.at[k], dev) for k, dev in enumerate((x_dev, y_dev, xy_dev))]
    for copy in dp_copies:
        copy.start()
    poll()

    @pl.loop(0, nb)
    def _(i):
        rows = row_block(i)
        sems.at(swap2 + i, pb.at[rows], pr.at[rows], c_dev).wait()
        xo, xt = ga[rows, :].astype(F32), gb[rows, :].astype(F32)
        mean = halves_mean(xo, xt)
        inv = lax.rsqrt(halves_mean(xo * xo, xt * xt) - mean * mean + norm_eps)
        ho, ht = (xo - mean) * inv, (xt - mean) * inv
        bo = (part[rows, 0:512] + pr[rows, 0:512].astype(F32)) * vec[0][0]
        bt = (part[rows, 512:1024] + pr[rows, 512:1024].astype(F32)) * vec[0][1]
        first, second = halves_mean(bo, bt), halves_mean(bo * ho, bt * ht)
        ga[rows, :] = (dm[rows, :] + inv * (bo - first - ho * second)).astype(BF)

    loc.later(ga, grad_out)
    for copy in dp_copies:
        copy.wait()
    vz[...] = (vsum[...] + vdp[0]) + (vdp[1] + vdp[2])
    z_copies = [sems.remote(vz.at[k], vzr.at[k], z_devs[k]) for k in (1, 2, 3)]
    for copy in z_copies:
        copy.start()
    poll()
    for copy in z_copies:
        copy.wait()
    vc[0] = (vz[0] + vzr[1]) + (vzr[2] + vzr[3])
    c_copy = sems.remote(vc.at[0], vc.at[1], c_dev)
    c_copy.start()
    poll()
    c_copy.wait()
    small_out[...] = vc[...]
    loc.close()
    scatter.close()


SCHEDULE = (
    (1021, 1011, 1031, 1010),
    (1020, 1001, 2010, 2020, 2110, 2120),
    (2030,),
    (2000,),
    (3010, 3020),
    (1030, 1000),
    (3110, 3120),
    (1131, 1101),
    (1311, 1130, 3030, 3000),
    (2130, 1321, 2100),
    (1310, 2310),
    (3130, 1211, 2320),
    (1331, 1100),
    (4000, 1320, 3310, 2210, 1210),
    (2330,),
    (1330, 1221, 1301, 3320, 3100, 4100),
    (1231, 3210, 1300),
    (3330, 1220, 1201),
    (2230, 2220, 1230, 2300),
    (1200, 2200, 3230, 3220, 3300, 4300, 3200, 4200),
)


def backward_all(seq, *args):
    tp = args[0].shape[1]
    nb = tp // BQ
    sds = jax.ShapeDtypeStruct
    vm = pltpu.VMEM
    halves = [half_block(m) for m in range(4)]
    n_remote = 4 * (8 + 4 + 3) - 4 + 9 + 2 * nb + 8
    scratch = [
        vm((tp, 2048), BF), vm((tp, 512), BF), vm((tp, 512), BF), vm((4, 2, 4, 128, 512), BF), vm((4, 4, 32, 1024), BF),
        vm((tp, 1024), F32), vm((tp, 1024), BF), vm((tp, 1024), BF), vm((2, SMALL, 1024), F32), vm((tp, 1024), BF),
        vm((tp, 512), F32), vm((128, tp), BF), vm((tp, 128), F32), vm((tp, 128), F32), vm((4, 8, 512), F32), vm((3, 4, 8, 512), F32),
        vm((4, 8, 512), F32), vm((4, 8, 512), F32), vm((2, 8, 512), F32), vm((2, 8, 512), F32),
    ]
    scratch += [vm((4, 4) + b, BF) for b in BLOCKS]
    scratch += [vm((4, 2) + b, BF) for b in BLOCKS]
    scratch += [vm((4,) + b, BF) for b in BLOCKS]
    scratch += [vm((3,) + b, BF) for b in BLOCKS]
    scratch += [vm(h, F32) for h in halves]
    scratch += [pltpu.SemaphoreType.DMA((n_remote,))] * 2 + [pltpu.SemaphoreType.DMA((tp // SMALL + 24,)), pltpu.SemaphoreType.REGULAR]
    return pl.pallas_call(
        functools.partial(backward_kernel, seq),
        out_shape=[sds((tp, 512), BF), sds((2, 8, 512), F32)]
        + [sds(d, F32) for d in ((2, 128, 512), (128, 1024), (2, 128, 128), (128, 768))],
        in_specs=[ANY] * 3 + [VMEM] * 4 + [ANY] * 10,
        out_specs=[ANY] + [VMEM] * 5,
        scratch_shapes=scratch,
        compiler_params=pltpu.CompilerParams(collective_id=1, has_side_effects=True, vmem_limit_bytes=63 << 20),
        cost_estimate=pl.CostEstimate(flops=40 * 10**9, bytes_accessed=100 * 10**6, transcendentals=10**7),
        name="backward",
    )(*args)


def local_chip(
    tokens, segment_ids, norm1_gain, norm1_shift, qkv_weight, qv_bias, out_weight, out_bias,
    norm2_gain, norm2_shift, up_weight, up_bias, down_weight, down_bias, cotangent,
):
    seq = segment_ids.shape[1]
    tp = -(-seq // BQ) * BQ
    c = lax.axis_index("gx")
    pad = ((0, tp - seq), (0, 0))
    both = jnp.pad(jnp.stack([tokens, cotangent]), ((0, 0),) + pad)
    vectors = (norm1_gain, norm1_shift, out_bias, norm2_gain, norm2_shift, down_bias)
    (wq, wo, wu, n1, x_oth, g_oth, vec_all, a1, big, lse, m, dh, gd, gu, rxu, usum, y) = forward_all(
        both, vectors, up_bias, qv_bias, segment_ids, qkv_weight.reshape(4, 128, 768), out_weight.reshape(2, 4, 32, 512),
        up_weight.reshape(4, 128, 1024), down_weight.reshape(4, 2, 128, 512),
    )
    grad, small, down_grad, up_grad, out_grad, qkv_grad = backward_all(
        seq, both, x_oth, g_oth, vec_all, n1, usum, lse, a1, big, m, dh, gd, gu, rxu, wq, wo, wu
    )

    def by_core(keep, got, axis):
        return jnp.where(c == 0, jnp.stack([keep, got], axis), jnp.stack([got, keep], axis))

    width = small[0]
    up_bias_grad = by_core(small[0, 6].reshape(4, 128), small[1, 6].reshape(4, 128), 1).reshape(1024)
    qv_bias_grad = by_core(small[0, 7, :256].reshape(2, 128), small[1, 7, :256].reshape(2, 128), 1).reshape(2, 256)
    return (
        y, grad[:seq], width[0], width[1], qkv_grad.reshape(1, 128, 3, 256), qv_bias_grad, out_grad.reshape(256, 1, 128), width[2],
        width[3], width[4], up_grad.reshape(1, 128, 1024), up_bias_grad, down_grad.reshape(1, 256, 512), width[5],
    )


def solution(mesh):
    sizes = dict(mesh.shape)
    chip_rows = sizes["dp"] == 4 and sizes["gx"] == 2 and sizes["gy"] == 4

    def whole(*args):
        rows, seq = args[1].shape
        fast = chip_rows and rows * seq == args[0].shape[0] and rows == 16
        body = local_chip if fast else local
        return jax.shard_map(
            body,
            mesh=mesh,
            in_specs=(
                P(("dp", "gy"), "gx"), P(("dp", "gx"), None), P("gx"), P("gx"), P("gx", None, "gy"), P(None, "gy"),
                P("gy", "gx"), P("gx"), P("gx"), P("gx"), P("gx", "gy"), P("gy"), P("gy", "gx"), P("gx"), P(("dp", "gy"), "gx"),
            ),
            out_specs=(
                P(("dp", "gy"), "gx"), P(("dp", "gy"), "gx"), P("gx"), P("gx"), P("gx", "dp", None, "gy"), P(None, "gy"),
                P("gy", "gx", "dp"), P("gx"), P("gx"), P("gx"), P("gx", "dp", "gy"), P("gy"), P("gy", "dp", "gx"), P("gx"),
            ),
            check_vma=False,
        )(*args)

    return whole
```
